32 devices in a mesh: dp: 8 (over y, x, core), mp: 4 (over z).
Axes of the slice: x: 2, y: 2, z: 4, core: 2. Of those that a mesh axis runs over, the one named last changes fastest.
Arguments:
- inputs: bfloat16 [6144, 512], P('dp'), may hold values from -6 to 6
- lengths: int32 [8], P('dp'), may hold values from 192 to 768, as said below
- filters: bfloat16 [768, 24], replicated, may hold values from -0.21875 to 0.21875
- first_gain: float32 [512], replicated, may hold values from 0.5 to 1.5
- stu_weight: bfloat16 [48, 512, 512], replicated, may hold values from -0.0390625 to 0.0390625
- ar_weight: bfloat16 [3, 512, 512], replicated, may hold values from -0.15625 to 0.15625
- second_gain: float32 [512], replicated, may hold values from 0.5 to 1.5
- gate_weight: bfloat16 [512, 2048], P(None, 'mp'), may hold values from -0.25 to 0.25
- up_weight: bfloat16 [512, 2048], P(None, 'mp'), may hold values from -0.25 to 0.25
- down_weight: bfloat16 [2048, 512], P('mp'), may hold values from -0.125 to 0.125
- cotangent: bfloat16 [6144, 512], P('dp'), may hold values from -6 to 6
Outputs:
- output: bfloat16 [6144, 512], P('dp')
- input_grad: float32 [6144, 512], P('dp')
- stu_grad: float32 [48, 512, 512], P('mp', 'dp')
- ar_grad: float32 [3, 512, 512], replicated
- first_gain_grad: float32 [512], replicated
- second_gain_grad: float32 [512], replicated
- gate_grad: float32 [512, 2048], P(None, 'mp')
- up_grad: float32 [512, 2048], P(None, 'mp')
- down_grad: float32 [2048, 512], P('mp')
The draws below stay inside these ranges and needn't reach their ends.
Inputs may be any that keep to these rules, and one draw needn't show every extreme that they name: `lengths`: one sequence in every draw has all 768 positions valid.
All inputs are finite; a program needn't handle non-finite values.
Results may differ from the reference program's by a relative error of at most 0.017.
Values may be sent and summed in bfloat16 or wider, within the bound.
No kernel may reach another device: no remote copies, remote signals or barrier semaphores. Data moves between devices by JAX's collectives and lax.ppermute only.
A program may use at most 384 MiB of HBM per device.

```python
import jax
import jax.numpy as jnp
from jax import lax

D = 512
FILT = 24
AR = 3
HID = 2048
SEQ_LEN = 768
SEQS = 8
TOKENS = 6144


def draw_lengths(key, part):
    key = jax.random.fold_in(key, 11)
    first_key, second_key = jax.random.split(key)
    values = jax.random.randint(first_key, (SEQS,), SEQ_LEN // 4, SEQ_LEN + 1).astype(jnp.int32)
    chosen = jax.random.randint(second_key, (), 0, SEQS)
    return values.at[chosen].set(SEQ_LEN).astype(jnp.int32)


def levels(rng, dims, cuts, low, top_value):
    loudness, own = 1.0, jax.random.fold_in(rng, 6)
    for axis_at, blocks in cuts:
        steps = jnp.exp(jax.random.uniform(jax.random.fold_in(own, axis_at), (blocks,), jnp.float32, low / len(cuts), top_value / len(cuts)))
        loudness = loudness * jnp.repeat(steps, dims[axis_at] // blocks).reshape([-1 if axis == axis_at else 1 for axis in range(len(dims))])
    return loudness


def normal_values(key, extent, scale, reach, shards=(), kind=jnp.bfloat16):
    array = scale * jax.random.normal(key, extent, jnp.float32)
    if shards:
        array = array * levels(key, extent, shards, -0.22, 0.18)
    return jnp.clip(array, -reach, reach).astype(kind)


def setup_inputs(seed: int = 0) -> dict:
    key_list = jax.random.split(jax.random.key(seed), 12)
    return {
        "inputs": normal_values(key_list[0], (TOKENS, D), 1.0, 6.0, ((0, 8),)),
        "lengths": draw_lengths(jax.random.fold_in(key_list[11], 71), 0),
        "filters": normal_values(key_list[2], (SEQ_LEN, FILT), SEQ_LEN ** -0.5, 0.21875),
        "first_gain": jnp.clip(1.0 + 0.1 * jax.random.normal(key_list[3], (D,), jnp.float32), 0.5, 1.5),
        "stu_weight": normal_values(key_list[4], (2 * FILT, D, D), (2 * FILT * D) ** -0.5, 0.0390625),
        "ar_weight": normal_values(key_list[5], (AR, D, D), (AR * D) ** -0.5, 0.15625),
        "second_gain": jnp.clip(1.0 + 0.1 * jax.random.normal(key_list[6], (D,), jnp.float32), 0.5, 1.5),
        "gate_weight": normal_values(key_list[7], (D, HID), D ** -0.5, 0.25, ((1, 4),)),
        "up_weight": normal_values(key_list[8], (D, HID), D ** -0.5, 0.25, ((1, 4),)),
        "down_weight": normal_values(key_list[9], (HID, D), HID ** -0.5, 0.125, ((0, 4),)),
        "cotangent": normal_values(key_list[10], (TOKENS, D), 1.0, 6.0, ((0, 8),)),
    }


EPS = 1e-05

@jax.custom_vjp
def low(v):
    return lax.optimization_barrier(v.astype(jnp.bfloat16)).astype(jnp.float32)

@jax.custom_vjp
def low_back(v):
    return v

def low_keep(v):
    return (low(v), None)

def low_pass(kept, grad):
    return (grad,)

def back_keep(v):
    return (v, None)

def back_low(kept, grad):
    return (low(grad),)
low.defvjp(low_keep, low_pass)
low_back.defvjp(back_keep, back_low)

def matmul(left, right):
    return jnp.dot(left, right, precision=lax.Precision.HIGHEST, preferred_element_type=jnp.float32)

def norm_rows(values, gain, mask):
    return mask * values * lax.rsqrt(lax.optimization_barrier(jnp.mean(values * values, axis=-1, keepdims=True)) + EPS) * gain

def spectral_conv(normed, filter_pair):
    length = normed.shape[0]
    fourier_in = jnp.fft.rfft(normed, n=2 * length, axis=0)
    fourier_filter = jnp.fft.rfft(filter_pair, n=2 * length, axis=0)
    product = fourier_in[:, None, :] * fourier_filter[:, :, None]
    result = jnp.fft.irfft(product, n=2 * length, axis=0)[:length]
    return result.reshape(length, -1)

def lagged(normed, order):
    length = normed.shape[0]
    return jnp.concatenate([jnp.pad(normed, ((lag, 0), (0, 0)))[:length] for lag in range(order)], axis=1)

def forward(source, first_gain, stu_weight, ar_weight, second_gain, gate_weight, up_weight, down_weight, filter_pair, mask):
    width = source.shape[1]
    normed = low(norm_rows(source, first_gain, mask))
    conv = low_back(low(spectral_conv(normed, filter_pair)))
    mixed = matmul(conv, stu_weight.reshape(-1, width)) + matmul(lagged(normed, ar_weight.shape[0]), ar_weight.reshape(-1, width))
    mixed = low_back(mixed)
    hidden_in = source + mixed
    normed_two = low(norm_rows(hidden_in, second_gain, mask))
    gate = low_back(matmul(normed_two, gate_weight))
    upper = low_back(matmul(normed_two, up_weight))
    act = low(jax.nn.gelu(gate) * upper)
    return hidden_in + matmul(act, down_weight)

def reference(inputs, lengths, filters, first_gain, stu_weight, ar_weight, second_gain, gate_weight, up_weight, down_weight, cotangent):
    filt = filters.astype(jnp.float32)
    signs = jnp.where(jnp.arange(filt.shape[0], dtype=jnp.int32) % 2 == 0, 1.0, -1.0).astype(jnp.float32)[:, None]
    filter_pair = jnp.concatenate([filt, filt * signs], axis=1)
    params = tuple((w.astype(jnp.float32) for w in (first_gain, stu_weight, ar_weight, second_gain, gate_weight, up_weight, down_weight)))
    count = lengths.shape[0]
    length = inputs.shape[0] // count
    width = inputs.shape[1]
    sources = inputs.astype(jnp.float32).reshape(count, length, width)
    cotangents = cotangent.astype(jnp.float32).reshape(count, length, width)

    def step(carry, item):
        source, cot_seq, valid = item
        mask = (jnp.arange(length, dtype=jnp.int32) < valid).astype(jnp.float32)[:, None]

        def run(values, *weights):
            return forward(values, *weights, filter_pair, mask)
        result, pull = jax.vjp(run, source, *params)
        grads = pull(cot_seq)
        carry = tuple((total + grad for total, grad in zip(carry, grads[1:])))
        return (carry, (result.astype(jnp.bfloat16), grads[0]))
    init = tuple((jnp.zeros_like(p) for p in params))
    sums, (results, input_grads) = lax.scan(step, init, (sources, cotangents, lengths))
    return (results.reshape(count * length, width), input_grads.reshape(count * length, width), sums[1], sums[2], sums[0], sums[3], sums[4], sums[5], sums[6])
```

```python
import functools

import jax
import jax.numpy as jnp
from jax import lax
from jax.experimental import pallas as pl
from jax.experimental.pallas import tpu as pltpu
from jax.sharding import PartitionSpec as P

EPS = 1e-05
BF = jnp.bfloat16
F32 = jnp.float32
SQRT_2_PI = 0.7978845608028654
CUBIC = 0.044715
VMEM_LIMIT = 56 << 20


def dot(left, right):
    return jnp.dot(left, right, preferred_element_type=F32)


def dot_cols(left, right):
    return lax.dot_general(left, right, (((1,), (1,)), ((), ())), preferred_element_type=F32)


def params():
    return pltpu.CompilerParams(vmem_limit_bytes=VMEM_LIMIT)


def cost(flops, nbytes):
    return pl.CostEstimate(flops=int(flops), bytes_accessed=int(nbytes), transcendentals=0)


def smem():
    return pl.BlockSpec(memory_space=pltpu.SMEM)


def whole(shape):
    zeros = (0,) * len(shape)
    return pl.BlockSpec(tuple(shape), lambda *_: zeros)


def toeplitz(base_row, rows):
    wide = jnp.broadcast_to(base_row, (rows, base_row.shape[1]))
    return pltpu.roll(wide, 0, 1, stride=1, stride_axis=0)


def parity_sign(shape):
    row = lax.broadcasted_iota(jnp.int32, shape, 0)
    return jnp.where(row % 2 == 0, 1.0, -1.0).astype(F32)


def norm_kernel(n, share, groups, meta, x_ref, gain_ref, u_ref, *rest):
    ut_refs, (scr, scr_t) = rest[:groups], rest[groups:]
    length, width = x_ref.shape
    block = width // groups
    m, d, valid = meta[0], meta[1], meta[2]
    x = x_ref[...].astype(F32)
    r1 = lax.rsqrt(jnp.mean(x * x, axis=-1, keepdims=True) + EPS)
    row = lax.broadcasted_iota(jnp.int32, (length, 1), 0)
    mask = (row < valid).astype(F32)
    u = mask * x * r1 * gain_ref[...]
    scr[...] = u.astype(BF)
    scr_t[...] = u.T.astype(BF)
    for r in range(n):
        start = pl.multiple_of(lax.rem(m + r, n) * share, 16)
        u_ref[r * share : (r + 1) * share, :] = scr[pl.ds(start, share), :]
    for r in range(groups):
        start = pl.multiple_of(((d // 2) ^ r) * block, 16)
        ut_refs[r][...] = scr_t[pl.ds(start, block), :]


def first_norm(meta, x, gain, n, groups):
    length, width = x.shape
    share = length // n
    block = width // groups
    return pl.pallas_call(
        functools.partial(norm_kernel, n, share, groups),
        in_specs=[smem(), whole(x.shape), whole((1, width))],
        out_specs=[whole(x.shape)] + [whole((block, length))] * groups,
        out_shape=[jax.ShapeDtypeStruct(x.shape, BF)]
        + [jax.ShapeDtypeStruct((block, length), BF)] * groups,
        scratch_shapes=[pltpu.VMEM((length, width), BF), pltpu.VMEM((width, length), BF)],
        compiler_params=params(),
        cost_estimate=cost(10 * x.size, 6 * x.size),
        name="first_norm",
    )(meta, x, gain)


def mix_kernel(
    kb, share, meta, filt_ref, x_ref, u_ref, wp_ref, wm_ref, ar_ref, gain_ref,
    hid_ref, nt_ref, t_ref, us_ref, acc_ref,
):
    j = pl.program_id(0)
    length, width = u_ref.shape
    m, valid_len = meta[0], meta[2]
    row = lax.broadcasted_iota(jnp.int32, (share, length), 0)
    col = lax.broadcasted_iota(jnp.int32, (share, length), 1)
    valid = (col <= row) | (col >= length - m * share)

    @pl.when(j == 0)
    def _():
        u = u_ref[...]
        us_ref[:, :width] = u
        us_ref[:, width:] = (u.astype(F32) * parity_sign((length, width))).astype(BF)
        total = jnp.zeros((share, width), F32)
        back = jnp.where(row - col < 0, row - col + length, row - col)
        for i in range(ar_ref.shape[0]):
            t = jnp.where(valid & (back == i), 1.0, 0.0).astype(BF)
            total = total + dot(dot(t, u).astype(BF), ar_ref[i])
        acc_ref[...] = total

    for b in range(kb):
        t = toeplitz(filt_ref[pl.ds(j * kb + b, 1), :], share)
        t_ref[b * share : (b + 1) * share, :] = jnp.where(valid, t, 0.0).astype(BF)
    c = dot(t_ref[...], us_ref[...])
    sign = parity_sign((share, width))
    total = acc_ref[...]
    for b in range(kb):
        rows = slice(b * share, (b + 1) * share)
        total = total + dot(c[rows, :width].astype(BF), wp_ref[b])
        total = total + dot((c[rows, width:] * sign).astype(BF), wm_ref[b])
    acc_ref[...] = total

    @pl.when(j == pl.num_programs(0) - 1)
    def _():
        start = pl.multiple_of(m * share, 16)
        x = x_ref[pl.ds(start, share), :].astype(F32)
        hidden = x + acc_ref[...]
        hid_ref[...] = hidden
        r2 = lax.rsqrt(jnp.mean(hidden * hidden, axis=-1, keepdims=True) + EPS)
        pos = m * share + lax.broadcasted_iota(jnp.int32, (share, 1), 0)
        mask = (pos < valid_len).astype(F32)
        nt_ref[...] = (mask * hidden * r2 * gain_ref[...]).astype(BF)


def spectral_mix(meta, rev, x, u, stu, ar, gain, share, kb):
    length, width = u.shape
    filt = rev.shape[0]
    steps = filt // kb
    w_spec = pl.BlockSpec((kb, width, width), lambda j: (j, 0, 0))
    w_spec_neg = pl.BlockSpec((kb, width, width), lambda j: (j + steps, 0, 0))
    return pl.pallas_call(
        functools.partial(mix_kernel, kb, share),
        grid=(steps,),
        in_specs=[
            smem(), whole(rev.shape), whole(x.shape), whole(u.shape),
            w_spec, w_spec_neg, whole(ar.shape), whole((1, width)),
        ],
        out_specs=[whole((share, width))] * 2,
        out_shape=[
            jax.ShapeDtypeStruct((share, width), F32),
            jax.ShapeDtypeStruct((share, width), BF),
        ],
        scratch_shapes=[
            pltpu.VMEM((kb * share, length), BF),
            pltpu.VMEM((length, 2 * width), BF),
            pltpu.VMEM((share, width), F32),
        ],
        compiler_params=params(),
        cost_estimate=cost(4 * filt * share * width * (length + width), 2 * stu.size),
        name="spectral_mix",
    )(meta, rev, x, u, stu, stu, ar, gain)


def ffn_kernel(meta, nt_ref, cot_ref, gw_ref, uw_ref, dw_ref, bn_ref, act_ref, bg_ref, bu_ref):
    nt = nt_ref[...]
    gate = dot(nt, gw_ref[...])
    upper = dot(nt, uw_ref[...])
    back_act = dot_cols(cot_ref[...], dw_ref[...])
    square = gate * gate
    th = jnp.tanh(SQRT_2_PI * (gate + CUBIC * square * gate))
    half = 0.5 * (1.0 + th)
    gelu = gate * half
    slope = half + 0.5 * gate * (1.0 - th * th) * (SQRT_2_PI * (1.0 + 3.0 * CUBIC * square))
    act_ref[...] = (gelu * upper).astype(BF)
    bg = (back_act * upper * slope).astype(BF)
    bu = (back_act * gelu).astype(BF)
    bg_ref[...] = bg
    bu_ref[...] = bu
    bn_ref[...] = (dot_cols(bg, gw_ref[...]) + dot_cols(bu, uw_ref[...])).astype(BF)


def feed_forward(meta, shift, n, nt, cot, gw, uw, dw):
    share, width = nt.shape
    hid = gw.shape[1]
    full = lambda shape: pl.BlockSpec(shape, lambda i, meta: (0, 0))
    return pl.pallas_call(
        ffn_kernel,
        grid_spec=pltpu.PrefetchScalarGridSpec(
            num_scalar_prefetch=1,
            grid=(1,),
            in_specs=[
                full(nt.shape),
                pl.BlockSpec((share, width), lambda i, meta: (lax.rem(meta[0] + shift, n), 0)),
                full(gw.shape), full(uw.shape), full(dw.shape),
            ],
            out_specs=[full((share, width))] + [full((share, hid))] * 3,
        ),
        out_shape=[jax.ShapeDtypeStruct((share, width), BF)]
        + [jax.ShapeDtypeStruct((share, hid), BF)] * 3,
        compiler_params=params(),
        cost_estimate=cost(10 * share * width * hid, 2 * (3 * width * hid + 6 * share * width)),
        name="feed_forward",
    )(meta, nt, cot, gw, uw, dw)


def ffn_grad_kernel(n, share, groups, meta, cot_ref, dw_ref, *refs):
    nt_refs, act_refs, bg_refs, bu_refs = (refs[i * n : (i + 1) * n] for i in range(4))
    rest = refs[4 * n :]
    out_refs, rest = rest[:n], rest[n:]
    m, d = meta[0], meta[1]
    nt = jnp.concatenate([ref[...] for ref in nt_refs], axis=0)
    act = jnp.concatenate([ref[...] for ref in act_refs], axis=0)
    bg = jnp.concatenate([ref[...] for ref in bg_refs], axis=0)
    bu = jnp.concatenate([ref[...] for ref in bu_refs], axis=0)
    cot = jnp.concatenate(
        [
            cot_ref[pl.ds(pl.multiple_of(lax.rem(m + r, n) * share, 16), share), :]
            for r in range(n)
        ],
        axis=0,
    )
    outs = dot(act, dw_ref[...]).astype(BF)
    for r in range(n):
        out_refs[r][...] = outs[r * share : (r + 1) * share, :]
    nt_t = nt.T
    act_t = act.T
    grads = (dot(nt_t, bg), dot(nt_t, bu), dot(act_t, cot))
    if groups:
        keep_ref, send_ref, scr = rest
        for i in range(3):
            scr[i] = grads[i]
        rows = scr.shape[1] // (2 * groups)
        core = lax.rem(d, 2)
        for r in range(groups):
            chip = ((d // 2) ^ r) * 2
            for i in range(3):
                mine = pl.multiple_of((chip + core) * rows, 16)
                other = pl.multiple_of((chip + 1 - core) * rows, 16)
                keep_ref[r, i] = scr[i, pl.ds(mine, rows), :]
                send_ref[r, i] = scr[i, pl.ds(other, rows), :].astype(BF)
    else:
        for ref, grad in zip(rest, grads):
            ref[...] = grad.astype(BF)


def ffn_grads(meta, cot, dw, nts, acts, bgs, bus, groups):
    n = len(nts)
    share, width = nts[0].shape
    hid = dw.shape[0]
    length = cot.shape[0]
    out_shape = [jax.ShapeDtypeStruct((share, width), BF)] * n
    scratch = []
    if groups:
        part = (groups, 3, width // (2 * groups), width)
        out_shape += [jax.ShapeDtypeStruct(part, F32), jax.ShapeDtypeStruct(part, BF)]
        scratch = [pltpu.VMEM((3, width, width), F32)]
    else:
        out_shape += [
            jax.ShapeDtypeStruct((width, hid), BF),
            jax.ShapeDtypeStruct((width, hid), BF),
            jax.ShapeDtypeStruct((hid, width), BF),
        ]
    args = [meta, cot, dw, *nts, *acts, *bgs, *bus]
    return pl.pallas_call(
        functools.partial(ffn_grad_kernel, n, share, groups),
        in_specs=[smem()] + [whole(a.shape) for a in args[1:]],
        out_specs=[whole(s.shape) for s in out_shape],
        out_shape=out_shape,
        scratch_shapes=scratch,
        compiler_params=params(),
        cost_estimate=cost(8 * length * width * hid, 12 * length * width),
        name="ffn_grads",
    )(*args)


def mid_kernel(n, share, meta, hid_ref, cot_ref, gain_ref, *refs):
    bn_refs, (bh_ref, b_ref, gg_ref) = refs[:n], refs[n:]
    m, valid_len = meta[0], meta[2]
    bn = bn_refs[0][...].astype(F32)
    for ref in bn_refs[1:]:
        bn = bn + ref[...].astype(F32)
    hidden = hid_ref[...]
    r2 = lax.rsqrt(jnp.mean(hidden * hidden, axis=-1, keepdims=True) + EPS)
    pos = m * share + lax.broadcasted_iota(jnp.int32, (share, 1), 0)
    bn = bn * (pos < valid_len).astype(F32)
    z = hidden * r2
    gg_ref[...] = jnp.broadcast_to(jnp.sum(bn * z, axis=0, keepdims=True), gg_ref.shape)
    q = bn * gain_ref[...]
    start = pl.multiple_of(m * share, 16)
    dout = cot_ref[pl.ds(start, share), :].astype(F32)
    back = dout + r2 * (q - z * jnp.mean(q * z, axis=-1, keepdims=True))
    bh_ref[...] = back
    b_ref[...] = back.astype(BF)


def mid_norm(meta, hidden, cot, gain, pieces):
    share, width = hidden.shape
    n = len(pieces)
    return pl.pallas_call(
        functools.partial(mid_kernel, n, share),
        in_specs=[smem(), whole(hidden.shape), whole(cot.shape), whole((1, width))]
        + [whole(hidden.shape)] * n,
        out_specs=[whole(hidden.shape)] * 2 + [whole((8, width))],
        out_shape=[
            jax.ShapeDtypeStruct(hidden.shape, F32),
            jax.ShapeDtypeStruct(hidden.shape, BF),
            jax.ShapeDtypeStruct((8, width), F32),
        ],
        compiler_params=params(),
        cost_estimate=cost(20 * hidden.size, 20 * hidden.size),
        name="second_norm_back",
    )(meta, hidden, cot, gain, *pieces)


def unmix_kernel(
    kb, share, n, meta, filt_ref, x_ref, bh_ref, gg_ref, gain_ref, wp_ref, wm_ref, ar_ref, *refs
):
    b_refs, (ig_ref, gain_out, t_ref, bs_ref, acc_ref) = refs[:n], refs[n:]
    j = pl.program_id(0)
    width = bh_ref.shape[1]
    length = n * share
    m, valid_len = meta[0], meta[2]
    row = lax.broadcasted_iota(jnp.int32, (share, length), 0)
    col = lax.broadcasted_iota(jnp.int32, (share, length), 1)
    valid = (col >= row) & (col < length - m * share)

    @pl.when(j == 0)
    def _():
        sign = parity_sign((share, width))
        for r in range(n):
            rows = slice(r * share, (r + 1) * share)
            b = b_refs[r][...]
            bs_ref[rows, :width] = b
            bs_ref[rows, width:] = (b.astype(F32) * sign).astype(BF)
        total = jnp.zeros((share, width), F32)
        for i in range(ar_ref.shape[0]):
            t = jnp.where(valid & (col - row == i), 1.0, 0.0).astype(BF)
            total = total + dot_cols(dot(t, bs_ref[:, :width]).astype(BF), ar_ref[i])
        acc_ref[...] = total

    for b in range(kb):
        t = toeplitz(filt_ref[pl.ds(j * kb + b, 1), :], share)
        t_ref[b * share : (b + 1) * share, :] = jnp.where(valid, t, 0.0).astype(BF)
    c = dot(t_ref[...], bs_ref[...])
    sign = parity_sign((share, width))
    total = acc_ref[...]
    for b in range(kb):
        rows = slice(b * share, (b + 1) * share)
        total = total + dot_cols(c[rows, :width].astype(BF), wp_ref[b])
        total = total + dot_cols((c[rows, width:] * sign).astype(BF), wm_ref[b])
    acc_ref[...] = total

    @pl.when(j == pl.num_programs(0) - 1)
    def _():
        start = pl.multiple_of(m * share, 16)
        x = x_ref[pl.ds(start, share), :].astype(F32)
        r1 = lax.rsqrt(jnp.mean(x * x, axis=-1, keepdims=True) + EPS)
        pos = m * share + lax.broadcasted_iota(jnp.int32, (share, 1), 0)
        masked = acc_ref[...] * (pos < valid_len).astype(F32)
        y = x * r1
        gain_out[0:8, :] = jnp.broadcast_to(jnp.sum(masked * y, axis=0, keepdims=True), (8, width))
        gain_out[8:16, :] = gg_ref[...]
        p = masked * gain_ref[...]
        ig = bh_ref[...] + r1 * (p - y * jnp.mean(p * y, axis=-1, keepdims=True))
        ig_ref[...] = ig.astype(BF)


def spectral_unmix(meta, filt, x, back_hidden, gg, gain, stu, ar, pieces, kb):
    share, width = back_hidden.shape
    n = len(pieces)
    length = n * share
    count = filt.shape[0]
    steps = count // kb
    w_spec = pl.BlockSpec((kb, width, width), lambda j: (j, 0, 0))
    w_spec_neg = pl.BlockSpec((kb, width, width), lambda j: (j + steps, 0, 0))
    return pl.pallas_call(
        functools.partial(unmix_kernel, kb, share, n),
        grid=(steps,),
        in_specs=[
            smem(), whole(filt.shape), whole(x.shape), whole(back_hidden.shape), whole(gg.shape),
            whole((1, width)), w_spec, w_spec_neg, whole(ar.shape),
        ]
        + [whole((share, width))] * n,
        out_specs=[whole((share, width)), whole((16, width))],
        out_shape=[
            jax.ShapeDtypeStruct((share, width), BF),
            jax.ShapeDtypeStruct((16, width), F32),
        ],
        scratch_shapes=[
            pltpu.VMEM((kb * share, length), BF),
            pltpu.VMEM((length, 2 * width), BF),
            pltpu.VMEM((share, width), F32),
        ],
        compiler_params=params(),
        cost_estimate=cost(4 * count * share * width * (length + width), 2 * stu.size),
        name="spectral_unmix",
    )(meta, filt, x, back_hidden, gg, gain, stu, stu, ar, *pieces)


def conv_kernel(groups, tile, filt_ref, *refs):
    ut_refs, conv_ref = refs[:groups], refs[groups]
    j = pl.program_id(0)
    length = filt_ref.shape[1]
    block = ut_refs[0].shape[0]
    count = length // tile
    strip = toeplitz(filt_ref[pl.ds(j, 1), :], tile)
    row = lax.broadcasted_iota(jnp.int32, (tile, length), 0)
    col = lax.broadcasted_iota(jnp.int32, (tile, length), 1)
    strip = jnp.where(col >= row, strip, 0.0).astype(BF)
    ut = jnp.concatenate([ref[...] for ref in ut_refs], axis=0)
    for c in range(count):
        total = None
        for b in range(c + 1):
            part = dot(
                ut[:, b * tile : (b + 1) * tile],
                strip[:, (c - b) * tile : (c - b + 1) * tile],
            )
            total = part if total is None else total + part
        total = total.astype(BF)
        for r in range(groups):
            conv_ref[0, r, :, c * tile : (c + 1) * tile] = total[r * block : (r + 1) * block, :]


def convolutions(filt, uts):
    count, length = filt.shape
    groups = len(uts)
    block = uts[0].shape[0]
    tile = 256 if length % 256 == 0 else length
    return pl.pallas_call(
        functools.partial(conv_kernel, groups, tile),
        grid=(count,),
        in_specs=[whole(filt.shape)] + [whole((block, length))] * groups,
        out_specs=pl.BlockSpec((1, groups, block, length), lambda j: (j, 0, 0, 0)),
        out_shape=jax.ShapeDtypeStruct((count, groups, block, length), BF),
        compiler_params=params(),
        cost_estimate=cost(
            4 * count * groups * block * length * length // 3, 2 * count * groups * block * length
        ),
        name="convolutions",
    )(filt, *uts)


def stu_kernel(n, share, groups, meta, conv_ref, *refs):
    b_refs = refs[: groups * n]
    keep_ref, send_ref, b_scr, acc = refs[groups * n :]
    g = pl.program_id(0)
    m, d = meta[0], meta[1]
    count, block = keep_ref.shape[0], 2 * keep_ref.shape[1]
    for s in range(groups):

        @pl.when(g == s)
        def _():
            for r in range(n):
                start = pl.multiple_of(lax.rem(m + r, n) * share, 16)
                b_scr[pl.ds(start, share), :] = b_refs[s * n + r][...]

    left = conv_ref[...].reshape(count * block, conv_ref.shape[-1])
    part = dot(left, b_scr[...]).reshape(count, block, -1)

    @pl.when(g == 0)
    def _():
        acc[...] = part

    @pl.when(g > 0)
    def _():
        acc[...] += part

    @pl.when(g == groups - 1)
    def _():
        rows = block // 2
        core = lax.rem(d, 2)
        mine = pl.multiple_of(core * rows, 16)
        other = pl.multiple_of((1 - core) * rows, 16)
        keep_ref[...] = acc[:, pl.ds(mine, rows), :]
        send_ref[...] = acc[:, pl.ds(other, rows), :].astype(BF)


def stu_grads(meta, conv, pieces):
    count, groups, block, length = conv.shape
    n = len(pieces[0])
    share, width = pieces[0][0].shape
    flat = [piece for group in pieces for piece in group]
    half = (count, block // 2, width)
    return pl.pallas_call(
        functools.partial(stu_kernel, n, share, groups),
        grid=(groups,),
        in_specs=[
            smem(),
            pl.BlockSpec((count, None, block, length), lambda g: (0, g, 0, 0)),
        ]
        + [whole((share, width))] * len(flat),
        out_specs=[whole(half)] * 2,
        out_shape=[jax.ShapeDtypeStruct(half, F32), jax.ShapeDtypeStruct(half, BF)],
        scratch_shapes=[
            pltpu.VMEM((length, width), BF),
            pltpu.VMEM((count, block, width), F32),
        ],
        compiler_params=params(),
        cost_estimate=cost(2 * conv.size * width, 2 * conv.size),
        name="stu_grads",
    )(meta, conv, *flat)


def stu_add_kernel(own, keep_ref, recv_ref, stu_ref, ar_ref):
    total = keep_ref[...] + recv_ref[...].astype(F32)
    stu_ref[...] = total[:own]
    ar_ref[...] = total[own:].astype(BF)


def stu_add(keep, recv, own):
    shape = keep.shape
    return pl.pallas_call(
        functools.partial(stu_add_kernel, own),
        in_specs=[whole(shape)] * 2,
        out_specs=[whole((own,) + shape[1:]), whole((shape[0] - own,) + shape[1:])],
        out_shape=[
            jax.ShapeDtypeStruct((own,) + shape[1:], F32),
            jax.ShapeDtypeStruct((shape[0] - own,) + shape[1:], BF),
        ],
        compiler_params=params(),
        cost_estimate=cost(keep.size, 10 * keep.size),
        name="stu_add",
    )(keep, recv)


def pair_add_kernel(keep_ref, recv_ref, *out_refs):
    for r, ref in enumerate(out_refs):
        ref[...] = (keep_ref[r] + recv_ref[r].astype(F32)).astype(ref.dtype)


def pair_add(keep, recv):
    groups = keep.shape[0]
    part = keep.shape[1:]
    return pl.pallas_call(
        pair_add_kernel,
        in_specs=[whole(keep.shape)] * 2,
        out_specs=[whole(part)] * groups,
        out_shape=[jax.ShapeDtypeStruct(part, F32)]
        + [jax.ShapeDtypeStruct(part, BF)] * (groups - 1),
        compiler_params=params(),
        cost_estimate=cost(keep.size, 8 * keep.size),
        name="pair_add",
    )(keep, recv)


def sum_kernel(*refs):
    total = refs[0][...].astype(F32)
    for ref in refs[1:-1]:
        total = total + ref[...].astype(F32)
    refs[-1][...] = total.astype(refs[-1].dtype)


def sum_pieces(pieces, dtype):
    shape = pieces[0].shape
    return pl.pallas_call(
        sum_kernel,
        in_specs=[whole(shape)] * len(pieces),
        out_specs=whole(shape),
        out_shape=jax.ShapeDtypeStruct(shape, dtype),
        compiler_params=params(),
        cost_estimate=cost(4 * pieces[0].size, 10 * pieces[0].size),
        name="sum_pieces",
    )(*pieces)


def gather_kernel(groups, count, meta, *refs):
    pieces, outs = refs[: 2 * groups], refs[2 * groups :]
    d = meta[1]
    rows = pieces[0].shape[1]
    core = lax.rem(d, 2)
    for r in range(groups):
        chip = ((d // 2) ^ r) * 2
        for half in range(2):
            which = chip + (core if half == 0 else 1 - core)
            start = pl.multiple_of(which * rows, 16)
            for i in range(count):
                if len(outs) == 1:
                    outs[0][i, pl.ds(start, rows), :] = pieces[half * groups + r][i].astype(F32)
                else:
                    outs[i][pl.ds(start, rows), :] = pieces[half * groups + r][i].astype(F32)


def gather_rows(meta, pieces, separate):
    groups = len(pieces) // 2
    count, rows, width = pieces[0].shape
    full = rows * 2 * groups
    if separate:
        out_shape = [jax.ShapeDtypeStruct((full, width), F32)] * count
    else:
        out_shape = [jax.ShapeDtypeStruct((count, full, width), F32)]
    return pl.pallas_call(
        functools.partial(gather_kernel, groups, count),
        in_specs=[smem()] + [whole(pieces[0].shape)] * len(pieces),
        out_specs=[whole(s.shape) for s in out_shape],
        out_shape=out_shape,
        compiler_params=params(),
        cost_estimate=cost(count * full * width, 6 * count * full * width),
        name="gather_rows",
    )(meta, *pieces)


def place_kernel(n, share, meta, *refs):
    pieces, out_ref = refs[:n], refs[n]
    m = meta[0]
    for r in range(n):
        start = pl.multiple_of(lax.rem(m + r, n) * share, 16)
        out_ref[pl.ds(start, share), :] = pieces[r][...].astype(out_ref.dtype)


def place_rows(meta, pieces, dtype):
    n = len(pieces)
    share, width = pieces[0].shape
    return pl.pallas_call(
        functools.partial(place_kernel, n, share),
        in_specs=[smem()] + [whole((share, width))] * n,
        out_specs=whole((n * share, width)),
        out_shape=jax.ShapeDtypeStruct((n * share, width), dtype),
        compiler_params=params(),
        cost_estimate=cost(n * share * width, 6 * n * share * width),
        name="place_rows",
    )(meta, *pieces)


def ordered_sum_kernel(n, slot, xor, meta, *refs):
    pieces, out_ref, scr = refs[:n], refs[n], refs[n + 1]
    me = meta[slot]
    for r in range(n):
        who = (me ^ r) if xor else lax.rem(me + r, n)
        scr[who] = pieces[r][...]
    total = scr[0]
    for r in range(1, n):
        total = total + scr[r]
    out_ref[...] = total


def ordered_sum(meta, pieces, slot, xor):
    n = len(pieces)
    shape = pieces[0].shape
    return pl.pallas_call(
        functools.partial(ordered_sum_kernel, n, slot, xor),
        in_specs=[smem()] + [whole(shape)] * n,
        out_specs=whole(shape),
        out_shape=jax.ShapeDtypeStruct(shape, F32),
        scratch_shapes=[pltpu.VMEM((n,) + shape, F32)],
        compiler_params=params(),
        cost_estimate=cost(n * pieces[0].size, 4 * n * pieces[0].size),
        name="ordered_sum",
    )(meta, *pieces)


def fetch_shifted(value, axis, n):
    return [value] + [
        lax.ppermute(value, axis, [(i, (i - r) % n) for i in range(n)]) for r in range(1, n)
    ]


def send_shifted(pieces, axis):
    n = len(pieces)
    return [pieces[0]] + [
        lax.ppermute(pieces[r], axis, [(i, (i + r) % n) for i in range(n)]) for r in range(1, n)
    ]


def swap(value, axis, n, bits):
    return lax.ppermute(value, axis, [(i, i ^ bits) for i in range(n)])


def gather_dp(meta, piece, n_dp, separate):
    same = [piece] + [swap(piece, "dp", n_dp, 2 * r) for r in range(1, n_dp // 2)]
    other = [swap(p, "dp", n_dp, 1) for p in same]
    return gather_rows(meta, same + other, separate)


def shards(
    inputs, lengths, filters, first_gain, stu_weight, ar_weight, second_gain,
    gate_weight, up_weight, down_weight, cotangent,
):
    n = lax.axis_size("mp")
    n_dp = lax.axis_size("dp")
    groups = n_dp // 2
    length, width = inputs.shape
    share = length // n
    filt_count = filters.shape[1]
    order = ar_weight.shape[0]
    own = stu_weight.shape[0] // n
    m = lax.axis_index("mp").astype(jnp.int32)
    d = lax.axis_index("dp").astype(jnp.int32)
    meta = jnp.stack([m, d, lengths[0].astype(jnp.int32)])
    gain_one = first_gain.reshape(1, width)
    gain_two = second_gain.reshape(1, width)

    taps = filters.T.astype(F32)
    signs = jnp.where(jnp.arange(length, dtype=jnp.int32) % 2 == 0, 1.0, -1.0).astype(F32)[None, :]
    rev_taps = jnp.concatenate([taps[:, :1], taps[:, :0:-1]], axis=1)
    pair = jnp.concatenate([taps, taps * signs], axis=0)
    lag_taps = (
        jnp.arange(length, dtype=jnp.int32)[None, :] == jnp.arange(order, dtype=jnp.int32)[:, None]
    ).astype(F32)
    own_taps = jnp.concatenate([lax.dynamic_slice_in_dim(pair, m * own, own, 0), lag_taps], axis=0)

    u, *ut_pieces = first_norm(meta, inputs, gain_one, n, groups)
    uts = [ut_pieces[0]] + [swap(ut_pieces[r], "dp", n_dp, 2 * r) for r in range(1, groups)]
    hidden, nt = spectral_mix(
        meta, rev_taps, inputs, u, stu_weight, ar_weight, gain_two, share, 4
    )
    nts = fetch_shifted(nt, "mp", n)
    conv = convolutions(own_taps, uts)

    parts = [
        feed_forward(meta, r, n, nts[r], cotangent, gate_weight, up_weight, down_weight)
        for r in range(n)
    ]
    bns = send_shifted([p[0] for p in parts], "mp")
    acts, bgs, bus = ([p[i] for p in parts] for i in (1, 2, 3))
    custom = n_dp == 8 and gate_weight.shape[1] == width
    grads = ffn_grads(
        meta, cotangent, down_weight, nts, acts, bgs, bus, groups if custom else 0
    )
    out_parts, grads = grads[:n], grads[n:]

    back_hidden, back_rows, second_part = mid_norm(meta, hidden, cotangent, gain_two, bns)
    backs = fetch_shifted(back_rows, "mp", n)
    all_backs = [backs] + [
        [swap(piece, "dp", n_dp, 2 * r) for piece in backs] for r in range(1, groups)
    ]
    ig, gains = spectral_unmix(
        meta, taps, inputs, back_hidden, second_part, gain_one, stu_weight, ar_weight, backs, 4
    )
    igs = fetch_shifted(ig, "mp", n)
    input_grad = place_rows(meta, igs, F32)

    out_sums = send_shifted(out_parts, "mp")
    out_rows = sum_pieces([hidden] + out_sums, BF)
    output = place_rows(meta, fetch_shifted(out_rows, "mp", n), BF)

    keep, send = stu_grads(meta, conv, all_backs)
    stu_grad, ar_part = stu_add(keep, swap(send, "dp", n_dp, 1), own)
    (ar_grad,) = gather_dp(meta, ar_part, n_dp, False)

    gains_dp = [gains] + [swap(gains, "dp", n_dp, r) for r in range(1, n_dp)]
    gains = ordered_sum(meta, gains_dp, 1, True)
    gains = ordered_sum(meta, fetch_shifted(gains, "mp", n), 0, False)

    if custom:
        keep, send = grads
        chunks = pair_add(keep, swap(send, "dp", n_dp, 1))
        chunks = [chunks[0]] + [swap(chunks[r], "dp", n_dp, 2 * r) for r in range(1, groups)]
        gate_grad, up_grad, down_grad = gather_dp(meta, sum_pieces(chunks, BF), n_dp, True)
    else:
        gate_grad, up_grad, down_grad = (lax.psum(g, "dp").astype(F32) for g in grads)
    return (
        output, input_grad, stu_grad, ar_grad, gains[0], gains[8], gate_grad, up_grad, down_grad,
    )


def solution(mesh):
    in_specs = (
        P("dp", None), P("dp"), P(), P(), P(), P(), P(),
        P(None, "mp"), P(None, "mp"), P("mp", None), P("dp", None),
    )
    out_specs = (
        P("dp", None), P("dp", None), P("mp", "dp", None), P(), P(), P(),
        P(None, "mp"), P(None, "mp"), P("mp", None),
    )
    return jax.shard_map(shards, mesh=mesh, in_specs=in_specs, out_specs=out_specs, check_vma=False)
```

```python
import functools

import jax
import jax.numpy as jnp
from jax import lax
from jax.experimental import pallas as pl
from jax.experimental.pallas import tpu as pltpu
from jax.sharding import PartitionSpec as P

EPS = 1e-05
BF = jnp.bfloat16
F32 = jnp.float32
SQRT_2_PI = 0.7978845608028654
CUBIC = 0.044715
VMEM_LIMIT = 24 << 20


def dot(left, right):
    return jnp.dot(left, right, preferred_element_type=F32)


def dot_cols(left, right):
    return lax.dot_general(left, right, (((1,), (1,)), ((), ())), preferred_element_type=F32)


def params(limit=VMEM_LIMIT):
    return pltpu.CompilerParams(vmem_limit_bytes=limit)


COST_SCALE = 1.0


def cost(flops, nbytes):
    return pl.CostEstimate(
        flops=int(COST_SCALE * flops), bytes_accessed=int(COST_SCALE * nbytes), transcendentals=0
    )


def smem():
    return pl.BlockSpec(memory_space=pltpu.SMEM)


def whole():
    return pl.BlockSpec(memory_space=pltpu.VMEM)


def lag_spec(ar, steps):
    order, width = ar.shape[:2]
    assert order <= steps
    return pl.BlockSpec((1, width, width), lambda j: (jnp.minimum(j, order - 1), 0, 0))


def toeplitz(base_row, rows):
    wide = jnp.broadcast_to(base_row, (rows, base_row.shape[1]))
    return pltpu.roll(wide, 0, 1, stride=1, stride_axis=0)


def put_columns(scr, value):
    for c in range(scr.shape[0]):
        scr[c] = value[:, c * 128 : (c + 1) * 128]


def every_second(scr, start, count):
    columns = [scr[c, pl.ds(start, count, stride=2), :] for c in range(scr.shape[0])]
    return columns[0] if len(columns) == 1 else jnp.concatenate(columns, axis=1)


def interleave(scr, value):
    half = value.shape[0] // 2
    for c in range(scr.shape[0]):
        columns = slice(c * 128, (c + 1) * 128)
        scr[c, pl.ds(0, half, stride=2), :] = value[:half, columns]
        scr[c, pl.ds(1, half, stride=2), :] = value[half:, columns]
    return jnp.concatenate([scr[c] for c in range(scr.shape[0])], axis=1)


def norm_kernel(
    n, share, len_ref, x_ref, gain_ref, filt_ref, u_ref, taps_ref, nat_ref, ut_ref, scr, scr_f
):
    length, width = x_ref.shape
    half = length // 2
    m = lax.axis_index("mp")
    x = x_ref[...].astype(F32)
    r1 = lax.rsqrt(jnp.mean(x * x, axis=-1, keepdims=True) + EPS)
    row = lax.broadcasted_iota(jnp.int32, (length, 1), 0)
    mask = (row < len_ref[0]).astype(F32)
    u = mask * x * r1 * gain_ref[...]
    put_columns(scr, u)
    ut_ref[...] = u.T.astype(BF)
    for r in range(n):
        start = lax.rem(m + r, n) * share
        for odd in range(2):
            u_ref[odd, r * (share // 2) : (r + 1) * (share // 2), :] = every_second(
                scr, start + odd, share // 2
            ).astype(BF)
    filt = filt_ref.shape[0]
    natural = filt_ref[...].astype(F32)
    nat_ref[...] = natural
    scr_f[0, :, :filt] = natural.T
    even = every_second(scr_f, 0, half).T[:filt]
    odd = every_second(scr_f, 1, half).T[:filt]
    i = lax.broadcasted_iota(jnp.int32, (half, half), 0)
    j = lax.broadcasted_iota(jnp.int32, (half, half), 1)
    flip = (i == jnp.where(j == 0, 0, half - j)).astype(F32).astype(BF)
    rev_even = dot(even.astype(BF), flip)
    rev_odd = dot(odd.astype(BF), flip)
    taps_ref[0] = rev_even
    taps_ref[1] = rev_odd
    taps_ref[2] = pltpu.roll(rev_odd, half - 1, 1)
    taps_ref[3] = even
    taps_ref[4] = odd
    taps_ref[5] = pltpu.roll(odd, 1, 1)


def first_norm(lengths, x, gain, filters, n):
    length, width = x.shape
    share = length // n
    filt = filters.shape[0]
    half = length // 2
    return pl.pallas_call(
        functools.partial(norm_kernel, n, share),
        in_specs=[smem()] + [whole()] * 3,
        out_specs=[whole()] * 4,
        out_shape=[
            jax.ShapeDtypeStruct((2, half, width), BF),
            jax.ShapeDtypeStruct((6, filt, half), F32),
            jax.ShapeDtypeStruct((filt, length), F32),
            jax.ShapeDtypeStruct((width, length), BF),
        ],
        scratch_shapes=[
            pltpu.VMEM((width // 128, length, 128), F32),
            pltpu.VMEM((1, length, 128), F32),
        ],
        compiler_params=params(),
        cost_estimate=cost(10 * x.size, 6 * x.size),
        name="first_norm",
    )(lengths, x, gain, filters)


def mix_kernel(
    kb, share, order, len_ref, taps_ref, x_ref, u_ref, wp_ref, wm_ref, ar_ref, gain_ref,
    hid_ref, nt_ref, ta_ref, tb_ref, c_ref, acc_ref, scr,
):
    j = pl.program_id(0)
    length, width = x_ref.shape
    half, rows = length // 2, share // 2
    m = lax.axis_index("mp")
    b = lax.broadcasted_iota(jnp.int32, (rows, half), 0)
    a = lax.broadcasted_iota(jnp.int32, (rows, half), 1)
    wrapped = a >= (length - m * share) // 2
    upto = (a <= b) | wrapped
    below = (a < b) | wrapped

    @pl.when(j == 0)
    def _():
        acc_ref[...] = jnp.zeros((share, width), F32)

    @pl.when(j < order)
    def _():
        parts = []
        for row_odd in range(2):
            part = None
            for col_odd in range(2):
                back = 2 * b + row_odd - 2 * a - col_odd
                valid = (back >= 0) | wrapped
                back = jnp.where(back < 0, back + length, back)
                t = jnp.where(valid & (back == j), 1.0, 0.0).astype(BF)
                one = dot(t, u_ref[col_odd])
                part = one if part is None else part + one
            parts.append(part)
        acc_ref[...] += dot(jnp.concatenate(parts, axis=0).astype(BF), ar_ref[0])

    for k in range(kb):
        even = toeplitz(taps_ref[0, pl.ds(j * kb + k, 1), :], rows)
        odd = toeplitz(taps_ref[1, pl.ds(j * kb + k, 1), :], rows)
        late = toeplitz(taps_ref[2, pl.ds(j * kb + k, 1), :], rows)
        even = jnp.where(upto, even, 0.0).astype(BF)
        at = k * share
        ta_ref[at : at + rows, :] = even
        ta_ref[at + rows : at + share, :] = jnp.where(upto, odd, 0.0).astype(BF)
        tb_ref[at : at + rows, :] = jnp.where(below, late, 0.0).astype(BF)
        tb_ref[at + rows : at + share, :] = even
    ca = dot(ta_ref[...], u_ref[0])
    cb = dot(tb_ref[...], u_ref[1])
    for k in range(kb):
        at = k * share
        pa, pb = ca[at : at + share], cb[at : at + share]
        c_ref[:, k * width : (k + 1) * width] = (pa + pb).astype(BF)
        c_ref[:rows, (kb + k) * width : (kb + k + 1) * width] = (pa[:rows] - pb[:rows]).astype(BF)
        c_ref[rows:, (kb + k) * width : (kb + k + 1) * width] = (pb[rows:] - pa[rows:]).astype(BF)
    total = dot(c_ref[:, : kb * width], wp_ref[...].reshape(kb * width, width))
    total = total + dot(c_ref[:, kb * width :], wm_ref[...].reshape(kb * width, width))
    acc_ref[...] += total

    @pl.when(j == pl.num_programs(0) - 1)
    def _():
        start = pl.multiple_of(m * share, 16)
        x = x_ref[pl.ds(start, share), :].astype(F32)
        hidden = x + interleave(scr, acc_ref[...])
        hid_ref[...] = hidden
        r2 = lax.rsqrt(jnp.mean(hidden * hidden, axis=-1, keepdims=True) + EPS)
        pos = m * share + lax.broadcasted_iota(jnp.int32, (share, 1), 0)
        mask = (pos < len_ref[0]).astype(F32)
        nt_ref[...] = (mask * hidden * r2 * gain_ref[...]).astype(BF)


def spectral_mix(lengths, taps, x, u, stu, ar, gain, share, kb):
    length, width = x.shape
    filt = taps.shape[1]
    steps = filt // kb
    w_spec = pl.BlockSpec((kb, width, width), lambda j: (j, 0, 0))
    w_spec_neg = pl.BlockSpec((kb, width, width), lambda j: (j + steps, 0, 0))
    return pl.pallas_call(
        functools.partial(mix_kernel, kb, share, ar.shape[0]),
        grid=(steps,),
        in_specs=[smem(), whole(), whole(), whole(), w_spec, w_spec_neg]
        + [lag_spec(ar, steps), whole()],
        out_specs=[whole()] * 2,
        out_shape=[
            jax.ShapeDtypeStruct((share, width), F32),
            jax.ShapeDtypeStruct((share, width), BF),
        ],
        scratch_shapes=[
            pltpu.VMEM((kb * share, length // 2), BF),
            pltpu.VMEM((kb * share, length // 2), BF),
            pltpu.VMEM((share, 2 * kb * width), BF),
            pltpu.VMEM((share, width), F32),
            pltpu.VMEM((width // 128, share, 128), F32),
        ],
        compiler_params=params(40 << 20),
        cost_estimate=cost(2 * filt * share * width * (length + 2 * width), 2 * stu.size),
        name="spectral_mix",
    )(lengths, taps, x, u, stu, stu, ar, gain)


def ffn_kernel(
    shift, n, nt_ref, cot_ref, gw_ref, uw_ref, dw_ref, bn_ref, act_ref, bg_ref, bu_ref
):
    share = nt_ref.shape[0]
    nt = nt_ref[...]
    gate = dot(nt, gw_ref[...])
    upper = dot(nt, uw_ref[...])
    start = pl.multiple_of(lax.rem(lax.axis_index("mp") + shift, n) * share, 16)
    back_act = dot_cols(cot_ref[pl.ds(start, share), :], dw_ref[...])
    square = gate * gate
    th = jnp.tanh(SQRT_2_PI * (gate + CUBIC * square * gate))
    half = 0.5 * (1.0 + th)
    gelu = gate * half
    slope = half + 0.5 * gate * (1.0 - th * th) * (SQRT_2_PI * (1.0 + 3.0 * CUBIC * square))
    act_ref[...] = (gelu * upper).astype(BF)
    bg = (back_act * upper * slope).astype(BF)
    bu = (back_act * gelu).astype(BF)
    bg_ref[...] = bg
    bu_ref[...] = bu
    bn_ref[...] = (dot_cols(bg, gw_ref[...]) + dot_cols(bu, uw_ref[...])).astype(BF)


def feed_forward(shift, n, nt, cot, gw, uw, dw):
    share, width = nt.shape
    hid = gw.shape[1]
    return pl.pallas_call(
        functools.partial(ffn_kernel, shift, n),
        in_specs=[whole()] * 5,
        out_specs=[whole()] * 4,
        out_shape=[jax.ShapeDtypeStruct((share, width), BF)]
        + [jax.ShapeDtypeStruct((share, hid), BF)] * 3,
        compiler_params=params(),
        cost_estimate=cost(10 * share * width * hid, 2 * (3 * width * hid + 6 * share * width)),
        name="feed_forward",
    )(nt, cot, gw, uw, dw)


def ffn_grad_kernel(n, share, groups, cot_ref, dw_ref, *refs):
    nt_refs, act_refs, bg_refs, bu_refs = (refs[i * n : (i + 1) * n] for i in range(4))
    out_refs, grad_refs = refs[4 * n : 5 * n], refs[5 * n :]
    m = lax.axis_index("mp")
    nt = jnp.concatenate([ref[...] for ref in nt_refs], axis=0)
    act = jnp.concatenate([ref[...] for ref in act_refs], axis=0)
    bg = jnp.concatenate([ref[...] for ref in bg_refs], axis=0)
    bu = jnp.concatenate([ref[...] for ref in bu_refs], axis=0)
    cot = jnp.concatenate(
        [
            cot_ref[pl.ds(pl.multiple_of(lax.rem(m + r, n) * share, 16), share), :]
            for r in range(n)
        ],
        axis=0,
    )
    outs = dot(act, dw_ref[...]).astype(BF)
    for r in range(n):
        out_refs[r][...] = outs[r * share : (r + 1) * share, :]
    nt_t = nt.T
    grads = (dot(nt_t, bg), dot(nt_t, bu), dot(act.T, cot))
    if not groups:
        for ref, grad in zip(grad_refs, grads):
            ref[...] = grad.astype(BF)
        return
    keep_ref, send_ref, scr = grad_refs
    for i in range(3):
        scr[i] = grads[i].astype(BF)
    rows = scr.shape[1] // (2 * groups)
    d = lax.axis_index("dp")
    core = lax.rem(d, 2)
    for r in range(groups):
        chip = ((d // 2) ^ r) * 2
        for i in range(3):
            mine = pl.multiple_of((chip + core) * rows, 16)
            other = pl.multiple_of((chip + 1 - core) * rows, 16)
            keep_ref[r, i] = scr[i, pl.ds(mine, rows), :]
            send_ref[r, i] = scr[i, pl.ds(other, rows), :]


def ffn_grads(cot, dw, nts, acts, bgs, bus, groups):
    n = len(nts)
    share, width = nts[0].shape
    hid = dw.shape[0]
    length = cot.shape[0]
    out_shape = [jax.ShapeDtypeStruct((share, width), BF)] * n
    scratch = []
    if groups:
        part = (groups, 3, width // (2 * groups), width)
        out_shape += [jax.ShapeDtypeStruct(part, BF)] * 2
        scratch = [pltpu.VMEM((3, width, width), BF)]
    else:
        out_shape += [
            jax.ShapeDtypeStruct((width, hid), BF),
            jax.ShapeDtypeStruct((width, hid), BF),
            jax.ShapeDtypeStruct((hid, width), BF),
        ]
    args = [cot, dw, *nts, *acts, *bgs, *bus]
    return pl.pallas_call(
        functools.partial(ffn_grad_kernel, n, share, groups),
        in_specs=[whole()] * len(args),
        out_specs=[whole()] * len(out_shape),
        out_shape=out_shape,
        scratch_shapes=scratch,
        compiler_params=params(),
        cost_estimate=cost(8 * length * width * hid, 12 * length * width),
        name="ffn_grads",
    )(*args)


def mid_kernel(n, share, len_ref, hid_ref, cot_ref, gain_ref, *refs):
    bn_refs, (bh_ref, b_ref, gg_ref) = refs[:n], refs[n:]
    m = lax.axis_index("mp")
    bn = bn_refs[0][...].astype(F32)
    for ref in bn_refs[1:]:
        bn = bn + ref[...].astype(F32)
    hidden = hid_ref[...]
    r2 = lax.rsqrt(jnp.mean(hidden * hidden, axis=-1, keepdims=True) + EPS)
    pos = m * share + lax.broadcasted_iota(jnp.int32, (share, 1), 0)
    bn = bn * (pos < len_ref[0]).astype(F32)
    z = hidden * r2
    gg_ref[...] = jnp.broadcast_to(jnp.sum(bn * z, axis=0, keepdims=True), gg_ref.shape)
    q = bn * gain_ref[...]
    start = pl.multiple_of(m * share, 16)
    dout = cot_ref[pl.ds(start, share), :].astype(F32)
    back = dout + r2 * (q - z * jnp.mean(q * z, axis=-1, keepdims=True))
    bh_ref[...] = back
    b_ref[...] = back.astype(BF)


def mid_norm(lengths, hidden, cot, gain, pieces):
    share, width = hidden.shape
    n = len(pieces)
    return pl.pallas_call(
        functools.partial(mid_kernel, n, share),
        in_specs=[smem()] + [whole()] * (3 + n),
        out_specs=[whole()] * 3,
        out_shape=[
            jax.ShapeDtypeStruct(hidden.shape, F32),
            jax.ShapeDtypeStruct(hidden.shape, BF),
            jax.ShapeDtypeStruct((8, width), F32),
        ],
        compiler_params=params(),
        cost_estimate=cost(20 * hidden.size, 20 * hidden.size),
        name="second_norm_back",
    )(lengths, hidden, cot, gain, *pieces)


def unmix_kernel(
    kb, share, n, order, len_ref, taps_ref, x_ref, bh_ref, gg_ref, gain_ref, wp_ref, wm_ref, ar_ref, *refs
):
    b_refs, (ig_ref, gain_out, ta_ref, tb_ref, be_ref, bo_ref, acc_ref, scr) = refs[:n], refs[n:]
    j = pl.program_id(0)
    width = bh_ref.shape[1]
    length = n * share
    half, rows = length // 2, share // 2
    m = lax.axis_index("mp")
    b = lax.broadcasted_iota(jnp.int32, (rows, half), 0)
    a = lax.broadcasted_iota(jnp.int32, (rows, half), 1)
    inside = a < (length - m * share) // 2
    upto = (a >= b) & inside
    below = (a > b) & inside

    @pl.when(j == 0)
    def _():
        for r in range(n):
            put_columns(scr, b_refs[r][...].astype(F32))
            be_ref[r * rows : (r + 1) * rows, :] = every_second(scr, 0, rows).astype(BF)
            bo_ref[r * rows : (r + 1) * rows, :] = every_second(scr, 1, rows).astype(BF)
        acc_ref[...] = jnp.zeros((share, width), F32)

    @pl.when(j < order)
    def _():
        parts = []
        for row_odd in range(2):
            part = None
            for col_odd, source in enumerate((be_ref, bo_ref)):
                ahead = 2 * a + col_odd - 2 * b - row_odd
                t = jnp.where(inside & (ahead == j), 1.0, 0.0).astype(BF)
                one = dot(t, source[...])
                part = one if part is None else part + one
            parts.append(part)
        acc_ref[...] += dot_cols(jnp.concatenate(parts, axis=0).astype(BF), ar_ref[0])

    for k in range(kb):
        even = toeplitz(taps_ref[3, pl.ds(j * kb + k, 1), :], rows)
        odd = toeplitz(taps_ref[4, pl.ds(j * kb + k, 1), :], rows)
        late = toeplitz(taps_ref[5, pl.ds(j * kb + k, 1), :], rows)
        even = jnp.where(upto, even, 0.0).astype(BF)
        at = k * share
        ta_ref[at : at + rows, :] = even
        ta_ref[at + rows : at + share, :] = jnp.where(below, late, 0.0).astype(BF)
        tb_ref[at : at + rows, :] = jnp.where(upto, odd, 0.0).astype(BF)
        tb_ref[at + rows : at + share, :] = even
    ca = dot(ta_ref[...], be_ref[...])
    cb = dot(tb_ref[...], bo_ref[...])
    total = acc_ref[...]
    for k in range(kb):
        at = k * share
        pa, pb = ca[at : at + share], cb[at : at + share]
        minus = jnp.concatenate([pa[:rows] - pb[:rows], pb[rows:] - pa[rows:]], axis=0)
        total = total + dot_cols((pa + pb).astype(BF), wp_ref[k])
        total = total + dot_cols(minus.astype(BF), wm_ref[k])
    acc_ref[...] = total

    @pl.when(j == pl.num_programs(0) - 1)
    def _():
        start = pl.multiple_of(m * share, 16)
        x = x_ref[pl.ds(start, share), :].astype(F32)
        r1 = lax.rsqrt(jnp.mean(x * x, axis=-1, keepdims=True) + EPS)
        pos = m * share + lax.broadcasted_iota(jnp.int32, (share, 1), 0)
        masked = interleave(scr, acc_ref[...]) * (pos < len_ref[0]).astype(F32)
        y = x * r1
        p = masked * gain_ref[...]
        ig = bh_ref[...] + r1 * (p - y * jnp.mean(p * y, axis=-1, keepdims=True))
        ig_ref[...] = ig.astype(BF)
        gain_out[0:8, :] = jnp.broadcast_to(jnp.sum(masked * y, axis=0, keepdims=True), (8, width))
        gain_out[8:16, :] = gg_ref[...]


def spectral_unmix(lengths, taps, x, back_hidden, gg, gain, stu, ar, pieces, kb):
    share, width = back_hidden.shape
    n = len(pieces)
    length = n * share
    count = taps.shape[1]
    steps = count // kb
    w_spec = pl.BlockSpec((kb, width, width), lambda j: (j, 0, 0))
    w_spec_neg = pl.BlockSpec((kb, width, width), lambda j: (j + steps, 0, 0))
    return pl.pallas_call(
        functools.partial(unmix_kernel, kb, share, n, ar.shape[0]),
        grid=(steps,),
        in_specs=[smem()]
        + [whole()] * 5
        + [w_spec, w_spec_neg, lag_spec(ar, steps)]
        + [whole()] * n,
        out_specs=[whole()] * 2,
        out_shape=[
            jax.ShapeDtypeStruct((share, width), BF),
            jax.ShapeDtypeStruct((16, width), F32),
        ],
        scratch_shapes=[
            pltpu.VMEM((kb * share, length // 2), BF),
            pltpu.VMEM((kb * share, length // 2), BF),
            pltpu.VMEM((length // 2, width), BF),
            pltpu.VMEM((length // 2, width), BF),
            pltpu.VMEM((share, width), F32),
            pltpu.VMEM((width // 128, share, 128), F32),
        ],
        compiler_params=params(40 << 20),
        cost_estimate=cost(2 * count * share * width * (length + 2 * width), 2 * stu.size),
        name="spectral_unmix",
    )(lengths, taps, x, back_hidden, gg, gain, stu, stu, ar, *pieces)


def conv_kernel(groups, tile, own, filt_ref, *refs):
    ut_refs, (conv_ref, tt_ref, ut_scr) = refs[:groups], refs[groups:]
    j = pl.program_id(0)
    filt, length = filt_ref.shape
    block = conv_ref.shape[1]
    count = length // tile
    chip = lax.axis_index("dp") // 2

    @pl.when(j == 0)
    def _():
        start = pl.multiple_of(chip * block, 16)
        for r in range(groups):
            ut_scr[r * block : (r + 1) * block, :] = ut_refs[r][pl.ds(start, block), :]

    which = lax.axis_index("mp") * own + j
    strip = toeplitz(filt_ref[pl.ds(lax.rem(which, filt), 1), :], tile)
    row = lax.broadcasted_iota(jnp.int32, (tile, length), 0)
    col = lax.broadcasted_iota(jnp.int32, (tile, length), 1)
    flip = ((col - row) % 2 == 1) & (which >= filt)
    strip = jnp.where(col >= row, jnp.where(flip, -strip, strip), 0.0).astype(BF)
    for b in range(count):
        tt_ref[b * tile : (b + 1) * tile, b * tile :] = strip[:, : length - b * tile]
    for c in range(count):
        end = (c + 1) * tile
        part = dot(ut_scr[:, :end], tt_ref[:end, c * tile : end]).astype(BF)
        for r in range(groups):
            start = pl.multiple_of((lax.rem(chip, groups) ^ r) * length + c * tile, 128)
            conv_ref[0, :, pl.ds(start, tile)] = part[r * block : (r + 1) * block, :]


def convolutions(filt, uts, own, chips):
    length = filt.shape[1]
    groups = len(uts)
    block = uts[0].shape[0] // chips
    tile = 256 if length % 256 == 0 else length
    return pl.pallas_call(
        functools.partial(conv_kernel, groups, tile, own),
        grid=(own,),
        in_specs=[whole()] * (1 + groups),
        out_specs=pl.BlockSpec((1, block, groups * length), lambda j: (j, 0, 0)),
        out_shape=jax.ShapeDtypeStruct((own, block, groups * length), BF),
        scratch_shapes=[
            pltpu.VMEM((length, length), BF),
            pltpu.VMEM((groups * block, length), BF),
        ],
        compiler_params=params(),
        cost_estimate=cost(
            4 * own * groups * block * length * length // 3, 2 * own * groups * block * length
        ),
        name="convolutions",
    )(filt, *uts)


def grads_kernel(steps, order, groups, rows, conv_ref, *refs):
    ut_refs, b_refs = refs[:groups], refs[groups : groups + len(rows)]
    keep_ref, send_ref, b_scr, lag_scr, scr = refs[groups + len(rows) :]
    g = pl.program_id(0)
    d = lax.axis_index("dp")
    chip, core = lax.rem(d // 2, groups), lax.rem(d, 2)
    step, block, depth = conv_ref.shape
    width, length = ut_refs[0].shape
    half = block // 2

    @pl.when(g == 0)
    def _():
        for ref, (r, at, size) in zip(b_refs, rows):
            start = pl.multiple_of((chip ^ r) * length + at, 16)
            b_scr[pl.ds(start, size), :] = ref[:size, :]

    @pl.when(g < steps)
    def _():
        part = dot(conv_ref[...].reshape(step * block, depth), b_scr[...])
        scr[...] = part.reshape(step, block, width)
        mine = pl.multiple_of(core * half, 16)
        other = pl.multiple_of((1 - core) * half, 16)
        keep_ref[pl.ds(g * step, step)] = scr[:, pl.ds(mine, half), :]
        for k in range(step):
            start = pl.multiple_of((g * step + k) * half, 16)
            send_ref[pl.ds(start, half), :] = scr[k, pl.ds(other, half), :].astype(BF)

    @pl.when(g >= steps)
    def _():
        lag = g - steps
        col = lax.broadcasted_iota(jnp.int32, (width, length), 1)
        for r in range(groups):
            value = pltpu.roll(ut_refs[r][...].astype(F32), lag, 1)
            start = pl.multiple_of((chip ^ r) * length, 128)
            lag_scr[:, pl.ds(start, length)] = jnp.where(col >= lag, value, 0.0).astype(BF)
        start = pl.multiple_of(steps * step * half + lag * width, 16)
        send_ref[pl.ds(start, width), :] = dot(lag_scr[...], b_scr[...]).astype(BF)


def matrix_grads(conv, uts, backs, rows, order):
    own, block, depth = conv.shape
    groups = len(uts)
    width = uts[0].shape[0]
    step = next(s for s in (4, 3, 2, 1) if own % s == 0)
    steps = own // step
    half = block // 2
    return pl.pallas_call(
        functools.partial(grads_kernel, steps, order, groups, rows),
        grid=(steps + order,),
        in_specs=[pl.BlockSpec((step, block, depth), lambda g: (jnp.minimum(g, steps - 1), 0, 0))]
        + [whole()] * (groups + len(backs)),
        out_specs=[whole()] * 2,
        out_shape=[
            jax.ShapeDtypeStruct((own, half, width), F32),
            jax.ShapeDtypeStruct((own * half + order * width, width), BF),
        ],
        scratch_shapes=[
            pltpu.VMEM((depth, width), BF),
            pltpu.VMEM((width, depth), BF),
            pltpu.VMEM((step, block, width), F32),
        ],
        compiler_params=params(),
        cost_estimate=cost(2 * (conv.size + order * width * depth) * width, 2 * conv.size),
        name="matrix_grads",
    )(conv, *uts, *backs)


def rows_message_kernel(ig_ref, hid_ref, *refs):
    share = ig_ref.shape[0]
    total = hid_ref[...]
    for ref in refs[:-1]:
        total = total + ref[...].astype(F32)
    refs[-1][:share, :] = ig_ref[...]
    refs[-1][share:, :] = total.astype(BF)


def rows_message(ig, hidden, pieces):
    share, width = ig.shape
    return pl.pallas_call(
        rows_message_kernel,
        in_specs=[whole()] * (2 + len(pieces)),
        out_specs=whole(),
        out_shape=jax.ShapeDtypeStruct((2 * share, width), BF),
        compiler_params=params(),
        cost_estimate=cost(4 * ig.size, 10 * ig.size),
        name="rows_message",
    )(ig, hidden, *pieces)


def finish_rows_kernel(n, share, *refs):
    pieces, (ig_ref, out_ref) = refs[:n], refs[n:]
    m = lax.axis_index("mp")
    for r in range(n):
        start = pl.multiple_of(lax.rem(m + r, n) * share, 16)
        ig_ref[pl.ds(start, share), :] = pieces[r][:share, :].astype(F32)
        out_ref[pl.ds(start, share), :] = pieces[r][share:, :]


def finish_rows(pieces):
    n = len(pieces)
    share, width = pieces[0].shape[0] // 2, pieces[0].shape[1]
    return pl.pallas_call(
        functools.partial(finish_rows_kernel, n, share),
        in_specs=[whole()] * n,
        out_specs=[whole()] * 2,
        out_shape=[
            jax.ShapeDtypeStruct((n * share, width), F32),
            jax.ShapeDtypeStruct((n * share, width), BF),
        ],
        compiler_params=params(),
        cost_estimate=cost(n * share * width, 6 * n * share * width),
        name="finish_rows",
    )(*pieces)


def ordered_sum_kernel(n, axis, step, *refs):
    pieces, (out_ref, scr) = refs[:n], refs[n:]
    me = lax.axis_index(axis)
    for r in range(n):
        who = lax.rem(me + r, n) if step == 0 else (me // step) ^ r
        scr[who] = pieces[r][...]
    total = scr[0]
    for r in range(1, n):
        total = total + scr[r]
    out_ref[...] = total


def ordered_sum(pieces, axis, step):
    n = len(pieces)
    shape = pieces[0].shape
    return pl.pallas_call(
        functools.partial(ordered_sum_kernel, n, axis, step),
        in_specs=[whole()] * n,
        out_specs=whole(),
        out_shape=jax.ShapeDtypeStruct(shape, F32),
        scratch_shapes=[pltpu.VMEM((n,) + shape, F32)],
        compiler_params=params(),
        cost_estimate=cost(n * pieces[0].size, 4 * n * pieces[0].size),
        name="ordered_sum",
    )(*pieces)


def halve_kernel(kept, sent, keep_ref, recv_ref, *out_refs):
    rows = recv_ref.shape[0] // keep_ref.shape[0]
    total = keep_ref[...].astype(F32) + recv_ref[...].astype(F32)
    for ref, which in zip(out_refs, (kept, sent)):
        for k, r in enumerate(which):
            ref[k] = total[r].astype(BF)


def halve(keep, recv, kept, sent):
    part = keep.shape[1:]
    return pl.pallas_call(
        functools.partial(halve_kernel, kept, sent),
        in_specs=[whole()] * 2,
        out_specs=[whole()] * 2,
        out_shape=[jax.ShapeDtypeStruct((len(w),) + part, BF) for w in (kept, sent)],
        compiler_params=params(),
        cost_estimate=cost(keep.size, 8 * keep.size),
        name="halve",
    )(keep, recv)


def pack_kernel(n, share, extra, *refs):
    pieces, rest = refs[:n], refs[n:]
    m = lax.axis_index("mp")
    out_refs = rest[1:] if extra else rest
    for r in range(n):
        start = pl.multiple_of(lax.rem(m + r, n) * share, 16)
        for ref in out_refs:
            ref[pl.ds(start, share), :] = pieces[r][...]
    if extra:
        rows = rest[0].shape[1]
        for k in range(rest[0].shape[0]):
            at = n * share + k * rows
            out_refs[1][at : at + rows, :] = rest[0][k]


def pack_rows(pieces, extra=None):
    n = len(pieces)
    share, width = pieces[0].shape
    shapes = [(n * share, width)]
    if extra is not None:
        shapes.append((n * share + extra.shape[0] * extra.shape[1], width))
    args = list(pieces) + ([] if extra is None else [extra])
    return pl.pallas_call(
        functools.partial(pack_kernel, n, share, extra is not None),
        in_specs=[whole()] * len(args),
        out_specs=[whole()] * len(shapes),
        out_shape=[jax.ShapeDtypeStruct(shape, BF) for shape in shapes],
        compiler_params=params(),
        cost_estimate=cost(n * share * width, 6 * n * share * width),
        name="pack_rows",
    )(*args)


def turn_kernel(keep_ref, x_ref, y_ref, keep_out, to_y, to_x):
    length = y_ref.shape[0]
    half, rows = length // 2, keep_ref.shape[1]
    keep_out[...] = keep_ref[0].astype(F32) + x_ref[length : length + rows, :].astype(F32)
    sent = keep_ref[1].astype(F32) + x_ref[length + rows :, :].astype(F32)
    to_y[:half, :] = x_ref[:half, :]
    to_y[half:, :] = sent.astype(BF)
    to_x[...] = y_ref[half:, :]


def turn(keep, over_x, over_y):
    length, width = over_y.shape
    rows = keep.shape[1]
    return pl.pallas_call(
        turn_kernel,
        in_specs=[whole()] * 3,
        out_specs=[whole()] * 3,
        out_shape=[
            jax.ShapeDtypeStruct((rows, width), F32),
            jax.ShapeDtypeStruct((length // 2 + rows, width), BF),
            jax.ShapeDtypeStruct((length // 2, width), BF),
        ],
        compiler_params=params(),
        cost_estimate=cost(over_x.size, 8 * over_x.size),
        name="turn",
    )(keep, over_x, over_y)


def last_sum_kernel(keep_ref, recv_ref, out_ref):
    at = recv_ref.shape[0] - keep_ref.shape[0]
    out_ref[...] = (keep_ref[...] + recv_ref[at:, :].astype(F32)).astype(BF)


def last_sum(keep, recv):
    return pl.pallas_call(
        last_sum_kernel,
        in_specs=[whole()] * 2,
        out_specs=whole(),
        out_shape=jax.ShapeDtypeStruct(keep.shape, BF),
        compiler_params=params(),
        cost_estimate=cost(keep.size, 8 * keep.size),
        name="last_sum",
    )(keep, recv)


def join_kernel(*refs):
    at = 0
    for ref in refs[:-1]:
        refs[-1][at : at + ref.shape[0], :] = ref[...]
        at += ref.shape[0]


def join_pieces(pieces):
    rows = sum(p.shape[0] for p in pieces)
    return pl.pallas_call(
        join_kernel,
        in_specs=[whole()] * len(pieces),
        out_specs=whole(),
        out_shape=jax.ShapeDtypeStruct((rows, pieces[0].shape[1]), pieces[0].dtype),
        compiler_params=params(),
        cost_estimate=cost(rows * pieces[0].shape[1], 4 * rows * pieces[0].shape[1]),
        name="join_pieces",
    )(*pieces)


def finish_kernel(chips, keep_ref, send_ref, recv_ref, stu_ref, ar_ref, *w_refs):
    own, half, width = keep_ref.shape
    d = lax.axis_index("dp")
    core = lax.rem(d, 2)
    groups, count = len(chips), len(w_refs)
    rows = width // (2 * groups) if groups else 0
    base = groups * count * rows
    for r in range(groups):
        chip = ((d // 2) ^ r) * 2
        for ref, which in ((send_ref, chip + core), (recv_ref, chip + 1 - core)):
            start = pl.multiple_of(which * rows, 16)
            for i, out in enumerate(w_refs):
                at = (chips[r] * count + i) * rows
                out[pl.ds(start, rows), :] = ref[at : at + rows, :].astype(F32)
    for k in range(own):
        at = base + k * half
        stu_ref[k] = keep_ref[k] + recv_ref[at : at + half, :].astype(F32)
    for i in range(ar_ref.shape[0]):
        at = base + own * half + i * width
        ar_ref[i] = send_ref[at : at + width, :].astype(F32) + recv_ref[
            at : at + width, :
        ].astype(F32)


def finish(keep, send, recv, order, chips):
    width = keep.shape[2]
    count = 3 if chips else 0
    return pl.pallas_call(
        functools.partial(finish_kernel, chips),
        in_specs=[whole()] * 3,
        out_specs=[whole()] * (2 + count),
        out_shape=[
            jax.ShapeDtypeStruct(keep.shape, F32),
            jax.ShapeDtypeStruct((order, width, width), F32),
        ]
        + [jax.ShapeDtypeStruct((width, width), F32)] * count,
        compiler_params=params(),
        cost_estimate=cost(keep.size, 10 * keep.size),
        name="finish",
    )(keep, send, recv)


def fetch_shifted(value, axis, n):
    return [value] + [
        lax.ppermute(value, axis, [(i, (i - r) % n) for i in range(n)]) for r in range(1, n)
    ]


def send_shifted(pieces, axis):
    n = len(pieces)
    return [pieces[0]] + [
        lax.ppermute(pieces[r], axis, [(i, (i + r) % n) for i in range(n)]) for r in range(1, n)
    ]


def swap(value, axis, n, bits):
    return lax.ppermute(value, axis, [(i, i ^ bits) for i in range(n)])


def merge_rows(value):
    return value.reshape(value.shape[0], -1, value.shape[-1])


def after(values, first):
    flat, tree = jax.tree.flatten(values)
    out = lax.optimization_barrier((*flat, *jax.tree.leaves(first)))
    return jax.tree.unflatten(tree, out[: len(flat)])


def shards(
    inputs, lengths, filters, first_gain, stu_weight, ar_weight, second_gain,
    gate_weight, up_weight, down_weight, cotangent,
):
    n = lax.axis_size("mp")
    n_dp = lax.axis_size("dp")
    groups = n_dp // 2
    length, width = inputs.shape
    share = length // n
    order = ar_weight.shape[0]
    own = stu_weight.shape[0] // n
    lengths = lengths.astype(jnp.int32)
    gain_one = first_gain.reshape(1, width)
    gain_two = second_gain.reshape(1, width)

    u, taps, natural, ut = first_norm(lengths, inputs, gain_one, filters.T, n)
    uts = [ut] + [swap(ut, "dp", n_dp, 2 * r) for r in range(1, 3)]
    hidden, nt = spectral_mix(lengths, taps, inputs, u, stu_weight, ar_weight, gain_two, share, 4)
    nts = fetch_shifted(nt, "mp", n)
    uts += [swap(after(ut, nt), "dp", n_dp, 2 * r) for r in range(3, groups)]
    weights = (cotangent, gate_weight, up_weight, down_weight)
    parts = [feed_forward(0, n, nts[0], *weights)]
    nts = [nts[0]] + after(after(nts[1:], parts[0][0]), uts[1:3])
    parts += [feed_forward(r, n, nts[r], *weights) for r in range(1, n)]
    bns = send_shifted([p[0] for p in parts], "mp")
    acts, bgs, bus = ([p[i] for p in parts] for i in (1, 2, 3))
    custom = n_dp == 8 and gate_weight.shape[1] == width
    grads = ffn_grads(cotangent, down_weight, nts, acts, bgs, bus, groups if custom else 0)
    out_parts, grads = grads[:n], grads[n:]
    bns = [bns[0]] + after(bns[1:], grads[0])
    back_hidden, back_rows, second_part = mid_norm(lengths, hidden, cotangent, gain_two, bns)
    backs = fetch_shifted(back_rows, "mp", n)
    uts = after(uts, back_rows)
    conv = [convolutions(natural, uts[r : r + 4], own, groups) for r in range(0, groups, 4)]
    backs = after(backs, conv)
    if custom:
        w_keep, w_send = grads
        w_send = swap(after(w_send, back_rows), "dp", n_dp, 1)
        w_keep, w_send = halve(w_keep, w_send, (0, 2), (1, 3))
        own_back, to_x = pack_rows(backs, merge_rows(w_send))
        over_x, over_y = swap(to_x, "dp", n_dp, 2), swap(own_back, "dp", n_dp, 4)
    else:
        (own_back,) = pack_rows(backs)
    out_sums = send_shifted(after(out_parts, own_back), "mp")
    ig, gains = spectral_unmix(
        lengths, taps, inputs, back_hidden, second_part, gain_one, stu_weight, ar_weight, backs, 4
    )
    conv, hidden = after((conv, hidden), ig)
    message = rows_message(ig, hidden, out_sums)
    messages = fetch_shifted(message, "mp", n)
    if custom:
        w_keep, to_y, to_x = turn(merge_rows(w_keep), after(over_x, message), over_y)
        from_y, from_x = swap(to_y, "dp", n_dp, 4), swap(to_x, "dp", n_dp, 2)
        all_backs = [own_back, over_x, over_y, from_y, from_x]
        half = length // 2
        rows = ((0, 0, length), (1, 0, length), (2, 0, length), (3, 0, half), (3, half, half))
        w_sum = last_sum(w_keep, from_y)
        conv = after(conv, w_sum)
    else:
        all_backs = [own_back] + [swap(own_back, "dp", n_dp, 2 * r) for r in range(1, groups)]
        rows = tuple((r, 0, length) for r in range(min(groups, 4)))

    gains = after(gains, all_backs[-1])
    gains = ordered_sum(fetch_shifted(gains, "mp", n), "mp", 0)
    gains = ordered_sum([gains, swap(gains, "dp", n_dp, 1)], "dp", 0)
    gains = [gains] + [swap(gains, "dp", n_dp, 2 * r) for r in range(1, groups)]
    gains = ordered_sum(gains, "dp", 2)

    conv = after(conv, (message, messages[n // 2]))
    if len(conv) == 1:
        keep, send = matrix_grads(conv[0], uts, all_backs, rows, order)
    else:
        some = [
            matrix_grads(c, uts[4 * k : 4 * k + 4], all_backs[4 * k : 4 * k + 4], rows, order)
            for k, c in enumerate(conv)
        ]
        keep = ordered_sum([k for k, _ in some], "dp", 8)
        send = ordered_sum([k.astype(F32) for _, k in some], "dp", 8).astype(BF)
    input_grad, output = finish_rows(after(messages, (gains, send)))
    if custom:
        w_pair = join_pieces([w_sum, swap(w_sum, "dp", n_dp, 4)])
        w_all = [w_pair, swap(w_pair, "dp", n_dp, 2)]
        send = join_pieces(after([*w_all, send], output))
    recv = swap(after(send, output), "dp", n_dp, 1)
    stu_grad, ar_grad, *w_grads = finish(keep, send, recv, order, (0, 2, 1, 3) if custom else ())
    if custom:
        gate_grad, up_grad, down_grad = w_grads
    else:
        gate_grad, up_grad, down_grad = (g.astype(F32) for g in lax.psum(tuple(grads), "dp"))
    return (
        output, input_grad, stu_grad, ar_grad, gains[0], gains[8], gate_grad, up_grad, down_grad,
    )


def solution(mesh):
    in_specs = (
        P("dp", None), P("dp"), P(), P(), P(), P(), P(),
        P(None, "mp"), P(None, "mp"), P("mp", None), P("dp", None),
    )
    out_specs = (
        P("dp", None), P("dp", None), P("mp", "dp", None), P(), P(), P(),
        P(None, "mp"), P(None, "mp"), P("mp", None),
    )
    return jax.shard_map(shards, mesh=mesh, in_specs=in_specs, out_specs=out_specs, check_vma=False)
```

```python
import functools

import jax
import jax.numpy as jnp
from jax import lax
from jax.experimental import pallas as pl
from jax.experimental.pallas import tpu as pltpu
from jax.sharding import PartitionSpec as P

EPS = 1e-05
BF = jnp.bfloat16
F32 = jnp.float32
SQRT_2_PI = 0.7978845608028654
CUBIC = 0.044715
VMEM_LIMIT = 20 << 20


def dot(left, right):
    return jnp.dot(left, right, preferred_element_type=F32)


def dot_cols(left, right):
    return lax.dot_general(left, right, (((1,), (1,)), ((), ())), preferred_element_type=F32)


def params(limit=VMEM_LIMIT):
    return pltpu.CompilerParams(vmem_limit_bytes=limit)


COST_SCALE = 1.0


def cost(flops, nbytes):
    return pl.CostEstimate(
        flops=int(COST_SCALE * flops), bytes_accessed=int(COST_SCALE * nbytes), transcendentals=0
    )


def smem():
    return pl.BlockSpec(memory_space=pltpu.SMEM)


def whole():
    return pl.BlockSpec(memory_space=pltpu.VMEM)


def outside():
    return pl.BlockSpec(memory_space=pltpu.HBM)


def toeplitz(base_row, rows):
    wide = jnp.broadcast_to(base_row, (rows, base_row.shape[1]))
    return pltpu.roll(wide, 0, 1, stride=1, stride_axis=0)


def put_columns(scr, value, at=0):
    for c in range(scr.shape[0]):
        scr[c, at : at + value.shape[0], :] = value[:, c * 128 : (c + 1) * 128]


def every_second(scr, start, count):
    columns = [scr[c, pl.ds(start, count, stride=2), :] for c in range(scr.shape[0])]
    return columns[0] if len(columns) == 1 else jnp.concatenate(columns, axis=1)


def interleave(scr, value):
    half = value.shape[0] // 2
    for c in range(scr.shape[0]):
        columns = slice(c * 128, (c + 1) * 128)
        scr[c, pl.ds(0, half, stride=2), :] = value[:half, columns]
        scr[c, pl.ds(1, half, stride=2), :] = value[half:, columns]
    count = value.shape[0]
    return jnp.concatenate([scr[c, :count, :] for c in range(scr.shape[0])], axis=1)


def norm_kernel(
    n, share, order, len_ref, x_ref, gain_ref, u_ref, ut_ref, own_ref, lag_ref, scr
):
    length, width = x_ref.shape
    m = lax.axis_index("mp")
    x = x_ref[...].astype(F32)
    r1 = lax.rsqrt(jnp.mean(x * x, axis=-1, keepdims=True) + EPS)
    row = lax.broadcasted_iota(jnp.int32, (length, 1), 0)
    mask = (row < len_ref[0]).astype(F32)
    u = mask * x * r1 * gain_ref[0:1, :]
    scr[:, :8, :] = jnp.zeros((scr.shape[0], 8, 128), F32)
    put_columns(scr, u, 8)
    ut_ref[...] = u.T.astype(BF)
    own_ref[...] = x_ref[pl.ds(pl.multiple_of(m * share, 16), share), :].astype(F32)
    for r in range(n):
        start = lax.rem(m + r, n) * share
        for odd in range(2):
            u_ref[odd, r * (share // 2) : (r + 1) * (share // 2), :] = every_second(
                scr, start + odd + 8, share // 2
            ).astype(BF)
    for lag in range(order):
        for odd in range(2):
            at = lag * width
            lag_ref[odd * (share // 2) : (odd + 1) * (share // 2), at : at + width] = every_second(
                scr, m * share + odd + 8 - lag, share // 2
            ).astype(BF)


def first_norm(lengths, x, gains, n, order):
    length, width = x.shape
    share = length // n
    return pl.pallas_call(
        functools.partial(norm_kernel, n, share, order),
        in_specs=[smem(), whole(), whole()],
        out_specs=[whole()] * 4,
        out_shape=[
            jax.ShapeDtypeStruct((2, length // 2, width), BF),
            jax.ShapeDtypeStruct((width, length), BF),
            jax.ShapeDtypeStruct((share, width), F32),
            jax.ShapeDtypeStruct((share, order * width), BF),
        ],
        scratch_shapes=[pltpu.VMEM((width // 128, length + 8, 128), F32)],
        compiler_params=params(),
        cost_estimate=cost(10 * x.size, 6 * x.size),
        name="first_norm",
    )(lengths, x, gains)


def taps_kernel(filt_ref, taps_ref, nat_ref, scr_f):
    filt, length = filt_ref.shape
    half = length // 2
    natural = filt_ref[...].astype(F32)
    nat_ref[...] = natural
    scr_f[0, :, :filt] = natural.T
    even = every_second(scr_f, 0, half).T[:filt]
    odd = every_second(scr_f, 1, half).T[:filt]
    i = lax.broadcasted_iota(jnp.int32, (half, half), 0)
    j = lax.broadcasted_iota(jnp.int32, (half, half), 1)
    flip = (i == jnp.where(j == 0, 0, half - j)).astype(F32).astype(BF)
    rev_even = dot(even.astype(BF), flip)
    rev_odd = dot(odd.astype(BF), flip)
    taps_ref[0] = rev_even
    taps_ref[1] = rev_odd
    taps_ref[2] = pltpu.roll(rev_odd, half - 1, 1)
    taps_ref[3] = even
    taps_ref[4] = odd
    taps_ref[5] = pltpu.roll(odd, 1, 1)


def filter_taps(filters):
    filt, length = filters.shape
    return pl.pallas_call(
        taps_kernel,
        in_specs=[whole()],
        out_specs=[whole()] * 2,
        out_shape=[
            jax.ShapeDtypeStruct((6, filt, length // 2), F32),
            jax.ShapeDtypeStruct((filt, length), F32),
        ],
        scratch_shapes=[pltpu.VMEM((1, length, 128), F32)],
        compiler_params=params(),
        cost_estimate=cost(10 * filters.size, 6 * filters.size),
        name="filter_taps",
    )(filters)


def fetch_matrices(j, steps, kb, stu_hbm, w_buf, sems):
    def copies(step):
        slot = lax.rem(step, 2)
        return [
            pltpu.make_async_copy(
                stu_hbm.at[pl.ds((sign * steps + step) * kb, kb)],
                w_buf.at[slot, sign],
                sems.at[slot, sign],
            )
            for sign in range(2)
        ]

    @pl.when(j == 0)
    def _():
        for copy in copies(j):
            copy.start()

    @pl.when(j + 1 < steps)
    def _():
        for copy in copies(j + 1):
            copy.start()

    def wait():
        for copy in copies(j):
            copy.wait()

    return lax.rem(j, 2), wait


def fetch_last(j, steps, src, dst, sem):
    copy = pltpu.make_async_copy(src, dst, sem)

    @pl.when(j == 0)
    def _():
        copy.start()

    @pl.when(j == steps - 1)
    def _():
        copy.wait()


def mix_kernel(
    kb, share, len_ref, taps_ref, x_ref, u_ref, lag_ref, gain_ref, stu_hbm, ar_hbm,
    hid_ref, nt_ref, ta_ref, tb_ref, c_ref, acc_ref, scr, w_buf, ar_ref, sems, ar_sem,
):
    j, steps = pl.program_id(0), pl.num_programs(0)
    half, width = u_ref.shape[1:]
    length, rows = 2 * half, share // 2
    m = lax.axis_index("mp")
    b = lax.broadcasted_iota(jnp.int32, (rows, half), 0)
    a = lax.broadcasted_iota(jnp.int32, (rows, half), 1)
    wrapped = a >= (length - m * share) // 2
    upto = (a <= b) | wrapped
    below = (a < b) | wrapped
    slot, wait = fetch_matrices(j, stu_hbm.shape[0] // (2 * kb), kb, stu_hbm, w_buf, sems)

    @pl.when(j == 0)
    def _():
        acc_ref[...] = jnp.zeros((share, width), F32)

    for k in range(kb):
        even = toeplitz(taps_ref[0, pl.ds(j * kb + k, 1), :], rows)
        odd = toeplitz(taps_ref[1, pl.ds(j * kb + k, 1), :], rows)
        late = toeplitz(taps_ref[2, pl.ds(j * kb + k, 1), :], rows)
        even = jnp.where(upto, even, 0.0).astype(BF)
        at = k * share
        ta_ref[at : at + rows, :] = even
        ta_ref[at + rows : at + share, :] = jnp.where(upto, odd, 0.0).astype(BF)
        tb_ref[at : at + rows, :] = jnp.where(below, late, 0.0).astype(BF)
        tb_ref[at + rows : at + share, :] = even
    ca = dot(ta_ref[...], u_ref[0])
    cb = dot(tb_ref[...], u_ref[1])
    for k in range(kb):
        at = k * share
        pa, pb = ca[at : at + share], cb[at : at + share]
        c_ref[:, k * width : (k + 1) * width] = (pa + pb).astype(BF)
        c_ref[:rows, (kb + k) * width : (kb + k + 1) * width] = (pa[:rows] - pb[:rows]).astype(BF)
        c_ref[rows:, (kb + k) * width : (kb + k + 1) * width] = (pb[rows:] - pa[rows:]).astype(BF)
    wait()
    acc_ref[...] += dot(c_ref[...], w_buf[slot].reshape(2 * kb * width, width))
    fetch_last(j, steps, ar_hbm, ar_ref, ar_sem)

    @pl.when(j == steps - 1)
    def _():
        total = acc_ref[...] + dot(lag_ref[...], ar_ref[...].reshape(lag_ref.shape[1], width))
        hidden = x_ref[...] + interleave(scr, total)
        hid_ref[...] = hidden
        r2 = lax.rsqrt(jnp.mean(hidden * hidden, axis=-1, keepdims=True) + EPS)
        pos = m * share + lax.broadcasted_iota(jnp.int32, (share, 1), 0)
        mask = (pos < len_ref[0]).astype(F32)
        nt_ref[...] = (mask * hidden * r2 * gain_ref[1:2, :]).astype(BF)


def matrix_scratch(kb, ar):
    width = ar.shape[1]
    return [
        pltpu.VMEM((2, 2, kb, width, width), BF),
        pltpu.VMEM(ar.shape, BF),
        pltpu.SemaphoreType.DMA((2, 2)),
        pltpu.SemaphoreType.DMA,
    ]


def spectral_mix(lengths, taps, x, u, lags, gains, stu, ar, share, kb):
    width = x.shape[1]
    length = 2 * u.shape[1]
    filt = taps.shape[1]
    return pl.pallas_call(
        functools.partial(mix_kernel, kb, share),
        grid=(filt // kb,),
        in_specs=[smem()] + [whole()] * 5 + [outside()] * 2,
        out_specs=[whole()] * 2,
        out_shape=[
            jax.ShapeDtypeStruct((share, width), F32),
            jax.ShapeDtypeStruct((share, width), BF),
        ],
        scratch_shapes=[
            pltpu.VMEM((kb * share, length // 2), BF),
            pltpu.VMEM((kb * share, length // 2), BF),
            pltpu.VMEM((share, 2 * kb * width), BF),
            pltpu.VMEM((share, width), F32),
            pltpu.VMEM((width // 128, share, 128), F32),
        ]
        + matrix_scratch(kb, ar),
        compiler_params=params(40 << 20),
        cost_estimate=cost(2 * filt * share * width * (length + 2 * width), 2 * stu.size),
        name="spectral_mix",
    )(lengths, taps, x, u, lags, gains, stu, ar)


def ffn_kernel(
    shift, n, nt_ref, cot_ref, gw_ref, uw_ref, dw_ref, bn_ref, act_ref, bg_ref, bu_ref
):
    share = nt_ref.shape[0]
    nt = nt_ref[...]
    gate = dot(nt, gw_ref[...])
    upper = dot(nt, uw_ref[...])
    start = pl.multiple_of(lax.rem(lax.axis_index("mp") + shift, n) * share, 16)
    back_act = dot_cols(cot_ref[pl.ds(start, share), :], dw_ref[...])
    square = gate * gate
    th = jnp.tanh(SQRT_2_PI * (gate + CUBIC * square * gate))
    half = 0.5 * (1.0 + th)
    gelu = gate * half
    slope = half + 0.5 * gate * (1.0 - th * th) * (SQRT_2_PI * (1.0 + 3.0 * CUBIC * square))
    act_ref[...] = (gelu * upper).astype(BF)
    bg = (back_act * upper * slope).astype(BF)
    bu = (back_act * gelu).astype(BF)
    bg_ref[...] = bg
    bu_ref[...] = bu
    bn_ref[...] = (dot_cols(bg, gw_ref[...]) + dot_cols(bu, uw_ref[...])).astype(BF)


def feed_forward(shift, n, nt, cot, gw, uw, dw):
    share, width = nt.shape
    hid = gw.shape[1]
    return pl.pallas_call(
        functools.partial(ffn_kernel, shift, n),
        in_specs=[whole()] * 5,
        out_specs=[whole()] * 4,
        out_shape=[jax.ShapeDtypeStruct((share, width), BF)]
        + [jax.ShapeDtypeStruct((share, hid), BF)] * 3,
        compiler_params=params(),
        cost_estimate=cost(10 * share * width * hid, 2 * (3 * width * hid + 6 * share * width)),
        name="feed_forward",
    )(nt, cot, gw, uw, dw)


def ffn_grad_kernel(n, share, groups, cot_ref, dw_ref, *refs):
    nt_refs, act_refs, bg_refs, bu_refs = (refs[i * n : (i + 1) * n] for i in range(4))
    out_refs, grad_refs = refs[4 * n : 5 * n], refs[5 * n :]
    m = lax.axis_index("mp")
    nt = jnp.concatenate([ref[...] for ref in nt_refs], axis=0)
    act = jnp.concatenate([ref[...] for ref in act_refs], axis=0)
    bg = jnp.concatenate([ref[...] for ref in bg_refs], axis=0)
    bu = jnp.concatenate([ref[...] for ref in bu_refs], axis=0)
    cot = jnp.concatenate(
        [
            cot_ref[pl.ds(pl.multiple_of(lax.rem(m + r, n) * share, 16), share), :]
            for r in range(n)
        ],
        axis=0,
    )
    outs = dot(act, dw_ref[...]).astype(BF)
    for r in range(n):
        out_refs[r][...] = outs[r * share : (r + 1) * share, :]
    nt_t = nt.T
    grads = (dot(nt_t, bg), dot(nt_t, bu), dot(act.T, cot))
    if not groups:
        for ref, grad in zip(grad_refs, grads):
            ref[...] = grad.astype(BF)
        return
    keep_ref, send_ref, scr = grad_refs
    for i in range(3):
        scr[i] = grads[i].astype(BF)
    rows = scr.shape[1] // (2 * groups)
    d = lax.axis_index("dp")
    core = lax.rem(d, 2)
    for r in range(groups):
        chip = ((d // 2) ^ r) * 2
        for i in range(3):
            mine = pl.multiple_of((chip + core) * rows, 16)
            other = pl.multiple_of((chip + 1 - core) * rows, 16)
            keep_ref[r, i] = scr[i, pl.ds(mine, rows), :]
            send_ref[r, i] = scr[i, pl.ds(other, rows), :]


def ffn_grads(cot, dw, nts, acts, bgs, bus, groups):
    n = len(nts)
    share, width = nts[0].shape
    hid = dw.shape[0]
    length = cot.shape[0]
    out_shape = [jax.ShapeDtypeStruct((share, width), BF)] * n
    scratch = []
    if groups:
        part = (groups, 3, width // (2 * groups), width)
        out_shape += [jax.ShapeDtypeStruct(part, BF)] * 2
        scratch = [pltpu.VMEM((3, width, width), BF)]
    else:
        out_shape += [
            jax.ShapeDtypeStruct((width, hid), BF),
            jax.ShapeDtypeStruct((width, hid), BF),
            jax.ShapeDtypeStruct((hid, width), BF),
        ]
    args = [cot, dw, *nts, *acts, *bgs, *bus]
    return pl.pallas_call(
        functools.partial(ffn_grad_kernel, n, share, groups),
        in_specs=[whole()] * len(args),
        out_specs=[whole()] * len(out_shape),
        out_shape=out_shape,
        scratch_shapes=scratch,
        compiler_params=params(),
        cost_estimate=cost(8 * length * width * hid, 12 * length * width),
        name="ffn_grads",
    )(*args)


def mid_kernel(n, share, len_ref, hid_ref, cot_ref, gain_ref, *refs):
    bn_refs, (bh_ref, b_ref, gg_ref) = refs[:n], refs[n:]
    m = lax.axis_index("mp")
    bn = bn_refs[0][...].astype(F32)
    for ref in bn_refs[1:]:
        bn = bn + ref[...].astype(F32)
    hidden = hid_ref[...]
    r2 = lax.rsqrt(jnp.mean(hidden * hidden, axis=-1, keepdims=True) + EPS)
    pos = m * share + lax.broadcasted_iota(jnp.int32, (share, 1), 0)
    bn = bn * (pos < len_ref[0]).astype(F32)
    z = hidden * r2
    gg_ref[...] = jnp.broadcast_to(jnp.sum(bn * z, axis=0, keepdims=True), gg_ref.shape)
    q = bn * gain_ref[1:2, :]
    start = pl.multiple_of(m * share, 16)
    dout = cot_ref[pl.ds(start, share), :].astype(F32)
    back = dout + r2 * (q - z * jnp.mean(q * z, axis=-1, keepdims=True))
    bh_ref[...] = back
    b_ref[...] = back.astype(BF)


def mid_norm(lengths, hidden, cot, gain, pieces):
    share, width = hidden.shape
    n = len(pieces)
    return pl.pallas_call(
        functools.partial(mid_kernel, n, share),
        in_specs=[smem()] + [whole()] * (3 + n),
        out_specs=[whole()] * 3,
        out_shape=[
            jax.ShapeDtypeStruct(hidden.shape, F32),
            jax.ShapeDtypeStruct(hidden.shape, BF),
            jax.ShapeDtypeStruct((8, width), F32),
        ],
        compiler_params=params(),
        cost_estimate=cost(20 * hidden.size, 20 * hidden.size),
        name="second_norm_back",
    )(lengths, hidden, cot, gain, *pieces)


def unmix_kernel(
    kb, share, n, len_ref, taps_ref, x_ref, bh_ref, gg_ref, gain_ref, stu_hbm, ar_hbm, *refs
):
    b_refs, (ig_ref, gain_out) = refs[:n], refs[n : n + 2]
    ta_ref, tb_ref, be_ref, bo_ref, lag_ref, acc_ref, scr = refs[n + 2 : n + 9]
    w_buf, ar_ref, sems, ar_sem = refs[n + 9 :]
    j, steps = pl.program_id(0), pl.num_programs(0)
    width = bh_ref.shape[1]
    length = n * share
    half, rows = length // 2, share // 2
    m = lax.axis_index("mp")
    b = lax.broadcasted_iota(jnp.int32, (rows, half), 0)
    a = lax.broadcasted_iota(jnp.int32, (rows, half), 1)
    inside = a < (length - m * share) // 2
    upto = (a >= b) & inside
    below = (a > b) & inside
    slot, wait = fetch_matrices(j, stu_hbm.shape[0] // (2 * kb), kb, stu_hbm, w_buf, sems)

    @pl.when(j == 0)
    def _():
        for r in reversed(range(n)):
            put_columns(scr, b_refs[r][...].astype(F32))
            be_ref[r * rows : (r + 1) * rows, :] = every_second(scr, 0, rows).astype(BF)
            bo_ref[r * rows : (r + 1) * rows, :] = every_second(scr, 1, rows).astype(BF)
        more = b_refs[1 % n][:16, :].astype(F32) * jnp.where(m == n - 1, 0.0, 1.0)
        put_columns(scr, more, share)
        order = lag_ref.shape[1] // width
        for lag in range(order):
            for odd in range(2):
                lag_ref[odd * rows : (odd + 1) * rows, lag * width : (lag + 1) * width] = (
                    every_second(scr, odd + lag, rows).astype(BF)
                )
        acc_ref[...] = jnp.zeros((share, width), F32)

    for k in range(kb):
        even = toeplitz(taps_ref[3, pl.ds(j * kb + k, 1), :], rows)
        odd = toeplitz(taps_ref[4, pl.ds(j * kb + k, 1), :], rows)
        late = toeplitz(taps_ref[5, pl.ds(j * kb + k, 1), :], rows)
        even = jnp.where(upto, even, 0.0).astype(BF)
        at = k * share
        ta_ref[at : at + rows, :] = even
        ta_ref[at + rows : at + share, :] = jnp.where(below, late, 0.0).astype(BF)
        tb_ref[at : at + rows, :] = jnp.where(upto, odd, 0.0).astype(BF)
        tb_ref[at + rows : at + share, :] = even
    ca = dot(ta_ref[...], be_ref[...])
    cb = dot(tb_ref[...], bo_ref[...])
    wait()
    total = acc_ref[...]
    for k in range(kb):
        at = k * share
        pa, pb = ca[at : at + share], cb[at : at + share]
        minus = jnp.concatenate([pa[:rows] - pb[:rows], pb[rows:] - pa[rows:]], axis=0)
        total = total + dot_cols((pa + pb).astype(BF), w_buf[slot, 0, k])
        total = total + dot_cols(minus.astype(BF), w_buf[slot, 1, k])
    acc_ref[...] = total
    fetch_last(j, steps, ar_hbm, ar_ref, ar_sem)

    @pl.when(j == steps - 1)
    def _():
        total = acc_ref[...]
        for lag in range(ar_ref.shape[0]):
            total = total + dot_cols(lag_ref[:, lag * width : (lag + 1) * width], ar_ref[lag])
        x = x_ref[...]
        r1 = lax.rsqrt(jnp.mean(x * x, axis=-1, keepdims=True) + EPS)
        pos = m * share + lax.broadcasted_iota(jnp.int32, (share, 1), 0)
        masked = interleave(scr, total) * (pos < len_ref[0]).astype(F32)
        y = x * r1
        p = masked * gain_ref[0:1, :]
        ig = bh_ref[...] + r1 * (p - y * jnp.mean(p * y, axis=-1, keepdims=True))
        ig_ref[...] = ig.astype(BF)
        gain_out[0:8, :] = jnp.broadcast_to(jnp.sum(masked * y, axis=0, keepdims=True), (8, width))
        gain_out[8:16, :] = gg_ref[...]


def spectral_unmix(lengths, taps, x, back_hidden, gg, gains, stu, ar, pieces, kb):
    share, width = back_hidden.shape
    n = len(pieces)
    length = n * share
    count = taps.shape[1]
    return pl.pallas_call(
        functools.partial(unmix_kernel, kb, share, n),
        grid=(count // kb,),
        in_specs=[smem()] + [whole()] * 5 + [outside()] * 2 + [whole()] * n,
        out_specs=[whole()] * 2,
        out_shape=[
            jax.ShapeDtypeStruct((share, width), BF),
            jax.ShapeDtypeStruct((16, width), F32),
        ],
        scratch_shapes=[
            pltpu.VMEM((kb * share, length // 2), BF),
            pltpu.VMEM((kb * share, length // 2), BF),
            pltpu.VMEM((length // 2, width), BF),
            pltpu.VMEM((length // 2, width), BF),
            pltpu.VMEM((share, ar.shape[0] * width), BF),
            pltpu.VMEM((share, width), F32),
            pltpu.VMEM((width // 128, share + 16, 128), F32),
        ]
        + matrix_scratch(kb, ar),
        compiler_params=params(30 << 20),
        cost_estimate=cost(2 * count * share * width * (length + 2 * width), 2 * stu.size),
        name="spectral_unmix",
    )(lengths, taps, x, back_hidden, gg, gains, stu, ar, *pieces)


def conv_kernel(groups, tile, own, filt_ref, *refs):
    ut_refs, (conv_ref, tt_ref, ut_scr) = refs[:groups], refs[groups:]
    j = pl.program_id(0)
    filt, length = filt_ref.shape
    block = conv_ref.shape[1]
    count = length // tile
    chip = lax.axis_index("dp") // 2

    @pl.when(j == 0)
    def _():
        start = pl.multiple_of(chip * block, 16)
        for r in range(groups):
            ut_scr[r * block : (r + 1) * block, :] = ut_refs[r][pl.ds(start, block), :]

    which = lax.axis_index("mp") * own + j
    strip = toeplitz(filt_ref[pl.ds(lax.rem(which, filt), 1), :], tile)
    row = lax.broadcasted_iota(jnp.int32, (tile, length), 0)
    col = lax.broadcasted_iota(jnp.int32, (tile, length), 1)
    flip = ((col - row) % 2 == 1) & (which >= filt)
    strip = jnp.where(col >= row, jnp.where(flip, -strip, strip), 0.0).astype(BF)
    for b in range(count):
        tt_ref[b * tile : (b + 1) * tile, b * tile :] = strip[:, : length - b * tile]
    for c in range(count):
        end = (c + 1) * tile
        part = dot(ut_scr[:, :end], tt_ref[:end, c * tile : end]).astype(BF)
        for r in range(groups):
            start = pl.multiple_of((lax.rem(chip, groups) ^ r) * length + c * tile, 128)
            conv_ref[0, :, pl.ds(start, tile)] = part[r * block : (r + 1) * block, :]


def convolutions(filt, uts, own, chips):
    length = filt.shape[1]
    groups = len(uts)
    block = uts[0].shape[0] // chips
    tile = 256 if length % 256 == 0 else length
    return pl.pallas_call(
        functools.partial(conv_kernel, groups, tile, own),
        grid=(own,),
        in_specs=[whole()] * (1 + groups),
        out_specs=pl.BlockSpec((1, block, groups * length), lambda j: (j, 0, 0)),
        out_shape=jax.ShapeDtypeStruct((own, block, groups * length), BF),
        scratch_shapes=[
            pltpu.VMEM((length, length), BF),
            pltpu.VMEM((groups * block, length), BF),
        ],
        compiler_params=params(),
        cost_estimate=cost(
            4 * own * groups * block * length * length // 3, 2 * own * groups * block * length
        ),
        name="convolutions",
    )(filt, *uts)


def lag_kernel(groups, *refs):
    ut_refs, out_refs = refs[:groups], refs[groups:]
    width, length = ut_refs[0].shape
    chip = lax.rem(lax.axis_index("dp") // 2, groups)
    col = lax.broadcasted_iota(jnp.int32, (width, length), 1)
    for r in range(groups):
        start = pl.multiple_of((chip ^ r) * length, 128)
        out_refs[0][:, pl.ds(start, length)] = ut_refs[r][...]
        value = ut_refs[r][...].astype(F32)
        for lag in range(1, len(out_refs)):
            moved = pltpu.roll(value, lag, 1)
            out_refs[lag][:, pl.ds(start, length)] = jnp.where(col >= lag, moved, 0.0).astype(BF)


def lagged(uts, order):
    groups = len(uts)
    width, length = uts[0].shape
    shape = jax.ShapeDtypeStruct((width, groups * length), BF)
    return pl.pallas_call(
        functools.partial(lag_kernel, groups),
        in_specs=[whole()] * groups,
        out_specs=[whole()] * order,
        out_shape=[shape] * order,
        compiler_params=params(),
        cost_estimate=cost(order * groups * width * length, 4 * order * groups * width * length),
        name="lagged",
    )(*uts)


def grads_kernel(steps, order, groups, rows, conv_ref, *refs):
    lag_refs, b_refs = refs[:order], refs[order : order + len(rows)]
    keep_ref, send_ref, b_scr, scr = refs[order + len(rows) :]
    g = pl.program_id(0)
    d = lax.axis_index("dp")
    chip, core = lax.rem(d // 2, groups), lax.rem(d, 2)
    step, block, depth = conv_ref.shape
    width, length = b_scr.shape[1], depth // groups
    half = block // 2

    @pl.when(g == 0)
    def _():
        for ref, (r, at, size) in zip(b_refs, rows):
            start = pl.multiple_of((chip ^ r) * length + at, 16)
            b_scr[pl.ds(start, size), :] = ref[:size, :]

    @pl.when(g < steps)
    def _():
        part = dot(conv_ref[...].reshape(step * block, depth), b_scr[...])
        scr[...] = part.reshape(step, block, width)
        mine = pl.multiple_of(core * half, 16)
        other = pl.multiple_of((1 - core) * half, 16)
        keep_ref[pl.ds(g * step, step)] = scr[:, pl.ds(mine, half), :]
        for k in range(step):
            start = pl.multiple_of((g * step + k) * half, 16)
            send_ref[pl.ds(start, half), :] = scr[k, pl.ds(other, half), :].astype(BF)

    for lag in range(order):

        @pl.when(g == steps + lag)
        def _():
            at = steps * step * half + lag * width
            send_ref[at : at + width, :] = dot(lag_refs[lag][...], b_scr[...]).astype(BF)


def matrix_grads(conv, lags, backs, rows):
    own, block, depth = conv.shape
    order, width = len(lags), lags[0].shape[0]
    groups = 1 + max(r for r, _, _ in rows)
    step = next(s for s in (4, 3, 2, 1) if own % s == 0)
    steps = own // step
    half = block // 2
    return pl.pallas_call(
        functools.partial(grads_kernel, steps, order, groups, rows),
        grid=(steps + order,),
        in_specs=[pl.BlockSpec((step, block, depth), lambda g: (jnp.minimum(g, steps - 1), 0, 0))]
        + [whole()] * (order + len(backs)),
        out_specs=[whole()] * 2,
        out_shape=[
            jax.ShapeDtypeStruct((own, half, width), F32),
            jax.ShapeDtypeStruct((own * half + order * width, width), BF),
        ],
        scratch_shapes=[
            pltpu.VMEM((depth, width), BF),
            pltpu.VMEM((step, block, width), F32),
        ],
        compiler_params=params(),
        cost_estimate=cost(2 * (conv.size + order * width * depth) * width, 2 * conv.size),
        name="matrix_grads",
    )(conv, *lags, *backs)


def rows_message_kernel(ig_ref, hid_ref, *refs):
    share = ig_ref.shape[0]
    total = hid_ref[...]
    for ref in refs[:-1]:
        total = total + ref[...].astype(F32)
    refs[-1][:share, :] = ig_ref[...]
    refs[-1][share:, :] = total.astype(BF)


def rows_message(ig, hidden, pieces):
    share, width = ig.shape
    return pl.pallas_call(
        rows_message_kernel,
        in_specs=[whole()] * (2 + len(pieces)),
        out_specs=whole(),
        out_shape=jax.ShapeDtypeStruct((2 * share, width), BF),
        compiler_params=params(),
        cost_estimate=cost(4 * ig.size, 10 * ig.size),
        name="rows_message",
    )(ig, hidden, *pieces)


def finish_rows_kernel(n, share, *refs):
    pieces, (ig_ref, out_ref) = refs[:n], refs[n:]
    m = lax.axis_index("mp")
    for r in range(n):
        start = pl.multiple_of(lax.rem(m + r, n) * share, 16)
        ig_ref[pl.ds(start, share), :] = pieces[r][:share, :].astype(F32)
        out_ref[pl.ds(start, share), :] = pieces[r][share:, :]


def finish_rows(pieces):
    n = len(pieces)
    share, width = pieces[0].shape[0] // 2, pieces[0].shape[1]
    return pl.pallas_call(
        functools.partial(finish_rows_kernel, n, share),
        in_specs=[whole()] * n,
        out_specs=[whole()] * 2,
        out_shape=[
            jax.ShapeDtypeStruct((n * share, width), F32),
            jax.ShapeDtypeStruct((n * share, width), BF),
        ],
        compiler_params=params(),
        cost_estimate=cost(n * share * width, 6 * n * share * width),
        name="finish_rows",
    )(*pieces)


def ordered_sum_kernel(n, axis, step, *refs):
    pieces, (out_ref, scr) = refs[:n], refs[n:]
    me = lax.axis_index(axis)
    for r in range(n):
        who = lax.rem(me + r, n) if step == 0 else (me // step) ^ r
        scr[who] = pieces[r][...]
    total = scr[0]
    for r in range(1, n):
        total = total + scr[r]
    out_ref[...] = total


def ordered_sum(pieces, axis, step):
    n = len(pieces)
    shape = pieces[0].shape
    return pl.pallas_call(
        functools.partial(ordered_sum_kernel, n, axis, step),
        in_specs=[whole()] * n,
        out_specs=whole(),
        out_shape=jax.ShapeDtypeStruct(shape, F32),
        scratch_shapes=[pltpu.VMEM((n,) + shape, F32)],
        compiler_params=params(),
        cost_estimate=cost(n * pieces[0].size, 4 * n * pieces[0].size),
        name="ordered_sum",
    )(*pieces)


def halve_kernel(kept, sent, keep_ref, recv_ref, *out_refs):
    rows = recv_ref.shape[0] // keep_ref.shape[0]
    total = keep_ref[...].astype(F32) + recv_ref[...].astype(F32)
    for ref, which in zip(out_refs, (kept, sent)):
        for k, r in enumerate(which):
            ref[k] = total[r].astype(BF)


def halve(keep, recv, kept, sent):
    part = keep.shape[1:]
    return pl.pallas_call(
        functools.partial(halve_kernel, kept, sent),
        in_specs=[whole()] * 2,
        out_specs=[whole()] * 2,
        out_shape=[jax.ShapeDtypeStruct((len(w),) + part, BF) for w in (kept, sent)],
        compiler_params=params(),
        cost_estimate=cost(keep.size, 8 * keep.size),
        name="halve",
    )(keep, recv)


def pack_kernel(n, share, extra, *refs):
    pieces, rest = refs[:n], refs[n:]
    m = lax.axis_index("mp")
    out_refs = rest[1:] if extra else rest
    for r in range(n):
        start = pl.multiple_of(lax.rem(m + r, n) * share, 16)
        for ref in out_refs:
            ref[pl.ds(start, share), :] = pieces[r][...]
    if extra:
        rows = rest[0].shape[1]
        for k in range(rest[0].shape[0]):
            at = n * share + k * rows
            out_refs[1][at : at + rows, :] = rest[0][k]


def pack_rows(pieces, extra=None):
    n = len(pieces)
    share, width = pieces[0].shape
    shapes = [(n * share, width)]
    if extra is not None:
        shapes.append((n * share + extra.shape[0] * extra.shape[1], width))
    args = list(pieces) + ([] if extra is None else [extra])
    return pl.pallas_call(
        functools.partial(pack_kernel, n, share, extra is not None),
        in_specs=[whole()] * len(args),
        out_specs=[whole()] * len(shapes),
        out_shape=[jax.ShapeDtypeStruct(shape, BF) for shape in shapes],
        compiler_params=params(),
        cost_estimate=cost(n * share * width, 6 * n * share * width),
        name="pack_rows",
    )(*args)


def turn_kernel(keep_ref, x_ref, y_ref, keep_out, to_y, to_x):
    length = y_ref.shape[0]
    half, rows = length // 2, keep_ref.shape[1]
    keep_out[...] = keep_ref[0].astype(F32) + x_ref[length : length + rows, :].astype(F32)
    sent = keep_ref[1].astype(F32) + x_ref[length + rows :, :].astype(F32)
    to_y[:half, :] = x_ref[:half, :]
    to_y[half:, :] = sent.astype(BF)
    to_x[...] = y_ref[half:, :]


def turn(keep, over_x, over_y):
    length, width = over_y.shape
    rows = keep.shape[1]
    return pl.pallas_call(
        turn_kernel,
        in_specs=[whole()] * 3,
        out_specs=[whole()] * 3,
        out_shape=[
            jax.ShapeDtypeStruct((rows, width), F32),
            jax.ShapeDtypeStruct((length // 2 + rows, width), BF),
            jax.ShapeDtypeStruct((length // 2, width), BF),
        ],
        compiler_params=params(),
        cost_estimate=cost(over_x.size, 8 * over_x.size),
        name="turn",
    )(keep, over_x, over_y)


def split_gains(both):
    high = both.astype(BF)
    low = (both - high.astype(F32)).astype(BF)
    return jnp.concatenate([high, low], axis=0)


def joined(gains):
    return gains[:16].astype(F32) + gains[16:].astype(F32)


def last_sum_kernel(keep_ref, recv_ref, gain_ref, out_ref):
    rows = keep_ref.shape[0]
    at = recv_ref.shape[0] - rows
    out_ref[:rows, :] = (keep_ref[...] + recv_ref[at:, :].astype(F32)).astype(BF)
    out_ref[rows:, :] = split_gains(gain_ref[...])


def last_sum(keep, recv, gains):
    rows, width = keep.shape
    return pl.pallas_call(
        last_sum_kernel,
        in_specs=[whole()] * 3,
        out_specs=whole(),
        out_shape=jax.ShapeDtypeStruct((rows + 32, width), BF),
        compiler_params=params(),
        cost_estimate=cost(keep.size, 8 * keep.size),
        name="last_sum",
    )(keep, recv, gains)


def pair_kernel(own_ref, recv_ref, out_ref):
    rows = own_ref.shape[0] - 32
    out_ref[:rows, :] = own_ref[:rows, :]
    out_ref[rows : 2 * rows, :] = recv_ref[:rows, :]
    out_ref[2 * rows :, :] = split_gains(joined(own_ref[rows:, :]) + joined(recv_ref[rows:, :]))


def pair_up(own, recv):
    rows, width = own.shape[0] - 32, own.shape[1]
    return pl.pallas_call(
        pair_kernel,
        in_specs=[whole()] * 2,
        out_specs=whole(),
        out_shape=jax.ShapeDtypeStruct((2 * rows + 32, width), BF),
        compiler_params=params(),
        cost_estimate=cost(own.size, 8 * own.size),
        name="pair_up",
    )(own, recv)


def join_kernel(*refs):
    at = 0
    for ref in refs[:-1]:
        refs[-1][at : at + ref.shape[0], :] = ref[...]
        at += ref.shape[0]


def join_pieces(pieces):
    rows = sum(p.shape[0] for p in pieces)
    return pl.pallas_call(
        join_kernel,
        in_specs=[whole()] * len(pieces),
        out_specs=whole(),
        out_shape=jax.ShapeDtypeStruct((rows, pieces[0].shape[1]), pieces[0].dtype),
        compiler_params=params(),
        cost_estimate=cost(rows * pieces[0].shape[1], 4 * rows * pieces[0].shape[1]),
        name="join_pieces",
    )(*pieces)


def finish_kernel(chips, keep_ref, send_ref, recv_ref, stu_ref, ar_ref, *more_refs):
    own, half, width = keep_ref.shape
    d = lax.axis_index("dp")
    core = lax.rem(d, 2)
    w_refs = more_refs[1:]
    groups, count = len(chips), len(w_refs)
    rows = width // (2 * groups) if groups else 0
    base = groups * count * rows
    if groups:
        gains = slice(base, base + 32)
        more_refs[0][...] = joined(send_ref[gains, :]) + joined(recv_ref[gains, :])
        base += 32
    for r in range(groups):
        chip = ((d // 2) ^ r) * 2
        for ref, which in ((send_ref, chip + core), (recv_ref, chip + 1 - core)):
            start = pl.multiple_of(which * rows, 16)
            for i, out in enumerate(w_refs):
                at = (chips[r] * count + i) * rows
                out[pl.ds(start, rows), :] = ref[at : at + rows, :].astype(F32)
    for k in range(own):
        at = base + k * half
        stu_ref[k] = keep_ref[k] + recv_ref[at : at + half, :].astype(F32)
    for i in range(ar_ref.shape[0]):
        at = base + own * half + i * width
        ar_ref[i] = send_ref[at : at + width, :].astype(F32) + recv_ref[
            at : at + width, :
        ].astype(F32)


def finish(keep, send, recv, order, chips):
    width = keep.shape[2]
    more = [jax.ShapeDtypeStruct((16, width), F32)] if chips else []
    more += [jax.ShapeDtypeStruct((width, width), F32)] * (3 if chips else 0)
    return pl.pallas_call(
        functools.partial(finish_kernel, chips),
        in_specs=[whole()] * 3,
        out_specs=[whole()] * (2 + len(more)),
        out_shape=[
            jax.ShapeDtypeStruct(keep.shape, F32),
            jax.ShapeDtypeStruct((order, width, width), F32),
        ]
        + more,
        compiler_params=params(),
        cost_estimate=cost(keep.size, 10 * keep.size),
        name="finish",
    )(keep, send, recv)


def fetch_shifted(value, axis, n):
    return [value] + [
        lax.ppermute(value, axis, [(i, (i - r) % n) for i in range(n)]) for r in range(1, n)
    ]


def send_shifted(pieces, axis):
    n = len(pieces)
    return [pieces[0]] + [
        lax.ppermute(pieces[r], axis, [(i, (i + r) % n) for i in range(n)]) for r in range(1, n)
    ]


def swap(value, axis, n, bits):
    return lax.ppermute(value, axis, [(i, i ^ bits) for i in range(n)])


def merge_rows(value):
    return value.reshape(value.shape[0], -1, value.shape[-1])


def after(values, first):
    flat, tree = jax.tree.flatten(values)
    out = lax.optimization_barrier((*flat, *jax.tree.leaves(first)))
    return jax.tree.unflatten(tree, out[: len(flat)])


def shards(
    inputs, lengths, filters, first_gain, stu_weight, ar_weight, second_gain,
    gate_weight, up_weight, down_weight, cotangent,
):
    n = lax.axis_size("mp")
    n_dp = lax.axis_size("dp")
    groups = n_dp // 2
    length, width = inputs.shape
    share = length // n
    order = ar_weight.shape[0]
    own = stu_weight.shape[0] // n
    lengths = lengths.astype(jnp.int32)
    both_gains = jnp.stack([first_gain, second_gain])

    u, ut, x_own, u_lags = first_norm(lengths, inputs, both_gains, n, order)
    taps, natural = filter_taps(filters.T)
    uts = [ut] + [swap(ut, "dp", n_dp, 2 * r) for r in range(1, 3)]
    hidden, nt = spectral_mix(
        lengths, taps, x_own, u, u_lags, both_gains, stu_weight, ar_weight, share, 4
    )
    nts = fetch_shifted(nt, "mp", n)
    weights = (cotangent, gate_weight, up_weight, down_weight)
    parts = {0: feed_forward(0, n, after(nt, uts[1:3]), *weights)}
    last = 0
    for r in sorted(range(1, n), key=lambda r: min(r, n - r)):
        first = parts[last][0]
        parts[r] = feed_forward(r, n, after(nts[r], first), *weights)
        last = r
    uts += [swap(after(ut, nt), "dp", n_dp, 2 * r) for r in range(3, groups)]
    parts = [parts[r] for r in range(n)]
    bns = send_shifted([p[0] for p in parts], "mp")
    acts, bgs, bus = ([p[i] for p in parts] for i in (1, 2, 3))
    custom = n_dp == 8 and gate_weight.shape[1] == width
    grads = ffn_grads(cotangent, down_weight, nts, acts, bgs, bus, groups if custom else 0)
    out_parts, grads = grads[:n], grads[n:]
    bns = [bns[0]] + after(bns[1:], grads[0])
    back_hidden, back_rows, second_part = mid_norm(lengths, hidden, cotangent, both_gains, bns)
    backs = fetch_shifted(back_rows, "mp", n)
    uts = after(uts, back_rows)
    conv = [convolutions(natural, uts[r : r + 4], own, groups) for r in range(0, groups, 4)]
    lags = [lagged(uts[r : r + 4], order) for r in range(0, groups, 4)]
    backs = after(backs, (conv, lags))
    if custom:
        w_keep, w_send = grads
        w_send = swap(after(w_send, back_rows), "dp", n_dp, 1)
        w_keep, w_send = halve(w_keep, w_send, (0, 2), (1, 3))
        own_back, to_x = pack_rows(backs, merge_rows(w_send))
        over_x, over_y = swap(to_x, "dp", n_dp, 2), swap(own_back, "dp", n_dp, 4)
    else:
        (own_back,) = pack_rows(backs)
    out_sums = send_shifted(after(out_parts, own_back), "mp")
    ig, gains = spectral_unmix(
        lengths, taps, x_own, back_hidden, second_part, both_gains, stu_weight, ar_weight, backs, 4
    )
    conv, hidden = after((conv, hidden), ig)
    message = rows_message(ig, hidden, out_sums)
    gains = ordered_sum(fetch_shifted(after(gains, message), "mp", n), "mp", 0)
    message = after(message, gains)
    messages = fetch_shifted(message, "mp", n)
    if custom:
        w_keep, to_y, to_x = turn(merge_rows(w_keep), after(over_x, message), over_y)
        from_y, from_x = swap(to_y, "dp", n_dp, 4), swap(to_x, "dp", n_dp, 2)
        all_backs = [own_back, over_x, over_y, from_y, from_x]
        half = length // 2
        rows = ((0, 0, length), (1, 0, length), (2, 0, length), (3, 0, half), (3, half, half))
        w_sum = last_sum(w_keep, from_y, gains)
        conv = after(conv, w_sum)
    else:
        all_backs = [own_back] + [swap(own_back, "dp", n_dp, 2 * r) for r in range(1, groups)]
        rows = tuple((r, 0, length) for r in range(min(groups, 4)))

    conv = after(conv, (message, messages[n // 2]))
    if len(conv) == 1:
        keep, send = matrix_grads(conv[0], lags[0], all_backs, rows)
    else:
        some = [
            matrix_grads(c, lags[k], all_backs[4 * k : 4 * k + 4], rows)
            for k, c in enumerate(conv)
        ]
        keep = ordered_sum([k for k, _ in some], "dp", 8)
        send = ordered_sum([k.astype(F32) for _, k in some], "dp", 8).astype(BF)
    input_grad, output = finish_rows(after(messages, (gains, send)))
    if custom:
        w_pair = pair_up(w_sum, swap(w_sum, "dp", n_dp, 4))
        w_all = pair_up(w_pair, after(swap(w_pair, "dp", n_dp, 2), messages))
        send = join_pieces([w_all, send])
    recv = after(swap(send, "dp", n_dp, 1), output)
    stu_grad, ar_grad, *more = finish(keep, send, recv, order, (0, 2, 1, 3) if custom else ())
    if custom:
        gains, gate_grad, up_grad, down_grad = more
    else:
        gains = ordered_sum([gains] + [swap(gains, "dp", n_dp, r) for r in range(1, n_dp)], "dp", 1)
        gate_grad, up_grad, down_grad = (g.astype(F32) for g in lax.psum(tuple(grads), "dp"))
    return (
        output, input_grad, stu_grad, ar_grad, gains[0], gains[8], gate_grad, up_grad, down_grad,
    )


def solution(mesh):
    in_specs = (
        P("dp", None), P("dp"), P(), P(), P(), P(), P(),
        P(None, "mp"), P(None, "mp"), P("mp", None), P("dp", None),
    )
    out_specs = (
        P("dp", None), P("dp", None), P("mp", "dp", None), P(), P(), P(),
        P(None, "mp"), P(None, "mp"), P("mp", None),
    )
    return jax.shard_map(shards, mesh=mesh, in_specs=in_specs, out_specs=out_specs, check_vma=False)
```

```python
import functools

import jax
import jax.numpy as jnp
from jax import lax
from jax.experimental import pallas as pl
from jax.experimental.pallas import tpu as pltpu
from jax.sharding import PartitionSpec as P

EPS = 1e-05
BF = jnp.bfloat16
F32 = jnp.float32
SQRT_2_PI = 0.7978845608028654
CUBIC = 0.044715
VMEM_LIMIT = 20 << 20


def dot(left, right):
    return jnp.dot(left, right, preferred_element_type=F32)


def dot_cols(left, right):
    return lax.dot_general(left, right, (((1,), (1,)), ((), ())), preferred_element_type=F32)


def params(limit=VMEM_LIMIT):
    return pltpu.CompilerParams(vmem_limit_bytes=limit)


COST_SCALE = 1.0


def cost(flops, nbytes):
    return pl.CostEstimate(
        flops=int(COST_SCALE * flops), bytes_accessed=int(COST_SCALE * nbytes), transcendentals=0
    )


def smem():
    return pl.BlockSpec(memory_space=pltpu.SMEM)


def whole():
    return pl.BlockSpec(memory_space=pltpu.VMEM)


def outside():
    return pl.BlockSpec(memory_space=pltpu.HBM)


def toeplitz(base_row, rows):
    wide = jnp.broadcast_to(base_row, (rows, base_row.shape[1]))
    return pltpu.roll(wide, 0, 1, stride=1, stride_axis=0)


def put_columns(scr, value, at=0):
    for c in range(scr.shape[0]):
        scr[c, at : at + value.shape[0], :] = value[:, c * 128 : (c + 1) * 128]


def every_second(scr, start, count):
    columns = [scr[c, pl.ds(start, count, stride=2), :] for c in range(scr.shape[0])]
    return columns[0] if len(columns) == 1 else jnp.concatenate(columns, axis=1)


def interleave(scr, value):
    half = value.shape[0] // 2
    for c in range(scr.shape[0]):
        columns = slice(c * 128, (c + 1) * 128)
        scr[c, pl.ds(0, half, stride=2), :] = value[:half, columns]
        scr[c, pl.ds(1, half, stride=2), :] = value[half:, columns]
    count = value.shape[0]
    return jnp.concatenate([scr[c, :count, :] for c in range(scr.shape[0])], axis=1)


def norm_kernel(
    n, share, order, len_ref, x_ref, gain_ref, filt_ref,
    u_ref, ut_ref, own_ref, lag_ref, taps_ref, nat_ref, scr, scr_f,
):
    length, width = x_ref.shape
    m = lax.axis_index("mp")
    filt = nat_ref.shape[0]
    x = x_ref[...].astype(F32)
    r1 = lax.rsqrt(jnp.mean(x * x, axis=-1, keepdims=True) + EPS)
    row = lax.broadcasted_iota(jnp.int32, (length, 1), 0)
    mask = (row < len_ref[0]).astype(F32)
    u = mask * x * r1 * gain_ref[0:1, :]
    scr[:, :8, :] = jnp.zeros((scr.shape[0], 8, 128), F32)
    put_columns(scr, u, 8)
    ut_ref[...] = u.T.astype(BF)
    own_ref[...] = x_ref[pl.ds(pl.multiple_of(m * share, 16), share), :].astype(F32)
    for r in range(n):
        start = lax.rem(m + r, n) * share
        for odd in range(2):
            u_ref[odd, r * (share // 2) : (r + 1) * (share // 2), :] = every_second(
                scr, start + odd + 8, share // 2
            ).astype(BF)
    for lag in range(order):
        for odd in range(2):
            at = lag * width
            lag_ref[odd * (share // 2) : (odd + 1) * (share // 2), at : at + width] = every_second(
                scr, m * share + odd + 8 - lag, share // 2
            ).astype(BF)
    half = length // 2
    natural = filt_ref[...].astype(F32)
    nat_ref[...] = natural
    scr_f[0, :, :filt] = natural.T
    even = every_second(scr_f, 0, half).T[:filt]
    odd = every_second(scr_f, 1, half).T[:filt]
    i = lax.broadcasted_iota(jnp.int32, (half, half), 0)
    j = lax.broadcasted_iota(jnp.int32, (half, half), 1)
    flip = (i == jnp.where(j == 0, 0, half - j)).astype(F32).astype(BF)
    rev_even = dot(even.astype(BF), flip)
    rev_odd = dot(odd.astype(BF), flip)
    taps_ref[0] = rev_even
    taps_ref[1] = rev_odd
    taps_ref[2] = pltpu.roll(rev_odd, half - 1, 1)
    taps_ref[3] = even
    taps_ref[4] = odd
    taps_ref[5] = pltpu.roll(odd, 1, 1)


def first_norm(lengths, x, gains, filters, n, order):
    length, width = x.shape
    share = length // n
    filt = filters.shape[0]
    return pl.pallas_call(
        functools.partial(norm_kernel, n, share, order),
        in_specs=[smem()] + [whole()] * 3,
        out_specs=[whole()] * 6,
        out_shape=[
            jax.ShapeDtypeStruct((2, length // 2, width), BF),
            jax.ShapeDtypeStruct((width, length), BF),
            jax.ShapeDtypeStruct((share, width), F32),
            jax.ShapeDtypeStruct((share, order * width), BF),
            jax.ShapeDtypeStruct((6, filt, length // 2), F32),
            jax.ShapeDtypeStruct((filt, length), F32),
        ],
        scratch_shapes=[
            pltpu.VMEM((width // 128, length + 8, 128), F32),
            pltpu.VMEM((1, length, 128), F32),
        ],
        compiler_params=params(),
        cost_estimate=cost(10 * x.size, 6 * x.size),
        name="first_norm",
    )(lengths, x, gains, filters)


def fetch_matrices(j, steps, kb, stu_hbm, w_buf, sems):
    def copies(step):
        slot = lax.rem(step, 2)
        return [
            pltpu.make_async_copy(
                stu_hbm.at[pl.ds((sign * steps + step) * kb, kb)],
                w_buf.at[slot, sign],
                sems.at[slot, sign],
            )
            for sign in range(2)
        ]

    @pl.when(j == 0)
    def _():
        for copy in copies(j):
            copy.start()

    @pl.when(j + 1 < steps)
    def _():
        for copy in copies(j + 1):
            copy.start()

    def wait():
        for copy in copies(j):
            copy.wait()

    return lax.rem(j, 2), wait


def fetch_last(j, steps, src, dst, sem):
    copy = pltpu.make_async_copy(src, dst, sem)

    @pl.when(j == 0)
    def _():
        copy.start()

    @pl.when(j == steps - 1)
    def _():
        copy.wait()


def mix_kernel(
    kb, share, len_ref, taps_ref, x_ref, u_ref, lag_ref, gain_ref, stu_hbm, ar_hbm,
    hid_ref, nt_ref, ta_ref, tb_ref, c_ref, acc_ref, scr, w_buf, ar_ref, sems, ar_sem,
):
    j, steps = pl.program_id(0), pl.num_programs(0)
    half, width = u_ref.shape[1:]
    length, rows = 2 * half, share // 2
    m = lax.axis_index("mp")
    b = lax.broadcasted_iota(jnp.int32, (rows, half), 0)
    a = lax.broadcasted_iota(jnp.int32, (rows, half), 1)
    wrapped = a >= (length - m * share) // 2
    upto = (a <= b) | wrapped
    below = (a < b) | wrapped
    slot, wait = fetch_matrices(j, stu_hbm.shape[0] // (2 * kb), kb, stu_hbm, w_buf, sems)

    @pl.when(j == 0)
    def _():
        acc_ref[...] = jnp.zeros((share, width), F32)

    for k in range(kb):
        even = toeplitz(taps_ref[0, pl.ds(j * kb + k, 1), :], rows)
        odd = toeplitz(taps_ref[1, pl.ds(j * kb + k, 1), :], rows)
        late = toeplitz(taps_ref[2, pl.ds(j * kb + k, 1), :], rows)
        even = jnp.where(upto, even, 0.0).astype(BF)
        at = k * share
        ta_ref[at : at + rows, :] = even
        ta_ref[at + rows : at + share, :] = jnp.where(upto, odd, 0.0).astype(BF)
        tb_ref[at : at + rows, :] = jnp.where(below, late, 0.0).astype(BF)
        tb_ref[at + rows : at + share, :] = even
    ca = dot(ta_ref[...], u_ref[0])
    cb = dot(tb_ref[...], u_ref[1])
    for k in range(kb):
        at = k * share
        pa, pb = ca[at : at + share], cb[at : at + share]
        c_ref[:, k * width : (k + 1) * width] = (pa + pb).astype(BF)
        c_ref[:rows, (kb + k) * width : (kb + k + 1) * width] = (pa[:rows] - pb[:rows]).astype(BF)
        c_ref[rows:, (kb + k) * width : (kb + k + 1) * width] = (pb[rows:] - pa[rows:]).astype(BF)
    wait()
    acc_ref[...] += dot(c_ref[...], w_buf[slot].reshape(2 * kb * width, width))
    fetch_last(j, steps, ar_hbm, ar_ref, ar_sem)

    @pl.when(j == steps - 1)
    def _():
        total = acc_ref[...] + dot(lag_ref[...], ar_ref[...].reshape(lag_ref.shape[1], width))
        hidden = x_ref[...] + interleave(scr, total)
        hid_ref[...] = hidden
        r2 = lax.rsqrt(jnp.mean(hidden * hidden, axis=-1, keepdims=True) + EPS)
        pos = m * share + lax.broadcasted_iota(jnp.int32, (share, 1), 0)
        mask = (pos < len_ref[0]).astype(F32)
        nt_ref[...] = (mask * hidden * r2 * gain_ref[1:2, :]).astype(BF)


def matrix_scratch(kb, ar):
    width = ar.shape[1]
    return [
        pltpu.VMEM((2, 2, kb, width, width), BF),
        pltpu.VMEM(ar.shape, BF),
        pltpu.SemaphoreType.DMA((2, 2)),
        pltpu.SemaphoreType.DMA,
    ]


def spectral_mix(lengths, taps, x, u, lags, gains, stu, ar, share, kb):
    width = x.shape[1]
    length = 2 * u.shape[1]
    filt = taps.shape[1]
    return pl.pallas_call(
        functools.partial(mix_kernel, kb, share),
        grid=(filt // kb,),
        in_specs=[smem()] + [whole()] * 5 + [outside()] * 2,
        out_specs=[whole()] * 2,
        out_shape=[
            jax.ShapeDtypeStruct((share, width), F32),
            jax.ShapeDtypeStruct((share, width), BF),
        ],
        scratch_shapes=[
            pltpu.VMEM((kb * share, length // 2), BF),
            pltpu.VMEM((kb * share, length // 2), BF),
            pltpu.VMEM((share, 2 * kb * width), BF),
            pltpu.VMEM((share, width), F32),
            pltpu.VMEM((width // 128, share, 128), F32),
        ]
        + matrix_scratch(kb, ar),
        compiler_params=params(40 << 20),
        cost_estimate=cost(2 * filt * share * width * (length + 2 * width), 2 * stu.size),
        name="spectral_mix",
    )(lengths, taps, x, u, lags, gains, stu, ar)


def ffn_kernel(
    shift, n, nt_ref, cot_ref, gw_ref, uw_ref, dw_ref, bn_ref, act_ref, bg_ref, bu_ref
):
    share = nt_ref.shape[0]
    nt = nt_ref[...]
    gate = dot(nt, gw_ref[...])
    upper = dot(nt, uw_ref[...])
    start = pl.multiple_of(lax.rem(lax.axis_index("mp") + shift, n) * share, 16)
    back_act = dot_cols(cot_ref[pl.ds(start, share), :], dw_ref[...])
    square = gate * gate
    th = jnp.tanh(SQRT_2_PI * (gate + CUBIC * square * gate))
    half = 0.5 * (1.0 + th)
    gelu = gate * half
    slope = half + 0.5 * gate * (1.0 - th * th) * (SQRT_2_PI * (1.0 + 3.0 * CUBIC * square))
    act_ref[...] = (gelu * upper).astype(BF)
    bg = (back_act * upper * slope).astype(BF)
    bu = (back_act * gelu).astype(BF)
    bg_ref[...] = bg
    bu_ref[...] = bu
    bn_ref[...] = (dot_cols(bg, gw_ref[...]) + dot_cols(bu, uw_ref[...])).astype(BF)


def feed_forward(shift, n, nt, cot, gw, uw, dw):
    share, width = nt.shape
    hid = gw.shape[1]
    return pl.pallas_call(
        functools.partial(ffn_kernel, shift, n),
        in_specs=[whole()] * 5,
        out_specs=[whole()] * 4,
        out_shape=[jax.ShapeDtypeStruct((share, width), BF)]
        + [jax.ShapeDtypeStruct((share, hid), BF)] * 3,
        compiler_params=params(),
        cost_estimate=cost(10 * share * width * hid, 2 * (3 * width * hid + 6 * share * width)),
        name="feed_forward",
    )(nt, cot, gw, uw, dw)


def ffn_grad_kernel(n, share, groups, cot_ref, dw_ref, *refs):
    nt_refs, act_refs, bg_refs, bu_refs = (refs[i * n : (i + 1) * n] for i in range(4))
    out_refs, grad_refs = refs[4 * n : 5 * n], refs[5 * n :]
    m = lax.axis_index("mp")
    nt = jnp.concatenate([ref[...] for ref in nt_refs], axis=0)
    act = jnp.concatenate([ref[...] for ref in act_refs], axis=0)
    bg = jnp.concatenate([ref[...] for ref in bg_refs], axis=0)
    bu = jnp.concatenate([ref[...] for ref in bu_refs], axis=0)
    cot = jnp.concatenate(
        [
            cot_ref[pl.ds(pl.multiple_of(lax.rem(m + r, n) * share, 16), share), :]
            for r in range(n)
        ],
        axis=0,
    )
    outs = dot(act, dw_ref[...]).astype(BF)
    for r in range(n):
        out_refs[r][...] = outs[r * share : (r + 1) * share, :]
    nt_t = nt.T
    grads = (dot(nt_t, bg), dot(nt_t, bu), dot(act.T, cot))
    if not groups:
        for ref, grad in zip(grad_refs, grads):
            ref[...] = grad.astype(BF)
        return
    keep_ref, send_ref, scr = grad_refs
    for i in range(3):
        scr[i] = grads[i].astype(BF)
    rows = scr.shape[1] // (2 * groups)
    d = lax.axis_index("dp")
    core = lax.rem(d, 2)
    for r in range(groups):
        chip = ((d // 2) ^ r) * 2
        for i in range(3):
            mine = pl.multiple_of((chip + core) * rows, 16)
            other = pl.multiple_of((chip + 1 - core) * rows, 16)
            at = (3 * r + i) * rows
            keep_ref[at : at + rows, :] = scr[i, pl.ds(mine, rows), :]
            send_ref[at : at + rows, :] = scr[i, pl.ds(other, rows), :]


def ffn_grads(cot, dw, nts, acts, bgs, bus, groups):
    n = len(nts)
    share, width = nts[0].shape
    hid = dw.shape[0]
    length = cot.shape[0]
    out_shape = [jax.ShapeDtypeStruct((share, width), BF)] * n
    scratch = []
    if groups:
        out_shape += [jax.ShapeDtypeStruct((3 * width // 2, width), BF)] * 2
        scratch = [pltpu.VMEM((3, width, width), BF)]
    else:
        out_shape += [
            jax.ShapeDtypeStruct((width, hid), BF),
            jax.ShapeDtypeStruct((width, hid), BF),
            jax.ShapeDtypeStruct((hid, width), BF),
        ]
    args = [cot, dw, *nts, *acts, *bgs, *bus]
    return pl.pallas_call(
        functools.partial(ffn_grad_kernel, n, share, groups),
        in_specs=[whole()] * len(args),
        out_specs=[whole()] * len(out_shape),
        out_shape=out_shape,
        scratch_shapes=scratch,
        compiler_params=params(),
        cost_estimate=cost(8 * length * width * hid, 12 * length * width),
        name="ffn_grads",
    )(*args)


def mid_kernel(n, share, len_ref, hid_ref, cot_ref, gain_ref, *refs):
    bn_refs, (bh_ref, b_ref, gg_ref) = refs[:n], refs[n:]
    m = lax.axis_index("mp")
    bn = bn_refs[0][...].astype(F32)
    for ref in bn_refs[1:]:
        bn = bn + ref[...].astype(F32)
    hidden = hid_ref[...]
    r2 = lax.rsqrt(jnp.mean(hidden * hidden, axis=-1, keepdims=True) + EPS)
    pos = m * share + lax.broadcasted_iota(jnp.int32, (share, 1), 0)
    bn = bn * (pos < len_ref[0]).astype(F32)
    z = hidden * r2
    gg_ref[...] = jnp.broadcast_to(jnp.sum(bn * z, axis=0, keepdims=True), gg_ref.shape)
    q = bn * gain_ref[1:2, :]
    start = pl.multiple_of(m * share, 16)
    dout = cot_ref[pl.ds(start, share), :].astype(F32)
    back = dout + r2 * (q - z * jnp.mean(q * z, axis=-1, keepdims=True))
    bh_ref[...] = back
    b_ref[...] = back.astype(BF)


def mid_norm(lengths, hidden, cot, gain, pieces):
    share, width = hidden.shape
    n = len(pieces)
    return pl.pallas_call(
        functools.partial(mid_kernel, n, share),
        in_specs=[smem()] + [whole()] * (3 + n),
        out_specs=[whole()] * 3,
        out_shape=[
            jax.ShapeDtypeStruct(hidden.shape, F32),
            jax.ShapeDtypeStruct(hidden.shape, BF),
            jax.ShapeDtypeStruct((8, width), F32),
        ],
        compiler_params=params(),
        cost_estimate=cost(20 * hidden.size, 20 * hidden.size),
        name="second_norm_back",
    )(lengths, hidden, cot, gain, *pieces)


def unmix_kernel(
    kb, share, n, len_ref, taps_ref, x_ref, bh_ref, gg_ref, gain_ref, stu_hbm, ar_hbm, *refs
):
    b_refs, (ig_ref, gain_out) = refs[:n], refs[n : n + 2]
    ta_ref, tb_ref, be_ref, bo_ref, lag_ref, acc_ref, scr = refs[n + 2 : n + 9]
    w_buf, ar_ref, sems, ar_sem = refs[n + 9 :]
    j, steps = pl.program_id(0), pl.num_programs(0)
    width = bh_ref.shape[1]
    length = n * share
    half, rows = length // 2, share // 2
    m = lax.axis_index("mp")
    b = lax.broadcasted_iota(jnp.int32, (rows, half), 0)
    a = lax.broadcasted_iota(jnp.int32, (rows, half), 1)
    inside = a < (length - m * share) // 2
    upto = (a >= b) & inside
    below = (a > b) & inside
    slot, wait = fetch_matrices(j, stu_hbm.shape[0] // (2 * kb), kb, stu_hbm, w_buf, sems)

    @pl.when(j == 0)
    def _():
        for r in reversed(range(n)):
            put_columns(scr, b_refs[r][...].astype(F32))
            be_ref[r * rows : (r + 1) * rows, :] = every_second(scr, 0, rows).astype(BF)
            bo_ref[r * rows : (r + 1) * rows, :] = every_second(scr, 1, rows).astype(BF)
        more = b_refs[1 % n][:16, :].astype(F32) * jnp.where(m == n - 1, 0.0, 1.0)
        put_columns(scr, more, share)
        order = lag_ref.shape[1] // width
        for lag in range(order):
            for odd in range(2):
                lag_ref[odd * rows : (odd + 1) * rows, lag * width : (lag + 1) * width] = (
                    every_second(scr, odd + lag, rows).astype(BF)
                )
        acc_ref[...] = jnp.zeros((share, width), F32)

    for k in range(kb):
        even = toeplitz(taps_ref[3, pl.ds(j * kb + k, 1), :], rows)
        odd = toeplitz(taps_ref[4, pl.ds(j * kb + k, 1), :], rows)
        late = toeplitz(taps_ref[5, pl.ds(j * kb + k, 1), :], rows)
        even = jnp.where(upto, even, 0.0).astype(BF)
        at = k * share
        ta_ref[at : at + rows, :] = even
        ta_ref[at + rows : at + share, :] = jnp.where(below, late, 0.0).astype(BF)
        tb_ref[at : at + rows, :] = jnp.where(upto, odd, 0.0).astype(BF)
        tb_ref[at + rows : at + share, :] = even
    ca = dot(ta_ref[...], be_ref[...])
    cb = dot(tb_ref[...], bo_ref[...])
    wait()
    total = acc_ref[...]
    for k in range(kb):
        at = k * share
        pa, pb = ca[at : at + share], cb[at : at + share]
        minus = jnp.concatenate([pa[:rows] - pb[:rows], pb[rows:] - pa[rows:]], axis=0)
        total = total + dot_cols((pa + pb).astype(BF), w_buf[slot, 0, k])
        total = total + dot_cols(minus.astype(BF), w_buf[slot, 1, k])
    acc_ref[...] = total
    fetch_last(j, steps, ar_hbm, ar_ref, ar_sem)

    @pl.when(j == steps - 1)
    def _():
        total = acc_ref[...]
        for lag in range(ar_ref.shape[0]):
            total = total + dot_cols(lag_ref[:, lag * width : (lag + 1) * width], ar_ref[lag])
        x = x_ref[...]
        r1 = lax.rsqrt(jnp.mean(x * x, axis=-1, keepdims=True) + EPS)
        pos = m * share + lax.broadcasted_iota(jnp.int32, (share, 1), 0)
        masked = interleave(scr, total) * (pos < len_ref[0]).astype(F32)
        y = x * r1
        p = masked * gain_ref[0:1, :]
        ig = bh_ref[...] + r1 * (p - y * jnp.mean(p * y, axis=-1, keepdims=True))
        ig_ref[...] = ig.astype(BF)
        gain_out[0:8, :] = jnp.broadcast_to(jnp.sum(masked * y, axis=0, keepdims=True), (8, width))
        gain_out[8:16, :] = gg_ref[...]


def spectral_unmix(lengths, taps, x, back_hidden, gg, gains, stu, ar, pieces, kb):
    share, width = back_hidden.shape
    n = len(pieces)
    length = n * share
    count = taps.shape[1]
    return pl.pallas_call(
        functools.partial(unmix_kernel, kb, share, n),
        grid=(count // kb,),
        in_specs=[smem()] + [whole()] * 5 + [outside()] * 2 + [whole()] * n,
        out_specs=[whole()] * 2,
        out_shape=[
            jax.ShapeDtypeStruct((share, width), BF),
            jax.ShapeDtypeStruct((16, width), F32),
        ],
        scratch_shapes=[
            pltpu.VMEM((kb * share, length // 2), BF),
            pltpu.VMEM((kb * share, length // 2), BF),
            pltpu.VMEM((length // 2, width), BF),
            pltpu.VMEM((length // 2, width), BF),
            pltpu.VMEM((share, ar.shape[0] * width), BF),
            pltpu.VMEM((share, width), F32),
            pltpu.VMEM((width // 128, share + 16, 128), F32),
        ]
        + matrix_scratch(kb, ar),
        compiler_params=params(30 << 20),
        cost_estimate=cost(2 * count * share * width * (length + 2 * width), 2 * stu.size),
        name="spectral_unmix",
    )(lengths, taps, x, back_hidden, gg, gains, stu, ar, *pieces)


def conv_kernel(groups, tile, own, filt_ref, *refs):
    ut_refs, (conv_ref, tt_ref, ut_scr) = refs[:groups], refs[groups:]
    j = pl.program_id(0)
    filt, length = filt_ref.shape
    block = conv_ref.shape[1]
    count = length // tile
    chip = lax.axis_index("dp") // 2

    @pl.when(j == 0)
    def _():
        start = pl.multiple_of(chip * block, 16)
        for r in range(groups):
            ut_scr[r * block : (r + 1) * block, :] = ut_refs[r][pl.ds(start, block), :]

    which = lax.axis_index("mp") * own + j
    strip = toeplitz(filt_ref[pl.ds(lax.rem(which, filt), 1), :], tile)
    row = lax.broadcasted_iota(jnp.int32, (tile, length), 0)
    col = lax.broadcasted_iota(jnp.int32, (tile, length), 1)
    flip = ((col - row) % 2 == 1) & (which >= filt)
    strip = jnp.where(col >= row, jnp.where(flip, -strip, strip), 0.0).astype(BF)
    for b in range(count):
        tt_ref[b * tile : (b + 1) * tile, b * tile :] = strip[:, : length - b * tile]
    for c in range(count):
        end = (c + 1) * tile
        part = dot(ut_scr[:, :end], tt_ref[:end, c * tile : end]).astype(BF)
        for r in range(groups):
            start = pl.multiple_of((lax.rem(chip, groups) ^ r) * length + c * tile, 128)
            conv_ref[0, :, pl.ds(start, tile)] = part[r * block : (r + 1) * block, :]


def convolutions(filt, uts, own, chips):
    length = filt.shape[1]
    groups = len(uts)
    block = uts[0].shape[0] // chips
    tile = 256 if length % 256 == 0 else length
    return pl.pallas_call(
        functools.partial(conv_kernel, groups, tile, own),
        grid=(own,),
        in_specs=[whole()] * (1 + groups),
        out_specs=pl.BlockSpec((1, block, groups * length), lambda j: (j, 0, 0)),
        out_shape=jax.ShapeDtypeStruct((own, block, groups * length), BF),
        scratch_shapes=[
            pltpu.VMEM((length, length), BF),
            pltpu.VMEM((groups * block, length), BF),
        ],
        compiler_params=params(),
        cost_estimate=cost(0, 0),
        name="convolutions",
    )(filt, *uts)


def lag_kernel(groups, *refs):
    ut_refs, out_refs = refs[:groups], refs[groups:]
    width, length = ut_refs[0].shape
    chip = lax.rem(lax.axis_index("dp") // 2, groups)
    col = lax.broadcasted_iota(jnp.int32, (width, length), 1)
    for r in range(groups):
        start = pl.multiple_of((chip ^ r) * length, 128)
        out_refs[0][:, pl.ds(start, length)] = ut_refs[r][...]
        value = ut_refs[r][...].astype(F32)
        for lag in range(1, len(out_refs)):
            moved = pltpu.roll(value, lag, 1)
            out_refs[lag][:, pl.ds(start, length)] = jnp.where(col >= lag, moved, 0.0).astype(BF)


def lagged(uts, order):
    groups = len(uts)
    width, length = uts[0].shape
    shape = jax.ShapeDtypeStruct((width, groups * length), BF)
    return pl.pallas_call(
        functools.partial(lag_kernel, groups),
        in_specs=[whole()] * groups,
        out_specs=[whole()] * order,
        out_shape=[shape] * order,
        compiler_params=params(),
        cost_estimate=cost(0, 0),
        name="lagged",
    )(*uts)


def grads_kernel(steps, order, groups, rows, conv_ref, *refs):
    lag_refs, b_refs = refs[:order], refs[order : order + len(rows)]
    keep_ref, send_ref, b_scr, scr = refs[order + len(rows) :]
    g = pl.program_id(0)
    d = lax.axis_index("dp")
    chip, core = lax.rem(d // 2, groups), lax.rem(d, 2)
    step, block, depth = conv_ref.shape
    width, length = b_scr.shape[1], depth // groups
    half = block // 2

    @pl.when(g == 0)
    def _():
        for ref, (r, at, size) in zip(b_refs, rows):
            start = pl.multiple_of((chip ^ r) * length + at, 16)
            b_scr[pl.ds(start, size), :] = ref[:size, :]

    @pl.when(g < steps)
    def _():
        part = dot(conv_ref[...].reshape(step * block, depth), b_scr[...])
        scr[...] = part.reshape(step, block, width)
        mine = pl.multiple_of(core * half, 16)
        other = pl.multiple_of((1 - core) * half, 16)
        keep_ref[pl.ds(g * step, step)] = scr[:, pl.ds(mine, half), :]
        for k in range(step):
            start = pl.multiple_of((g * step + k) * half, 16)
            send_ref[pl.ds(start, half), :] = scr[k, pl.ds(other, half), :].astype(BF)

    for lag in range(order):

        @pl.when(g == steps + lag)
        def _():
            at = steps * step * half + lag * width
            send_ref[at : at + width, :] = dot(lag_refs[lag][...], b_scr[...]).astype(BF)


def matrix_grads(conv, lags, backs, rows):
    own, block, depth = conv.shape
    order, width = len(lags), lags[0].shape[0]
    groups = 1 + max(r for r, _, _ in rows)
    step = next(s for s in (4, 3, 2, 1) if own % s == 0)
    steps = own // step
    half = block // 2
    return pl.pallas_call(
        functools.partial(grads_kernel, steps, order, groups, rows),
        grid=(steps + order,),
        in_specs=[pl.BlockSpec((step, block, depth), lambda g: (jnp.minimum(g, steps - 1), 0, 0))]
        + [whole()] * (order + len(backs)),
        out_specs=[whole()] * 2,
        out_shape=[
            jax.ShapeDtypeStruct((own, half, width), F32),
            jax.ShapeDtypeStruct((own * half + order * width, width), BF),
        ],
        scratch_shapes=[
            pltpu.VMEM((depth, width), BF),
            pltpu.VMEM((step, block, width), F32),
        ],
        compiler_params=params(),
        cost_estimate=cost(0, 0),
        name="matrix_grads",
    )(conv, *lags, *backs)


def rows_message_kernel(ig_ref, hid_ref, *refs):
    share = ig_ref.shape[0]
    total = hid_ref[...]
    for ref in refs[:-1]:
        total = total + ref[...].astype(F32)
    refs[-1][:share, :] = ig_ref[...]
    refs[-1][share:, :] = total.astype(BF)


def rows_message(ig, hidden, pieces):
    share, width = ig.shape
    return pl.pallas_call(
        rows_message_kernel,
        in_specs=[whole()] * (2 + len(pieces)),
        out_specs=whole(),
        out_shape=jax.ShapeDtypeStruct((2 * share, width), BF),
        compiler_params=params(),
        cost_estimate=cost(4 * ig.size, 10 * ig.size),
        name="rows_message",
    )(ig, hidden, *pieces)


def finish_rows_kernel(n, share, *refs):
    pieces, (ig_ref, out_ref) = refs[:n], refs[n:]
    m = lax.axis_index("mp")
    for r in range(n):
        start = pl.multiple_of(lax.rem(m + r, n) * share, 16)
        ig_ref[pl.ds(start, share), :] = pieces[r][:share, :].astype(F32)
        out_ref[pl.ds(start, share), :] = pieces[r][share:, :]


def finish_rows(pieces):
    n = len(pieces)
    share, width = pieces[0].shape[0] // 2, pieces[0].shape[1]
    return pl.pallas_call(
        functools.partial(finish_rows_kernel, n, share),
        in_specs=[whole()] * n,
        out_specs=[whole()] * 2,
        out_shape=[
            jax.ShapeDtypeStruct((n * share, width), F32),
            jax.ShapeDtypeStruct((n * share, width), BF),
        ],
        compiler_params=params(),
        cost_estimate=cost(n * share * width, 6 * n * share * width),
        name="finish_rows",
    )(*pieces)


def ordered_sum_kernel(n, axis, step, *refs):
    pieces, (out_ref, scr) = refs[:n], refs[n:]
    me = lax.axis_index(axis)
    for r in range(n):
        who = lax.rem(me + r, n) if step == 0 else (me // step) ^ r
        scr[who] = pieces[r][...]
    total = scr[0]
    for r in range(1, n):
        total = total + scr[r]
    out_ref[...] = total


def ordered_sum(pieces, axis, step):
    n = len(pieces)
    shape = pieces[0].shape
    return pl.pallas_call(
        functools.partial(ordered_sum_kernel, n, axis, step),
        in_specs=[whole()] * n,
        out_specs=whole(),
        out_shape=jax.ShapeDtypeStruct(shape, F32),
        scratch_shapes=[pltpu.VMEM((n,) + shape, F32)],
        compiler_params=params(),
        cost_estimate=cost(n * pieces[0].size, 4 * n * pieces[0].size),
        name="ordered_sum",
    )(*pieces)


def cores_sum_kernel(keep_ref, recv_ref, sum_ref, to_x, to_y):
    total = (keep_ref[...].astype(F32) + recv_ref[...].astype(F32)).astype(BF)
    sum_ref[...] = total
    half = total.shape[0] // 8
    for k, r in enumerate((1, 3)):
        to_x[k * half : (k + 1) * half, :] = total[2 * r * half : (2 * r + 1) * half]
    for k, r in enumerate((2, 3)):
        to_y[k * half : (k + 1) * half, :] = total[(2 * r + 1) * half : (2 * r + 2) * half]


def cores_sum(keep, recv):
    size, width = keep.shape
    return pl.pallas_call(
        cores_sum_kernel,
        in_specs=[whole()] * 2,
        out_specs=[whole()] * 3,
        out_shape=[jax.ShapeDtypeStruct((rows, width), BF) for rows in (size, size // 4, size // 4)],
        compiler_params=params(),
        cost_estimate=cost(keep.size, 8 * keep.size),
        name="cores_sum",
    )(keep, recv)


def pack_kernel(n, share, extras, *refs):
    pieces, extra_refs, out_refs = refs[:n], refs[n : n + extras], refs[n + extras :]
    m = lax.axis_index("mp")
    for r in range(n):
        start = pl.multiple_of(lax.rem(m + r, n) * share, 16)
        for ref in out_refs:
            ref[pl.ds(start, share), :] = pieces[r][...]
    for ref, extra in zip(out_refs[1:], extra_refs):
        ref[n * share :, :] = extra[...]


def pack_rows(pieces, extras=()):
    n = len(pieces)
    share, width = pieces[0].shape
    rows = [n * share] + [n * share + extra.shape[0] for extra in extras]
    return pl.pallas_call(
        functools.partial(pack_kernel, n, share, len(extras)),
        in_specs=[whole()] * (n + len(extras)),
        out_specs=[whole()] * len(rows),
        out_shape=[jax.ShapeDtypeStruct((r, width), BF) for r in rows],
        compiler_params=params(),
        cost_estimate=cost(n * share * width, 6 * n * share * width),
        name="pack_rows",
    )(*pieces, *extras)


def turn_kernel(x_ref, y_ref, sum_ref, gain_ref, part_ref, to_y, to_x):
    size = part_ref.shape[0] // 2
    half = size // 2
    length = x_ref.shape[0] - size
    gains = split_gains(gain_ref[...])
    for ref, came, at, chunks in ((to_y, x_ref, 0, (0, 2)), (to_x, y_ref, 1, (0, 1))):
        start = at * length // 2
        ref[: length // 2, :] = came[start : start + length // 2, :]
        for k, r in enumerate(chunks):
            own = sum_ref[(2 * r + at) * half : (2 * r + at + 1) * half, :].astype(F32)
            there = length + k * half
            total = (own + came[there : there + half, :].astype(F32)).astype(BF)
            part_ref[at * size + k * half : at * size + (k + 1) * half, :] = total
            ref[length // 2 + k * half : length // 2 + (k + 1) * half, :] = total
        ref[length // 2 + size :, :] = gains


def turn(over_x, over_y, sums, gains):
    size, width = sums.shape[0] // 4, sums.shape[1]
    rows = (over_x.shape[0] - size) // 2 + size + 32
    return pl.pallas_call(
        turn_kernel,
        in_specs=[whole()] * 4,
        out_specs=[whole()] * 3,
        out_shape=[
            jax.ShapeDtypeStruct((2 * size, width), BF),
            jax.ShapeDtypeStruct((rows, width), BF),
            jax.ShapeDtypeStruct((rows, width), BF),
        ],
        compiler_params=params(),
        cost_estimate=cost(over_x.size, 8 * over_x.size),
        name="turn",
    )(over_x, over_y, sums, gains)


def chunks_kernel(part_ref, from_y, from_x, to_x, to_y):
    size = part_ref.shape[0] // 2
    half = size // 2
    at = from_y.shape[0] - 32 - size
    for ref, came, start in ((to_x, from_y, 0), (to_y, from_x, size)):
        for k in range(2):
            there = at + (1 - k) * half
            ref[k * half : (k + 1) * half, :] = (
                part_ref[start + k * half : start + (k + 1) * half, :].astype(F32)
                + came[there : there + half, :].astype(F32)
            ).astype(BF)
    to_x[size:, :] = from_y[at + size :, :]


def whole_chunks(parts, from_y, from_x):
    size, width = parts.shape[0] // 2, parts.shape[1]
    return pl.pallas_call(
        chunks_kernel,
        in_specs=[whole()] * 3,
        out_specs=[whole()] * 2,
        out_shape=[
            jax.ShapeDtypeStruct((size + 32, width), BF),
            jax.ShapeDtypeStruct((size, width), BF),
        ],
        compiler_params=params(),
        cost_estimate=cost(parts.size, 8 * parts.size),
        name="whole_chunks",
    )(parts, from_y, from_x)


def split_gains(both):
    high = both.astype(BF)
    low = (both - high.astype(F32)).astype(BF)
    return jnp.concatenate([high, low], axis=0)


def joined(gains):
    return gains[:16].astype(F32) + gains[16:].astype(F32)


def chips_sum_kernel(gain_ref, from_x, from_y, recv_ref, out_ref, scr):
    chip = lax.axis_index("dp") // 2
    scr[chip] = joined(split_gains(gain_ref[...]))
    for ref, bits in ((from_x, 1), (from_y, 2), (recv_ref, 3)):
        scr[chip ^ bits] = joined(ref[ref.shape[0] - 32 :, :])
    out_ref[...] = ((scr[0] + scr[1]) + scr[2]) + scr[3]


def chips_sum(gains, from_x, from_y, recv):
    return pl.pallas_call(
        chips_sum_kernel,
        in_specs=[whole()] * 4,
        out_specs=whole(),
        out_shape=jax.ShapeDtypeStruct(gains.shape, F32),
        scratch_shapes=[pltpu.VMEM((4,) + gains.shape, F32)],
        compiler_params=params(),
        cost_estimate=cost(4 * gains.size, 16 * gains.size),
        name="chips_sum",
    )(gains, from_x, from_y, recv)


def join_kernel(counts, *refs):
    at = 0
    for ref, count in zip(refs, counts):
        refs[-1][at : at + count, :] = ref[:count, :]
        at += count


def join_pieces(pieces, counts):
    rows = sum(counts)
    return pl.pallas_call(
        functools.partial(join_kernel, counts),
        in_specs=[whole()] * len(pieces),
        out_specs=whole(),
        out_shape=jax.ShapeDtypeStruct((rows, pieces[0].shape[1]), pieces[0].dtype),
        compiler_params=params(),
        cost_estimate=cost(rows * pieces[0].shape[1], 4 * rows * pieces[0].shape[1]),
        name="join_pieces",
    )(*pieces)


def finish_kernel(custom, keep_ref, send_ref, recv_ref, stu_ref, ar_ref, *w_refs):
    own, half, width = keep_ref.shape
    base = 0
    if custom:
        d = lax.axis_index("dp")
        core = lax.rem(d, 2)
        rows = width // 8
        part = 3 * rows // 2
        base = 8 * part
        for r in range(4):
            chip = ((d // 2) ^ r) * 2
            upper, lower = (0, 4, 1, 5)[r] * part, (2, 3, 6, 7)[r] * part
            for ref, which in ((send_ref, chip + core), (recv_ref, chip + 1 - core)):
                start = pl.multiple_of(which * rows, 16)
                chunk = jnp.concatenate(
                    [ref[upper : upper + part, :], ref[lower : lower + part, :]], axis=0
                ).astype(F32)
                for i, out in enumerate(w_refs):
                    out[pl.ds(start, rows), :] = chunk[i * rows : (i + 1) * rows]
    for k in range(own):
        at = base + k * half
        stu_ref[k] = keep_ref[k] + recv_ref[at : at + half, :].astype(F32)
    for i in range(ar_ref.shape[0]):
        at = base + own * half + i * width
        ar_ref[i] = send_ref[at : at + width, :].astype(F32) + recv_ref[
            at : at + width, :
        ].astype(F32)


def finish(keep, send, recv, order, custom):
    width = keep.shape[2]
    more = [jax.ShapeDtypeStruct((width, width), F32)] * (3 if custom else 0)
    return pl.pallas_call(
        functools.partial(finish_kernel, custom),
        in_specs=[whole()] * 3,
        out_specs=[whole()] * (2 + len(more)),
        out_shape=[
            jax.ShapeDtypeStruct(keep.shape, F32),
            jax.ShapeDtypeStruct((order, width, width), F32),
        ]
        + more,
        compiler_params=params(),
        cost_estimate=cost(keep.size, 10 * keep.size),
        name="finish",
    )(keep, send, recv)


def fetch_shifted(value, axis, n):
    pieces = {0: value}
    for r in sorted(range(1, n), key=lambda r: min(r, n - r)):
        pieces[r] = lax.ppermute(value, axis, [(i, (i - r) % n) for i in range(n)])
    return [pieces[r] for r in range(n)]


def send_shifted(pieces, axis):
    n = len(pieces)
    moved = {0: pieces[0]}
    for r in sorted(range(1, n), key=lambda r: min(r, n - r)):
        moved[r] = lax.ppermute(pieces[r], axis, [(i, (i + r) % n) for i in range(n)])
    return [moved[r] for r in range(n)]


def swap(value, axis, n, bits):
    return lax.ppermute(value, axis, [(i, i ^ bits) for i in range(n)])


def after(values, first):
    flat, tree = jax.tree.flatten(values)
    out = lax.optimization_barrier((*flat, *jax.tree.leaves(first)))
    return jax.tree.unflatten(tree, out[: len(flat)])


def shards(
    inputs, lengths, filters, first_gain, stu_weight, ar_weight, second_gain,
    gate_weight, up_weight, down_weight, cotangent,
):
    n = lax.axis_size("mp")
    n_dp = lax.axis_size("dp")
    groups = n_dp // 2
    length, width = inputs.shape
    share = length // n
    order = ar_weight.shape[0]
    own = stu_weight.shape[0] // n
    lengths = lengths.astype(jnp.int32)
    both_gains = jnp.stack([first_gain, second_gain])

    u, ut, x_own, u_lags, taps, natural = first_norm(
        lengths, inputs, both_gains, filters.T, n, order
    )
    uts = [ut] + [swap(ut, "dp", n_dp, 2 * r) for r in range(1, 3)]
    hidden, nt = spectral_mix(
        lengths, taps, x_own, u, u_lags, both_gains, stu_weight, ar_weight, share, 4
    )
    nts = fetch_shifted(nt, "mp", n)
    weights = (cotangent, gate_weight, up_weight, down_weight)
    parts = {0: feed_forward(0, n, after(nt, uts[1:3]), *weights)}
    last = 0
    for r in sorted(range(1, n), key=lambda r: -min(r, n - r)):
        first = parts[last][0]
        parts[r] = feed_forward(r, n, after(nts[r], first), *weights)
        last = r
    uts += [swap(after(ut, nt), "dp", n_dp, 2 * r) for r in range(3, groups)]
    parts = [parts[r] for r in range(n)]
    bns = send_shifted([p[0] for p in parts], "mp")
    acts, bgs, bus = ([p[i] for p in parts] for i in (1, 2, 3))
    custom = n_dp == 8 and gate_weight.shape[1] == width
    grads = ffn_grads(cotangent, down_weight, nts, acts, bgs, bus, groups if custom else 0)
    out_parts, grads = grads[:n], grads[n:]
    bns = [bns[0]] + after(bns[1:], (grads[0], uts))
    back_hidden, back_rows, second_part = mid_norm(lengths, hidden, cotangent, both_gains, bns)
    backs = fetch_shifted(back_rows, "mp", n)
    if custom:
        w_keep, w_send = grads
        w_parts, to_x, to_y = cores_sum(w_keep, swap(after(w_send, back_rows), "dp", n_dp, 1))
        own_back, to_x, to_y = pack_rows(backs, (to_x, to_y))
        over_x, over_y = swap(to_x, "dp", n_dp, 2), swap(to_y, "dp", n_dp, 4)
    else:
        (own_back,) = pack_rows(backs)
    out_sums = send_shifted(after(out_parts, own_back), "mp")
    ig, gains = spectral_unmix(
        lengths, taps, x_own, back_hidden, second_part, both_gains, stu_weight, ar_weight, backs, 4
    )
    uts, hidden = after((uts, hidden), ig)
    conv = [convolutions(natural, uts[r : r + 4], own, groups) for r in range(0, groups, 4)]
    lags = [lagged(uts[r : r + 4], order) for r in range(0, groups, 4)]
    message = rows_message(ig, hidden, out_sums)
    messages = fetch_shifted(message, "mp", n)
    if custom:
        w_parts, to_y, to_x = turn(after(over_x, message), over_y, w_parts, gains)
        from_y, from_x = swap(to_y, "dp", n_dp, 4), swap(to_x, "dp", n_dp, 2)
        all_backs = [own_back, over_x, over_y, from_y, from_x]
        half = length // 2
        rows = ((0, 0, length), (1, 0, length), (2, 0, length), (3, 0, half), (3, half, half))
        to_x, to_y = whole_chunks(after(w_parts, conv), from_y, from_x)
        w_all = [to_x, to_y, swap(to_x, "dp", n_dp, 2), swap(to_y, "dp", n_dp, 4)]
        gains = chips_sum(gains, from_x, from_y, w_all[2])
        gains = ordered_sum([gains, swap(gains, "dp", n_dp, 1)], "dp", 0)
    else:
        all_backs = [own_back] + [swap(own_back, "dp", n_dp, 2 * r) for r in range(1, groups)]
        rows = tuple((r, 0, length) for r in range(min(groups, 4)))
        gains = ordered_sum([gains] + [swap(gains, "dp", n_dp, r) for r in range(1, n_dp)], "dp", 1)
    gains_dp = gains
    gains = fetch_shifted(gains, "mp", n)

    conv = after(conv, message)
    if len(conv) == 1:
        keep, send = matrix_grads(conv[0], lags[0], all_backs, rows)
    else:
        some = [
            matrix_grads(c, lags[k], all_backs[4 * k : 4 * k + 4], rows)
            for k, c in enumerate(conv)
        ]
        keep = ordered_sum([k for k, _ in some], "dp", 8)
        send = ordered_sum([k.astype(F32) for _, k in some], "dp", 8).astype(BF)
    input_grad, output = finish_rows(after(messages, send))
    if custom:
        w_all = after(w_all, (messages, gains_dp))
        counts = [w_all[1].shape[0]] * 4 + [send.shape[0]]
        send = join_pieces([*w_all, send], counts)
    recv = after(swap(send, "dp", n_dp, 1), output)
    stu_grad, ar_grad, *w_grads = finish(keep, send, recv, order, custom)
    gains = ordered_sum(after(gains, stu_grad), "mp", 0)
    if custom:
        gate_grad, up_grad, down_grad = w_grads
    else:
        gate_grad, up_grad, down_grad = (g.astype(F32) for g in lax.psum(tuple(grads), "dp"))
    return (
        output, input_grad, stu_grad, ar_grad, gains[0], gains[8], gate_grad, up_grad, down_grad,
    )


def solution(mesh):
    in_specs = (
        P("dp", None), P("dp"), P(), P(), P(), P(), P(),
        P(None, "mp"), P(None, "mp"), P("mp", None), P("dp", None),
    )
    out_specs = (
        P("dp", None), P("dp", None), P("mp", "dp", None), P(), P(), P(),
        P(None, "mp"), P(None, "mp"), P("mp", None),
    )
    return jax.shard_map(shards, mesh=mesh, in_specs=in_specs, out_specs=out_specs, check_vma=False)
```

```python
import functools

import jax
import jax.numpy as jnp
from jax import lax
from jax.experimental import pallas as pl
from jax.experimental.pallas import tpu as pltpu
from jax.sharding import PartitionSpec as P

EPS = 1e-05
BF = jnp.bfloat16
F32 = jnp.float32
SQRT_2_PI = 0.7978845608028654
CUBIC = 0.044715
VMEM_LIMIT = 20 << 20


def dot(left, right):
    return jnp.dot(left, right, preferred_element_type=F32)


def dot_cols(left, right):
    return lax.dot_general(left, right, (((1,), (1,)), ((), ())), preferred_element_type=F32)


def params(limit=VMEM_LIMIT):
    return pltpu.CompilerParams(vmem_limit_bytes=limit)


COST_SCALE = 1.0


def cost(flops, nbytes):
    return pl.CostEstimate(
        flops=int(COST_SCALE * flops), bytes_accessed=int(COST_SCALE * nbytes), transcendentals=0
    )


def smem():
    return pl.BlockSpec(memory_space=pltpu.SMEM)


def whole():
    return pl.BlockSpec(memory_space=pltpu.VMEM)


def outside():
    return pl.BlockSpec(memory_space=pltpu.HBM)


def toeplitz(base_row, rows):
    wide = jnp.broadcast_to(base_row, (rows, base_row.shape[1]))
    return pltpu.roll(wide, 0, 1, stride=1, stride_axis=0)


def put_columns(scr, value, at=0):
    for c in range(scr.shape[0]):
        scr[c, at : at + value.shape[0], :] = value[:, c * 128 : (c + 1) * 128]


def every_second(scr, start, count):
    columns = [scr[c, pl.ds(start, count, stride=2), :] for c in range(scr.shape[0])]
    return columns[0] if len(columns) == 1 else jnp.concatenate(columns, axis=1)


def interleave(scr, value):
    half = value.shape[0] // 2
    for c in range(scr.shape[0]):
        columns = slice(c * 128, (c + 1) * 128)
        scr[c, pl.ds(0, half, stride=2), :] = value[:half, columns]
        scr[c, pl.ds(1, half, stride=2), :] = value[half:, columns]
    count = value.shape[0]
    return jnp.concatenate([scr[c, :count, :] for c in range(scr.shape[0])], axis=1)


def norm_kernel(
    n, share, order, len_ref, x_ref, gain_ref, filt_ref,
    u_ref, ut_ref, own_ref, lag_ref, taps_ref, nat_ref, scr, scr_f,
):
    length, width = x_ref.shape
    m = lax.axis_index("mp")
    filt = nat_ref.shape[0]
    x = x_ref[...].astype(F32)
    r1 = lax.rsqrt(jnp.mean(x * x, axis=-1, keepdims=True) + EPS)
    row = lax.broadcasted_iota(jnp.int32, (length, 1), 0)
    mask = (row < len_ref[0]).astype(F32)
    u = mask * x * r1 * gain_ref[0:1, :]
    scr[:, :8, :] = jnp.zeros((scr.shape[0], 8, 128), F32)
    put_columns(scr, u, 8)
    ut_ref[...] = u.T.astype(BF)
    own_ref[...] = x_ref[pl.ds(pl.multiple_of(m * share, 16), share), :].astype(F32)
    for r in range(n):
        start = lax.rem(m + r, n) * share
        for odd in range(2):
            u_ref[odd, r * (share // 2) : (r + 1) * (share // 2), :] = every_second(
                scr, start + odd + 8, share // 2
            ).astype(BF)
    for lag in range(order):
        for odd in range(2):
            at = lag * width
            lag_ref[odd * (share // 2) : (odd + 1) * (share // 2), at : at + width] = every_second(
                scr, m * share + odd + 8 - lag, share // 2
            ).astype(BF)
    half = length // 2
    natural = filt_ref[...].astype(F32)
    nat_ref[...] = natural
    scr_f[0, :, :filt] = natural.T
    even = every_second(scr_f, 0, half).T[:filt]
    odd = every_second(scr_f, 1, half).T[:filt]
    i = lax.broadcasted_iota(jnp.int32, (half, half), 0)
    j = lax.broadcasted_iota(jnp.int32, (half, half), 1)
    flip = (i == jnp.where(j == 0, 0, half - j)).astype(F32).astype(BF)
    rev_even = dot(even.astype(BF), flip)
    rev_odd = dot(odd.astype(BF), flip)
    taps_ref[0] = rev_even
    taps_ref[1] = rev_odd
    taps_ref[2] = pltpu.roll(rev_odd, half - 1, 1)
    taps_ref[3] = even
    taps_ref[4] = odd
    taps_ref[5] = pltpu.roll(odd, 1, 1)


def first_norm(lengths, x, gains, filters, n, order):
    length, width = x.shape
    share = length // n
    filt = filters.shape[0]
    return pl.pallas_call(
        functools.partial(norm_kernel, n, share, order),
        in_specs=[smem()] + [whole()] * 3,
        out_specs=[whole()] * 6,
        out_shape=[
            jax.ShapeDtypeStruct((2, length // 2, width), BF),
            jax.ShapeDtypeStruct((width, length), BF),
            jax.ShapeDtypeStruct((share, width), F32),
            jax.ShapeDtypeStruct((share, order * width), BF),
            jax.ShapeDtypeStruct((6, filt, length // 2), F32),
            jax.ShapeDtypeStruct((filt, length), F32),
        ],
        scratch_shapes=[
            pltpu.VMEM((width // 128, length + 8, 128), F32),
            pltpu.VMEM((1, length, 128), F32),
        ],
        compiler_params=params(),
        cost_estimate=cost(10 * x.size, 6 * x.size),
        name="first_norm",
    )(lengths, x, gains, filters)


def fetch_matrices(j, steps, kb, stu_hbm, w_buf, sems):
    def copies(step):
        slot = lax.rem(step, 2)
        return [
            pltpu.make_async_copy(
                stu_hbm.at[pl.ds((sign * steps + step) * kb, kb)],
                w_buf.at[slot, sign],
                sems.at[slot, sign],
            )
            for sign in range(2)
        ]

    @pl.when(j == 0)
    def _():
        for copy in copies(j):
            copy.start()

    @pl.when(j + 1 < steps)
    def _():
        for copy in copies(j + 1):
            copy.start()

    def wait():
        for copy in copies(j):
            copy.wait()

    return lax.rem(j, 2), wait


def fetch_last(j, steps, src, dst, sem):
    copy = pltpu.make_async_copy(src, dst, sem)

    @pl.when(j == 0)
    def _():
        copy.start()

    @pl.when(j == steps - 1)
    def _():
        copy.wait()


def mix_kernel(
    kb, share, len_ref, taps_ref, x_ref, u_ref, lag_ref, gain_ref, stu_hbm, ar_hbm,
    hid_ref, nt_ref, ta_ref, tb_ref, c_ref, acc_ref, scr, w_buf, ar_ref, sems, ar_sem,
):
    j, steps = pl.program_id(0), pl.num_programs(0)
    half, width = u_ref.shape[1:]
    length, rows = 2 * half, share // 2
    m = lax.axis_index("mp")
    b = lax.broadcasted_iota(jnp.int32, (rows, half), 0)
    a = lax.broadcasted_iota(jnp.int32, (rows, half), 1)
    wrapped = a >= (length - m * share) // 2
    upto = (a <= b) | wrapped
    below = (a < b) | wrapped
    slot, wait = fetch_matrices(j, stu_hbm.shape[0] // (2 * kb), kb, stu_hbm, w_buf, sems)

    @pl.when(j == 0)
    def _():
        acc_ref[...] = jnp.zeros((share, width), F32)

    for k in range(kb):
        even = toeplitz(taps_ref[0, pl.ds(j * kb + k, 1), :], rows)
        odd = toeplitz(taps_ref[1, pl.ds(j * kb + k, 1), :], rows)
        late = toeplitz(taps_ref[2, pl.ds(j * kb + k, 1), :], rows)
        even = jnp.where(upto, even, 0.0).astype(BF)
        at = k * share
        ta_ref[at : at + rows, :] = even
        ta_ref[at + rows : at + share, :] = jnp.where(upto, odd, 0.0).astype(BF)
        tb_ref[at : at + rows, :] = jnp.where(below, late, 0.0).astype(BF)
        tb_ref[at + rows : at + share, :] = even
    ca = dot(ta_ref[...], u_ref[0])
    cb = dot(tb_ref[...], u_ref[1])
    for k in range(kb):
        at = k * share
        pa, pb = ca[at : at + share], cb[at : at + share]
        c_ref[:, k * width : (k + 1) * width] = (pa + pb).astype(BF)
        c_ref[:rows, (kb + k) * width : (kb + k + 1) * width] = (pa[:rows] - pb[:rows]).astype(BF)
        c_ref[rows:, (kb + k) * width : (kb + k + 1) * width] = (pb[rows:] - pa[rows:]).astype(BF)
    wait()
    acc_ref[...] += dot(c_ref[...], w_buf[slot].reshape(2 * kb * width, width))
    fetch_last(j, steps, ar_hbm, ar_ref, ar_sem)

    @pl.when(j == steps - 1)
    def _():
        total = acc_ref[...] + dot(lag_ref[...], ar_ref[...].reshape(lag_ref.shape[1], width))
        hidden = x_ref[...] + interleave(scr, total)
        hid_ref[...] = hidden
        r2 = lax.rsqrt(jnp.mean(hidden * hidden, axis=-1, keepdims=True) + EPS)
        pos = m * share + lax.broadcasted_iota(jnp.int32, (share, 1), 0)
        mask = (pos < len_ref[0]).astype(F32)
        nt_ref[...] = (mask * hidden * r2 * gain_ref[1:2, :]).astype(BF)


def matrix_scratch(kb, ar):
    width = ar.shape[1]
    return [
        pltpu.VMEM((2, 2, kb, width, width), BF),
        pltpu.VMEM(ar.shape, BF),
        pltpu.SemaphoreType.DMA((2, 2)),
        pltpu.SemaphoreType.DMA,
    ]


def spectral_mix(lengths, taps, x, u, lags, gains, stu, ar, share, kb):
    width = x.shape[1]
    length = 2 * u.shape[1]
    filt = taps.shape[1]
    return pl.pallas_call(
        functools.partial(mix_kernel, kb, share),
        grid=(filt // kb,),
        in_specs=[smem()] + [whole()] * 5 + [outside()] * 2,
        out_specs=[whole()] * 2,
        out_shape=[
            jax.ShapeDtypeStruct((share, width), F32),
            jax.ShapeDtypeStruct((share, width), BF),
        ],
        scratch_shapes=[
            pltpu.VMEM((kb * share, length // 2), BF),
            pltpu.VMEM((kb * share, length // 2), BF),
            pltpu.VMEM((share, 2 * kb * width), BF),
            pltpu.VMEM((share, width), F32),
            pltpu.VMEM((width // 128, share, 128), F32),
        ]
        + matrix_scratch(kb, ar),
        compiler_params=params(50 << 20),
        cost_estimate=cost(2 * filt * share * width * (length + 2 * width), 2 * stu.size),
        name="spectral_mix",
    )(lengths, taps, x, u, lags, gains, stu, ar)


def ffn_kernel(
    shift, n, nt_ref, cot_ref, gw_ref, uw_ref, dw_ref, bn_ref, act_ref, bg_ref, bu_ref
):
    share = nt_ref.shape[0]
    nt = nt_ref[...]
    gate = dot(nt, gw_ref[...])
    upper = dot(nt, uw_ref[...])
    start = pl.multiple_of(lax.rem(lax.axis_index("mp") + shift, n) * share, 16)
    back_act = dot_cols(cot_ref[pl.ds(start, share), :], dw_ref[...])
    square = gate * gate
    th = jnp.tanh(SQRT_2_PI * (gate + CUBIC * square * gate))
    half = 0.5 * (1.0 + th)
    gelu = gate * half
    slope = half + 0.5 * gate * (1.0 - th * th) * (SQRT_2_PI * (1.0 + 3.0 * CUBIC * square))
    act_ref[...] = (gelu * upper).astype(BF)
    bg = (back_act * upper * slope).astype(BF)
    bu = (back_act * gelu).astype(BF)
    bg_ref[...] = bg
    bu_ref[...] = bu
    bn_ref[...] = (dot_cols(bg, gw_ref[...]) + dot_cols(bu, uw_ref[...])).astype(BF)


def feed_forward(shift, n, nt, cot, gw, uw, dw):
    share, width = nt.shape
    hid = gw.shape[1]
    return pl.pallas_call(
        functools.partial(ffn_kernel, shift, n),
        in_specs=[whole()] * 5,
        out_specs=[whole()] * 4,
        out_shape=[jax.ShapeDtypeStruct((share, width), BF)]
        + [jax.ShapeDtypeStruct((share, hid), BF)] * 3,
        compiler_params=params(),
        cost_estimate=cost(10 * share * width * hid, 2 * (3 * width * hid + 6 * share * width)),
        name="feed_forward",
    )(nt, cot, gw, uw, dw)


def ffn_grad_kernel(n, share, groups, cot_ref, dw_ref, *refs):
    nt_refs, act_refs, bg_refs, bu_refs = (refs[i * n : (i + 1) * n] for i in range(4))
    out_refs, grad_refs = refs[4 * n : 5 * n], refs[5 * n :]
    m = lax.axis_index("mp")
    nt = jnp.concatenate([ref[...] for ref in nt_refs], axis=0)
    act = jnp.concatenate([ref[...] for ref in act_refs], axis=0)
    bg = jnp.concatenate([ref[...] for ref in bg_refs], axis=0)
    bu = jnp.concatenate([ref[...] for ref in bu_refs], axis=0)
    cot = jnp.concatenate(
        [
            cot_ref[pl.ds(pl.multiple_of(lax.rem(m + r, n) * share, 16), share), :]
            for r in range(n)
        ],
        axis=0,
    )
    outs = dot(act, dw_ref[...]).astype(BF)
    for r in range(n):
        out_refs[r][...] = outs[r * share : (r + 1) * share, :]
    nt_t = nt.T
    grads = (dot(nt_t, bg), dot(nt_t, bu), dot(act.T, cot))
    if not groups:
        for ref, grad in zip(grad_refs, grads):
            ref[...] = grad.astype(BF)
        return
    keep_ref, send_ref, scr = grad_refs
    for i in range(3):
        scr[i] = grads[i].astype(BF)
    rows = scr.shape[1] // (2 * groups)
    d = lax.axis_index("dp")
    core = lax.rem(d, 2)
    for r in range(groups):
        chip = ((d // 2) ^ r) * 2
        for i in range(3):
            mine = pl.multiple_of((chip + core) * rows, 16)
            other = pl.multiple_of((chip + 1 - core) * rows, 16)
            at = (3 * r + i) * rows
            keep_ref[at : at + rows, :] = scr[i, pl.ds(mine, rows), :]
            send_ref[at : at + rows, :] = scr[i, pl.ds(other, rows), :]


def ffn_grads(cot, dw, nts, acts, bgs, bus, groups):
    n = len(nts)
    share, width = nts[0].shape
    hid = dw.shape[0]
    length = cot.shape[0]
    out_shape = [jax.ShapeDtypeStruct((share, width), BF)] * n
    scratch = []
    if groups:
        out_shape += [jax.ShapeDtypeStruct((3 * width // 2, width), BF)] * 2
        scratch = [pltpu.VMEM((3, width, width), BF)]
    else:
        out_shape += [
            jax.ShapeDtypeStruct((width, hid), BF),
            jax.ShapeDtypeStruct((width, hid), BF),
            jax.ShapeDtypeStruct((hid, width), BF),
        ]
    args = [cot, dw, *nts, *acts, *bgs, *bus]
    return pl.pallas_call(
        functools.partial(ffn_grad_kernel, n, share, groups),
        in_specs=[whole()] * len(args),
        out_specs=[whole()] * len(out_shape),
        out_shape=out_shape,
        scratch_shapes=scratch,
        compiler_params=params(),
        cost_estimate=cost(8 * length * width * hid, 12 * length * width),
        name="ffn_grads",
    )(*args)


def mid_kernel(n, share, len_ref, hid_ref, cot_ref, gain_ref, *refs):
    bn_refs, (bh_ref, b_ref, gg_ref) = refs[:n], refs[n:]
    m = lax.axis_index("mp")
    bn = bn_refs[0][...].astype(F32)
    for ref in bn_refs[1:]:
        bn = bn + ref[...].astype(F32)
    hidden = hid_ref[...]
    r2 = lax.rsqrt(jnp.mean(hidden * hidden, axis=-1, keepdims=True) + EPS)
    pos = m * share + lax.broadcasted_iota(jnp.int32, (share, 1), 0)
    bn = bn * (pos < len_ref[0]).astype(F32)
    z = hidden * r2
    gg_ref[...] = jnp.broadcast_to(jnp.sum(bn * z, axis=0, keepdims=True), gg_ref.shape)
    q = bn * gain_ref[1:2, :]
    start = pl.multiple_of(m * share, 16)
    dout = cot_ref[pl.ds(start, share), :].astype(F32)
    back = dout + r2 * (q - z * jnp.mean(q * z, axis=-1, keepdims=True))
    bh_ref[...] = back
    b_ref[...] = back.astype(BF)


def first_sum_kernel(a_ref, b_ref, out_ref):
    out_ref[...] = a_ref[...].astype(F32) + b_ref[...].astype(F32)


def first_sum(a, b):
    return pl.pallas_call(
        first_sum_kernel,
        in_specs=[whole()] * 2,
        out_specs=whole(),
        out_shape=jax.ShapeDtypeStruct(a.shape, F32),
        compiler_params=params(),
        cost_estimate=cost(a.size, 8 * a.size),
        name="first_sum",
    )(a, b)


def mid_norm(lengths, hidden, cot, gain, pieces):
    share, width = hidden.shape
    n = len(pieces)
    return pl.pallas_call(
        functools.partial(mid_kernel, n, share),
        in_specs=[smem()] + [whole()] * (3 + n),
        out_specs=[whole()] * 3,
        out_shape=[
            jax.ShapeDtypeStruct(hidden.shape, F32),
            jax.ShapeDtypeStruct(hidden.shape, BF),
            jax.ShapeDtypeStruct((8, width), F32),
        ],
        compiler_params=params(),
        cost_estimate=cost(20 * hidden.size, 20 * hidden.size),
        name="second_norm_back",
    )(lengths, hidden, cot, gain, *pieces)


def unmix_kernel(
    kb, share, n, len_ref, taps_ref, x_ref, bh_ref, gg_ref, gain_ref, stu_hbm, ar_hbm, *refs
):
    b_refs, (ig_ref, gain_out) = refs[:n], refs[n : n + 2]
    ta_ref, tb_ref, be_ref, bo_ref, lag_ref, acc_ref, scr = refs[n + 2 : n + 9]
    w_buf, ar_ref, sems, ar_sem = refs[n + 9 :]
    j, steps = pl.program_id(0), pl.num_programs(0)
    width = bh_ref.shape[1]
    length = n * share
    half, rows = length // 2, share // 2
    m = lax.axis_index("mp")
    b = lax.broadcasted_iota(jnp.int32, (rows, half), 0)
    a = lax.broadcasted_iota(jnp.int32, (rows, half), 1)
    inside = a < (length - m * share) // 2
    upto = (a >= b) & inside
    below = (a > b) & inside
    slot, wait = fetch_matrices(j, stu_hbm.shape[0] // (2 * kb), kb, stu_hbm, w_buf, sems)

    @pl.when(j == 0)
    def _():
        for r in reversed(range(n)):
            put_columns(scr, b_refs[r][...].astype(F32))
            be_ref[r * rows : (r + 1) * rows, :] = every_second(scr, 0, rows).astype(BF)
            bo_ref[r * rows : (r + 1) * rows, :] = every_second(scr, 1, rows).astype(BF)
        more = b_refs[1 % n][:16, :].astype(F32) * jnp.where(m == n - 1, 0.0, 1.0)
        put_columns(scr, more, share)
        order = lag_ref.shape[1] // width
        for lag in range(order):
            for odd in range(2):
                lag_ref[odd * rows : (odd + 1) * rows, lag * width : (lag + 1) * width] = (
                    every_second(scr, odd + lag, rows).astype(BF)
                )
        acc_ref[...] = jnp.zeros((share, width), F32)

    for k in range(kb):
        even = toeplitz(taps_ref[3, pl.ds(j * kb + k, 1), :], rows)
        odd = toeplitz(taps_ref[4, pl.ds(j * kb + k, 1), :], rows)
        late = toeplitz(taps_ref[5, pl.ds(j * kb + k, 1), :], rows)
        even = jnp.where(upto, even, 0.0).astype(BF)
        at = k * share
        ta_ref[at : at + rows, :] = even
        ta_ref[at + rows : at + share, :] = jnp.where(below, late, 0.0).astype(BF)
        tb_ref[at : at + rows, :] = jnp.where(upto, odd, 0.0).astype(BF)
        tb_ref[at + rows : at + share, :] = even
    ca = dot(ta_ref[...], be_ref[...])
    cb = dot(tb_ref[...], bo_ref[...])
    wait()
    total = acc_ref[...]
    for k in range(kb):
        at = k * share
        pa, pb = ca[at : at + share], cb[at : at + share]
        minus = jnp.concatenate([pa[:rows] - pb[:rows], pb[rows:] - pa[rows:]], axis=0)
        total = total + dot_cols((pa + pb).astype(BF), w_buf[slot, 0, k])
        total = total + dot_cols(minus.astype(BF), w_buf[slot, 1, k])
    acc_ref[...] = total
    fetch_last(j, steps, ar_hbm, ar_ref, ar_sem)

    @pl.when(j == steps - 1)
    def _():
        total = acc_ref[...]
        for lag in range(ar_ref.shape[0]):
            total = total + dot_cols(lag_ref[:, lag * width : (lag + 1) * width], ar_ref[lag])
        x = x_ref[...]
        r1 = lax.rsqrt(jnp.mean(x * x, axis=-1, keepdims=True) + EPS)
        pos = m * share + lax.broadcasted_iota(jnp.int32, (share, 1), 0)
        masked = interleave(scr, total) * (pos < len_ref[0]).astype(F32)
        y = x * r1
        p = masked * gain_ref[0:1, :]
        ig = bh_ref[...] + r1 * (p - y * jnp.mean(p * y, axis=-1, keepdims=True))
        ig_ref[...] = ig.astype(BF)
        gain_out[0:8, :] = jnp.broadcast_to(jnp.sum(masked * y, axis=0, keepdims=True), (8, width))
        gain_out[8:16, :] = gg_ref[...]


def spectral_unmix(lengths, taps, x, back_hidden, gg, gains, stu, ar, pieces, kb):
    share, width = back_hidden.shape
    n = len(pieces)
    length = n * share
    count = taps.shape[1]
    return pl.pallas_call(
        functools.partial(unmix_kernel, kb, share, n),
        grid=(count // kb,),
        in_specs=[smem()] + [whole()] * 5 + [outside()] * 2 + [whole()] * n,
        out_specs=[whole()] * 2,
        out_shape=[
            jax.ShapeDtypeStruct((share, width), BF),
            jax.ShapeDtypeStruct((16, width), F32),
        ],
        scratch_shapes=[
            pltpu.VMEM((kb * share, length // 2), BF),
            pltpu.VMEM((kb * share, length // 2), BF),
            pltpu.VMEM((length // 2, width), BF),
            pltpu.VMEM((length // 2, width), BF),
            pltpu.VMEM((share, ar.shape[0] * width), BF),
            pltpu.VMEM((share, width), F32),
            pltpu.VMEM((width // 128, share + 16, 128), F32),
        ]
        + matrix_scratch(kb, ar),
        compiler_params=params(30 << 20),
        cost_estimate=cost(2 * count * share * width * (length + 2 * width), 2 * stu.size),
        name="spectral_unmix",
    )(lengths, taps, x, back_hidden, gg, gains, stu, ar, *pieces)


def conv_kernel(groups, tile, own, first, filt_ref, *refs):
    ut_refs, (conv_ref, tt_ref, ut_scr) = refs[:groups], refs[groups:]
    j = pl.program_id(0)
    filt, length = filt_ref.shape
    block = conv_ref.shape[1]
    count = length // tile
    chip = lax.axis_index("dp") // 2

    @pl.when(j == 0)
    def _():
        start = pl.multiple_of(chip * block, 16)
        for r in range(groups):
            ut_scr[r * block : (r + 1) * block, :] = ut_refs[r][pl.ds(start, block), :]

    which = lax.axis_index("mp") * own + first + j
    strip = toeplitz(filt_ref[pl.ds(lax.rem(which, filt), 1), :], tile)
    row = lax.broadcasted_iota(jnp.int32, (tile, length), 0)
    col = lax.broadcasted_iota(jnp.int32, (tile, length), 1)
    flip = ((col - row) % 2 == 1) & (which >= filt)
    strip = jnp.where(col >= row, jnp.where(flip, -strip, strip), 0.0).astype(BF)
    for b in range(count):
        tt_ref[b * tile : (b + 1) * tile, b * tile :] = strip[:, : length - b * tile]
    for c in range(count):
        end = (c + 1) * tile
        part = dot(ut_scr[:, :end], tt_ref[:end, c * tile : end]).astype(BF)
        for r in range(groups):
            start = pl.multiple_of((lax.rem(chip, groups) ^ r) * length + c * tile, 128)
            conv_ref[0, :, pl.ds(start, tile)] = part[r * block : (r + 1) * block, :]


def convolutions(filt, uts, own, chips, first, last):
    length = filt.shape[1]
    groups = len(uts)
    block = uts[0].shape[0] // chips
    tile = 256 if length % 256 == 0 else length
    return pl.pallas_call(
        functools.partial(conv_kernel, groups, tile, own, first),
        grid=(last - first,),
        in_specs=[whole()] * (1 + groups),
        out_specs=pl.BlockSpec((1, block, groups * length), lambda j: (j, 0, 0)),
        out_shape=jax.ShapeDtypeStruct((last - first, block, groups * length), BF),
        scratch_shapes=[
            pltpu.VMEM((length, length), BF),
            pltpu.VMEM((groups * block, length), BF),
        ],
        compiler_params=params(),
        cost_estimate=cost(0, 0),
        name="convolutions",
    )(filt, *uts)


def lag_kernel(groups, *refs):
    ut_refs, out_refs = refs[:groups], refs[groups:]
    width, length = ut_refs[0].shape
    chip = lax.rem(lax.axis_index("dp") // 2, groups)
    col = lax.broadcasted_iota(jnp.int32, (width, length), 1)
    for r in range(groups):
        start = pl.multiple_of((chip ^ r) * length, 128)
        out_refs[0][:, pl.ds(start, length)] = ut_refs[r][...]
        value = ut_refs[r][...].astype(F32)
        for lag in range(1, len(out_refs)):
            moved = pltpu.roll(value, lag, 1)
            out_refs[lag][:, pl.ds(start, length)] = jnp.where(col >= lag, moved, 0.0).astype(BF)


def lagged(uts, order):
    groups = len(uts)
    width, length = uts[0].shape
    shape = jax.ShapeDtypeStruct((width, groups * length), BF)
    return pl.pallas_call(
        functools.partial(lag_kernel, groups),
        in_specs=[whole()] * groups,
        out_specs=[whole()] * order,
        out_shape=[shape] * order,
        compiler_params=params(),
        cost_estimate=cost(0, 0),
        name="lagged",
    )(*uts)


def grads_kernel(steps, order, groups, rows, conv_ref, conv_two_ref, *refs):
    lag_refs, b_refs = refs[:order], refs[order : order + len(rows)]
    keep_ref, send_ref, b_scr, scr = refs[order + len(rows) :]
    g = pl.program_id(0)
    d = lax.axis_index("dp")
    chip, core = lax.rem(d // 2, groups), lax.rem(d, 2)
    step, block, depth = conv_ref.shape
    width, length = b_scr.shape[1], depth // groups
    half = block // 2

    @pl.when(g == 0)
    def _():
        for ref, (r, at, size) in zip(b_refs, rows):
            start = pl.multiple_of((chip ^ r) * length + at, 16)
            b_scr[pl.ds(start, size), :] = ref[:size, :]

    for k, ref in enumerate((conv_ref, conv_two_ref)):

        @pl.when((g >= k * steps // 2) & (g < (k + 1) * steps // 2))
        def _():
            part = dot(ref[...].reshape(step * block, depth), b_scr[...])
            scr[...] = part.reshape(step, block, width)

    @pl.when(g < steps)
    def _():
        mine = pl.multiple_of(core * half, 16)
        other = pl.multiple_of((1 - core) * half, 16)
        keep_ref[pl.ds(g * step, step)] = scr[:, pl.ds(mine, half), :]
        for k in range(step):
            start = pl.multiple_of((g * step + k) * half, 16)
            send_ref[pl.ds(start, half), :] = scr[k, pl.ds(other, half), :].astype(BF)

    for lag in range(order):

        @pl.when(g == steps + lag)
        def _():
            at = steps * step * half + lag * width
            send_ref[at : at + width, :] = dot(lag_refs[lag][...], b_scr[...]).astype(BF)


def matrix_grads(convs, lags, backs, rows):
    part, block, depth = convs[0].shape
    own = 2 * part
    order, width = len(lags), lags[0].shape[0]
    groups = 1 + max(r for r, _, _ in rows)
    step = next(s for s in (3, 2, 1) if part % s == 0)
    steps = own // step
    half = block // 2
    return pl.pallas_call(
        functools.partial(grads_kernel, steps, order, groups, rows),
        grid=(steps + order,),
        in_specs=[
            pl.BlockSpec((step, block, depth), lambda g: (jnp.minimum(g, steps // 2 - 1), 0, 0)),
            pl.BlockSpec(
                (step, block, depth), lambda g: (jnp.clip(g - steps // 2, 0, steps // 2 - 1), 0, 0)
            ),
        ]
        + [whole()] * (order + len(backs)),
        out_specs=[whole()] * 2,
        out_shape=[
            jax.ShapeDtypeStruct((own, half, width), F32),
            jax.ShapeDtypeStruct((own * half + order * width, width), BF),
        ],
        scratch_shapes=[
            pltpu.VMEM((depth, width), BF),
            pltpu.VMEM((step, block, width), F32),
        ],
        compiler_params=params(),
        cost_estimate=cost(0, 0),
        name="matrix_grads",
    )(*convs, *lags, *backs)


def rows_message_kernel(ig_ref, hid_ref, *refs):
    share = ig_ref.shape[0]
    total = hid_ref[...]
    for ref in refs[:-1]:
        total = total + ref[...].astype(F32)
    refs[-1][:share, :] = ig_ref[...]
    refs[-1][share:, :] = total.astype(BF)


def rows_message(ig, hidden, pieces):
    share, width = ig.shape
    return pl.pallas_call(
        rows_message_kernel,
        in_specs=[whole()] * (2 + len(pieces)),
        out_specs=whole(),
        out_shape=jax.ShapeDtypeStruct((2 * share, width), BF),
        compiler_params=params(),
        cost_estimate=cost(4 * ig.size, 10 * ig.size),
        name="rows_message",
    )(ig, hidden, *pieces)


def finish_rows_kernel(n, share, *refs):
    pieces, (ig_ref, out_ref) = refs[:n], refs[n:]
    m = lax.axis_index("mp")
    for r in range(n):
        start = pl.multiple_of(lax.rem(m + r, n) * share, 16)
        ig_ref[pl.ds(start, share), :] = pieces[r][:share, :].astype(F32)
        out_ref[pl.ds(start, share), :] = pieces[r][share:, :]


def finish_rows(pieces):
    n = len(pieces)
    share, width = pieces[0].shape[0] // 2, pieces[0].shape[1]
    return pl.pallas_call(
        functools.partial(finish_rows_kernel, n, share),
        in_specs=[whole()] * n,
        out_specs=[whole()] * 2,
        out_shape=[
            jax.ShapeDtypeStruct((n * share, width), F32),
            jax.ShapeDtypeStruct((n * share, width), BF),
        ],
        compiler_params=params(),
        cost_estimate=cost(n * share * width, 6 * n * share * width),
        name="finish_rows",
    )(*pieces)


def ordered_sum_kernel(n, axis, step, *refs):
    pieces, (out_ref, scr) = refs[:n], refs[n:]
    me = lax.axis_index(axis)
    for r in range(n):
        who = lax.rem(me + r, n) if step == 0 else (me // step) ^ r
        scr[who] = pieces[r][...]
    total = scr[0]
    for r in range(1, n):
        total = total + scr[r]
    out_ref[...] = total


def ordered_sum(pieces, axis, step):
    n = len(pieces)
    shape = pieces[0].shape
    return pl.pallas_call(
        functools.partial(ordered_sum_kernel, n, axis, step),
        in_specs=[whole()] * n,
        out_specs=whole(),
        out_shape=jax.ShapeDtypeStruct(shape, F32),
        scratch_shapes=[pltpu.VMEM((n,) + shape, F32)],
        compiler_params=params(),
        cost_estimate=cost(n * pieces[0].size, 4 * n * pieces[0].size),
        name="ordered_sum",
    )(*pieces)


def cores_sum_kernel(keep_ref, recv_ref, sum_ref, to_x, to_y):
    total = (keep_ref[...].astype(F32) + recv_ref[...].astype(F32)).astype(BF)
    sum_ref[...] = total
    half = total.shape[0] // 8
    for k, r in enumerate((1, 3)):
        to_x[k * half : (k + 1) * half, :] = total[2 * r * half : (2 * r + 1) * half]
    for k, r in enumerate((2, 3)):
        to_y[k * half : (k + 1) * half, :] = total[(2 * r + 1) * half : (2 * r + 2) * half]


def cores_sum(keep, recv):
    size, width = keep.shape
    return pl.pallas_call(
        cores_sum_kernel,
        in_specs=[whole()] * 2,
        out_specs=[whole()] * 3,
        out_shape=[jax.ShapeDtypeStruct((rows, width), BF) for rows in (size, size // 4, size // 4)],
        compiler_params=params(),
        cost_estimate=cost(keep.size, 8 * keep.size),
        name="cores_sum",
    )(keep, recv)


def pack_kernel(n, share, extras, *refs):
    pieces, extra_refs, out_refs = refs[:n], refs[n : n + extras], refs[n + extras :]
    m = lax.axis_index("mp")
    for r in range(n):
        start = pl.multiple_of(lax.rem(m + r, n) * share, 16)
        for ref in out_refs:
            ref[pl.ds(start, share), :] = pieces[r][...]
    for ref, extra in zip(out_refs[1:], extra_refs):
        ref[n * share :, :] = extra[...]


def pack_rows(pieces, extras=()):
    n = len(pieces)
    share, width = pieces[0].shape
    rows = [n * share] + [n * share + extra.shape[0] for extra in extras]
    return pl.pallas_call(
        functools.partial(pack_kernel, n, share, len(extras)),
        in_specs=[whole()] * (n + len(extras)),
        out_specs=[whole()] * len(rows),
        out_shape=[jax.ShapeDtypeStruct((r, width), BF) for r in rows],
        compiler_params=params(),
        cost_estimate=cost(n * share * width, 6 * n * share * width),
        name="pack_rows",
    )(*pieces, *extras)


def turn_kernel(x_ref, y_ref, sum_ref, gain_ref, part_ref, to_y, to_x):
    size = part_ref.shape[0] // 2
    half = size // 2
    length = x_ref.shape[0] - size
    gains = split_gains(gain_ref[...])
    for ref, came, at, chunks in ((to_y, x_ref, 0, (0, 2)), (to_x, y_ref, 1, (0, 1))):
        start = at * length // 2
        ref[: length // 2, :] = came[start : start + length // 2, :]
        for k, r in enumerate(chunks):
            own = sum_ref[(2 * r + at) * half : (2 * r + at + 1) * half, :].astype(F32)
            there = length + k * half
            total = (own + came[there : there + half, :].astype(F32)).astype(BF)
            part_ref[at * size + k * half : at * size + (k + 1) * half, :] = total
            ref[length // 2 + k * half : length // 2 + (k + 1) * half, :] = total
        ref[length // 2 + size :, :] = gains


def turn(over_x, over_y, sums, gains):
    size, width = sums.shape[0] // 4, sums.shape[1]
    rows = (over_x.shape[0] - size) // 2 + size + 32
    return pl.pallas_call(
        turn_kernel,
        in_specs=[whole()] * 4,
        out_specs=[whole()] * 3,
        out_shape=[
            jax.ShapeDtypeStruct((2 * size, width), BF),
            jax.ShapeDtypeStruct((rows, width), BF),
            jax.ShapeDtypeStruct((rows, width), BF),
        ],
        compiler_params=params(),
        cost_estimate=cost(over_x.size, 8 * over_x.size),
        name="turn",
    )(over_x, over_y, sums, gains)


def chunks_kernel(part_ref, from_y, from_x, to_x, to_y):
    size = part_ref.shape[0] // 2
    half = size // 2
    at = from_y.shape[0] - 32 - size
    for ref, came, start in ((to_x, from_y, 0), (to_y, from_x, size)):
        for k in range(2):
            there = at + (1 - k) * half
            ref[k * half : (k + 1) * half, :] = (
                part_ref[start + k * half : start + (k + 1) * half, :].astype(F32)
                + came[there : there + half, :].astype(F32)
            ).astype(BF)
    to_x[size:, :] = from_y[at + size :, :]


def whole_chunks(parts, from_y, from_x):
    size, width = parts.shape[0] // 2, parts.shape[1]
    return pl.pallas_call(
        chunks_kernel,
        in_specs=[whole()] * 3,
        out_specs=[whole()] * 2,
        out_shape=[
            jax.ShapeDtypeStruct((size + 32, width), BF),
            jax.ShapeDtypeStruct((size, width), BF),
        ],
        compiler_params=params(),
        cost_estimate=cost(parts.size, 8 * parts.size),
        name="whole_chunks",
    )(parts, from_y, from_x)


def split_gains(both):
    high = both.astype(BF)
    low = (both - high.astype(F32)).astype(BF)
    return jnp.concatenate([high, low], axis=0)


def joined(gains):
    return gains[:16].astype(F32) + gains[16:].astype(F32)


def chips_sum_kernel(gain_ref, from_x, from_y, recv_ref, out_ref, scr):
    chip = lax.axis_index("dp") // 2
    scr[chip] = joined(split_gains(gain_ref[...]))
    for ref, bits in ((from_x, 1), (from_y, 2), (recv_ref, 3)):
        scr[chip ^ bits] = joined(ref[ref.shape[0] - 32 :, :])
    out_ref[...] = ((scr[0] + scr[1]) + scr[2]) + scr[3]


def chips_sum(gains, from_x, from_y, recv):
    return pl.pallas_call(
        chips_sum_kernel,
        in_specs=[whole()] * 4,
        out_specs=whole(),
        out_shape=jax.ShapeDtypeStruct(gains.shape, F32),
        scratch_shapes=[pltpu.VMEM((4,) + gains.shape, F32)],
        compiler_params=params(),
        cost_estimate=cost(4 * gains.size, 16 * gains.size),
        name="chips_sum",
    )(gains, from_x, from_y, recv)


def join_kernel(counts, *refs):
    at = 0
    for ref, count in zip(refs, counts):
        refs[-1][at : at + count, :] = ref[:count, :]
        at += count


def join_pieces(pieces, counts):
    rows = sum(counts)
    return pl.pallas_call(
        functools.partial(join_kernel, counts),
        in_specs=[whole()] * len(pieces),
        out_specs=whole(),
        out_shape=jax.ShapeDtypeStruct((rows, pieces[0].shape[1]), pieces[0].dtype),
        compiler_params=params(),
        cost_estimate=cost(rows * pieces[0].shape[1], 4 * rows * pieces[0].shape[1]),
        name="join_pieces",
    )(*pieces)


def finish_kernel(custom, keep_ref, send_ref, recv_ref, stu_ref, ar_ref, *w_refs):
    own, half, width = keep_ref.shape
    base = 0
    if custom:
        d = lax.axis_index("dp")
        core = lax.rem(d, 2)
        rows = width // 8
        part = 3 * rows // 2
        base = 8 * part
        for r in range(4):
            chip = ((d // 2) ^ r) * 2
            upper, lower = (0, 4, 1, 5)[r] * part, (2, 3, 6, 7)[r] * part
            for ref, which in ((send_ref, chip + core), (recv_ref, chip + 1 - core)):
                start = pl.multiple_of(which * rows, 16)
                chunk = jnp.concatenate(
                    [ref[upper : upper + part, :], ref[lower : lower + part, :]], axis=0
                ).astype(F32)
                for i, out in enumerate(w_refs):
                    out[pl.ds(start, rows), :] = chunk[i * rows : (i + 1) * rows]
    for k in range(own):
        at = base + k * half
        stu_ref[k] = keep_ref[k] + recv_ref[at : at + half, :].astype(F32)
    for i in range(ar_ref.shape[0]):
        at = base + own * half + i * width
        ar_ref[i] = send_ref[at : at + width, :].astype(F32) + recv_ref[
            at : at + width, :
        ].astype(F32)


def finish(keep, send, recv, order, custom):
    width = keep.shape[2]
    more = [jax.ShapeDtypeStruct((width, width), F32)] * (3 if custom else 0)
    return pl.pallas_call(
        functools.partial(finish_kernel, custom),
        in_specs=[whole()] * 3,
        out_specs=[whole()] * (2 + len(more)),
        out_shape=[
            jax.ShapeDtypeStruct(keep.shape, F32),
            jax.ShapeDtypeStruct((order, width, width), F32),
        ]
        + more,
        compiler_params=params(),
        cost_estimate=cost(keep.size, 10 * keep.size),
        name="finish",
    )(keep, send, recv)


def fetch_shifted(value, axis, n):
    pieces = {0: value}
    for r in sorted(range(1, n), key=lambda r: min(r, n - r)):
        pieces[r] = lax.ppermute(value, axis, [(i, (i - r) % n) for i in range(n)])
    return [pieces[r] for r in range(n)]


def send_shifted(pieces, axis):
    n = len(pieces)
    moved = {0: pieces[0]}
    for r in sorted(range(1, n), key=lambda r: min(r, n - r)):
        moved[r] = lax.ppermute(pieces[r], axis, [(i, (i + r) % n) for i in range(n)])
    return [moved[r] for r in range(n)]


def swap(value, axis, n, bits):
    return lax.ppermute(value, axis, [(i, i ^ bits) for i in range(n)])


def after(values, first):
    flat, tree = jax.tree.flatten(values)
    out = lax.optimization_barrier((*flat, *jax.tree.leaves(first)))
    return jax.tree.unflatten(tree, out[: len(flat)])


def shards(
    inputs, lengths, filters, first_gain, stu_weight, ar_weight, second_gain,
    gate_weight, up_weight, down_weight, cotangent,
):
    n = lax.axis_size("mp")
    n_dp = lax.axis_size("dp")
    groups = n_dp // 2
    length, width = inputs.shape
    share = length // n
    order = ar_weight.shape[0]
    own = stu_weight.shape[0] // n
    lengths = lengths.astype(jnp.int32)
    both_gains = jnp.stack([first_gain, second_gain])

    u, ut, x_own, u_lags, taps, natural = first_norm(
        lengths, inputs, both_gains, filters.T, n, order
    )
    uts = [ut] + [swap(ut, "dp", n_dp, 2 * r) for r in range(1, 3)]
    hidden, nt = spectral_mix(
        lengths, taps, x_own, u, u_lags, both_gains, stu_weight, ar_weight, share, 8
    )
    nts = fetch_shifted(nt, "mp", n)
    weights = (cotangent, gate_weight, up_weight, down_weight)
    parts = {0: feed_forward(0, n, after(nt, uts[1:3]), *weights)}
    last = 0
    for r in sorted(range(1, n), key=lambda r: -min(r, n - r)):
        first = parts[last][0]
        parts[r] = feed_forward(r, n, after(nts[r], first), *weights)
        last = r
    uts += [swap(after(ut, nt), "dp", n_dp, 2 * r) for r in range(3, groups)]
    parts = [parts[r] for r in range(n)]
    bns = send_shifted([p[0] for p in parts], "mp")
    acts, bgs, bus = ([p[i] for p in parts] for i in (1, 2, 3))
    custom = n_dp == 8 and gate_weight.shape[1] == width
    grads = ffn_grads(cotangent, down_weight, nts, acts, bgs, bus, groups if custom else 0)
    out_parts, grads = grads[:n], grads[n:]
    bns[1 : n // 2] = after(bns[1 : n // 2], (grads[0], uts))
    far = n // 2
    bns = [first_sum(bns[0], bns[far])] + [bns[r] for r in range(1, n) if r != far]
    back_hidden, back_rows, second_part = mid_norm(lengths, hidden, cotangent, both_gains, bns)
    backs = fetch_shifted(back_rows, "mp", n)
    uts = after(uts, back_rows)
    fours = [uts[r : r + 4] for r in range(0, groups, 4)]
    lags = [lagged(some, order) for some in fours]
    conv = [convolutions(natural, some, own, groups, 0, own // 2) for some in fours]
    backs = after(backs, (lags, conv))
    if custom:
        w_keep, w_send = grads
        w_parts, to_x, to_y = cores_sum(w_keep, swap(after(w_send, back_rows), "dp", n_dp, 1))
        own_back, to_x, to_y = pack_rows(backs, (to_x, to_y))
        over_x, over_y = swap(to_x, "dp", n_dp, 2), swap(to_y, "dp", n_dp, 4)
    else:
        (own_back,) = pack_rows(backs)
    out_sums = send_shifted(after(out_parts, own_back), "mp")
    ig, gains = spectral_unmix(
        lengths, taps, x_own, back_hidden, second_part, both_gains, stu_weight, ar_weight, backs, 8
    )
    uts, hidden = after((uts, hidden), ig)
    fours = [uts[r : r + 4] for r in range(0, groups, 4)]
    conv_two = [convolutions(natural, some, own, groups, own // 2, own) for some in fours]
    message = rows_message(ig, hidden, out_sums)
    messages = fetch_shifted(message, "mp", n)
    if custom:
        w_parts, to_y, to_x = turn(after(over_x, message), over_y, w_parts, gains)
        from_y, from_x = swap(to_y, "dp", n_dp, 4), swap(to_x, "dp", n_dp, 2)
        all_backs = [own_back, over_x, over_y, from_y, from_x]
        half = length // 2
        rows = ((0, 0, length), (1, 0, length), (2, 0, length), (3, 0, half), (3, half, half))
        to_x, to_y = whole_chunks(after(w_parts, conv_two), from_y, from_x)
        w_all = [to_x, to_y, swap(to_x, "dp", n_dp, 2), swap(to_y, "dp", n_dp, 4)]
        gains = chips_sum(gains, from_x, from_y, w_all[2])
        gains = ordered_sum([gains, swap(gains, "dp", n_dp, 1)], "dp", 0)
    else:
        all_backs = [own_back] + [swap(own_back, "dp", n_dp, 2 * r) for r in range(1, groups)]
        rows = tuple((r, 0, length) for r in range(min(groups, 4)))
        gains = ordered_sum([gains] + [swap(gains, "dp", n_dp, r) for r in range(1, n_dp)], "dp", 1)
    gains_dp = gains
    gains = fetch_shifted(gains, "mp", n)

    conv = after(list(zip(conv, conv_two)), message)
    if len(conv) == 1:
        keep, send = matrix_grads(conv[0], lags[0], all_backs, rows)
    else:
        some = [
            matrix_grads(c, lags[k], all_backs[4 * k : 4 * k + 4], rows)
            for k, c in enumerate(conv)
        ]
        keep = ordered_sum([k for k, _ in some], "dp", 8)
        send = ordered_sum([k.astype(F32) for _, k in some], "dp", 8).astype(BF)
    input_grad, output = finish_rows(after(messages, send))
    if custom:
        w_all = after(w_all, (messages, gains_dp))
        counts = [w_all[1].shape[0]] * 4 + [send.shape[0]]
        send = join_pieces([*w_all, send], counts)
    recv = after(swap(send, "dp", n_dp, 1), output)
    stu_grad, ar_grad, *w_grads = finish(keep, send, recv, order, custom)
    gains = ordered_sum(after(gains, stu_grad), "mp", 0)
    if custom:
        gate_grad, up_grad, down_grad = w_grads
    else:
        gate_grad, up_grad, down_grad = (g.astype(F32) for g in lax.psum(tuple(grads), "dp"))
    return (
        output, input_grad, stu_grad, ar_grad, gains[0], gains[8], gate_grad, up_grad, down_grad,
    )


def solution(mesh):
    in_specs = (
        P("dp", None), P("dp"), P(), P(), P(), P(), P(),
        P(None, "mp"), P(None, "mp"), P("mp", None), P("dp", None),
    )
    out_specs = (
        P("dp", None), P("dp", None), P("mp", "dp", None), P(), P(), P(),
        P(None, "mp"), P(None, "mp"), P("mp", None),
    )
    return jax.shard_map(shards, mesh=mesh, in_specs=in_specs, out_specs=out_specs, check_vma=False)
```

```python
import functools

import jax
import jax.numpy as jnp
from jax import lax
from jax.experimental import pallas as pl
from jax.experimental.pallas import tpu as pltpu
from jax.sharding import PartitionSpec as P

EPS = 1e-05
BF = jnp.bfloat16
F32 = jnp.float32
SQRT_2_PI = 0.7978845608028654
CUBIC = 0.044715
VMEM_LIMIT = 20 << 20


def dot(left, right):
    return jnp.dot(left, right, preferred_element_type=F32)


def dot_cols(left, right):
    return lax.dot_general(left, right, (((1,), (1,)), ((), ())), preferred_element_type=F32)


def params(limit=VMEM_LIMIT):
    return pltpu.CompilerParams(vmem_limit_bytes=limit)


COST_SCALE = 1.0


def cost(flops, nbytes):
    return pl.CostEstimate(
        flops=int(COST_SCALE * flops), bytes_accessed=int(COST_SCALE * nbytes), transcendentals=0
    )


def smem():
    return pl.BlockSpec(memory_space=pltpu.SMEM)


def whole():
    return pl.BlockSpec(memory_space=pltpu.VMEM)


def outside():
    return pl.BlockSpec(memory_space=pltpu.HBM)


def toeplitz(base_row, rows, first=0, step=1):
    wide = jnp.broadcast_to(base_row, (rows, base_row.shape[1]))
    return pltpu.roll(wide, first, 1, stride=step, stride_axis=0)


def put_columns(scr, value, at=0):
    for c in range(scr.shape[0]):
        scr[c, at : at + value.shape[0], :] = value[:, c * 128 : (c + 1) * 128]


def every_nth(scr, start, count, step):
    columns = [scr[c, pl.ds(start, count, stride=step), :] for c in range(scr.shape[0])]
    return columns[0] if len(columns) == 1 else jnp.concatenate(columns, axis=1)


def put_every_nth(scr, value, start, step):
    for c in range(scr.shape[0]):
        columns = slice(c * 128, (c + 1) * 128)
        scr[c, pl.ds(start, value.shape[0], stride=step), :] = value[:, columns]


def columns_of(scr, count):
    return jnp.concatenate([scr[c, :count, :] for c in range(scr.shape[0])], axis=1)


def norm_kernel(
    n, share, order, len_ref, x_ref, gain_ref, filt_ref,
    u_ref, ut_ref, ut_two_ref, own_ref, lag_ref, taps_ref, nat_ref, scr, scr_f,
):
    length, width = x_ref.shape
    m = lax.axis_index("mp")
    filt = nat_ref.shape[0]
    x = x_ref[...].astype(F32)
    r1 = lax.rsqrt(jnp.mean(x * x, axis=-1, keepdims=True) + EPS)
    row = lax.broadcasted_iota(jnp.int32, (length, 1), 0)
    mask = (row < len_ref[0]).astype(F32)
    u = mask * x * r1 * gain_ref[0:1, :]
    scr[:, :8, :] = jnp.zeros((scr.shape[0], 8, 128), F32)
    put_columns(scr, u, 8)
    ut = u.T.astype(BF)
    ut_ref[...] = ut
    ut_two_ref[:width, :] = ut
    ut_two_ref[width:, :] = jnp.zeros((ut_two_ref.shape[0] - width, length), BF)
    for odd in range(2):
        u_ref[odd] = every_nth(scr, odd + 8, length // 2, 2).astype(BF)
    for lag in range(order):
        rows = every_nth(scr, m + 8 - lag, share, n)
        lag_ref[:, lag * width : (lag + 1) * width] = rows.astype(BF)
    put_columns(scr, x, 8)
    own_ref[...] = every_nth(scr, m + 8, share, n)
    half = length // 2
    natural = filt_ref[...].astype(F32)
    nat_ref[...] = natural
    scr_f[0, :length, :filt] = natural.T
    even = every_nth(scr_f, 0, half, 2).T[:filt]
    odd = every_nth(scr_f, 1, half, 2).T[:filt]
    i = lax.broadcasted_iota(jnp.int32, (half, half), 0)
    j = lax.broadcasted_iota(jnp.int32, (half, half), 1)
    flip = (i == jnp.where(j == 0, 0, half - j)).astype(F32).astype(BF)
    rev_even = dot(even.astype(BF), flip)
    rev_odd = dot(odd.astype(BF), flip)
    shift, is_odd = m // 2, lax.rem(m, 2)
    one, two = jnp.where(is_odd == 0, rev_even, rev_odd), jnp.where(is_odd == 0, rev_odd, rev_even)
    taps_ref[0] = pltpu.roll(one, shift, 1)
    taps_ref[1] = pltpu.roll(two, lax.rem(shift + half - 1 + is_odd, half), 1)
    one, two = jnp.where(is_odd == 0, even, odd), jnp.where(is_odd == 0, odd, even)
    taps_ref[2] = pltpu.roll(one, shift + is_odd, 1)
    taps_ref[3] = pltpu.roll(two, shift, 1)


def first_norm(lengths, x, gains, filters, n, order):
    length, width = x.shape
    share = length // n
    filt = filters.shape[0]
    return pl.pallas_call(
        functools.partial(norm_kernel, n, share, order),
        in_specs=[smem()] + [whole()] * 3,
        out_specs=[whole()] * 7,
        out_shape=[
            jax.ShapeDtypeStruct((2, length // 2, width), BF),
            jax.ShapeDtypeStruct((width, length), BF),
            jax.ShapeDtypeStruct((width + 16, length), BF),
            jax.ShapeDtypeStruct((share, width), F32),
            jax.ShapeDtypeStruct((share, order * width), BF),
            jax.ShapeDtypeStruct((4, filt, length // 2), F32),
            jax.ShapeDtypeStruct((filt, length), F32),
        ],
        scratch_shapes=[
            pltpu.VMEM((width // 128, length + 24, 128), F32),
            pltpu.VMEM((1, length + 8, 128), F32),
        ],
        compiler_params=params(),
        cost_estimate=cost(10 * x.size, 6 * x.size),
        name="first_norm",
    )(lengths, x, gains, filters)


def fetch_matrices(j, steps, kb, stu_hbm, w_buf, sems):
    def copies(step):
        slot = lax.rem(step, 2)
        return [
            pltpu.make_async_copy(
                stu_hbm.at[pl.ds((sign * steps + step) * kb, kb)],
                w_buf.at[slot, sign],
                sems.at[slot, sign],
            )
            for sign in range(2)
        ]

    @pl.when(j == 0)
    def _():
        for copy in copies(j):
            copy.start()

    @pl.when(j + 1 < steps)
    def _():
        for copy in copies(j + 1):
            copy.start()

    def wait():
        for copy in copies(j):
            copy.wait()

    return lax.rem(j, 2), wait


def fetch_last(j, steps, src, dst, sem):
    copy = pltpu.make_async_copy(src, dst, sem)

    @pl.when(j == 0)
    def _():
        copy.start()

    @pl.when(j == steps - 1)
    def _():
        copy.wait()


def mix_kernel(
    kb, n, len_ref, taps_ref, x_ref, u_ref, lag_ref, gain_ref, stu_hbm, ar_hbm,
    hid_ref, nt_ref, ta_ref, tb_ref, tc_ref, td_ref, c_ref, acc_ref, w_buf, ar_ref, sems, ar_sem,
):
    j, steps = pl.program_id(0), pl.num_programs(0)
    half, width = u_ref.shape[1:]
    share, step = x_ref.shape[0], n // 2
    m = lax.axis_index("mp")
    shift, is_odd = m // 2, lax.rem(m, 2)
    depth = ta_ref.shape[1]
    first = ta_ref.shape[0] // kb
    rest = share - first
    row = lax.broadcasted_iota(jnp.int32, (share, half), 0) * step + shift
    col = lax.broadcasted_iota(jnp.int32, (share, half), 1)
    upto, below = col <= row, col <= row - 1 + is_odd
    slot, wait = fetch_matrices(j, stu_hbm.shape[0] // (2 * kb), kb, stu_hbm, w_buf, sems)

    @pl.when(j == 0)
    def _():
        acc_ref[...] = jnp.zeros((share, width), F32)

    for k in range(kb):
        for which, valid, short, full in ((0, upto, ta_ref, tc_ref), (1, below, tb_ref, td_ref)):
            base = taps_ref[which, pl.ds(j * kb + k, 1), :]
            t = toeplitz(base, first, 0, step)
            t = jnp.where(valid[:first], t, 0.0).astype(BF)
            short[k * first : (k + 1) * first, :] = t[:, :depth]
            t = toeplitz(base, rest, step * first, step)
            full[k * rest : (k + 1) * rest, :] = jnp.where(valid[first:], t, 0.0).astype(BF)
    ca, cb = dot(ta_ref[...], u_ref[0, :depth]), dot(tb_ref[...], u_ref[1, :depth])
    cc, cd = dot(tc_ref[...], u_ref[0]), dot(td_ref[...], u_ref[1])
    sign = jnp.where(is_odd == 0, 1.0, -1.0)
    for k in range(kb):
        plus = slice(k * width, (k + 1) * width)
        minus = slice((kb + k) * width, (kb + k + 1) * width)
        pa, pb = ca[k * first : (k + 1) * first], cb[k * first : (k + 1) * first]
        c_ref[:first, plus] = (pa + pb).astype(BF)
        c_ref[:first, minus] = ((pa - pb) * sign).astype(BF)
        pa, pb = cc[k * rest : (k + 1) * rest], cd[k * rest : (k + 1) * rest]
        c_ref[first:, plus] = (pa + pb).astype(BF)
        c_ref[first:, minus] = ((pa - pb) * sign).astype(BF)
    wait()
    acc_ref[...] += dot(c_ref[...], w_buf[slot].reshape(2 * kb * width, width))
    fetch_last(j, steps, ar_hbm, ar_ref, ar_sem)

    @pl.when(j == steps - 1)
    def _():
        total = acc_ref[...] + dot(lag_ref[...], ar_ref[...].reshape(lag_ref.shape[1], width))
        hidden = x_ref[...] + total
        hid_ref[...] = hidden
        r2 = lax.rsqrt(jnp.mean(hidden * hidden, axis=-1, keepdims=True) + EPS)
        pos = n * lax.broadcasted_iota(jnp.int32, (share, 1), 0) + m
        mask = (pos < len_ref[0]).astype(F32)
        nt_ref[...] = (mask * hidden * r2 * gain_ref[1:2, :]).astype(BF)


def matrix_scratch(kb, ar):
    width = ar.shape[1]
    return [
        pltpu.VMEM((2, 2, kb, width, width), BF),
        pltpu.VMEM(ar.shape, BF),
        pltpu.SemaphoreType.DMA((2, 2)),
        pltpu.SemaphoreType.DMA,
    ]


def spectral_mix(lengths, taps, x, u, lags, gains, stu, ar, n, kb):
    share, width = x.shape
    half = u.shape[1]
    filt = taps.shape[1]
    depth = min(256, half)
    first = depth // (n // 2)
    return pl.pallas_call(
        functools.partial(mix_kernel, kb, n),
        grid=(filt // kb,),
        in_specs=[smem()] + [whole()] * 5 + [outside()] * 2,
        out_specs=[whole()] * 2,
        out_shape=[
            jax.ShapeDtypeStruct((share, width), F32),
            jax.ShapeDtypeStruct((share, width), BF),
        ],
        scratch_shapes=[pltpu.VMEM((kb * first, depth), BF)] * 2
        + [pltpu.VMEM((kb * (share - first), half), BF)] * 2
        + [pltpu.VMEM((share, 2 * kb * width), BF), pltpu.VMEM((share, width), F32)]
        + matrix_scratch(kb, ar),
        compiler_params=params(51 << 20),
        cost_estimate=cost(0, 0),
        name="spectral_mix",
    )(lengths, taps, x, u, lags, gains, stu, ar)


def dealt_kernel(n, in_ref, out_ref, scr):
    share = out_ref.shape[0] // n
    put_columns(scr, in_ref[...].astype(F32))
    for m in range(n):
        out_ref[m * share : (m + 1) * share, :] = every_nth(scr, m, share, n).astype(BF)


def dealt_rows(value, n):
    length, width = value.shape
    return pl.pallas_call(
        functools.partial(dealt_kernel, n),
        in_specs=[whole()],
        out_specs=whole(),
        out_shape=jax.ShapeDtypeStruct(value.shape, BF),
        scratch_shapes=[pltpu.VMEM((width // 128, length + 16, 128), F32)],
        compiler_params=params(),
        cost_estimate=cost(value.size, 4 * value.size),
        name="dealt_rows",
    )(value)


def half_kernel(gate_hbm, up_hbm, down_hbm, out_ref, sems):
    rows = gate_hbm.shape[0] // 2
    start = pl.multiple_of(lax.rem(lax.axis_index("dp"), 2) * rows, 16)
    copies = [
        pltpu.make_async_copy(src.at[pl.ds(start, rows)], out_ref.at[k], sems.at[k])
        for k, src in enumerate((gate_hbm, up_hbm, down_hbm))
    ]
    for copy in copies:
        copy.start()
    for copy in copies:
        copy.wait()


def half_weights(gate, up, down):
    rows, width = gate.shape
    return pl.pallas_call(
        half_kernel,
        in_specs=[outside()] * 3,
        out_specs=whole(),
        out_shape=jax.ShapeDtypeStruct((3, rows // 2, width), BF),
        scratch_shapes=[pltpu.SemaphoreType.DMA((3,))],
        compiler_params=params(),
        cost_estimate=cost(0, 6 * gate.size),
        name="half_weights",
    )(gate, up, down)


def both_halves_kernel(own_ref, other_ref, *out_refs):
    rows = own_ref.shape[1]
    core = lax.rem(lax.axis_index("dp"), 2)
    for ref, which in ((own_ref, core), (other_ref, 1 - core)):
        start = pl.multiple_of(which * rows, 16)
        for k, out in enumerate(out_refs):
            out[pl.ds(start, rows), :] = ref[k]


def both_halves(own, other):
    count, rows, width = own.shape
    return pl.pallas_call(
        both_halves_kernel,
        in_specs=[whole()] * 2,
        out_specs=[whole()] * count,
        out_shape=[jax.ShapeDtypeStruct((2 * rows, width), BF)] * count,
        compiler_params=params(),
        cost_estimate=cost(0, 4 * own.size),
        name="both_halves",
    )(own, other)


def hidden_part(nt, cot, gw, uw, dw):
    gate = dot(nt, gw)
    upper = dot(nt, uw)
    back_act = dot_cols(cot, dw)
    square = gate * gate
    th = jnp.tanh(SQRT_2_PI * (gate + CUBIC * square * gate))
    half = 0.5 * (1.0 + th)
    gelu = gate * half
    slope = half + 0.5 * gate * (1.0 - th * th) * (SQRT_2_PI * (1.0 + 3.0 * CUBIC * square))
    act = (gelu * upper).astype(BF)
    return act, (back_act * upper * slope).astype(BF), (back_act * gelu).astype(BF)


def rows_of(cot_ref, which, share):
    return cot_ref[pl.ds(pl.multiple_of(which * share, 16), share), :]


def ffn_kernel(shift, n, nt_ref, cot_ref, *refs):
    w_refs, (bn_ref, out_ref, act_ref, bg_ref, bu_ref) = refs[:6], refs[6:]
    nt = nt_ref[...]
    cot = rows_of(cot_ref, lax.rem(lax.axis_index("mp") + shift, n), nt.shape[0])
    bn, out = 0.0, 0.0
    for k in range(2):
        gw, uw, dw = (ref[...] for ref in w_refs[3 * k : 3 * k + 3])
        act, bg, bu = hidden_part(nt, cot, gw, uw, dw)
        bn = bn + dot_cols(bg, gw) + dot_cols(bu, uw)
        out = out + dot(act, dw)
        if k == 0:
            act_ref[...] = act
            bg_ref[...] = bg
            bu_ref[...] = bu
    bn_ref[...] = bn.astype(BF)
    out_ref[...] = out.astype(BF)


def feed_forward(shift, n, nt, cot, own, other):
    share, width = nt.shape
    hid = own[0].shape[1]
    return pl.pallas_call(
        functools.partial(ffn_kernel, shift, n),
        in_specs=[whole()] * 8,
        out_specs=[whole()] * 5,
        out_shape=[jax.ShapeDtypeStruct((share, width), BF)] * 2
        + [jax.ShapeDtypeStruct((share, hid), BF)] * 3,
        compiler_params=params(),
        cost_estimate=cost(24 * share * width * hid, 2 * (6 * width * hid + 6 * share * width)),
        name="feed_forward",
    )(nt, cot, *own, *other)


def hidden_kernel(shift, n, nt_ref, cot_ref, gw_ref, uw_ref, dw_ref, act_ref, bg_ref, bu_ref):
    nt = nt_ref[...]
    which = lax.rem((lax.axis_index("mp") ^ 1) + shift, n)
    cot = rows_of(cot_ref, which, nt.shape[0])
    act_ref[...], bg_ref[...], bu_ref[...] = hidden_part(
        nt, cot, gw_ref[...], uw_ref[...], dw_ref[...]
    )


def hidden_rows(shift, n, nt, cot, own):
    share, width = nt.shape
    hid = own[0].shape[1]
    return pl.pallas_call(
        functools.partial(hidden_kernel, shift, n),
        in_specs=[whole()] * 5,
        out_specs=[whole()] * 3,
        out_shape=[jax.ShapeDtypeStruct((share, hid), BF)] * 3,
        compiler_params=params(),
        cost_estimate=cost(6 * share * width * hid, 2 * (3 * width * hid + 6 * share * width)),
        name="hidden_rows",
    )(nt, cot, *own)


def ffn_grad_kernel(n, share, groups, cot_ref, *refs):
    nt_refs, act_refs, bg_refs, bu_refs = (refs[i * n : (i + 1) * n] for i in range(4))
    grad_refs = refs[4 * n :]
    m = lax.axis_index("mp")
    nt = jnp.concatenate([ref[...] for ref in nt_refs], axis=0)
    act = jnp.concatenate([ref[...] for ref in act_refs], axis=0)
    bg = jnp.concatenate([ref[...] for ref in bg_refs], axis=0)
    bu = jnp.concatenate([ref[...] for ref in bu_refs], axis=0)
    cot = jnp.concatenate(
        [
            rows_of(cot_ref, lax.rem(first + shift, n), share)
            for first in (m, m ^ 1)
            for shift in range(0, n, 2)
        ],
        axis=0,
    )
    nt_t = nt.T
    grads = (dot(nt_t, bg), dot(nt_t, bu), dot(act.T, cot))
    if not groups:
        for ref, grad in zip(grad_refs, grads):
            ref[...] = grad.astype(BF)
        return
    keep_ref, send_ref, scr = grad_refs
    for i in range(3):
        scr[i] = grads[i].astype(BF)
    rows = scr.shape[1] // (2 * groups)
    d = lax.axis_index("dp")
    core = lax.rem(d, 2)
    for r in range(groups):
        chip = ((d // 2) ^ r) * 2
        for i in range(3):
            mine = pl.multiple_of((chip + core) * rows, 16)
            other = pl.multiple_of((chip + 1 - core) * rows, 16)
            at = (3 * r + i) * rows
            keep_ref[at : at + rows, :] = scr[i, pl.ds(mine, rows), :]
            send_ref[at : at + rows, :] = scr[i, pl.ds(other, rows), :]


def ffn_grads(cot, nts, acts, bgs, bus, groups):
    n = len(nts)
    share, width = nts[0].shape
    hid = acts[0].shape[1]
    length = cot.shape[0]
    scratch = []
    if groups:
        out_shape = [jax.ShapeDtypeStruct((3 * width // 2, width), BF)] * 2
        scratch = [pltpu.VMEM((3, width, width), BF)]
    else:
        out_shape = [
            jax.ShapeDtypeStruct((width, hid), BF),
            jax.ShapeDtypeStruct((width, hid), BF),
            jax.ShapeDtypeStruct((hid, width), BF),
        ]
    args = [cot, *nts, *acts, *bgs, *bus]
    return pl.pallas_call(
        functools.partial(ffn_grad_kernel, n, share, groups),
        in_specs=[whole()] * len(args),
        out_specs=[whole()] * len(out_shape),
        out_shape=out_shape,
        scratch_shapes=scratch,
        compiler_params=params(),
        cost_estimate=cost(6 * length * width * hid, 12 * length * width),
        name="ffn_grads",
    )(*args)


def mid_kernel(n, share, mp, len_ref, hid_ref, cot_ref, gain_ref, *refs):
    bn_refs, (bh_ref, b_ref, gg_ref) = refs[:n], refs[n:]
    m = lax.axis_index("mp")
    bn = bn_refs[0][...].astype(F32)
    for ref in bn_refs[1:]:
        bn = bn + ref[...].astype(F32)
    hidden = hid_ref[...]
    r2 = lax.rsqrt(jnp.mean(hidden * hidden, axis=-1, keepdims=True) + EPS)
    pos = mp * lax.broadcasted_iota(jnp.int32, (share, 1), 0) + m
    bn = bn * (pos < len_ref[0]).astype(F32)
    z = hidden * r2
    gg_ref[...] = jnp.broadcast_to(jnp.sum(bn * z, axis=0, keepdims=True), gg_ref.shape)
    q = bn * gain_ref[1:2, :]
    start = pl.multiple_of(m * share, 16)
    dout = cot_ref[pl.ds(start, share), :].astype(F32)
    back = dout + r2 * (q - z * jnp.mean(q * z, axis=-1, keepdims=True))
    bh_ref[...] = back
    b_ref[...] = back.astype(BF)


def mid_norm(lengths, hidden, cot, gain, pieces):
    share, width = hidden.shape
    n = len(pieces)
    return pl.pallas_call(
        functools.partial(mid_kernel, n, share, cot.shape[0] // share),
        in_specs=[smem()] + [whole()] * (3 + n),
        out_specs=[whole()] * 3,
        out_shape=[
            jax.ShapeDtypeStruct(hidden.shape, F32),
            jax.ShapeDtypeStruct(hidden.shape, BF),
            jax.ShapeDtypeStruct((8, width), F32),
        ],
        compiler_params=params(),
        cost_estimate=cost(20 * hidden.size, 20 * hidden.size),
        name="second_norm_back",
    )(lengths, hidden, cot, gain, *pieces)


def unmix_kernel(
    kb, n, len_ref, taps_ref, x_ref, bh_ref, gg_ref, gain_ref, stu_hbm, ar_hbm, *refs
):
    b_refs, (ig_ref, gain_out) = refs[:n], refs[n : n + 2]
    ta_ref, tb_ref, tc_ref, td_ref, b_scr, lag_ref, acc_ref, scr = refs[n + 2 : n + 10]
    w_buf, ar_ref, sems, ar_sem = refs[n + 10 :]
    j, steps = pl.program_id(0), pl.num_programs(0)
    share, width = bh_ref.shape
    half, step = n * share // 2, n // 2
    m = lax.axis_index("mp")
    shift, is_odd = m // 2, lax.rem(m, 2)
    depth = tc_ref.shape[1]
    start = half - depth
    first = ta_ref.shape[0] // kb
    rest = share - first
    row = lax.broadcasted_iota(jnp.int32, (share, half), 0) * step + shift
    col = lax.broadcasted_iota(jnp.int32, (share, half), 1)
    above, upto = col >= row + is_odd, col >= row
    slot, wait = fetch_matrices(j, stu_hbm.shape[0] // (2 * kb), kb, stu_hbm, w_buf, sems)

    @pl.when(j == 0)
    def _():
        for r in range(n):
            c = lax.rem(m + r, n)
            value = b_refs[r][...].astype(F32)
            put_every_nth(scr.at[lax.rem(c, 2)], value, c // 2, step)
            if r < lag_ref.shape[1] // width:
                moved = pltpu.roll(value, share - 1, 0)
                last = lax.broadcasted_iota(jnp.int32, (share, 1), 0) == share - 1
                moved = jnp.where(last, 0.0, moved)
                value = jnp.where(m + r >= n, moved, value)
                lag_ref[:, r * width : (r + 1) * width] = value.astype(BF)
        for odd in range(2):
            b_scr[odd] = columns_of(scr.at[odd], half).astype(BF)
        acc_ref[...] = jnp.zeros((share, width), F32)

    for k in range(kb):
        for which, valid, full, short in ((2, above, ta_ref, tc_ref), (3, upto, tb_ref, td_ref)):
            base = taps_ref[which, pl.ds(j * kb + k, 1), :]
            t = toeplitz(base, first, 0, step)
            full[k * first : (k + 1) * first, :] = jnp.where(valid[:first], t, 0.0).astype(BF)
            t = toeplitz(base, rest, step * first, step)
            t = jnp.where(valid[first:], t, 0.0).astype(BF)
            short[k * rest : (k + 1) * rest, :] = t[:, start:]
    ca, cb = dot(ta_ref[...], b_scr[0]), dot(tb_ref[...], b_scr[1])
    cc, cd = dot(tc_ref[...], b_scr[0, start:]), dot(td_ref[...], b_scr[1, start:])
    sign = jnp.where(is_odd == 0, 1.0, -1.0)
    wait()
    total = acc_ref[...]
    for k in range(kb):
        upper, lower = slice(k * first, (k + 1) * first), slice(k * rest, (k + 1) * rest)
        pa = jnp.concatenate([ca[upper], cc[lower]], axis=0)
        pb = jnp.concatenate([cb[upper], cd[lower]], axis=0)
        total = total + dot_cols((pa + pb).astype(BF), w_buf[slot, 0, k])
        total = total + dot_cols(((pa - pb) * sign).astype(BF), w_buf[slot, 1, k])
    acc_ref[...] = total
    fetch_last(j, steps, ar_hbm, ar_ref, ar_sem)

    @pl.when(j == steps - 1)
    def _():
        total = acc_ref[...]
        for lag in range(ar_ref.shape[0]):
            total = total + dot_cols(lag_ref[:, lag * width : (lag + 1) * width], ar_ref[lag])
        x = x_ref[...]
        r1 = lax.rsqrt(jnp.mean(x * x, axis=-1, keepdims=True) + EPS)
        pos = n * lax.broadcasted_iota(jnp.int32, (share, 1), 0) + m
        masked = total * (pos < len_ref[0]).astype(F32)
        y = x * r1
        p = masked * gain_ref[0:1, :]
        ig = bh_ref[...] + r1 * (p - y * jnp.mean(p * y, axis=-1, keepdims=True))
        ig_ref[...] = ig.astype(BF)
        gain_out[0:8, :] = jnp.broadcast_to(jnp.sum(masked * y, axis=0, keepdims=True), (8, width))
        gain_out[8:16, :] = gg_ref[...]


def spectral_unmix(lengths, taps, x, back_hidden, gg, gains, stu, ar, pieces, kb):
    share, width = back_hidden.shape
    n = len(pieces)
    half = n * share // 2
    count = taps.shape[1]
    depth = min(256, half)
    first = (half - depth) // (n // 2)
    return pl.pallas_call(
        functools.partial(unmix_kernel, kb, n),
        grid=(count // kb,),
        in_specs=[smem()] + [whole()] * 5 + [outside()] * 2 + [whole()] * n,
        out_specs=[whole()] * 2,
        out_shape=[
            jax.ShapeDtypeStruct((share, width), BF),
            jax.ShapeDtypeStruct((16, width), F32),
        ],
        scratch_shapes=[pltpu.VMEM((kb * first, half), BF)] * 2
        + [pltpu.VMEM((kb * (share - first), depth), BF)] * 2
        + [
            pltpu.VMEM((2, half, width), BF),
            pltpu.VMEM((share, ar.shape[0] * width), BF),
            pltpu.VMEM((share, width), F32),
            pltpu.VMEM((2, width // 128, half + 8, 128), F32),
        ]
        + matrix_scratch(kb, ar),
        compiler_params=params(30 << 20),
        cost_estimate=cost(4 * count * share * width * (half + width), 2 * stu.size),
        name="spectral_unmix",
    )(lengths, taps, x, back_hidden, gg, gains, stu, ar, *pieces)


def conv_kernel(groups, tile, own, first, filt_ref, *refs):
    ut_refs, (conv_ref, tt_ref, ut_scr) = refs[:groups], refs[groups:]
    j = pl.program_id(0)
    filt, length = filt_ref.shape
    block = conv_ref.shape[1]
    count = length // tile
    chip = lax.axis_index("dp") // 2

    @pl.when(j == 0)
    def _():
        start = pl.multiple_of(chip * block, 16)
        for r in range(groups):
            ut_scr[r * block : (r + 1) * block, :] = ut_refs[r][pl.ds(start, block), :]

    which = lax.axis_index("mp") * own + first + j
    strip = toeplitz(filt_ref[pl.ds(lax.rem(which, filt), 1), :], tile)
    row = lax.broadcasted_iota(jnp.int32, (tile, length), 0)
    col = lax.broadcasted_iota(jnp.int32, (tile, length), 1)
    flip = ((col - row) % 2 == 1) & (which >= filt)
    strip = jnp.where(col >= row, jnp.where(flip, -strip, strip), 0.0).astype(BF)
    for b in range(count):
        tt_ref[b * tile : (b + 1) * tile, b * tile :] = strip[:, : length - b * tile]
    for c in range(count):
        end = (c + 1) * tile
        part = dot(ut_scr[:, :end], tt_ref[:end, c * tile : end]).astype(BF)
        for r in range(groups):
            start = pl.multiple_of((lax.rem(chip, groups) ^ r) * length + c * tile, 128)
            conv_ref[0, :, pl.ds(start, tile)] = part[r * block : (r + 1) * block, :]


def convolutions(filt, uts, own, chips, first, last):
    length = filt.shape[1]
    groups = len(uts)
    block = uts[0].shape[0] // chips
    tile = 256 if length % 256 == 0 else length
    return pl.pallas_call(
        functools.partial(conv_kernel, groups, tile, own, first),
        grid=(last - first,),
        in_specs=[whole()] * (1 + groups),
        out_specs=pl.BlockSpec((1, block, groups * length), lambda j: (j, 0, 0)),
        out_shape=jax.ShapeDtypeStruct((last - first, block, groups * length), BF),
        scratch_shapes=[
            pltpu.VMEM((length, length), BF),
            pltpu.VMEM((groups * block, length), BF),
        ],
        compiler_params=params(),
        cost_estimate=cost(0, 0),
        name="convolutions",
    )(filt, *uts)


def lag_kernel(groups, *refs):
    ut_refs, out_refs = refs[:groups], refs[groups:]
    width, length = ut_refs[0].shape
    chip = lax.rem(lax.axis_index("dp") // 2, groups)
    col = lax.broadcasted_iota(jnp.int32, (width, length), 1)
    for r in range(groups):
        start = pl.multiple_of((chip ^ r) * length, 128)
        out_refs[0][:, pl.ds(start, length)] = ut_refs[r][:width, :]
        value = ut_refs[r][:width, :].astype(F32)
        for lag in range(1, len(out_refs)):
            moved = pltpu.roll(value, lag, 1)
            out_refs[lag][:, pl.ds(start, length)] = jnp.where(col >= lag, moved, 0.0).astype(BF)


def lagged(uts, order):
    groups = len(uts)
    width, length = uts[0].shape
    shape = jax.ShapeDtypeStruct((width, groups * length), BF)
    return pl.pallas_call(
        functools.partial(lag_kernel, groups),
        in_specs=[whole()] * groups,
        out_specs=[whole()] * order,
        out_shape=[shape] * order,
        compiler_params=params(),
        cost_estimate=cost(0, 0),
        name="lagged",
    )(*uts)


def grads_kernel(steps, order, groups, rows, conv_ref, conv_two_ref, *refs):
    lag_refs, b_refs = refs[:order], refs[order : order + len(rows)]
    keep_ref, send_ref, b_scr, scr = refs[order + len(rows) :]
    g = pl.program_id(0)
    d = lax.axis_index("dp")
    chip, core = lax.rem(d // 2, groups), lax.rem(d, 2)
    step, block, depth = conv_ref.shape
    width, length = b_scr.shape[1], depth // groups
    half = block // 2

    @pl.when(g == 0)
    def _():
        for ref, (r, at, size) in zip(b_refs, rows):
            start = pl.multiple_of((chip ^ r) * length + at, 16)
            b_scr[pl.ds(start, size), :] = ref[:size, :]

    for k, ref in enumerate((conv_ref, conv_two_ref)):

        @pl.when((g >= k * steps // 2) & (g < (k + 1) * steps // 2))
        def _():
            part = dot(ref[...].reshape(step * block, depth), b_scr[...])
            scr[...] = part.reshape(step, block, width)

    @pl.when(g < steps)
    def _():
        mine = pl.multiple_of(core * half, 16)
        other = pl.multiple_of((1 - core) * half, 16)
        keep_ref[pl.ds(g * step, step)] = scr[:, pl.ds(mine, half), :]
        for k in range(step):
            start = pl.multiple_of((g * step + k) * half, 16)
            send_ref[pl.ds(start, half), :] = scr[k, pl.ds(other, half), :].astype(BF)

    for lag in range(order):

        @pl.when(g == steps + lag)
        def _():
            at = steps * step * half + lag * width
            send_ref[at : at + width, :] = dot(lag_refs[lag][...], b_scr[...]).astype(BF)


def matrix_grads(convs, lags, backs, rows):
    part, block, depth = convs[0].shape
    own = 2 * part
    order, width = len(lags), lags[0].shape[0]
    groups = 1 + max(r for r, _, _ in rows)
    step = next(s for s in (3, 2, 1) if part % s == 0)
    steps = own // step
    half = block // 2
    return pl.pallas_call(
        functools.partial(grads_kernel, steps, order, groups, rows),
        grid=(steps + order,),
        in_specs=[
            pl.BlockSpec((step, block, depth), lambda g: (jnp.minimum(g, steps // 2 - 1), 0, 0)),
            pl.BlockSpec(
                (step, block, depth), lambda g: (jnp.clip(g - steps // 2, 0, steps // 2 - 1), 0, 0)
            ),
        ]
        + [whole()] * (order + len(backs)),
        out_specs=[whole()] * 2,
        out_shape=[
            jax.ShapeDtypeStruct((own, half, width), F32),
            jax.ShapeDtypeStruct((own * half + order * width, width), BF),
        ],
        scratch_shapes=[
            pltpu.VMEM((depth, width), BF),
            pltpu.VMEM((step, block, width), F32),
        ],
        compiler_params=params(),
        cost_estimate=cost(0, 0),
        name="matrix_grads",
    )(*convs, *lags, *backs)


def rows_message_kernel(ig_ref, hid_ref, *refs):
    share = ig_ref.shape[0]
    total = hid_ref[...]
    for ref in refs[:-1]:
        total = total + ref[...].astype(F32)
    refs[-1][:share, :] = ig_ref[...]
    refs[-1][share:, :] = total.astype(BF)


def rows_message(ig, hidden, pieces):
    share, width = ig.shape
    return pl.pallas_call(
        rows_message_kernel,
        in_specs=[whole()] * (2 + len(pieces)),
        out_specs=whole(),
        out_shape=jax.ShapeDtypeStruct((2 * share, width), BF),
        compiler_params=params(),
        cost_estimate=cost(4 * ig.size, 10 * ig.size),
        name="rows_message",
    )(ig, hidden, *pieces)


def finish_rows_kernel(n, share, *refs):
    pieces, (ig_ref, out_ref, scr) = refs[:n], refs[n:]
    m = lax.axis_index("mp")
    for at, ref in ((0, ig_ref), (share, out_ref)):
        for r in range(n):
            value = pieces[r][at : at + share, :].astype(F32)
            put_every_nth(scr, value, lax.rem(m + r, n), n)
        ref[...] = columns_of(scr, n * share).astype(ref.dtype)


def finish_rows(pieces):
    n = len(pieces)
    share, width = pieces[0].shape[0] // 2, pieces[0].shape[1]
    return pl.pallas_call(
        functools.partial(finish_rows_kernel, n, share),
        in_specs=[whole()] * n,
        out_specs=[whole()] * 2,
        out_shape=[
            jax.ShapeDtypeStruct((n * share, width), F32),
            jax.ShapeDtypeStruct((n * share, width), BF),
        ],
        scratch_shapes=[pltpu.VMEM((width // 128, n * share + 16, 128), F32)],
        compiler_params=params(),
        cost_estimate=cost(1e9, 1e9),
        name="finish_rows",
    )(*pieces)


def ordered_sum_kernel(n, axis, step, *refs):
    pieces, (out_ref, scr) = refs[:n], refs[n:]
    me = lax.axis_index(axis)
    for r in range(n):
        who = lax.rem(me + r, n) if step == 0 else (me // step) ^ r
        scr[who] = pieces[r][...]
    total = scr[0]
    for r in range(1, n):
        total = total + scr[r]
    out_ref[...] = total


def ordered_sum(pieces, axis, step):
    n = len(pieces)
    shape = pieces[0].shape
    return pl.pallas_call(
        functools.partial(ordered_sum_kernel, n, axis, step),
        in_specs=[whole()] * n,
        out_specs=whole(),
        out_shape=jax.ShapeDtypeStruct(shape, F32),
        scratch_shapes=[pltpu.VMEM((n,) + shape, F32)],
        compiler_params=params(),
        cost_estimate=cost(n * pieces[0].size, 4 * n * pieces[0].size),
        name="ordered_sum",
    )(*pieces)


def cores_sum_kernel(keep_ref, recv_ref, upper_ref, lower_ref):
    total = (keep_ref[...].astype(F32) + recv_ref[...].astype(F32)).astype(BF)
    half = total.shape[0] // 8
    for r in range(4):
        at = 2 * r * half
        upper_ref[r * half : (r + 1) * half, :] = total[at : at + half]
        lower_ref[r * half : (r + 1) * half, :] = total[at + half : at + 2 * half]


def cores_sum(keep, recv):
    size, width = keep.shape
    return pl.pallas_call(
        cores_sum_kernel,
        in_specs=[whole()] * 2,
        out_specs=[whole()] * 2,
        out_shape=[jax.ShapeDtypeStruct((size // 2, width), BF)] * 2,
        compiler_params=params(),
        cost_estimate=cost(keep.size, 8 * keep.size),
        name="cores_sum",
    )(keep, recv)


def pack_kernel(n, share, *refs):
    pieces, (out_ref, scr) = refs[:n], refs[n:]
    m = lax.axis_index("mp")
    for r in range(n):
        put_every_nth(scr, pieces[r][...].astype(F32), lax.rem(m + r, n), n)
    out_ref[...] = columns_of(scr, n * share).astype(BF)


def pack_rows(pieces):
    n = len(pieces)
    share, width = pieces[0].shape
    return pl.pallas_call(
        functools.partial(pack_kernel, n, share),
        in_specs=[whole()] * n,
        out_specs=whole(),
        out_shape=jax.ShapeDtypeStruct((n * share, width), BF),
        scratch_shapes=[pltpu.VMEM((width // 128, n * share + 16, 128), F32)],
        compiler_params=params(),
        cost_estimate=cost(n * share * width, 6 * n * share * width),
        name="pack_rows",
    )(*pieces)


def turn_kernel(x_ref, y_ref, upper_ref, lower_ref, gain_ref, to_y, to_x):
    half, size = x_ref.shape[0] // 2, upper_ref.shape[0]
    gains = split_gains(gain_ref[...])
    for ref, rows, w_ref in ((to_y, x_ref[:half, :], lower_ref), (to_x, y_ref[half:, :], upper_ref)):
        ref[:half, :] = rows
        ref[half : half + size, :] = w_ref[...]
        ref[half + size :, :] = gains


def turn(over_x, over_y, upper, lower, gains):
    rows = over_x.shape[0] // 2 + upper.shape[0] + 32
    return pl.pallas_call(
        turn_kernel,
        in_specs=[whole()] * 5,
        out_specs=[whole()] * 2,
        out_shape=[jax.ShapeDtypeStruct((rows, over_x.shape[1]), BF)] * 2,
        compiler_params=params(),
        cost_estimate=cost(over_x.size, 8 * over_x.size),
        name="turn",
    )(over_x, over_y, upper, lower, gains)


def half_sums_kernel(upper_ref, lower_ref, from_y, from_x, to_y, to_x):
    size = to_y.shape[0]
    half = size // 4
    at = from_y.shape[0] - 32 - size
    for ref, own, came, bits in ((to_y, upper_ref, from_x, 1), (to_x, lower_ref, from_y, 2)):
        for r in range(4):
            there = at + (r ^ bits) * half
            ref[r * half : (r + 1) * half, :] = (
                own[r * half : (r + 1) * half, :].astype(F32)
                + came[there : there + half, :].astype(F32)
            ).astype(BF)
    to_x[size:, :] = from_y[at + size :, :]


def half_sums(upper, lower, from_y, from_x):
    size, width = upper.shape
    return pl.pallas_call(
        half_sums_kernel,
        in_specs=[whole()] * 4,
        out_specs=[whole()] * 2,
        out_shape=[jax.ShapeDtypeStruct((rows, width), BF) for rows in (size, size + 32)],
        compiler_params=params(),
        cost_estimate=cost(upper.size, 8 * upper.size),
        name="half_sums",
    )(upper, lower, from_y, from_x)


def chunks_kernel(upper_ref, from_y, lower_ref, from_x, more_ref, out_ref):
    half = upper_ref.shape[0] // 4
    for own, came, bits, lower in ((upper_ref, from_y, 2, 0), (lower_ref, from_x, 1, 1)):
        for r in range(4):
            at, there = (2 * r + lower) * half, (r ^ bits) * half
            out_ref[at : at + half, :] = (
                own[r * half : (r + 1) * half, :].astype(F32)
                + came[there : there + half, :].astype(F32)
            ).astype(BF)
    out_ref[8 * half :, :] = more_ref[...]


def whole_chunks(upper, from_y, lower, from_x, more):
    size, width = upper.shape
    return pl.pallas_call(
        chunks_kernel,
        in_specs=[whole()] * 5,
        out_specs=whole(),
        out_shape=jax.ShapeDtypeStruct((2 * size + more.shape[0], width), BF),
        compiler_params=params(),
        cost_estimate=cost(upper.size, 8 * upper.size),
        name="whole_chunks",
    )(upper, from_y, lower, from_x, more)


def split_gains(both):
    high = both.astype(BF)
    low = (both - high.astype(F32)).astype(BF)
    return jnp.concatenate([high, low], axis=0)


def joined(gains):
    return gains[:16].astype(F32) + gains[16:].astype(F32)


def chips_sum_kernel(gain_ref, from_x, from_y, recv_ref, out_ref, scr):
    chip = lax.axis_index("dp") // 2
    scr[chip] = joined(split_gains(gain_ref[...]))
    for ref, bits in ((from_x, 1), (from_y, 2), (recv_ref, 3)):
        scr[chip ^ bits] = joined(ref[ref.shape[0] - 32 :, :])
    out_ref[...] = ((scr[0] + scr[1]) + scr[2]) + scr[3]


def chips_sum(gains, from_x, from_y, recv):
    return pl.pallas_call(
        chips_sum_kernel,
        in_specs=[whole()] * 4,
        out_specs=whole(),
        out_shape=jax.ShapeDtypeStruct(gains.shape, F32),
        scratch_shapes=[pltpu.VMEM((4,) + gains.shape, F32)],
        compiler_params=params(),
        cost_estimate=cost(4 * gains.size, 16 * gains.size),
        name="chips_sum",
    )(gains, from_x, from_y, recv)


def finish_kernel(custom, keep_ref, send_ref, recv_ref, stu_ref, ar_ref, *w_refs):
    own, half, width = keep_ref.shape
    base = 0
    if custom:
        d = lax.axis_index("dp")
        core = lax.rem(d, 2)
        rows = width // 8
        base = 12 * rows
        for r in range(4):
            chip = ((d // 2) ^ r) * 2
            for ref, which in ((send_ref, chip + core), (recv_ref, chip + 1 - core)):
                start = pl.multiple_of(which * rows, 16)
                for i, out in enumerate(w_refs):
                    at = (3 * r + i) * rows
                    out[pl.ds(start, rows), :] = ref[at : at + rows, :].astype(F32)
    for k in range(own):
        at = base + k * half
        stu_ref[k] = keep_ref[k] + recv_ref[at : at + half, :].astype(F32)
    for i in range(ar_ref.shape[0]):
        at = base + own * half + i * width
        ar_ref[i] = send_ref[at : at + width, :].astype(F32) + recv_ref[
            at : at + width, :
        ].astype(F32)


def finish(keep, send, recv, order, custom):
    width = keep.shape[2]
    more = [jax.ShapeDtypeStruct((width, width), F32)] * (3 if custom else 0)
    return pl.pallas_call(
        functools.partial(finish_kernel, custom),
        in_specs=[whole()] * 3,
        out_specs=[whole()] * (2 + len(more)),
        out_shape=[
            jax.ShapeDtypeStruct(keep.shape, F32),
            jax.ShapeDtypeStruct((order, width, width), F32),
        ]
        + more,
        compiler_params=params(),
        cost_estimate=cost(keep.size, 10 * keep.size),
        name="finish",
    )(keep, send, recv)


def fetch_shifted(value, axis, n, step=1):
    pieces = {0: value}
    for r in sorted(range(step, n, step), key=lambda r: min(r, n - r)):
        pieces[r] = lax.ppermute(value, axis, [(i, (i - r) % n) for i in range(n)])
    return [pieces[r] for r in range(0, n, step)]


def send_shifted(pieces, axis, n, step):
    moved = {0: pieces[0]}
    for r in sorted(range(step, n, step), key=lambda r: min(r, n - r)):
        moved[r] = lax.ppermute(pieces[r // step], axis, [(i, (i + r) % n) for i in range(n)])
    return [moved[r] for r in range(0, n, step)]


def swap(value, axis, n, bits):
    return lax.ppermute(value, axis, [(i, i ^ bits) for i in range(n)])


def swap_sum(value, n):
    return ordered_sum([value, swap(value, "dp", n, 1)], "dp", 0)


def after(values, first):
    flat, tree = jax.tree.flatten(values)
    out = lax.optimization_barrier((*flat, *jax.tree.leaves(first)))
    return jax.tree.unflatten(tree, out[: len(flat)])


def shards(
    inputs, lengths, filters, first_gain, stu_weight, ar_weight, second_gain,
    gate_weight, up_weight, down_weight, cotangent,
):
    n = lax.axis_size("mp")
    n_dp = lax.axis_size("dp")
    groups = n_dp // 2
    length, width = inputs.shape
    share = length // n
    order = ar_weight.shape[0]
    own = stu_weight.shape[0] // n
    lengths = lengths.astype(jnp.int32)
    both_gains = jnp.stack([first_gain, second_gain])

    own_w = (gate_weight, up_weight, down_weight)
    custom = n_dp == 8 and gate_weight.shape[1] == width
    if custom:
        half_w = half_weights(*own_w)
        both_gains = after(both_gains, half_w)
        half_w = swap(half_w, "mp", n, 1)
    u, ut, ut_two, x_own, u_lags, taps, natural = first_norm(
        lengths, inputs, both_gains, filters.T, n, order
    )
    uts = [ut, swap(ut, "dp", n_dp, 2), swap(ut_two, "dp", n_dp, 4)]
    hidden, nt = spectral_mix(
        lengths, taps, x_own, u, u_lags, both_gains, stu_weight, ar_weight, n, 8
    )
    cotangent = dealt_rows(cotangent, n)
    nts = fetch_shifted(nt, "mp", n, 2)
    others = [swap(piece, "mp", n, 1) for piece in nts]
    if custom:
        other_w = both_halves(half_w, swap(after(half_w, nt), "dp", n_dp, 1))
    else:
        other_w = [swap(w, "mp", n, 1) for w in own_w]
    parts = [feed_forward(0, n, after(nt, uts[1:3]), cotangent, own_w, other_w)]
    for k in range(1, n // 2):
        piece = after(nts[k], parts[-1][0])
        parts.append(feed_forward(2 * k, n, piece, cotangent, own_w, other_w))
    uts += [swap(after(ut, nt), "dp", n_dp, 2 * r) for r in range(3, groups)]
    bns = send_shifted([p[0] for p in parts], "mp", n, 2)
    out_parts = [p[1] for p in parts]
    bns[1:] = after(bns[1:], uts)
    back_hidden, back_rows, second_part = mid_norm(lengths, hidden, cotangent, both_gains, bns)
    backs = fetch_shifted(back_rows, "mp", n)
    more = [
        hidden_rows(2 * k, n, after(piece, back_rows), cotangent, own_w)
        for k, piece in enumerate(others)
    ]
    acts, bgs, bus = ([p[i + 2] for p in parts] + [p[i] for p in more] for i in range(3))
    grads = ffn_grads(cotangent, nts + others, acts, bgs, bus, groups if custom else 0)
    uts = after(uts, back_rows)
    fours = [uts[r : r + 4] for r in range(0, groups, 4)]
    lags = [lagged(some, order) for some in fours]
    conv = [convolutions(natural, some, own, groups, 0, own // 2) for some in fours]
    backs = after(backs, (lags, conv))
    own_back = pack_rows(backs)
    if custom:
        over_x, over_y = swap(own_back, "dp", n_dp, 2), swap(own_back, "dp", n_dp, 4)
        w_came = swap(after(grads[1], own_back), "dp", n_dp, 1)
    out_sums = send_shifted(after(out_parts, own_back), "mp", n, 2)
    ig, gains = spectral_unmix(
        lengths, taps, x_own, back_hidden, second_part, both_gains, stu_weight, ar_weight, backs, 8
    )
    uts, hidden = after((uts, hidden), ig)
    fours = [uts[r : r + 4] for r in range(0, groups, 4)]
    conv_two = [convolutions(natural, some, own, groups, own // 2, own) for some in fours]
    message = rows_message(ig, hidden, out_sums)
    messages = fetch_shifted(message, "mp", n)
    if custom:
        upper, lower = cores_sum(grads[0], after(w_came, message))
        to_y, to_x = turn(after(over_x, message), over_y, upper, lower, gains)
        from_y, from_x = swap(to_y, "dp", n_dp, 4), swap(to_x, "dp", n_dp, 2)
        all_backs = [own_back, over_x, over_y, from_y, from_x]
        half = length // 2
        rows = ((0, 0, length), (1, 0, length), (2, 0, length), (3, 0, half), (3, half, half))
        upper, lower = half_sums(after(upper, conv_two), lower, from_y, from_x)
        from_y_two, from_x_two = swap(upper, "dp", n_dp, 4), swap(lower, "dp", n_dp, 2)
        conv_two = after(conv_two, upper)
        gains_parts = (gains, from_x, from_y)
    else:
        all_backs = [own_back] + [swap(own_back, "dp", n_dp, 2 * r) for r in range(1, groups)]
        rows = tuple((r, 0, length) for r in range(min(groups, 4)))
        gains = ordered_sum([gains] + [swap(gains, "dp", n_dp, r) for r in range(1, n_dp)], "dp", 1)
    conv = after(list(zip(conv, conv_two)), message)
    if len(conv) == 1:
        keep, send = matrix_grads(conv[0], lags[0], all_backs, rows)
    else:
        some = [
            matrix_grads(c, lags[k], all_backs[4 * k : 4 * k + 4], rows)
            for k, c in enumerate(conv)
        ]
        keep = ordered_sum([k for k, _ in some], "dp", 8)
        send = ordered_sum([k.astype(F32) for _, k in some], "dp", 8).astype(BF)
    input_grad, output = finish_rows(after(messages, send))
    if custom:
        from_y_two, from_x_two = after((from_y_two, from_x_two), output)
        gains = swap_sum(chips_sum(*gains_parts, after(from_x_two, send)), n_dp)
        send = whole_chunks(upper, from_y_two, lower, from_x_two, after(send, gains))
    gains = fetch_shifted(gains, "mp", n)
    recv = swap(send, "dp", n_dp, 1)
    stu_grad, ar_grad, *w_grads = finish(keep, send, recv, order, custom)
    gains = ordered_sum(after(gains, stu_grad), "mp", 0)
    if custom:
        gate_grad, up_grad, down_grad = w_grads
    else:
        gate_grad, up_grad, down_grad = (g.astype(F32) for g in lax.psum(tuple(grads), "dp"))
    return (
        output, input_grad, stu_grad, ar_grad, gains[0], gains[8], gate_grad, up_grad, down_grad,
    )


def solution(mesh):
    in_specs = (
        P("dp", None), P("dp"), P(), P(), P(), P(), P(),
        P(None, "mp"), P(None, "mp"), P("mp", None), P("dp", None),
    )
    out_specs = (
        P("dp", None), P("dp", None), P("mp", "dp", None), P(), P(), P(),
        P(None, "mp"), P(None, "mp"), P("mp", None),
    )
    return jax.shard_map(shards, mesh=mesh, in_specs=in_specs, out_specs=out_specs, check_vma=False)
```

```python
import functools

import jax
import jax.numpy as jnp
from jax import lax
from jax.experimental import pallas as pl
from jax.experimental.pallas import tpu as pltpu
from jax.sharding import PartitionSpec as P

EPS = 1e-05
BF = jnp.bfloat16
F32 = jnp.float32
SQRT_2_PI = 0.7978845608028654
CUBIC = 0.044715
VMEM_LIMIT = 20 << 20


def dot(left, right):
    return jnp.dot(left, right, preferred_element_type=F32)


def dot_cols(left, right):
    return lax.dot_general(left, right, (((1,), (1,)), ((), ())), preferred_element_type=F32)


def params(limit=VMEM_LIMIT):
    return pltpu.CompilerParams(vmem_limit_bytes=limit)


COST_SCALE = 1.0


def cost(flops, nbytes):
    return pl.CostEstimate(
        flops=int(COST_SCALE * flops), bytes_accessed=int(COST_SCALE * nbytes), transcendentals=0
    )


def smem():
    return pl.BlockSpec(memory_space=pltpu.SMEM)


def whole():
    return pl.BlockSpec(memory_space=pltpu.VMEM)


def outside():
    return pl.BlockSpec(memory_space=pltpu.HBM)


def toeplitz(base_row, rows, first=0, step=1):
    wide = jnp.broadcast_to(base_row, (rows, base_row.shape[1]))
    return pltpu.roll(wide, first, 1, stride=step, stride_axis=0)


def put_columns(scr, value, at=0):
    for c in range(scr.shape[0]):
        scr[c, at : at + value.shape[0], :] = value[:, c * 128 : (c + 1) * 128]


def every_nth(scr, start, count, step):
    columns = [scr[c, pl.ds(start, count, stride=step), :] for c in range(scr.shape[0])]
    return columns[0] if len(columns) == 1 else jnp.concatenate(columns, axis=1)


def put_every_nth(scr, value, start, step):
    for c in range(scr.shape[0]):
        columns = slice(c * 128, (c + 1) * 128)
        scr[c, pl.ds(start, value.shape[0], stride=step), :] = value[:, columns]


def columns_of(scr, count):
    return jnp.concatenate([scr[c, :count, :] for c in range(scr.shape[0])], axis=1)


def norm_kernel(
    n, share, order, len_ref, x_ref, gain_ref, filt_ref,
    u_ref, ut_ref, ut_two_ref, own_ref, lag_ref, taps_ref, nat_ref, scr, scr_f,
):
    length, width = x_ref.shape
    m = lax.axis_index("mp")
    filt = nat_ref.shape[0]
    x = x_ref[...].astype(F32)
    r1 = lax.rsqrt(jnp.mean(x * x, axis=-1, keepdims=True) + EPS)
    row = lax.broadcasted_iota(jnp.int32, (length, 1), 0)
    mask = (row < len_ref[0]).astype(F32)
    u = mask * x * r1 * gain_ref[0:1, :]
    scr[:, :8, :] = jnp.zeros((scr.shape[0], 8, 128), F32)
    put_columns(scr, u, 8)
    ut = u.T.astype(BF)
    ut_ref[...] = ut
    ut_two_ref[:width, :] = ut
    ut_two_ref[width:, :] = jnp.zeros((ut_two_ref.shape[0] - width, length), BF)
    for odd in range(2):
        u_ref[odd] = every_nth(scr, odd + 8, length // 2, 2).astype(BF)
    for lag in range(order):
        rows = every_nth(scr, m + 8 - lag, share, n)
        lag_ref[:, lag * width : (lag + 1) * width] = rows.astype(BF)
    put_columns(scr, x, 8)
    own_ref[...] = every_nth(scr, m + 8, share, n)
    half = length // 2
    natural = filt_ref[...].astype(F32)
    nat_ref[...] = natural
    scr_f[0, :length, :filt] = natural.T
    even = every_nth(scr_f, 0, half, 2).T[:filt]
    odd = every_nth(scr_f, 1, half, 2).T[:filt]
    i = lax.broadcasted_iota(jnp.int32, (half, half), 0)
    j = lax.broadcasted_iota(jnp.int32, (half, half), 1)
    flip = (i == jnp.where(j == 0, 0, half - j)).astype(F32).astype(BF)
    rev_even = dot(even.astype(BF), flip)
    rev_odd = dot(odd.astype(BF), flip)
    shift, is_odd = m // 2, lax.rem(m, 2)
    one, two = jnp.where(is_odd == 0, rev_even, rev_odd), jnp.where(is_odd == 0, rev_odd, rev_even)
    taps_ref[0] = pltpu.roll(one, shift, 1)
    taps_ref[1] = pltpu.roll(two, lax.rem(shift + half - 1 + is_odd, half), 1)
    one, two = jnp.where(is_odd == 0, even, odd), jnp.where(is_odd == 0, odd, even)
    taps_ref[2] = pltpu.roll(one, shift + is_odd, 1)
    taps_ref[3] = pltpu.roll(two, shift, 1)


def first_norm(lengths, x, gains, filters, n, order):
    length, width = x.shape
    share = length // n
    filt = filters.shape[0]
    return pl.pallas_call(
        functools.partial(norm_kernel, n, share, order),
        in_specs=[smem()] + [whole()] * 3,
        out_specs=[whole()] * 7,
        out_shape=[
            jax.ShapeDtypeStruct((2, length // 2, width), BF),
            jax.ShapeDtypeStruct((width, length), BF),
            jax.ShapeDtypeStruct((width + 16, length), BF),
            jax.ShapeDtypeStruct((share, width), F32),
            jax.ShapeDtypeStruct((share, order * width), BF),
            jax.ShapeDtypeStruct((4, filt, length // 2), F32),
            jax.ShapeDtypeStruct((filt, length), F32),
        ],
        scratch_shapes=[
            pltpu.VMEM((width // 128, length + 24, 128), F32),
            pltpu.VMEM((1, length + 8, 128), F32),
        ],
        compiler_params=params(),
        cost_estimate=cost(10 * x.size, 6 * x.size),
        name="first_norm",
    )(lengths, x, gains, filters)


def fetch_matrices(j, steps, kb, stu_hbm, w_buf, sems):
    def copies(step):
        slot = lax.rem(step, 2)
        return [
            pltpu.make_async_copy(
                stu_hbm.at[pl.ds((sign * steps + step) * kb, kb)],
                w_buf.at[slot, sign],
                sems.at[slot, sign],
            )
            for sign in range(2)
        ]

    @pl.when(j == 0)
    def _():
        for copy in copies(j):
            copy.start()

    @pl.when(j + 1 < steps)
    def _():
        for copy in copies(j + 1):
            copy.start()

    def wait():
        for copy in copies(j):
            copy.wait()

    return lax.rem(j, 2), wait


def fetch_last(j, steps, src, dst, sem):
    copy = pltpu.make_async_copy(src, dst, sem)

    @pl.when(j == 0)
    def _():
        copy.start()

    @pl.when(j == steps - 1)
    def _():
        copy.wait()


def mix_kernel(
    kb, n, len_ref, taps_ref, x_ref, u_ref, lag_ref, gain_ref, stu_hbm, ar_hbm,
    hid_ref, nt_ref, ta_ref, tb_ref, tc_ref, td_ref, c_ref, acc_ref, w_buf, ar_ref, sems, ar_sem,
):
    j, steps = pl.program_id(0), pl.num_programs(0)
    half, width = u_ref.shape[1:]
    share, step = x_ref.shape[0], n // 2
    m = lax.axis_index("mp")
    shift, is_odd = m // 2, lax.rem(m, 2)
    depth = ta_ref.shape[1]
    first = ta_ref.shape[0] // kb
    rest = share - first
    row = lax.broadcasted_iota(jnp.int32, (share, half), 0) * step + shift
    col = lax.broadcasted_iota(jnp.int32, (share, half), 1)
    upto, below = col <= row, col <= row - 1 + is_odd
    slot, wait = fetch_matrices(j, stu_hbm.shape[0] // (2 * kb), kb, stu_hbm, w_buf, sems)

    @pl.when(j == 0)
    def _():
        acc_ref[...] = jnp.zeros((share, width), F32)

    for k in range(kb):
        for which, valid, short, full in ((0, upto, ta_ref, tc_ref), (1, below, tb_ref, td_ref)):
            base = taps_ref[which, pl.ds(j * kb + k, 1), :]
            t = toeplitz(base, first, 0, step)
            t = jnp.where(valid[:first], t, 0.0).astype(BF)
            short[k * first : (k + 1) * first, :] = t[:, :depth]
            t = toeplitz(base, rest, step * first, step)
            full[k * rest : (k + 1) * rest, :] = jnp.where(valid[first:], t, 0.0).astype(BF)
    ca, cb = dot(ta_ref[...], u_ref[0, :depth]), dot(tb_ref[...], u_ref[1, :depth])
    cc, cd = dot(tc_ref[...], u_ref[0]), dot(td_ref[...], u_ref[1])
    sign = jnp.where(is_odd == 0, 1.0, -1.0)
    for k in range(kb):
        plus = slice(k * width, (k + 1) * width)
        minus = slice((kb + k) * width, (kb + k + 1) * width)
        pa, pb = ca[k * first : (k + 1) * first], cb[k * first : (k + 1) * first]
        c_ref[:first, plus] = (pa + pb).astype(BF)
        c_ref[:first, minus] = ((pa - pb) * sign).astype(BF)
        pa, pb = cc[k * rest : (k + 1) * rest], cd[k * rest : (k + 1) * rest]
        c_ref[first:, plus] = (pa + pb).astype(BF)
        c_ref[first:, minus] = ((pa - pb) * sign).astype(BF)
    wait()
    acc_ref[...] += dot(c_ref[...], w_buf[slot].reshape(2 * kb * width, width))
    fetch_last(j, steps, ar_hbm, ar_ref, ar_sem)

    @pl.when(j == steps - 1)
    def _():
        total = acc_ref[...] + dot(lag_ref[...], ar_ref[...].reshape(lag_ref.shape[1], width))
        hidden = x_ref[...] + total
        hid_ref[...] = hidden
        r2 = lax.rsqrt(jnp.mean(hidden * hidden, axis=-1, keepdims=True) + EPS)
        pos = n * lax.broadcasted_iota(jnp.int32, (share, 1), 0) + m
        mask = (pos < len_ref[0]).astype(F32)
        nt_ref[...] = (mask * hidden * r2 * gain_ref[1:2, :]).astype(BF)


def matrix_scratch(kb, ar):
    width = ar.shape[1]
    return [
        pltpu.VMEM((2, 2, kb, width, width), BF),
        pltpu.VMEM(ar.shape, BF),
        pltpu.SemaphoreType.DMA((2, 2)),
        pltpu.SemaphoreType.DMA,
    ]


def spectral_mix(lengths, taps, x, u, lags, gains, stu, ar, n, kb):
    share, width = x.shape
    half = u.shape[1]
    filt = taps.shape[1]
    depth = min(256, half)
    first = depth // (n // 2)
    return pl.pallas_call(
        functools.partial(mix_kernel, kb, n),
        grid=(filt // kb,),
        in_specs=[smem()] + [whole()] * 5 + [outside()] * 2,
        out_specs=[whole()] * 2,
        out_shape=[
            jax.ShapeDtypeStruct((share, width), F32),
            jax.ShapeDtypeStruct((share, width), BF),
        ],
        scratch_shapes=[pltpu.VMEM((kb * first, depth), BF)] * 2
        + [pltpu.VMEM((kb * (share - first), half), BF)] * 2
        + [pltpu.VMEM((share, 2 * kb * width), BF), pltpu.VMEM((share, width), F32)]
        + matrix_scratch(kb, ar),
        compiler_params=params(51 << 20),
        cost_estimate=cost(0, 0),
        name="spectral_mix",
    )(lengths, taps, x, u, lags, gains, stu, ar)


def dealt_kernel(n, in_ref, out_ref, scr):
    share = out_ref.shape[0] // n
    put_columns(scr, in_ref[...].astype(F32))
    for m in range(n):
        out_ref[m * share : (m + 1) * share, :] = every_nth(scr, m, share, n).astype(BF)


def dealt_rows(value, n):
    length, width = value.shape
    return pl.pallas_call(
        functools.partial(dealt_kernel, n),
        in_specs=[whole()],
        out_specs=whole(),
        out_shape=jax.ShapeDtypeStruct(value.shape, BF),
        scratch_shapes=[pltpu.VMEM((width // 128, length + 16, 128), F32)],
        compiler_params=params(),
        cost_estimate=cost(value.size, 4 * value.size),
        name="dealt_rows",
    )(value)


def half_kernel(gate_hbm, up_hbm, down_hbm, out_ref, sems):
    rows = gate_hbm.shape[0] // 2
    start = pl.multiple_of(lax.rem(lax.axis_index("dp"), 2) * rows, 16)
    copies = [
        pltpu.make_async_copy(src.at[pl.ds(start, rows)], out_ref.at[k], sems.at[k])
        for k, src in enumerate((gate_hbm, up_hbm, down_hbm))
    ]
    for copy in copies:
        copy.start()
    for copy in copies:
        copy.wait()


def half_weights(gate, up, down):
    rows, width = gate.shape
    return pl.pallas_call(
        half_kernel,
        in_specs=[outside()] * 3,
        out_specs=whole(),
        out_shape=jax.ShapeDtypeStruct((3, rows // 2, width), BF),
        scratch_shapes=[pltpu.SemaphoreType.DMA((3,))],
        compiler_params=params(58 << 20),
        cost_estimate=cost(0, 6 * gate.size),
        name="half_weights",
    )(gate, up, down)


def both_halves_kernel(own_ref, other_ref, *out_refs):
    rows = own_ref.shape[1]
    core = lax.rem(lax.axis_index("dp"), 2)
    for ref, which in ((own_ref, core), (other_ref, 1 - core)):
        start = pl.multiple_of(which * rows, 16)
        for k, out in enumerate(out_refs):
            out[pl.ds(start, rows), :] = ref[k]


def both_halves(own, other):
    count, rows, width = own.shape
    return pl.pallas_call(
        both_halves_kernel,
        in_specs=[whole()] * 2,
        out_specs=[whole()] * count,
        out_shape=[jax.ShapeDtypeStruct((2 * rows, width), BF)] * count,
        compiler_params=params(),
        cost_estimate=cost(0, 4 * own.size),
        name="both_halves",
    )(own, other)


def hidden_part(nt, cot, gw, uw, dw):
    gate = dot(nt, gw)
    upper = dot(nt, uw)
    back_act = dot_cols(cot, dw)
    square = gate * gate
    th = jnp.tanh(SQRT_2_PI * (gate + CUBIC * square * gate))
    half = 0.5 * (1.0 + th)
    gelu = gate * half
    slope = half + 0.5 * gate * (1.0 - th * th) * (SQRT_2_PI * (1.0 + 3.0 * CUBIC * square))
    act = (gelu * upper).astype(BF)
    return act, (back_act * upper * slope).astype(BF), (back_act * gelu).astype(BF)


def rows_of(cot_ref, which, share):
    return cot_ref[pl.ds(pl.multiple_of(which * share, 16), share), :]


def ffn_kernel(shift, n, nt_ref, cot_ref, *refs):
    w_refs, (bn_ref, out_ref, act_ref, bg_ref, bu_ref) = refs[:6], refs[6:]
    nt = nt_ref[...]
    cot = rows_of(cot_ref, lax.rem(lax.axis_index("mp") + shift, n), nt.shape[0])
    bn, out = 0.0, 0.0
    for k in range(2):
        gw, uw, dw = (ref[...] for ref in w_refs[3 * k : 3 * k + 3])
        act, bg, bu = hidden_part(nt, cot, gw, uw, dw)
        bn = bn + dot_cols(bg, gw) + dot_cols(bu, uw)
        out = out + dot(act, dw)
        if k == 0:
            act_ref[...] = act
            bg_ref[...] = bg
            bu_ref[...] = bu
    bn_ref[...] = bn.astype(BF)
    out_ref[...] = out.astype(BF)


def feed_forward(shift, n, nt, cot, own, other):
    share, width = nt.shape
    hid = own[0].shape[1]
    return pl.pallas_call(
        functools.partial(ffn_kernel, shift, n),
        in_specs=[whole()] * 8,
        out_specs=[whole()] * 5,
        out_shape=[jax.ShapeDtypeStruct((share, width), BF)] * 2
        + [jax.ShapeDtypeStruct((share, hid), BF)] * 3,
        compiler_params=params(),
        cost_estimate=cost(24 * share * width * hid, 2 * (6 * width * hid + 6 * share * width)),
        name="feed_forward",
    )(nt, cot, *own, *other)


def hidden_kernel(shift, n, nt_ref, cot_ref, gw_ref, uw_ref, dw_ref, act_ref, bg_ref, bu_ref):
    nt = nt_ref[...]
    which = lax.rem((lax.axis_index("mp") ^ 1) + shift, n)
    cot = rows_of(cot_ref, which, nt.shape[0])
    act_ref[...], bg_ref[...], bu_ref[...] = hidden_part(
        nt, cot, gw_ref[...], uw_ref[...], dw_ref[...]
    )


def hidden_rows(shift, n, nt, cot, own):
    share, width = nt.shape
    hid = own[0].shape[1]
    return pl.pallas_call(
        functools.partial(hidden_kernel, shift, n),
        in_specs=[whole()] * 5,
        out_specs=[whole()] * 3,
        out_shape=[jax.ShapeDtypeStruct((share, hid), BF)] * 3,
        compiler_params=params(),
        cost_estimate=cost(6 * share * width * hid, 2 * (3 * width * hid + 6 * share * width)),
        name="hidden_rows",
    )(nt, cot, *own)


def ffn_grad_kernel(n, share, groups, cot_ref, *refs):
    nt_refs, act_refs, bg_refs, bu_refs = (refs[i * n : (i + 1) * n] for i in range(4))
    grad_refs = refs[4 * n :]
    m = lax.axis_index("mp")
    nt = jnp.concatenate([ref[...] for ref in nt_refs], axis=0)
    act = jnp.concatenate([ref[...] for ref in act_refs], axis=0)
    bg = jnp.concatenate([ref[...] for ref in bg_refs], axis=0)
    bu = jnp.concatenate([ref[...] for ref in bu_refs], axis=0)
    cot = jnp.concatenate(
        [
            rows_of(cot_ref, lax.rem(first + shift, n), share)
            for first in (m, m ^ 1)
            for shift in range(0, n, 2)
        ],
        axis=0,
    )
    nt_t = nt.T
    grads = (dot(nt_t, bg), dot(nt_t, bu), dot(act.T, cot))
    if not groups:
        for ref, grad in zip(grad_refs, grads):
            ref[...] = grad.astype(BF)
        return
    keep_ref, send_ref, scr = grad_refs
    for i in range(3):
        scr[i] = grads[i].astype(BF)
    rows = scr.shape[1] // (2 * groups)
    d = lax.axis_index("dp")
    core = lax.rem(d, 2)
    for r in range(groups):
        chip = ((d // 2) ^ r) * 2
        for i in range(3):
            mine = pl.multiple_of((chip + core) * rows, 16)
            other = pl.multiple_of((chip + 1 - core) * rows, 16)
            at = (3 * r + i) * rows
            keep_ref[at : at + rows, :] = scr[i, pl.ds(mine, rows), :]
            send_ref[at : at + rows, :] = scr[i, pl.ds(other, rows), :]


def ffn_grads(cot, nts, acts, bgs, bus, groups):
    n = len(nts)
    share, width = nts[0].shape
    hid = acts[0].shape[1]
    length = cot.shape[0]
    scratch = []
    if groups:
        out_shape = [jax.ShapeDtypeStruct((3 * width // 2, width), BF)] * 2
        scratch = [pltpu.VMEM((3, width, width), BF)]
    else:
        out_shape = [
            jax.ShapeDtypeStruct((width, hid), BF),
            jax.ShapeDtypeStruct((width, hid), BF),
            jax.ShapeDtypeStruct((hid, width), BF),
        ]
    args = [cot, *nts, *acts, *bgs, *bus]
    return pl.pallas_call(
        functools.partial(ffn_grad_kernel, n, share, groups),
        in_specs=[whole()] * len(args),
        out_specs=[whole()] * len(out_shape),
        out_shape=out_shape,
        scratch_shapes=scratch,
        compiler_params=params(),
        cost_estimate=cost(6 * length * width * hid, 12 * length * width),
        name="ffn_grads",
    )(*args)


def mid_kernel(n, share, mp, len_ref, hid_ref, cot_ref, gain_ref, *refs):
    bn_refs, (bh_ref, b_ref, gg_ref) = refs[:n], refs[n:]
    m = lax.axis_index("mp")
    bn = bn_refs[0][...].astype(F32)
    for ref in bn_refs[1:]:
        bn = bn + ref[...].astype(F32)
    hidden = hid_ref[...]
    r2 = lax.rsqrt(jnp.mean(hidden * hidden, axis=-1, keepdims=True) + EPS)
    pos = mp * lax.broadcasted_iota(jnp.int32, (share, 1), 0) + m
    bn = bn * (pos < len_ref[0]).astype(F32)
    z = hidden * r2
    gg_ref[...] = jnp.broadcast_to(jnp.sum(bn * z, axis=0, keepdims=True), gg_ref.shape)
    q = bn * gain_ref[1:2, :]
    start = pl.multiple_of(m * share, 16)
    dout = cot_ref[pl.ds(start, share), :].astype(F32)
    back = dout + r2 * (q - z * jnp.mean(q * z, axis=-1, keepdims=True))
    bh_ref[...] = back
    b_ref[...] = back.astype(BF)


def mid_norm(lengths, hidden, cot, gain, pieces):
    share, width = hidden.shape
    n = len(pieces)
    return pl.pallas_call(
        functools.partial(mid_kernel, n, share, cot.shape[0] // share),
        in_specs=[smem()] + [whole()] * (3 + n),
        out_specs=[whole()] * 3,
        out_shape=[
            jax.ShapeDtypeStruct(hidden.shape, F32),
            jax.ShapeDtypeStruct(hidden.shape, BF),
            jax.ShapeDtypeStruct((8, width), F32),
        ],
        compiler_params=params(),
        cost_estimate=cost(20 * hidden.size, 20 * hidden.size),
        name="second_norm_back",
    )(lengths, hidden, cot, gain, *pieces)


def unmix_kernel(
    kb, n, len_ref, taps_ref, x_ref, bh_ref, gg_ref, gain_ref, stu_hbm, ar_hbm, *refs
):
    b_refs, (ig_ref, gain_out) = refs[:n], refs[n : n + 2]
    ta_ref, tb_ref, tc_ref, td_ref, b_scr, lag_ref, acc_ref, scr = refs[n + 2 : n + 10]
    w_buf, ar_ref, sems, ar_sem = refs[n + 10 :]
    j, steps = pl.program_id(0), pl.num_programs(0)
    share, width = bh_ref.shape
    half, step = n * share // 2, n // 2
    m = lax.axis_index("mp")
    shift, is_odd = m // 2, lax.rem(m, 2)
    depth = tc_ref.shape[1]
    start = half - depth
    first = ta_ref.shape[0] // kb
    rest = share - first
    row = lax.broadcasted_iota(jnp.int32, (share, half), 0) * step + shift
    col = lax.broadcasted_iota(jnp.int32, (share, half), 1)
    above, upto = col >= row + is_odd, col >= row
    slot, wait = fetch_matrices(j, stu_hbm.shape[0] // (2 * kb), kb, stu_hbm, w_buf, sems)

    @pl.when(j == 0)
    def _():
        for r in range(n):
            c = lax.rem(m + r, n)
            value = b_refs[r][...].astype(F32)
            put_every_nth(scr.at[lax.rem(c, 2)], value, c // 2, step)
            if r < lag_ref.shape[1] // width:
                moved = pltpu.roll(value, share - 1, 0)
                last = lax.broadcasted_iota(jnp.int32, (share, 1), 0) == share - 1
                moved = jnp.where(last, 0.0, moved)
                value = jnp.where(m + r >= n, moved, value)
                lag_ref[:, r * width : (r + 1) * width] = value.astype(BF)
        for odd in range(2):
            b_scr[odd] = columns_of(scr.at[odd], half).astype(BF)
        acc_ref[...] = jnp.zeros((share, width), F32)

    for k in range(kb):
        for which, valid, full, short in ((2, above, ta_ref, tc_ref), (3, upto, tb_ref, td_ref)):
            base = taps_ref[which, pl.ds(j * kb + k, 1), :]
            t = toeplitz(base, first, 0, step)
            full[k * first : (k + 1) * first, :] = jnp.where(valid[:first], t, 0.0).astype(BF)
            t = toeplitz(base, rest, step * first, step)
            t = jnp.where(valid[first:], t, 0.0).astype(BF)
            short[k * rest : (k + 1) * rest, :] = t[:, start:]
    ca, cb = dot(ta_ref[...], b_scr[0]), dot(tb_ref[...], b_scr[1])
    cc, cd = dot(tc_ref[...], b_scr[0, start:]), dot(td_ref[...], b_scr[1, start:])
    sign = jnp.where(is_odd == 0, 1.0, -1.0)
    wait()
    total = acc_ref[...]
    for k in range(kb):
        upper, lower = slice(k * first, (k + 1) * first), slice(k * rest, (k + 1) * rest)
        pa = jnp.concatenate([ca[upper], cc[lower]], axis=0)
        pb = jnp.concatenate([cb[upper], cd[lower]], axis=0)
        total = total + dot_cols((pa + pb).astype(BF), w_buf[slot, 0, k])
        total = total + dot_cols(((pa - pb) * sign).astype(BF), w_buf[slot, 1, k])
    acc_ref[...] = total
    fetch_last(j, steps, ar_hbm, ar_ref, ar_sem)

    @pl.when(j == steps - 1)
    def _():
        total = acc_ref[...]
        for lag in range(ar_ref.shape[0]):
            total = total + dot_cols(lag_ref[:, lag * width : (lag + 1) * width], ar_ref[lag])
        x = x_ref[...]
        r1 = lax.rsqrt(jnp.mean(x * x, axis=-1, keepdims=True) + EPS)
        pos = n * lax.broadcasted_iota(jnp.int32, (share, 1), 0) + m
        masked = total * (pos < len_ref[0]).astype(F32)
        y = x * r1
        p = masked * gain_ref[0:1, :]
        ig = bh_ref[...] + r1 * (p - y * jnp.mean(p * y, axis=-1, keepdims=True))
        ig_ref[...] = ig.astype(BF)
        gain_out[0:8, :] = jnp.broadcast_to(jnp.sum(masked * y, axis=0, keepdims=True), (8, width))
        gain_out[8:16, :] = gg_ref[...]


def spectral_unmix(lengths, taps, x, back_hidden, gg, gains, stu, ar, pieces, kb):
    share, width = back_hidden.shape
    n = len(pieces)
    half = n * share // 2
    count = taps.shape[1]
    depth = min(256, half)
    first = (half - depth) // (n // 2)
    return pl.pallas_call(
        functools.partial(unmix_kernel, kb, n),
        grid=(count // kb,),
        in_specs=[smem()] + [whole()] * 5 + [outside()] * 2 + [whole()] * n,
        out_specs=[whole()] * 2,
        out_shape=[
            jax.ShapeDtypeStruct((share, width), BF),
            jax.ShapeDtypeStruct((16, width), F32),
        ],
        scratch_shapes=[pltpu.VMEM((kb * first, half), BF)] * 2
        + [pltpu.VMEM((kb * (share - first), depth), BF)] * 2
        + [
            pltpu.VMEM((2, half, width), BF),
            pltpu.VMEM((share, ar.shape[0] * width), BF),
            pltpu.VMEM((share, width), F32),
            pltpu.VMEM((2, width // 128, half + 8, 128), F32),
        ]
        + matrix_scratch(kb, ar),
        compiler_params=params(30 << 20),
        cost_estimate=cost(4 * count * share * width * (half + width), 2 * stu.size),
        name="spectral_unmix",
    )(lengths, taps, x, back_hidden, gg, gains, stu, ar, *pieces)


def conv_kernel(groups, tile, own, first, filt_ref, *refs):
    ut_refs, (conv_ref, tt_ref, ut_scr) = refs[:groups], refs[groups:]
    j = pl.program_id(0)
    filt, length = filt_ref.shape
    block = conv_ref.shape[1]
    count = length // tile
    chip = lax.axis_index("dp") // 2

    @pl.when(j == 0)
    def _():
        start = pl.multiple_of(chip * block, 16)
        for r in range(groups):
            ut_scr[r * block : (r + 1) * block, :] = ut_refs[r][pl.ds(start, block), :]

    which = lax.axis_index("mp") * own + first + j
    strip = toeplitz(filt_ref[pl.ds(lax.rem(which, filt), 1), :], tile)
    row = lax.broadcasted_iota(jnp.int32, (tile, length), 0)
    col = lax.broadcasted_iota(jnp.int32, (tile, length), 1)
    flip = ((col - row) % 2 == 1) & (which >= filt)
    strip = jnp.where(col >= row, jnp.where(flip, -strip, strip), 0.0).astype(BF)
    for b in range(count):
        tt_ref[b * tile : (b + 1) * tile, b * tile :] = strip[:, : length - b * tile]
    for c in range(count):
        end = (c + 1) * tile
        part = dot(ut_scr[:, :end], tt_ref[:end, c * tile : end]).astype(BF)
        for r in range(groups):
            start = pl.multiple_of((lax.rem(chip, groups) ^ r) * length + c * tile, 128)
            conv_ref[0, :, pl.ds(start, tile)] = part[r * block : (r + 1) * block, :]


def convolutions(filt, uts, own, chips, first, last):
    length = filt.shape[1]
    groups = len(uts)
    block = uts[0].shape[0] // chips
    tile = 256 if length % 256 == 0 else length
    return pl.pallas_call(
        functools.partial(conv_kernel, groups, tile, own, first),
        grid=(last - first,),
        in_specs=[whole()] * (1 + groups),
        out_specs=pl.BlockSpec((1, block, groups * length), lambda j: (j, 0, 0)),
        out_shape=jax.ShapeDtypeStruct((last - first, block, groups * length), BF),
        scratch_shapes=[
            pltpu.VMEM((length, length), BF),
            pltpu.VMEM((groups * block, length), BF),
        ],
        compiler_params=params(),
        cost_estimate=cost(0, 0),
        name="convolutions",
    )(filt, *uts)


def lag_kernel(groups, *refs):
    ut_refs, out_refs = refs[:groups], refs[groups:]
    width, length = ut_refs[0].shape
    chip = lax.rem(lax.axis_index("dp") // 2, groups)
    col = lax.broadcasted_iota(jnp.int32, (width, length), 1)
    for r in range(groups):
        start = pl.multiple_of((chip ^ r) * length, 128)
        out_refs[0][:, pl.ds(start, length)] = ut_refs[r][:width, :]
        value = ut_refs[r][:width, :].astype(F32)
        for lag in range(1, len(out_refs)):
            moved = pltpu.roll(value, lag, 1)
            out_refs[lag][:, pl.ds(start, length)] = jnp.where(col >= lag, moved, 0.0).astype(BF)


def lagged(uts, order):
    groups = len(uts)
    width, length = uts[0].shape
    shape = jax.ShapeDtypeStruct((width, groups * length), BF)
    return pl.pallas_call(
        functools.partial(lag_kernel, groups),
        in_specs=[whole()] * groups,
        out_specs=[whole()] * order,
        out_shape=[shape] * order,
        compiler_params=params(),
        cost_estimate=cost(0, 0),
        name="lagged",
    )(*uts)


def grads_kernel(steps, order, groups, rows, conv_ref, conv_two_ref, *refs):
    lag_refs, b_refs = refs[:order], refs[order : order + len(rows)]
    keep_ref, send_ref, b_scr, scr = refs[order + len(rows) :]
    g = pl.program_id(0)
    d = lax.axis_index("dp")
    chip, core = lax.rem(d // 2, groups), lax.rem(d, 2)
    step, block, depth = conv_ref.shape
    width, length = b_scr.shape[1], depth // groups
    half = block // 2

    @pl.when(g == 0)
    def _():
        for ref, (r, at, size) in zip(b_refs, rows):
            start = pl.multiple_of((chip ^ r) * length + at, 16)
            b_scr[pl.ds(start, size), :] = ref[:size, :]

    for k, ref in enumerate((conv_ref, conv_two_ref)):

        @pl.when((g >= k * steps // 2) & (g < (k + 1) * steps // 2))
        def _():
            part = dot(ref[...].reshape(step * block, depth), b_scr[...])
            scr[...] = part.reshape(step, block, width)

    @pl.when(g < steps)
    def _():
        mine = pl.multiple_of(core * half, 16)
        other = pl.multiple_of((1 - core) * half, 16)
        keep_ref[pl.ds(g * step, step)] = scr[:, pl.ds(mine, half), :]
        for k in range(step):
            start = pl.multiple_of((g * step + k) * half, 16)
            send_ref[pl.ds(start, half), :] = scr[k, pl.ds(other, half), :].astype(BF)

    for lag in range(order):

        @pl.when(g == steps + lag)
        def _():
            at = steps * step * half + lag * width
            send_ref[at : at + width, :] = dot(lag_refs[lag][...], b_scr[...]).astype(BF)


def matrix_grads(convs, lags, backs, rows):
    part, block, depth = convs[0].shape
    own = 2 * part
    order, width = len(lags), lags[0].shape[0]
    groups = 1 + max(r for r, _, _ in rows)
    step = next(s for s in (3, 2, 1) if part % s == 0)
    steps = own // step
    half = block // 2
    return pl.pallas_call(
        functools.partial(grads_kernel, steps, order, groups, rows),
        grid=(steps + order,),
        in_specs=[
            pl.BlockSpec((step, block, depth), lambda g: (jnp.minimum(g, steps // 2 - 1), 0, 0)),
            pl.BlockSpec(
                (step, block, depth), lambda g: (jnp.clip(g - steps // 2, 0, steps // 2 - 1), 0, 0)
            ),
        ]
        + [whole()] * (order + len(backs)),
        out_specs=[whole()] * 2,
        out_shape=[
            jax.ShapeDtypeStruct((own, half, width), F32),
            jax.ShapeDtypeStruct((own * half + order * width, width), BF),
        ],
        scratch_shapes=[
            pltpu.VMEM((depth, width), BF),
            pltpu.VMEM((step, block, width), F32),
        ],
        compiler_params=params(),
        cost_estimate=cost(0, 0),
        name="matrix_grads",
    )(*convs, *lags, *backs)


def rows_message_kernel(ig_ref, hid_ref, *refs):
    share = ig_ref.shape[0]
    total = hid_ref[...]
    for ref in refs[:-1]:
        total = total + ref[...].astype(F32)
    refs[-1][:share, :] = ig_ref[...]
    refs[-1][share:, :] = total.astype(BF)


def rows_message(ig, hidden, pieces):
    share, width = ig.shape
    return pl.pallas_call(
        rows_message_kernel,
        in_specs=[whole()] * (2 + len(pieces)),
        out_specs=whole(),
        out_shape=jax.ShapeDtypeStruct((2 * share, width), BF),
        compiler_params=params(),
        cost_estimate=cost(4 * ig.size, 10 * ig.size),
        name="rows_message",
    )(ig, hidden, *pieces)


def finish_rows_kernel(n, share, *refs):
    pieces, (ig_ref, out_ref, scr) = refs[:n], refs[n:]
    m = lax.axis_index("mp")
    for at, ref in ((0, ig_ref), (share, out_ref)):
        for r in range(n):
            value = pieces[r][at : at + share, :].astype(F32)
            put_every_nth(scr, value, lax.rem(m + r, n), n)
        ref[...] = columns_of(scr, n * share).astype(ref.dtype)


def finish_rows(pieces):
    n = len(pieces)
    share, width = pieces[0].shape[0] // 2, pieces[0].shape[1]
    return pl.pallas_call(
        functools.partial(finish_rows_kernel, n, share),
        in_specs=[whole()] * n,
        out_specs=[whole()] * 2,
        out_shape=[
            jax.ShapeDtypeStruct((n * share, width), F32),
            jax.ShapeDtypeStruct((n * share, width), BF),
        ],
        scratch_shapes=[pltpu.VMEM((width // 128, n * share + 16, 128), F32)],
        compiler_params=params(),
        cost_estimate=cost(1e9, 1e9),
        name="finish_rows",
    )(*pieces)


def ordered_sum_kernel(n, axis, step, *refs):
    pieces, (out_ref, scr) = refs[:n], refs[n:]
    me = lax.axis_index(axis)
    for r in range(n):
        who = lax.rem(me + r, n) if step == 0 else (me // step) ^ r
        scr[who] = pieces[r][...]
    total = scr[0]
    for r in range(1, n):
        total = total + scr[r]
    out_ref[...] = total


def ordered_sum(pieces, axis, step):
    n = len(pieces)
    shape = pieces[0].shape
    return pl.pallas_call(
        functools.partial(ordered_sum_kernel, n, axis, step),
        in_specs=[whole()] * n,
        out_specs=whole(),
        out_shape=jax.ShapeDtypeStruct(shape, F32),
        scratch_shapes=[pltpu.VMEM((n,) + shape, F32)],
        compiler_params=params(),
        cost_estimate=cost(n * pieces[0].size, 4 * n * pieces[0].size),
        name="ordered_sum",
    )(*pieces)


def cores_sum_kernel(keep_ref, recv_ref, upper_ref, lower_ref):
    total = (keep_ref[...].astype(F32) + recv_ref[...].astype(F32)).astype(BF)
    half = total.shape[0] // 8
    for r in range(4):
        at = 2 * r * half
        upper_ref[r * half : (r + 1) * half, :] = total[at : at + half]
        lower_ref[r * half : (r + 1) * half, :] = total[at + half : at + 2 * half]


def cores_sum(keep, recv):
    size, width = keep.shape
    return pl.pallas_call(
        cores_sum_kernel,
        in_specs=[whole()] * 2,
        out_specs=[whole()] * 2,
        out_shape=[jax.ShapeDtypeStruct((size // 2, width), BF)] * 2,
        compiler_params=params(),
        cost_estimate=cost(keep.size, 8 * keep.size),
        name="cores_sum",
    )(keep, recv)


def pack_kernel(n, share, *refs):
    pieces, (out_ref, scr) = refs[:n], refs[n:]
    m = lax.axis_index("mp")
    for r in range(n):
        put_every_nth(scr, pieces[r][...].astype(F32), lax.rem(m + r, n), n)
    out_ref[...] = columns_of(scr, n * share).astype(BF)


def pack_rows(pieces):
    n = len(pieces)
    share, width = pieces[0].shape
    return pl.pallas_call(
        functools.partial(pack_kernel, n, share),
        in_specs=[whole()] * n,
        out_specs=whole(),
        out_shape=jax.ShapeDtypeStruct((n * share, width), BF),
        scratch_shapes=[pltpu.VMEM((width // 128, n * share + 16, 128), F32)],
        compiler_params=params(),
        cost_estimate=cost(n * share * width, 6 * n * share * width),
        name="pack_rows",
    )(*pieces)


def turn_kernel(x_ref, y_ref, upper_ref, lower_ref, gain_ref, to_y, to_x):
    half, size = x_ref.shape[0] // 2, upper_ref.shape[0]
    gains = split_gains(gain_ref[...])
    for ref, rows, w_ref in ((to_y, x_ref[:half, :], lower_ref), (to_x, y_ref[half:, :], upper_ref)):
        ref[:half, :] = rows
        ref[half : half + size, :] = w_ref[...]
        ref[half + size :, :] = gains


def turn(over_x, over_y, upper, lower, gains):
    rows = over_x.shape[0] // 2 + upper.shape[0] + 32
    return pl.pallas_call(
        turn_kernel,
        in_specs=[whole()] * 5,
        out_specs=[whole()] * 2,
        out_shape=[jax.ShapeDtypeStruct((rows, over_x.shape[1]), BF)] * 2,
        compiler_params=params(),
        cost_estimate=cost(over_x.size, 8 * over_x.size),
        name="turn",
    )(over_x, over_y, upper, lower, gains)


def half_sums_kernel(upper_ref, lower_ref, from_y, from_x, to_y, to_x):
    size = to_y.shape[0]
    half = size // 4
    at = from_y.shape[0] - 32 - size
    for ref, own, came, bits in ((to_y, upper_ref, from_x, 1), (to_x, lower_ref, from_y, 2)):
        for r in range(4):
            there = at + (r ^ bits) * half
            ref[r * half : (r + 1) * half, :] = (
                own[r * half : (r + 1) * half, :].astype(F32)
                + came[there : there + half, :].astype(F32)
            ).astype(BF)
    to_x[size:, :] = from_y[at + size :, :]


def half_sums(upper, lower, from_y, from_x):
    size, width = upper.shape
    return pl.pallas_call(
        half_sums_kernel,
        in_specs=[whole()] * 4,
        out_specs=[whole()] * 2,
        out_shape=[jax.ShapeDtypeStruct((rows, width), BF) for rows in (size, size + 32)],
        compiler_params=params(),
        cost_estimate=cost(upper.size, 8 * upper.size),
        name="half_sums",
    )(upper, lower, from_y, from_x)


def chunks_kernel(upper_ref, from_y, lower_ref, from_x, more_ref, out_ref):
    half = upper_ref.shape[0] // 4
    for own, came, bits, lower in ((upper_ref, from_y, 2, 0), (lower_ref, from_x, 1, 1)):
        for r in range(4):
            at, there = (2 * r + lower) * half, (r ^ bits) * half
            out_ref[at : at + half, :] = (
                own[r * half : (r + 1) * half, :].astype(F32)
                + came[there : there + half, :].astype(F32)
            ).astype(BF)
    out_ref[8 * half :, :] = more_ref[...]


def whole_chunks(upper, from_y, lower, from_x, more):
    size, width = upper.shape
    return pl.pallas_call(
        chunks_kernel,
        in_specs=[whole()] * 5,
        out_specs=whole(),
        out_shape=jax.ShapeDtypeStruct((2 * size + more.shape[0], width), BF),
        compiler_params=params(),
        cost_estimate=cost(upper.size, 8 * upper.size),
        name="whole_chunks",
    )(upper, from_y, lower, from_x, more)


def split_gains(both):
    high = both.astype(BF)
    low = (both - high.astype(F32)).astype(BF)
    return jnp.concatenate([high, low], axis=0)


def joined(gains):
    return gains[:16].astype(F32) + gains[16:].astype(F32)


def chips_sum_kernel(gain_ref, from_x, from_y, recv_ref, out_ref, scr):
    chip = lax.axis_index("dp") // 2
    scr[chip] = joined(split_gains(gain_ref[...]))
    for ref, bits in ((from_x, 1), (from_y, 2), (recv_ref, 3)):
        scr[chip ^ bits] = joined(ref[ref.shape[0] - 32 :, :])
    out_ref[...] = ((scr[0] + scr[1]) + scr[2]) + scr[3]


def chips_sum(gains, from_x, from_y, recv):
    return pl.pallas_call(
        chips_sum_kernel,
        in_specs=[whole()] * 4,
        out_specs=whole(),
        out_shape=jax.ShapeDtypeStruct(gains.shape, F32),
        scratch_shapes=[pltpu.VMEM((4,) + gains.shape, F32)],
        compiler_params=params(),
        cost_estimate=cost(4 * gains.size, 16 * gains.size),
        name="chips_sum",
    )(gains, from_x, from_y, recv)


def finish_kernel(custom, keep_ref, send_ref, recv_ref, stu_ref, ar_ref, *w_refs):
    own, half, width = keep_ref.shape
    base = 0
    if custom:
        d = lax.axis_index("dp")
        core = lax.rem(d, 2)
        rows = width // 8
        base = 12 * rows
        for r in range(4):
            chip = ((d // 2) ^ r) * 2
            for ref, which in ((send_ref, chip + core), (recv_ref, chip + 1 - core)):
                start = pl.multiple_of(which * rows, 16)
                for i, out in enumerate(w_refs):
                    at = (3 * r + i) * rows
                    out[pl.ds(start, rows), :] = ref[at : at + rows, :].astype(F32)
    for k in range(own):
        at = base + k * half
        stu_ref[k] = keep_ref[k] + recv_ref[at : at + half, :].astype(F32)
    for i in range(ar_ref.shape[0]):
        at = base + own * half + i * width
        ar_ref[i] = send_ref[at : at + width, :].astype(F32) + recv_ref[
            at : at + width, :
        ].astype(F32)


def finish(keep, send, recv, order, custom):
    width = keep.shape[2]
    more = [jax.ShapeDtypeStruct((width, width), F32)] * (3 if custom else 0)
    return pl.pallas_call(
        functools.partial(finish_kernel, custom),
        in_specs=[whole()] * 3,
        out_specs=[whole()] * (2 + len(more)),
        out_shape=[
            jax.ShapeDtypeStruct(keep.shape, F32),
            jax.ShapeDtypeStruct((order, width, width), F32),
        ]
        + more,
        compiler_params=params(),
        cost_estimate=cost(keep.size, 10 * keep.size),
        name="finish",
    )(keep, send, recv)


def fetch_shifted(value, axis, n, step=1):
    pieces = {0: value}
    for r in sorted(range(step, n, step), key=lambda r: min(r, n - r)):
        pieces[r] = lax.ppermute(value, axis, [(i, (i - r) % n) for i in range(n)])
    return [pieces[r] for r in range(0, n, step)]


def send_shifted(pieces, axis, n, step):
    moved = {0: pieces[0]}
    for r in sorted(range(step, n, step), key=lambda r: min(r, n - r)):
        moved[r] = lax.ppermute(pieces[r // step], axis, [(i, (i + r) % n) for i in range(n)])
    return [moved[r] for r in range(0, n, step)]


def swap(value, axis, n, bits):
    return lax.ppermute(value, axis, [(i, i ^ bits) for i in range(n)])


def swap_sum(value, n):
    return ordered_sum([value, swap(value, "dp", n, 1)], "dp", 0)


def after(values, first):
    flat, tree = jax.tree.flatten(values)
    out = lax.optimization_barrier((*flat, *jax.tree.leaves(first)))
    return jax.tree.unflatten(tree, out[: len(flat)])


def shards(
    inputs, lengths, filters, first_gain, stu_weight, ar_weight, second_gain,
    gate_weight, up_weight, down_weight, cotangent,
):
    n = lax.axis_size("mp")
    n_dp = lax.axis_size("dp")
    groups = n_dp // 2
    length, width = inputs.shape
    share = length // n
    order = ar_weight.shape[0]
    own = stu_weight.shape[0] // n
    lengths = lengths.astype(jnp.int32)
    both_gains = jnp.stack([first_gain, second_gain])

    own_w = (gate_weight, up_weight, down_weight)
    custom = n_dp == 8 and gate_weight.shape[1] == width
    if custom:
        half_w = half_weights(*own_w)
        both_gains = after(both_gains, half_w)
        half_w = swap(half_w, "mp", n, 1)
    u, ut, ut_two, x_own, u_lags, taps, natural = first_norm(
        lengths, inputs, both_gains, filters.T, n, order
    )
    uts = [ut, swap(ut, "dp", n_dp, 2), swap(ut_two, "dp", n_dp, 4)]
    hidden, nt = spectral_mix(
        lengths, taps, x_own, u, u_lags, both_gains, stu_weight, ar_weight, n, 8
    )
    cotangent = dealt_rows(cotangent, n)
    nts = fetch_shifted(nt, "mp", n, 2)
    others = [swap(piece, "mp", n, 1) for piece in nts]
    if custom:
        other_w = both_halves(half_w, swap(after(half_w, nt), "dp", n_dp, 1))
    else:
        other_w = [swap(w, "mp", n, 1) for w in own_w]
    parts = [feed_forward(0, n, after(nt, uts[1:3]), cotangent, own_w, other_w)]
    for k in range(1, n // 2):
        piece = after(nts[k], parts[-1][0])
        parts.append(feed_forward(2 * k, n, piece, cotangent, own_w, other_w))
    uts += [swap(after(ut, nt), "dp", n_dp, 2 * r) for r in range(3, groups)]
    bns = send_shifted([p[0] for p in parts], "mp", n, 2)
    out_parts = [p[1] for p in parts]
    bns[1:] = after(bns[1:], uts)
    back_hidden, back_rows, second_part = mid_norm(lengths, hidden, cotangent, both_gains, bns)
    backs = fetch_shifted(back_rows, "mp", n)
    more = [
        hidden_rows(2 * k, n, after(piece, back_rows), cotangent, own_w)
        for k, piece in enumerate(others)
    ]
    acts, bgs, bus = ([p[i + 2] for p in parts] + [p[i] for p in more] for i in range(3))
    grads = ffn_grads(cotangent, nts + others, acts, bgs, bus, groups if custom else 0)
    uts = after(uts, back_rows)
    fours = [uts[r : r + 4] for r in range(0, groups, 4)]
    lags = [lagged(some, order) for some in fours]
    conv = [convolutions(natural, some, own, groups, 0, own // 2) for some in fours]
    backs = after(backs, (lags, conv))
    own_back = pack_rows(backs)
    if custom:
        over_x, over_y = swap(own_back, "dp", n_dp, 2), swap(own_back, "dp", n_dp, 4)
        w_came = swap(after(grads[1], own_back), "dp", n_dp, 1)
    out_sums = send_shifted(after(out_parts, own_back), "mp", n, 2)
    ig, gains = spectral_unmix(
        lengths, taps, x_own, back_hidden, second_part, both_gains, stu_weight, ar_weight, backs, 8
    )
    uts, hidden = after((uts, hidden), ig)
    fours = [uts[r : r + 4] for r in range(0, groups, 4)]
    conv_two = [convolutions(natural, some, own, groups, own // 2, own) for some in fours]
    message = rows_message(ig, hidden, out_sums)
    messages = fetch_shifted(message, "mp", n)
    if custom:
        upper, lower = cores_sum(grads[0], after(w_came, message))
        to_y, to_x = turn(after(over_x, message), over_y, upper, lower, gains)
        from_y, from_x = swap(to_y, "dp", n_dp, 4), swap(to_x, "dp", n_dp, 2)
        all_backs = [own_back, over_x, over_y, from_y, from_x]
        half = length // 2
        rows = ((0, 0, length), (1, 0, length), (2, 0, length), (3, 0, half), (3, half, half))
        upper, lower = half_sums(after(upper, conv_two), lower, from_y, from_x)
        from_y_two, from_x_two = swap(upper, "dp", n_dp, 4), swap(lower, "dp", n_dp, 2)
        conv_two = after(conv_two, upper)
        gains_parts = (gains, from_x, from_y)
    else:
        all_backs = [own_back] + [swap(own_back, "dp", n_dp, 2 * r) for r in range(1, groups)]
        rows = tuple((r, 0, length) for r in range(min(groups, 4)))
        gains = ordered_sum([gains] + [swap(gains, "dp", n_dp, r) for r in range(1, n_dp)], "dp", 1)
    conv = after(list(zip(conv, conv_two)), message)
    if len(conv) == 1:
        keep, send = matrix_grads(conv[0], lags[0], all_backs, rows)
    else:
        some = [
            matrix_grads(c, lags[k], all_backs[4 * k : 4 * k + 4], rows)
            for k, c in enumerate(conv)
        ]
        keep = ordered_sum([k for k, _ in some], "dp", 8)
        send = ordered_sum([k.astype(F32) for _, k in some], "dp", 8).astype(BF)
    input_grad, output = finish_rows(after(messages, send))
    if custom:
        from_y_two, from_x_two = after((from_y_two, from_x_two), output)
        gains = swap_sum(chips_sum(*gains_parts, after(from_x_two, send)), n_dp)
        send = whole_chunks(upper, from_y_two, lower, from_x_two, after(send, gains))
    gains = fetch_shifted(gains, "mp", n)
    recv = swap(send, "dp", n_dp, 1)
    stu_grad, ar_grad, *w_grads = finish(keep, send, recv, order, custom)
    gains = ordered_sum(after(gains, stu_grad), "mp", 0)
    if custom:
        gate_grad, up_grad, down_grad = w_grads
    else:
        gate_grad, up_grad, down_grad = (g.astype(F32) for g in lax.psum(tuple(grads), "dp"))
    return (
        output, input_grad, stu_grad, ar_grad, gains[0], gains[8], gate_grad, up_grad, down_grad,
    )


def solution(mesh):
    in_specs = (
        P("dp", None), P("dp"), P(), P(), P(), P(), P(),
        P(None, "mp"), P(None, "mp"), P("mp", None), P("dp", None),
    )
    out_specs = (
        P("dp", None), P("dp", None), P("mp", "dp", None), P(), P(), P(),
        P(None, "mp"), P(None, "mp"), P("mp", None),
    )
    return jax.shard_map(shards, mesh=mesh, in_specs=in_specs, out_specs=out_specs, check_vma=False)
```

```python
import functools

import jax
import jax.numpy as jnp
from jax import lax
from jax.experimental import pallas as pl
from jax.experimental.pallas import tpu as pltpu
from jax.sharding import PartitionSpec as P

EPS = 1e-05
BF = jnp.bfloat16
F32 = jnp.float32
SQRT_2_PI = 0.7978845608028654
CUBIC = 0.044715
VMEM_LIMIT = 20 << 20


def dot(left, right):
    return jnp.dot(left, right, preferred_element_type=F32)


def dot_cols(left, right):
    return lax.dot_general(left, right, (((1,), (1,)), ((), ())), preferred_element_type=F32)


def params(limit=VMEM_LIMIT):
    return pltpu.CompilerParams(vmem_limit_bytes=limit)


COST_SCALE = 1.0


def cost(flops, nbytes):
    return pl.CostEstimate(
        flops=int(COST_SCALE * flops), bytes_accessed=int(COST_SCALE * nbytes), transcendentals=0
    )


def smem():
    return pl.BlockSpec(memory_space=pltpu.SMEM)


def whole():
    return pl.BlockSpec(memory_space=pltpu.VMEM)


def outside():
    return pl.BlockSpec(memory_space=pltpu.HBM)


def toeplitz(base_row, rows, first=0, step=1):
    wide = jnp.broadcast_to(base_row, (rows, base_row.shape[1]))
    return pltpu.roll(wide, first, 1, stride=step, stride_axis=0)


def put_columns(scr, value, at=0):
    for c in range(scr.shape[0]):
        scr[c, at : at + value.shape[0], :] = value[:, c * 128 : (c + 1) * 128]


def every_nth(scr, start, count, step):
    columns = [scr[c, pl.ds(start, count, stride=step), :] for c in range(scr.shape[0])]
    return columns[0] if len(columns) == 1 else jnp.concatenate(columns, axis=1)


def put_every_nth(scr, value, start, step):
    for c in range(scr.shape[0]):
        columns = slice(c * 128, (c + 1) * 128)
        scr[c, pl.ds(start, value.shape[0], stride=step), :] = value[:, columns]


def columns_of(scr, count):
    return jnp.concatenate([scr[c, :count, :] for c in range(scr.shape[0])], axis=1)


def norm_kernel(
    n, share, order, len_ref, x_ref, gain_ref, filt_ref,
    u_ref, ut_ref, ut_two_ref, own_ref, lag_ref, taps_ref, nat_ref, scr, scr_f,
):
    length, width = x_ref.shape
    m = lax.axis_index("mp")
    filt = nat_ref.shape[0]
    x = x_ref[...].astype(F32)
    r1 = lax.rsqrt(jnp.mean(x * x, axis=-1, keepdims=True) + EPS)
    row = lax.broadcasted_iota(jnp.int32, (length, 1), 0)
    mask = (row < len_ref[0]).astype(F32)
    u = mask * x * r1 * gain_ref[0:1, :]
    scr[:, :8, :] = jnp.zeros((scr.shape[0], 8, 128), F32)
    put_columns(scr, u, 8)
    ut = u.T.astype(BF)
    ut_ref[...] = ut
    ut_two_ref[:width, :] = ut
    ut_two_ref[width:, :] = jnp.zeros((ut_two_ref.shape[0] - width, length), BF)
    for odd in range(2):
        u_ref[odd] = every_nth(scr, odd + 8, length // 2, 2).astype(BF)
    for lag in range(order):
        rows = every_nth(scr, m + 8 - lag, share, n)
        lag_ref[:, lag * width : (lag + 1) * width] = rows.astype(BF)
    put_columns(scr, x, 8)
    own_ref[...] = every_nth(scr, m + 8, share, n)
    half = length // 2
    natural = filt_ref[...].astype(F32)
    nat_ref[...] = natural
    scr_f[0, :length, :filt] = natural.T
    even = every_nth(scr_f, 0, half, 2).T[:filt]
    odd = every_nth(scr_f, 1, half, 2).T[:filt]
    i = lax.broadcasted_iota(jnp.int32, (half, half), 0)
    j = lax.broadcasted_iota(jnp.int32, (half, half), 1)
    flip = (i == jnp.where(j == 0, 0, half - j)).astype(F32).astype(BF)
    rev_even = dot(even.astype(BF), flip)
    rev_odd = dot(odd.astype(BF), flip)
    shift, is_odd = m // 2, lax.rem(m, 2)
    one, two = jnp.where(is_odd == 0, rev_even, rev_odd), jnp.where(is_odd == 0, rev_odd, rev_even)
    taps_ref[0] = pltpu.roll(one, shift, 1)
    taps_ref[1] = pltpu.roll(two, lax.rem(shift + half - 1 + is_odd, half), 1)
    one, two = jnp.where(is_odd == 0, even, odd), jnp.where(is_odd == 0, odd, even)
    taps_ref[2] = pltpu.roll(one, shift + is_odd, 1)
    taps_ref[3] = pltpu.roll(two, shift, 1)


def first_norm(lengths, x, gains, filters, n, order):
    length, width = x.shape
    share = length // n
    filt = filters.shape[0]
    return pl.pallas_call(
        functools.partial(norm_kernel, n, share, order),
        in_specs=[smem()] + [whole()] * 3,
        out_specs=[whole()] * 7,
        out_shape=[
            jax.ShapeDtypeStruct((2, length // 2, width), BF),
            jax.ShapeDtypeStruct((width, length), BF),
            jax.ShapeDtypeStruct((width + 16, length), BF),
            jax.ShapeDtypeStruct((share, width), F32),
            jax.ShapeDtypeStruct((share, order * width), BF),
            jax.ShapeDtypeStruct((4, filt, length // 2), F32),
            jax.ShapeDtypeStruct((filt, length), F32),
        ],
        scratch_shapes=[
            pltpu.VMEM((width // 128, length + 24, 128), F32),
            pltpu.VMEM((1, length + 8, 128), F32),
        ],
        compiler_params=params(),
        cost_estimate=cost(10 * x.size, 6 * x.size),
        name="first_norm",
    )(lengths, x, gains, filters)


def fetch_matrices(j, steps, kb, stu_hbm, w_buf, sems):
    def copies(step):
        slot = lax.rem(step, 2)
        return [
            pltpu.make_async_copy(
                stu_hbm.at[pl.ds((sign * steps + step) * kb, kb)],
                w_buf.at[slot, sign],
                sems.at[slot, sign],
            )
            for sign in range(2)
        ]

    @pl.when(j == 0)
    def _():
        for copy in copies(j):
            copy.start()

    @pl.when(j + 1 < steps)
    def _():
        for copy in copies(j + 1):
            copy.start()

    def wait():
        for copy in copies(j):
            copy.wait()

    return lax.rem(j, 2), wait


def fetch_last(j, steps, src, dst, sem):
    copy = pltpu.make_async_copy(src, dst, sem)

    @pl.when(j == 0)
    def _():
        copy.start()

    @pl.when(j == steps - 1)
    def _():
        copy.wait()


def mix_kernel(
    kb, n, len_ref, taps_ref, x_ref, u_ref, lag_ref, gain_ref, stu_hbm, ar_hbm,
    hid_ref, nt_ref, ta_ref, tb_ref, tc_ref, td_ref, c_ref, acc_ref, w_buf, ar_ref, sems, ar_sem,
):
    j, steps = pl.program_id(0), pl.num_programs(0)
    half, width = u_ref.shape[1:]
    share, step = x_ref.shape[0], n // 2
    m = lax.axis_index("mp")
    shift, is_odd = m // 2, lax.rem(m, 2)
    depth = ta_ref.shape[1]
    first = ta_ref.shape[0] // kb
    rest = share - first
    row = lax.broadcasted_iota(jnp.int32, (share, half), 0) * step + shift
    col = lax.broadcasted_iota(jnp.int32, (share, half), 1)
    upto, below = col <= row, col <= row - 1 + is_odd
    slot, wait = fetch_matrices(j, stu_hbm.shape[0] // (2 * kb), kb, stu_hbm, w_buf, sems)

    @pl.when(j == 0)
    def _():
        acc_ref[...] = jnp.zeros((share, width), F32)

    for k in range(kb):
        for which, valid, short, full in ((0, upto, ta_ref, tc_ref), (1, below, tb_ref, td_ref)):
            base = taps_ref[which, pl.ds(j * kb + k, 1), :]
            t = toeplitz(base, first, 0, step)
            t = jnp.where(valid[:first], t, 0.0).astype(BF)
            short[k * first : (k + 1) * first, :] = t[:, :depth]
            t = toeplitz(base, rest, step * first, step)
            full[k * rest : (k + 1) * rest, :] = jnp.where(valid[first:], t, 0.0).astype(BF)
    ca, cb = dot(ta_ref[...], u_ref[0, :depth]), dot(tb_ref[...], u_ref[1, :depth])
    cc, cd = dot(tc_ref[...], u_ref[0]), dot(td_ref[...], u_ref[1])
    sign = jnp.where(is_odd == 0, 1.0, -1.0)
    for k in range(kb):
        plus = slice(k * width, (k + 1) * width)
        minus = slice((kb + k) * width, (kb + k + 1) * width)
        pa, pb = ca[k * first : (k + 1) * first], cb[k * first : (k + 1) * first]
        c_ref[:first, plus] = (pa + pb).astype(BF)
        c_ref[:first, minus] = ((pa - pb) * sign).astype(BF)
        pa, pb = cc[k * rest : (k + 1) * rest], cd[k * rest : (k + 1) * rest]
        c_ref[first:, plus] = (pa + pb).astype(BF)
        c_ref[first:, minus] = ((pa - pb) * sign).astype(BF)
    wait()
    acc_ref[...] += dot(c_ref[...], w_buf[slot].reshape(2 * kb * width, width))
    fetch_last(j, steps, ar_hbm, ar_ref, ar_sem)

    @pl.when(j == steps - 1)
    def _():
        total = acc_ref[...] + dot(lag_ref[...], ar_ref[...].reshape(lag_ref.shape[1], width))
        hidden = x_ref[...] + total
        hid_ref[...] = hidden
        r2 = lax.rsqrt(jnp.mean(hidden * hidden, axis=-1, keepdims=True) + EPS)
        pos = n * lax.broadcasted_iota(jnp.int32, (share, 1), 0) + m
        mask = (pos < len_ref[0]).astype(F32)
        nt_ref[...] = (mask * hidden * r2 * gain_ref[1:2, :]).astype(BF)


def matrix_scratch(kb, ar):
    width = ar.shape[1]
    return [
        pltpu.VMEM((2, 2, kb, width, width), BF),
        pltpu.VMEM(ar.shape, BF),
        pltpu.SemaphoreType.DMA((2, 2)),
        pltpu.SemaphoreType.DMA,
    ]


def spectral_mix(lengths, taps, x, u, lags, gains, stu, ar, n, kb):
    share, width = x.shape
    half = u.shape[1]
    filt = taps.shape[1]
    depth = min(256, half)
    first = depth // (n // 2)
    return pl.pallas_call(
        functools.partial(mix_kernel, kb, n),
        grid=(filt // kb,),
        in_specs=[smem()] + [whole()] * 5 + [outside()] * 2,
        out_specs=[whole()] * 2,
        out_shape=[
            jax.ShapeDtypeStruct((share, width), F32),
            jax.ShapeDtypeStruct((share, width), BF),
        ],
        scratch_shapes=[pltpu.VMEM((kb * first, depth), BF)] * 2
        + [pltpu.VMEM((kb * (share - first), half), BF)] * 2
        + [pltpu.VMEM((share, 2 * kb * width), BF), pltpu.VMEM((share, width), F32)]
        + matrix_scratch(kb, ar),
        compiler_params=params(51 << 20),
        cost_estimate=cost(0, 0),
        name="spectral_mix",
    )(lengths, taps, x, u, lags, gains, stu, ar)


def dealt_kernel(n, in_ref, out_ref, scr):
    share = out_ref.shape[0] // n
    put_columns(scr, in_ref[...].astype(F32))
    for m in range(n):
        out_ref[m * share : (m + 1) * share, :] = every_nth(scr, m, share, n).astype(BF)


def dealt_rows(value, n):
    length, width = value.shape
    return pl.pallas_call(
        functools.partial(dealt_kernel, n),
        in_specs=[whole()],
        out_specs=whole(),
        out_shape=jax.ShapeDtypeStruct(value.shape, BF),
        scratch_shapes=[pltpu.VMEM((width // 128, length + 16, 128), F32)],
        compiler_params=params(),
        cost_estimate=cost(value.size, 4 * value.size),
        name="dealt_rows",
    )(value)


def half_kernel(gate_hbm, up_hbm, down_hbm, out_ref, sems):
    rows = gate_hbm.shape[0] // 2
    start = pl.multiple_of(lax.rem(lax.axis_index("dp"), 2) * rows, 16)
    copies = [
        pltpu.make_async_copy(src.at[pl.ds(start, rows)], out_ref.at[k], sems.at[k])
        for k, src in enumerate((gate_hbm, up_hbm, down_hbm))
    ]
    for copy in copies:
        copy.start()
    for copy in copies:
        copy.wait()


def half_weights(gate, up, down):
    rows, width = gate.shape
    return pl.pallas_call(
        half_kernel,
        in_specs=[outside()] * 3,
        out_specs=whole(),
        out_shape=jax.ShapeDtypeStruct((3, rows // 2, width), BF),
        scratch_shapes=[pltpu.SemaphoreType.DMA((3,))],
        compiler_params=params(58 << 20),
        cost_estimate=cost(0, 6 * gate.size),
        name="half_weights",
    )(gate, up, down)


def both_halves_kernel(own_ref, other_ref, *out_refs):
    rows = own_ref.shape[1]
    core = lax.rem(lax.axis_index("dp"), 2)
    for ref, which in ((own_ref, core), (other_ref, 1 - core)):
        start = pl.multiple_of(which * rows, 16)
        for k, out in enumerate(out_refs):
            out[pl.ds(start, rows), :] = ref[k]


def both_halves(own, other):
    count, rows, width = own.shape
    return pl.pallas_call(
        both_halves_kernel,
        in_specs=[whole()] * 2,
        out_specs=[whole()] * count,
        out_shape=[jax.ShapeDtypeStruct((2 * rows, width), BF)] * count,
        compiler_params=params(),
        cost_estimate=cost(0, 4 * own.size),
        name="both_halves",
    )(own, other)


def hidden_part(nt, cot, gw, uw, dw):
    gate = dot(nt, gw)
    upper = dot(nt, uw)
    back_act = dot_cols(cot, dw)
    square = gate * gate
    th = jnp.tanh(SQRT_2_PI * (gate + CUBIC * square * gate))
    half = 0.5 * (1.0 + th)
    gelu = gate * half
    slope = half + 0.5 * gate * (1.0 - th * th) * (SQRT_2_PI * (1.0 + 3.0 * CUBIC * square))
    act = (gelu * upper).astype(BF)
    return act, (back_act * upper * slope).astype(BF), (back_act * gelu).astype(BF)


def rows_of(cot_ref, which, share):
    return cot_ref[pl.ds(pl.multiple_of(which * share, 16), share), :]


def ffn_kernel(shift, n, nt_ref, cot_ref, *refs):
    w_refs, (bn_ref, out_ref, act_ref, bg_ref, bu_ref) = refs[:6], refs[6:]
    nt = nt_ref[...]
    cot = rows_of(cot_ref, lax.rem(lax.axis_index("mp") + shift, n), nt.shape[0])
    bn, out = 0.0, 0.0
    for k in range(2):
        gw, uw, dw = (ref[...] for ref in w_refs[3 * k : 3 * k + 3])
        act, bg, bu = hidden_part(nt, cot, gw, uw, dw)
        bn = bn + dot_cols(bg, gw) + dot_cols(bu, uw)
        out = out + dot(act, dw)
        if k == 0:
            act_ref[...] = act
            bg_ref[...] = bg
            bu_ref[...] = bu
    bn_ref[...] = bn.astype(BF)
    out_ref[...] = out.astype(BF)


def feed_forward(shift, n, nt, cot, own, other):
    share, width = nt.shape
    hid = own[0].shape[1]
    return pl.pallas_call(
        functools.partial(ffn_kernel, shift, n),
        in_specs=[whole()] * 8,
        out_specs=[whole()] * 5,
        out_shape=[jax.ShapeDtypeStruct((share, width), BF)] * 2
        + [jax.ShapeDtypeStruct((share, hid), BF)] * 3,
        compiler_params=params(),
        cost_estimate=cost(24 * share * width * hid, 2 * (6 * width * hid + 6 * share * width)),
        name="feed_forward",
    )(nt, cot, *own, *other)


def hidden_kernel(shift, n, nt_ref, cot_ref, gw_ref, uw_ref, dw_ref, act_ref, bg_ref, bu_ref):
    nt = nt_ref[...]
    which = lax.rem((lax.axis_index("mp") ^ 1) + shift, n)
    cot = rows_of(cot_ref, which, nt.shape[0])
    act_ref[...], bg_ref[...], bu_ref[...] = hidden_part(
        nt, cot, gw_ref[...], uw_ref[...], dw_ref[...]
    )


def hidden_rows(shift, n, nt, cot, own):
    share, width = nt.shape
    hid = own[0].shape[1]
    return pl.pallas_call(
        functools.partial(hidden_kernel, shift, n),
        in_specs=[whole()] * 5,
        out_specs=[whole()] * 3,
        out_shape=[jax.ShapeDtypeStruct((share, hid), BF)] * 3,
        compiler_params=params(),
        cost_estimate=cost(6 * share * width * hid, 2 * (3 * width * hid + 6 * share * width)),
        name="hidden_rows",
    )(nt, cot, *own)


def ffn_grad_kernel(n, share, groups, cot_ref, *refs):
    nt_refs, act_refs, bg_refs, bu_refs = (refs[i * n : (i + 1) * n] for i in range(4))
    grad_refs = refs[4 * n :]
    m = lax.axis_index("mp")
    nt = jnp.concatenate([ref[...] for ref in nt_refs], axis=0)
    act = jnp.concatenate([ref[...] for ref in act_refs], axis=0)
    bg = jnp.concatenate([ref[...] for ref in bg_refs], axis=0)
    bu = jnp.concatenate([ref[...] for ref in bu_refs], axis=0)
    cot = jnp.concatenate(
        [
            rows_of(cot_ref, lax.rem(first + shift, n), share)
            for first in (m, m ^ 1)
            for shift in range(0, n, 2)
        ],
        axis=0,
    )
    nt_t = nt.T
    grads = (dot(nt_t, bg), dot(nt_t, bu), dot(act.T, cot))
    if not groups:
        for ref, grad in zip(grad_refs, grads):
            ref[...] = grad.astype(BF)
        return
    keep_ref, send_ref, scr = grad_refs
    for i in range(3):
        scr[i] = grads[i].astype(BF)
    rows = scr.shape[1] // (2 * groups)
    d = lax.axis_index("dp")
    core = lax.rem(d, 2)
    for r in range(groups):
        chip = ((d // 2) ^ r) * 2
        for i in range(3):
            mine = pl.multiple_of((chip + core) * rows, 16)
            other = pl.multiple_of((chip + 1 - core) * rows, 16)
            at = (3 * r + i) * rows
            keep_ref[at : at + rows, :] = scr[i, pl.ds(mine, rows), :]
            send_ref[at : at + rows, :] = scr[i, pl.ds(other, rows), :]


def ffn_grads(cot, nts, acts, bgs, bus, groups):
    n = len(nts)
    share, width = nts[0].shape
    hid = acts[0].shape[1]
    length = cot.shape[0]
    scratch = []
    if groups:
        out_shape = [jax.ShapeDtypeStruct((3 * width // 2, width), BF)] * 2
        scratch = [pltpu.VMEM((3, width, width), BF)]
    else:
        out_shape = [
            jax.ShapeDtypeStruct((width, hid), BF),
            jax.ShapeDtypeStruct((width, hid), BF),
            jax.ShapeDtypeStruct((hid, width), BF),
        ]
    args = [cot, *nts, *acts, *bgs, *bus]
    return pl.pallas_call(
        functools.partial(ffn_grad_kernel, n, share, groups),
        in_specs=[whole()] * len(args),
        out_specs=[whole()] * len(out_shape),
        out_shape=out_shape,
        scratch_shapes=scratch,
        compiler_params=params(),
        cost_estimate=cost(6 * length * width * hid, 12 * length * width),
        name="ffn_grads",
    )(*args)


def mid_kernel(n, share, mp, len_ref, hid_ref, cot_ref, gain_ref, *refs):
    bn_refs, (bh_ref, b_ref, gg_ref) = refs[:n], refs[n:]
    m = lax.axis_index("mp")
    bn = bn_refs[0][...].astype(F32)
    for ref in bn_refs[1:]:
        bn = bn + ref[...].astype(F32)
    hidden = hid_ref[...]
    r2 = lax.rsqrt(jnp.mean(hidden * hidden, axis=-1, keepdims=True) + EPS)
    pos = mp * lax.broadcasted_iota(jnp.int32, (share, 1), 0) + m
    bn = bn * (pos < len_ref[0]).astype(F32)
    z = hidden * r2
    gg_ref[...] = jnp.broadcast_to(jnp.sum(bn * z, axis=0, keepdims=True), gg_ref.shape)
    q = bn * gain_ref[1:2, :]
    start = pl.multiple_of(m * share, 16)
    dout = cot_ref[pl.ds(start, share), :].astype(F32)
    back = dout + r2 * (q - z * jnp.mean(q * z, axis=-1, keepdims=True))
    bh_ref[...] = back
    b_ref[...] = back.astype(BF)


def mid_norm(lengths, hidden, cot, gain, pieces):
    share, width = hidden.shape
    n = len(pieces)
    return pl.pallas_call(
        functools.partial(mid_kernel, n, share, cot.shape[0] // share),
        in_specs=[smem()] + [whole()] * (3 + n),
        out_specs=[whole()] * 3,
        out_shape=[
            jax.ShapeDtypeStruct(hidden.shape, F32),
            jax.ShapeDtypeStruct(hidden.shape, BF),
            jax.ShapeDtypeStruct((8, width), F32),
        ],
        compiler_params=params(),
        cost_estimate=cost(20 * hidden.size, 20 * hidden.size),
        name="second_norm_back",
    )(lengths, hidden, cot, gain, *pieces)


def unmix_kernel(
    kb, n, len_ref, taps_ref, x_ref, bh_ref, gg_ref, gain_ref, stu_hbm, ar_hbm, *refs
):
    b_refs, (ig_ref, gain_out) = refs[:n], refs[n : n + 2]
    ta_ref, tb_ref, tc_ref, td_ref, b_scr, lag_ref, acc_ref, scr = refs[n + 2 : n + 10]
    w_buf, ar_ref, sems, ar_sem = refs[n + 10 :]
    j, steps = pl.program_id(0), pl.num_programs(0)
    share, width = bh_ref.shape
    half, step = n * share // 2, n // 2
    m = lax.axis_index("mp")
    shift, is_odd = m // 2, lax.rem(m, 2)
    depth = tc_ref.shape[1]
    start = half - depth
    first = ta_ref.shape[0] // kb
    rest = share - first
    row = lax.broadcasted_iota(jnp.int32, (share, half), 0) * step + shift
    col = lax.broadcasted_iota(jnp.int32, (share, half), 1)
    above, upto = col >= row + is_odd, col >= row
    slot, wait = fetch_matrices(j, stu_hbm.shape[0] // (2 * kb), kb, stu_hbm, w_buf, sems)

    @pl.when(j == 0)
    def _():
        for r in range(n):
            c = lax.rem(m + r, n)
            value = b_refs[r][...].astype(F32)
            put_every_nth(scr.at[lax.rem(c, 2)], value, c // 2, step)
            if r < lag_ref.shape[1] // width:
                moved = pltpu.roll(value, share - 1, 0)
                last = lax.broadcasted_iota(jnp.int32, (share, 1), 0) == share - 1
                moved = jnp.where(last, 0.0, moved)
                value = jnp.where(m + r >= n, moved, value)
                lag_ref[:, r * width : (r + 1) * width] = value.astype(BF)
        for odd in range(2):
            b_scr[odd] = columns_of(scr.at[odd], half).astype(BF)
        acc_ref[...] = jnp.zeros((share, width), F32)

    for k in range(kb):
        for which, valid, full, short in ((2, above, ta_ref, tc_ref), (3, upto, tb_ref, td_ref)):
            base = taps_ref[which, pl.ds(j * kb + k, 1), :]
            t = toeplitz(base, first, 0, step)
            full[k * first : (k + 1) * first, :] = jnp.where(valid[:first], t, 0.0).astype(BF)
            t = toeplitz(base, rest, step * first, step)
            t = jnp.where(valid[first:], t, 0.0).astype(BF)
            short[k * rest : (k + 1) * rest, :] = t[:, start:]
    ca, cb = dot(ta_ref[...], b_scr[0]), dot(tb_ref[...], b_scr[1])
    cc, cd = dot(tc_ref[...], b_scr[0, start:]), dot(td_ref[...], b_scr[1, start:])
    sign = jnp.where(is_odd == 0, 1.0, -1.0)
    wait()
    total = acc_ref[...]
    for k in range(kb):
        upper, lower = slice(k * first, (k + 1) * first), slice(k * rest, (k + 1) * rest)
        pa = jnp.concatenate([ca[upper], cc[lower]], axis=0)
        pb = jnp.concatenate([cb[upper], cd[lower]], axis=0)
        total = total + dot_cols((pa + pb).astype(BF), w_buf[slot, 0, k])
        total = total + dot_cols(((pa - pb) * sign).astype(BF), w_buf[slot, 1, k])
    acc_ref[...] = total
    fetch_last(j, steps, ar_hbm, ar_ref, ar_sem)

    @pl.when(j == steps - 1)
    def _():
        total = acc_ref[...]
        for lag in range(ar_ref.shape[0]):
            total = total + dot_cols(lag_ref[:, lag * width : (lag + 1) * width], ar_ref[lag])
        x = x_ref[...]
        r1 = lax.rsqrt(jnp.mean(x * x, axis=-1, keepdims=True) + EPS)
        pos = n * lax.broadcasted_iota(jnp.int32, (share, 1), 0) + m
        masked = total * (pos < len_ref[0]).astype(F32)
        y = x * r1
        p = masked * gain_ref[0:1, :]
        ig = bh_ref[...] + r1 * (p - y * jnp.mean(p * y, axis=-1, keepdims=True))
        ig_ref[...] = ig.astype(BF)
        gain_out[0:8, :] = jnp.broadcast_to(jnp.sum(masked * y, axis=0, keepdims=True), (8, width))
        gain_out[8:16, :] = gg_ref[...]


def spectral_unmix(lengths, taps, x, back_hidden, gg, gains, stu, ar, pieces, kb):
    share, width = back_hidden.shape
    n = len(pieces)
    half = n * share // 2
    count = taps.shape[1]
    depth = min(256, half)
    first = (half - depth) // (n // 2)
    return pl.pallas_call(
        functools.partial(unmix_kernel, kb, n),
        grid=(count // kb,),
        in_specs=[smem()] + [whole()] * 5 + [outside()] * 2 + [whole()] * n,
        out_specs=[whole()] * 2,
        out_shape=[
            jax.ShapeDtypeStruct((share, width), BF),
            jax.ShapeDtypeStruct((16, width), F32),
        ],
        scratch_shapes=[pltpu.VMEM((kb * first, half), BF)] * 2
        + [pltpu.VMEM((kb * (share - first), depth), BF)] * 2
        + [
            pltpu.VMEM((2, half, width), BF),
            pltpu.VMEM((share, ar.shape[0] * width), BF),
            pltpu.VMEM((share, width), F32),
            pltpu.VMEM((2, width // 128, half + 8, 128), F32),
        ]
        + matrix_scratch(kb, ar),
        compiler_params=params(30 << 20),
        cost_estimate=cost(4 * count * share * width * (half + width), 2 * stu.size),
        name="spectral_unmix",
    )(lengths, taps, x, back_hidden, gg, gains, stu, ar, *pieces)


def conv_kernel(groups, tile, own, first, filt_ref, *refs):
    ut_refs, (conv_ref, tt_ref, ut_scr) = refs[:groups], refs[groups:]
    j = pl.program_id(0)
    filt, length = filt_ref.shape
    block = conv_ref.shape[1]
    count = length // tile
    chip = lax.axis_index("dp") // 2

    @pl.when(j == 0)
    def _():
        start = pl.multiple_of(chip * block, 16)
        for r in range(groups):
            ut_scr[r * block : (r + 1) * block, :] = ut_refs[r][pl.ds(start, block), :]

    which = lax.axis_index("mp") * own + first + j
    strip = toeplitz(filt_ref[pl.ds(lax.rem(which, filt), 1), :], tile)
    row = lax.broadcasted_iota(jnp.int32, (tile, length), 0)
    col = lax.broadcasted_iota(jnp.int32, (tile, length), 1)
    flip = ((col - row) % 2 == 1) & (which >= filt)
    strip = jnp.where(col >= row, jnp.where(flip, -strip, strip), 0.0).astype(BF)
    for b in range(count):
        tt_ref[b * tile : (b + 1) * tile, b * tile :] = strip[:, : length - b * tile]
    for c in range(count):
        end = (c + 1) * tile
        part = dot(ut_scr[:, :end], tt_ref[:end, c * tile : end]).astype(BF)
        for r in range(groups):
            start = pl.multiple_of((lax.rem(chip, groups) ^ r) * length + c * tile, 128)
            conv_ref[0, :, pl.ds(start, tile)] = part[r * block : (r + 1) * block, :]


def convolutions(filt, uts, own, chips, first, last):
    length = filt.shape[1]
    groups = len(uts)
    block = uts[0].shape[0] // chips
    tile = 256 if length % 256 == 0 else length
    return pl.pallas_call(
        functools.partial(conv_kernel, groups, tile, own, first),
        grid=(last - first,),
        in_specs=[whole()] * (1 + groups),
        out_specs=pl.BlockSpec((1, block, groups * length), lambda j: (j, 0, 0)),
        out_shape=jax.ShapeDtypeStruct((last - first, block, groups * length), BF),
        scratch_shapes=[
            pltpu.VMEM((length, length), BF),
            pltpu.VMEM((groups * block, length), BF),
        ],
        compiler_params=params(),
        cost_estimate=cost(0, 0),
        name="convolutions",
    )(filt, *uts)


def lag_kernel(groups, *refs):
    ut_refs, out_refs = refs[:groups], refs[groups:]
    width, length = ut_refs[0].shape
    chip = lax.rem(lax.axis_index("dp") // 2, groups)
    col = lax.broadcasted_iota(jnp.int32, (width, length), 1)
    for r in range(groups):
        start = pl.multiple_of((chip ^ r) * length, 128)
        out_refs[0][:, pl.ds(start, length)] = ut_refs[r][:width, :]
        value = ut_refs[r][:width, :].astype(F32)
        for lag in range(1, len(out_refs)):
            moved = pltpu.roll(value, lag, 1)
            out_refs[lag][:, pl.ds(start, length)] = jnp.where(col >= lag, moved, 0.0).astype(BF)


def lagged(uts, order):
    groups = len(uts)
    width, length = uts[0].shape
    shape = jax.ShapeDtypeStruct((width, groups * length), BF)
    return pl.pallas_call(
        functools.partial(lag_kernel, groups),
        in_specs=[whole()] * groups,
        out_specs=[whole()] * order,
        out_shape=[shape] * order,
        compiler_params=params(),
        cost_estimate=cost(0, 0),
        name="lagged",
    )(*uts)


def grads_kernel(steps, order, groups, rows, conv_ref, conv_two_ref, *refs):
    lag_refs, b_refs = refs[:order], refs[order : order + len(rows)]
    keep_ref, send_ref, b_scr, scr = refs[order + len(rows) :]
    g = pl.program_id(0)
    d = lax.axis_index("dp")
    chip, core = lax.rem(d // 2, groups), lax.rem(d, 2)
    step, block, depth = conv_ref.shape
    width, length = b_scr.shape[1], depth // groups
    half = block // 2

    @pl.when(g == 0)
    def _():
        for ref, (r, at, size) in zip(b_refs, rows):
            start = pl.multiple_of((chip ^ r) * length + at, 16)
            b_scr[pl.ds(start, size), :] = ref[:size, :]

    for k, ref in enumerate((conv_ref, conv_two_ref)):

        @pl.when((g >= k * steps // 2) & (g < (k + 1) * steps // 2))
        def _():
            part = dot(ref[...].reshape(step * block, depth), b_scr[...])
            scr[...] = part.reshape(step, block, width)

    @pl.when(g < steps)
    def _():
        mine = pl.multiple_of(core * half, 16)
        other = pl.multiple_of((1 - core) * half, 16)
        keep_ref[pl.ds(g * step, step)] = scr[:, pl.ds(mine, half), :]
        for k in range(step):
            start = pl.multiple_of((g * step + k) * half, 16)
            send_ref[pl.ds(start, half), :] = scr[k, pl.ds(other, half), :].astype(BF)

    for lag in range(order):

        @pl.when(g == steps + lag)
        def _():
            at = steps * step * half + lag * width
            send_ref[at : at + width, :] = dot(lag_refs[lag][...], b_scr[...]).astype(BF)


def matrix_grads(convs, lags, backs, rows):
    part, block, depth = convs[0].shape
    own = 2 * part
    order, width = len(lags), lags[0].shape[0]
    groups = 1 + max(r for r, _, _ in rows)
    step = next(s for s in (3, 2, 1) if part % s == 0)
    steps = own // step
    half = block // 2
    return pl.pallas_call(
        functools.partial(grads_kernel, steps, order, groups, rows),
        grid=(steps + order,),
        in_specs=[
            pl.BlockSpec((step, block, depth), lambda g: (jnp.minimum(g, steps // 2 - 1), 0, 0)),
            pl.BlockSpec(
                (step, block, depth), lambda g: (jnp.clip(g - steps // 2, 0, steps // 2 - 1), 0, 0)
            ),
        ]
        + [whole()] * (order + len(backs)),
        out_specs=[whole()] * 2,
        out_shape=[
            jax.ShapeDtypeStruct((own, half, width), F32),
            jax.ShapeDtypeStruct((own * half + order * width, width), BF),
        ],
        scratch_shapes=[
            pltpu.VMEM((depth, width), BF),
            pltpu.VMEM((step, block, width), F32),
        ],
        compiler_params=params(),
        cost_estimate=cost(0, 0),
        name="matrix_grads",
    )(*convs, *lags, *backs)


def rows_message_kernel(ig_ref, hid_ref, *refs):
    share = ig_ref.shape[0]
    total = hid_ref[...]
    for ref in refs[:-1]:
        total = total + ref[...].astype(F32)
    refs[-1][:share, :] = ig_ref[...]
    refs[-1][share:, :] = total.astype(BF)


def rows_message(ig, hidden, pieces):
    share, width = ig.shape
    return pl.pallas_call(
        rows_message_kernel,
        in_specs=[whole()] * (2 + len(pieces)),
        out_specs=whole(),
        out_shape=jax.ShapeDtypeStruct((2 * share, width), BF),
        compiler_params=params(),
        cost_estimate=cost(4 * ig.size, 10 * ig.size),
        name="rows_message",
    )(ig, hidden, *pieces)


def finish_rows_kernel(n, share, at, *refs):
    pieces, (out_ref, scr) = refs[:n], refs[n:]
    m = lax.axis_index("mp")
    for r in range(n):
        value = pieces[r][at : at + share, :].astype(F32)
        put_every_nth(scr, value, lax.rem(m + r, n), n)
    out_ref[...] = columns_of(scr, n * share).astype(out_ref.dtype)


def finish_rows(pieces, at, dtype, weight):
    n = len(pieces)
    share, width = pieces[0].shape[0] // 2, pieces[0].shape[1]
    return pl.pallas_call(
        functools.partial(finish_rows_kernel, n, share, at),
        in_specs=[whole()] * n,
        out_specs=whole(),
        out_shape=jax.ShapeDtypeStruct((n * share, width), dtype),
        scratch_shapes=[pltpu.VMEM((width // 128, n * share + 16, 128), F32)],
        compiler_params=params(),
        cost_estimate=cost(weight, weight),
        name="finish_rows",
    )(*pieces)


def ordered_sum_kernel(n, axis, step, *refs):
    pieces, (out_ref, scr) = refs[:n], refs[n:]
    me = lax.axis_index(axis)
    for r in range(n):
        who = lax.rem(me + r, n) if step == 0 else (me // step) ^ r
        scr[who] = pieces[r][...]
    total = scr[0]
    for r in range(1, n):
        total = total + scr[r]
    out_ref[...] = total


def ordered_sum(pieces, axis, step):
    n = len(pieces)
    shape = pieces[0].shape
    return pl.pallas_call(
        functools.partial(ordered_sum_kernel, n, axis, step),
        in_specs=[whole()] * n,
        out_specs=whole(),
        out_shape=jax.ShapeDtypeStruct(shape, F32),
        scratch_shapes=[pltpu.VMEM((n,) + shape, F32)],
        compiler_params=params(),
        cost_estimate=cost(n * pieces[0].size, 4 * n * pieces[0].size),
        name="ordered_sum",
    )(*pieces)


def cores_sum_kernel(keep_ref, recv_ref, upper_ref, lower_ref):
    total = (keep_ref[...].astype(F32) + recv_ref[...].astype(F32)).astype(BF)
    half = total.shape[0] // 8
    for r in range(4):
        at = 2 * r * half
        upper_ref[r * half : (r + 1) * half, :] = total[at : at + half]
        lower_ref[r * half : (r + 1) * half, :] = total[at + half : at + 2 * half]


def cores_sum(keep, recv):
    size, width = keep.shape
    return pl.pallas_call(
        cores_sum_kernel,
        in_specs=[whole()] * 2,
        out_specs=[whole()] * 2,
        out_shape=[jax.ShapeDtypeStruct((size // 2, width), BF)] * 2,
        compiler_params=params(),
        cost_estimate=cost(keep.size, 8 * keep.size),
        name="cores_sum",
    )(keep, recv)


def pack_kernel(n, share, *refs):
    pieces, (out_ref, scr) = refs[:n], refs[n:]
    m = lax.axis_index("mp")
    for r in range(n):
        put_every_nth(scr, pieces[r][...].astype(F32), lax.rem(m + r, n), n)
    out_ref[...] = columns_of(scr, n * share).astype(BF)


def pack_rows(pieces):
    n = len(pieces)
    share, width = pieces[0].shape
    return pl.pallas_call(
        functools.partial(pack_kernel, n, share),
        in_specs=[whole()] * n,
        out_specs=whole(),
        out_shape=jax.ShapeDtypeStruct((n * share, width), BF),
        scratch_shapes=[pltpu.VMEM((width // 128, n * share + 16, 128), F32)],
        compiler_params=params(),
        cost_estimate=cost(n * share * width, 6 * n * share * width),
        name="pack_rows",
    )(*pieces)


def turn_kernel(x_ref, y_ref, upper_ref, lower_ref, gain_ref, to_y, to_x):
    half, size = x_ref.shape[0] // 2, upper_ref.shape[0]
    gains = split_gains(gain_ref[...])
    for ref, rows, w_ref in ((to_y, x_ref[:half, :], lower_ref), (to_x, y_ref[half:, :], upper_ref)):
        ref[:half, :] = rows
        ref[half : half + size, :] = w_ref[...]
        ref[half + size :, :] = gains


def turn(over_x, over_y, upper, lower, gains):
    rows = over_x.shape[0] // 2 + upper.shape[0] + 32
    return pl.pallas_call(
        turn_kernel,
        in_specs=[whole()] * 5,
        out_specs=[whole()] * 2,
        out_shape=[jax.ShapeDtypeStruct((rows, over_x.shape[1]), BF)] * 2,
        compiler_params=params(),
        cost_estimate=cost(over_x.size, 8 * over_x.size),
        name="turn",
    )(over_x, over_y, upper, lower, gains)


def half_sums_kernel(upper_ref, lower_ref, from_y, from_x, to_y, to_x):
    size = to_y.shape[0]
    half = size // 4
    at = from_y.shape[0] - 32 - size
    for ref, own, came, bits in ((to_y, upper_ref, from_x, 1), (to_x, lower_ref, from_y, 2)):
        for r in range(4):
            there = at + (r ^ bits) * half
            ref[r * half : (r + 1) * half, :] = (
                own[r * half : (r + 1) * half, :].astype(F32)
                + came[there : there + half, :].astype(F32)
            ).astype(BF)
    to_x[size:, :] = from_y[at + size :, :]


def half_sums(upper, lower, from_y, from_x):
    size, width = upper.shape
    return pl.pallas_call(
        half_sums_kernel,
        in_specs=[whole()] * 4,
        out_specs=[whole()] * 2,
        out_shape=[jax.ShapeDtypeStruct((rows, width), BF) for rows in (size, size + 32)],
        compiler_params=params(),
        cost_estimate=cost(upper.size, 8 * upper.size),
        name="half_sums",
    )(upper, lower, from_y, from_x)


def chunks_kernel(upper_ref, from_y, lower_ref, from_x, more_ref, out_ref):
    half = upper_ref.shape[0] // 4
    for own, came, bits, lower in ((upper_ref, from_y, 2, 0), (lower_ref, from_x, 1, 1)):
        for r in range(4):
            at, there = (2 * r + lower) * half, (r ^ bits) * half
            out_ref[at : at + half, :] = (
                own[r * half : (r + 1) * half, :].astype(F32)
                + came[there : there + half, :].astype(F32)
            ).astype(BF)
    out_ref[8 * half :, :] = more_ref[...]


def whole_chunks(upper, from_y, lower, from_x, more):
    size, width = upper.shape
    return pl.pallas_call(
        chunks_kernel,
        in_specs=[whole()] * 5,
        out_specs=whole(),
        out_shape=jax.ShapeDtypeStruct((2 * size + more.shape[0], width), BF),
        compiler_params=params(),
        cost_estimate=cost(upper.size, 8 * upper.size),
        name="whole_chunks",
    )(upper, from_y, lower, from_x, more)


def split_gains(both):
    high = both.astype(BF)
    low = (both - high.astype(F32)).astype(BF)
    return jnp.concatenate([high, low], axis=0)


def joined(gains):
    return gains[:16].astype(F32) + gains[16:].astype(F32)


def chips_sum_kernel(gain_ref, from_x, from_y, recv_ref, out_ref, scr):
    chip = lax.axis_index("dp") // 2
    scr[chip] = joined(split_gains(gain_ref[...]))
    for ref, bits in ((from_x, 1), (from_y, 2), (recv_ref, 3)):
        scr[chip ^ bits] = joined(ref[ref.shape[0] - 32 :, :])
    out_ref[...] = ((scr[0] + scr[1]) + scr[2]) + scr[3]


def chips_sum(gains, from_x, from_y, recv):
    return pl.pallas_call(
        chips_sum_kernel,
        in_specs=[whole()] * 4,
        out_specs=whole(),
        out_shape=jax.ShapeDtypeStruct(gains.shape, F32),
        scratch_shapes=[pltpu.VMEM((4,) + gains.shape, F32)],
        compiler_params=params(),
        cost_estimate=cost(4 * gains.size, 16 * gains.size),
        name="chips_sum",
    )(gains, from_x, from_y, recv)


def finish_kernel(custom, keep_ref, send_ref, recv_ref, stu_ref, ar_ref, *w_refs):
    own, half, width = keep_ref.shape
    base = 0
    if custom:
        d = lax.axis_index("dp")
        core = lax.rem(d, 2)
        rows = width // 8
        base = 12 * rows
        for r in range(4):
            chip = ((d // 2) ^ r) * 2
            for ref, which in ((send_ref, chip + core), (recv_ref, chip + 1 - core)):
                start = pl.multiple_of(which * rows, 16)
                for i, out in enumerate(w_refs):
                    at = (3 * r + i) * rows
                    out[pl.ds(start, rows), :] = ref[at : at + rows, :].astype(F32)
    for k in range(own):
        at = base + k * half
        stu_ref[k] = keep_ref[k] + recv_ref[at : at + half, :].astype(F32)
    for i in range(ar_ref.shape[0]):
        at = base + own * half + i * width
        ar_ref[i] = send_ref[at : at + width, :].astype(F32) + recv_ref[
            at : at + width, :
        ].astype(F32)


def finish(keep, send, recv, order, custom):
    width = keep.shape[2]
    more = [jax.ShapeDtypeStruct((width, width), F32)] * (3 if custom else 0)
    return pl.pallas_call(
        functools.partial(finish_kernel, custom),
        in_specs=[whole()] * 3,
        out_specs=[whole()] * (2 + len(more)),
        out_shape=[
            jax.ShapeDtypeStruct(keep.shape, F32),
            jax.ShapeDtypeStruct((order, width, width), F32),
        ]
        + more,
        compiler_params=params(),
        cost_estimate=cost(keep.size, 10 * keep.size),
        name="finish",
    )(keep, send, recv)


def fetch_shifted(value, axis, n, step=1):
    pieces = {0: value}
    for r in sorted(range(step, n, step), key=lambda r: min(r, n - r)):
        pieces[r] = lax.ppermute(value, axis, [(i, (i - r) % n) for i in range(n)])
    return [pieces[r] for r in range(0, n, step)]


def send_shifted(pieces, axis, n, step):
    moved = {0: pieces[0]}
    for r in sorted(range(step, n, step), key=lambda r: min(r, n - r)):
        moved[r] = lax.ppermute(pieces[r // step], axis, [(i, (i + r) % n) for i in range(n)])
    return [moved[r] for r in range(0, n, step)]


def swap(value, axis, n, bits):
    return lax.ppermute(value, axis, [(i, i ^ bits) for i in range(n)])


def swap_sum(value, n):
    return ordered_sum([value, swap(value, "dp", n, 1)], "dp", 0)


def after(values, first):
    flat, tree = jax.tree.flatten(values)
    out = lax.optimization_barrier((*flat, *jax.tree.leaves(first)))
    return jax.tree.unflatten(tree, out[: len(flat)])


def shards(
    inputs, lengths, filters, first_gain, stu_weight, ar_weight, second_gain,
    gate_weight, up_weight, down_weight, cotangent,
):
    n = lax.axis_size("mp")
    n_dp = lax.axis_size("dp")
    groups = n_dp // 2
    length, width = inputs.shape
    share = length // n
    order = ar_weight.shape[0]
    own = stu_weight.shape[0] // n
    lengths = lengths.astype(jnp.int32)
    both_gains = jnp.stack([first_gain, second_gain])

    own_w = (gate_weight, up_weight, down_weight)
    custom = n_dp == 8 and gate_weight.shape[1] == width
    if custom:
        half_w = half_weights(*own_w)
        both_gains = after(both_gains, half_w)
        half_w = swap(half_w, "mp", n, 1)
    u, ut, ut_two, x_own, u_lags, taps, natural = first_norm(
        lengths, inputs, both_gains, filters.T, n, order
    )
    uts = [ut, swap(ut, "dp", n_dp, 2), swap(ut_two, "dp", n_dp, 4)]
    hidden, nt = spectral_mix(
        lengths, taps, x_own, u, u_lags, both_gains, stu_weight, ar_weight, n, 8
    )
    cotangent = dealt_rows(cotangent, n)
    nts = fetch_shifted(nt, "mp", n, 2)
    others = [swap(piece, "mp", n, 1) for piece in nts]
    if custom:
        other_w = both_halves(half_w, swap(after(half_w, nt), "dp", n_dp, 1))
    else:
        other_w = [swap(w, "mp", n, 1) for w in own_w]
    parts = [feed_forward(0, n, after(nt, uts[1:3]), cotangent, own_w, other_w)]
    for k in range(1, n // 2):
        piece = after(nts[k], parts[-1][0])
        parts.append(feed_forward(2 * k, n, piece, cotangent, own_w, other_w))
    uts += [swap(after(ut, nt), "dp", n_dp, 2 * r) for r in range(3, groups)]
    bns = send_shifted([p[0] for p in parts], "mp", n, 2)
    out_parts = [p[1] for p in parts]
    bns[1:] = after(bns[1:], uts)
    back_hidden, back_rows, second_part = mid_norm(lengths, hidden, cotangent, both_gains, bns)
    backs = fetch_shifted(back_rows, "mp", n)
    more = [
        hidden_rows(2 * k, n, after(piece, back_rows), cotangent, own_w)
        for k, piece in enumerate(others)
    ]
    acts, bgs, bus = ([p[i + 2] for p in parts] + [p[i] for p in more] for i in range(3))
    grads = ffn_grads(cotangent, nts + others, acts, bgs, bus, groups if custom else 0)
    uts = after(uts, back_rows)
    fours = [uts[r : r + 4] for r in range(0, groups, 4)]
    lags = [lagged(some, order) for some in fours]
    conv = [convolutions(natural, some, own, groups, 0, own // 2) for some in fours]
    backs = after(backs, (lags, conv))
    own_back = pack_rows(backs)
    if custom:
        over_x, over_y = swap(own_back, "dp", n_dp, 2), swap(own_back, "dp", n_dp, 4)
        w_came = swap(after(grads[1], own_back), "dp", n_dp, 1)
    out_sums = send_shifted(after(out_parts, own_back), "mp", n, 2)
    ig, gains = spectral_unmix(
        lengths, taps, x_own, back_hidden, second_part, both_gains, stu_weight, ar_weight, backs, 8
    )
    uts, hidden = after((uts, hidden), ig)
    fours = [uts[r : r + 4] for r in range(0, groups, 4)]
    conv_two = [convolutions(natural, some, own, groups, own // 2, own) for some in fours]
    message = rows_message(ig, hidden, out_sums)
    messages = fetch_shifted(message, "mp", n)
    if custom:
        upper, lower = cores_sum(grads[0], after(w_came, message))
        to_y, to_x = turn(after(over_x, message), over_y, upper, lower, gains)
        from_y, from_x = swap(to_y, "dp", n_dp, 4), swap(to_x, "dp", n_dp, 2)
        all_backs = [own_back, over_x, over_y, from_y, from_x]
        half = length // 2
        rows = ((0, 0, length), (1, 0, length), (2, 0, length), (3, 0, half), (3, half, half))
        upper, lower = half_sums(after(upper, conv_two), lower, from_y, from_x)
        from_y_two, from_x_two = swap(upper, "dp", n_dp, 4), swap(lower, "dp", n_dp, 2)
        conv_two = after(conv_two, upper)
        gains_parts = (gains, from_x, from_y)
    else:
        all_backs = [own_back] + [swap(own_back, "dp", n_dp, 2 * r) for r in range(1, groups)]
        rows = tuple((r, 0, length) for r in range(min(groups, 4)))
        gains = ordered_sum([gains] + [swap(gains, "dp", n_dp, r) for r in range(1, n_dp)], "dp", 1)
    conv = after(list(zip(conv, conv_two)), message)
    if len(conv) == 1:
        keep, send = matrix_grads(conv[0], lags[0], all_backs, rows)
    else:
        some = [
            matrix_grads(c, lags[k], all_backs[4 * k : 4 * k + 4], rows)
            for k, c in enumerate(conv)
        ]
        keep = ordered_sum([k for k, _ in some], "dp", 8)
        send = ordered_sum([k.astype(F32) for _, k in some], "dp", 8).astype(BF)
    messages = after(messages, send)
    output = finish_rows(messages, share, BF, 1e9)
    input_grad = finish_rows(after(messages, output), 0, F32, 1e6)
    if custom:
        from_y_two, from_x_two = after((from_y_two, from_x_two), output)
        gains = chips_sum(*gains_parts, after(from_x_two, send))
        gains = [gains, after(swap(gains, "dp", n_dp, 1), input_grad)]
        gains = ordered_sum(gains, "dp", 0)
        send = whole_chunks(upper, from_y_two, lower, from_x_two, after(send, gains))
    gains = fetch_shifted(gains, "mp", n)
    recv = swap(send, "dp", n_dp, 1)
    stu_grad, ar_grad, *w_grads = finish(keep, send, recv, order, custom)
    gains = ordered_sum(after(gains, stu_grad), "mp", 0)
    if custom:
        gate_grad, up_grad, down_grad = w_grads
    else:
        gate_grad, up_grad, down_grad = (g.astype(F32) for g in lax.psum(tuple(grads), "dp"))
    return (
        output, input_grad, stu_grad, ar_grad, gains[0], gains[8], gate_grad, up_grad, down_grad,
    )


def solution(mesh):
    in_specs = (
        P("dp", None), P("dp"), P(), P(), P(), P(), P(),
        P(None, "mp"), P(None, "mp"), P("mp", None), P("dp", None),
    )
    out_specs = (
        P("dp", None), P("dp", None), P("mp", "dp", None), P(), P(), P(),
        P(None, "mp"), P(None, "mp"), P("mp", None),
    )
    return jax.shard_map(shards, mesh=mesh, in_specs=in_specs, out_specs=out_specs, check_vma=False)
```

```python
import functools

import jax
import jax.numpy as jnp
from jax import lax
from jax.experimental import pallas as pl
from jax.experimental.pallas import tpu as pltpu
from jax.sharding import PartitionSpec as P

EPS = 1e-05
BF = jnp.bfloat16
F32 = jnp.float32
SQRT_2_PI = 0.7978845608028654
CUBIC = 0.044715
VMEM_LIMIT = 20 << 20


def dot(left, right):
    return jnp.dot(left, right, preferred_element_type=F32)


def dot_cols(left, right):
    return lax.dot_general(left, right, (((1,), (1,)), ((), ())), preferred_element_type=F32)


def params(limit=VMEM_LIMIT):
    return pltpu.CompilerParams(vmem_limit_bytes=limit)


COST_SCALE = 1.0


def cost(flops, nbytes):
    return pl.CostEstimate(
        flops=int(COST_SCALE * flops), bytes_accessed=int(COST_SCALE * nbytes), transcendentals=0
    )


def smem():
    return pl.BlockSpec(memory_space=pltpu.SMEM)


def whole():
    return pl.BlockSpec(memory_space=pltpu.VMEM)


def outside():
    return pl.BlockSpec(memory_space=pltpu.HBM)


def toeplitz(base_row, rows, first=0, step=1):
    wide = jnp.broadcast_to(base_row, (rows, base_row.shape[1]))
    return pltpu.roll(wide, first, 1, stride=step, stride_axis=0)


def put_columns(scr, value, at=0):
    for c in range(scr.shape[0]):
        scr[c, at : at + value.shape[0], :] = value[:, c * 128 : (c + 1) * 128]


def every_nth(scr, start, count, step):
    columns = [scr[c, pl.ds(start, count, stride=step), :] for c in range(scr.shape[0])]
    return columns[0] if len(columns) == 1 else jnp.concatenate(columns, axis=1)


def put_every_nth(scr, value, start, step):
    for c in range(scr.shape[0]):
        columns = slice(c * 128, (c + 1) * 128)
        scr[c, pl.ds(start, value.shape[0], stride=step), :] = value[:, columns]


def columns_of(scr, count):
    return jnp.concatenate([scr[c, :count, :] for c in range(scr.shape[0])], axis=1)


def norm_kernel(
    n, share, order, len_ref, x_ref, gain_ref, filt_ref,
    u_ref, ut_ref, ut_two_ref, own_ref, lag_ref, taps_ref, nat_ref, scr, scr_f,
):
    length, width = x_ref.shape
    m = lax.axis_index("mp")
    filt = nat_ref.shape[0]
    x = x_ref[...].astype(F32)
    r1 = lax.rsqrt(jnp.mean(x * x, axis=-1, keepdims=True) + EPS)
    row = lax.broadcasted_iota(jnp.int32, (length, 1), 0)
    mask = (row < len_ref[0]).astype(F32)
    u = mask * x * r1 * gain_ref[0:1, :]
    scr[:, :8, :] = jnp.zeros((scr.shape[0], 8, 128), F32)
    put_columns(scr, u, 8)
    ut = u.T.astype(BF)
    ut_ref[...] = ut
    ut_two_ref[:width, :] = ut
    ut_two_ref[width:, :] = jnp.zeros((ut_two_ref.shape[0] - width, length), BF)
    for odd in range(2):
        u_ref[odd] = every_nth(scr, odd + 8, length // 2, 2).astype(BF)
    for lag in range(order):
        rows = every_nth(scr, m + 8 - lag, share, n)
        lag_ref[:, lag * width : (lag + 1) * width] = rows.astype(BF)
    put_columns(scr, x, 8)
    own_ref[...] = every_nth(scr, m + 8, share, n)
    half = length // 2
    natural = filt_ref[...].astype(F32)
    nat_ref[...] = natural
    scr_f[0, :length, :filt] = natural.T
    even = every_nth(scr_f, 0, half, 2).T[:filt]
    odd = every_nth(scr_f, 1, half, 2).T[:filt]
    i = lax.broadcasted_iota(jnp.int32, (half, half), 0)
    j = lax.broadcasted_iota(jnp.int32, (half, half), 1)
    flip = (i == jnp.where(j == 0, 0, half - j)).astype(F32).astype(BF)
    rev_even = dot(even.astype(BF), flip)
    rev_odd = dot(odd.astype(BF), flip)
    shift, is_odd = m // 2, lax.rem(m, 2)
    one, two = jnp.where(is_odd == 0, rev_even, rev_odd), jnp.where(is_odd == 0, rev_odd, rev_even)
    taps_ref[0] = pltpu.roll(one, shift, 1)
    taps_ref[1] = pltpu.roll(two, lax.rem(shift + half - 1 + is_odd, half), 1)
    one, two = jnp.where(is_odd == 0, even, odd), jnp.where(is_odd == 0, odd, even)
    taps_ref[2] = pltpu.roll(one, shift + is_odd, 1)
    taps_ref[3] = pltpu.roll(two, shift, 1)


def first_norm(lengths, x, gains, filters, n, order):
    length, width = x.shape
    share = length // n
    filt = filters.shape[0]
    return pl.pallas_call(
        functools.partial(norm_kernel, n, share, order),
        in_specs=[smem()] + [whole()] * 3,
        out_specs=[whole()] * 7,
        out_shape=[
            jax.ShapeDtypeStruct((2, length // 2, width), BF),
            jax.ShapeDtypeStruct((width, length), BF),
            jax.ShapeDtypeStruct((width + 16, length), BF),
            jax.ShapeDtypeStruct((share, width), F32),
            jax.ShapeDtypeStruct((share, order * width), BF),
            jax.ShapeDtypeStruct((4, filt, length // 2), F32),
            jax.ShapeDtypeStruct((filt, length), F32),
        ],
        scratch_shapes=[
            pltpu.VMEM((width // 128, length + 24, 128), F32),
            pltpu.VMEM((1, length + 8, 128), F32),
        ],
        compiler_params=params(),
        cost_estimate=cost(10 * x.size, 6 * x.size),
        name="first_norm",
    )(lengths, x, gains, filters)


def fetch_matrices(j, steps, kb, stu_hbm, w_buf, sems):
    def copies(step):
        slot = lax.rem(step, 2)
        return [
            pltpu.make_async_copy(
                stu_hbm.at[pl.ds((sign * steps + step) * kb, kb)],
                w_buf.at[slot, sign],
                sems.at[slot, sign],
            )
            for sign in range(2)
        ]

    @pl.when(j == 0)
    def _():
        for copy in copies(j):
            copy.start()

    @pl.when(j + 1 < steps)
    def _():
        for copy in copies(j + 1):
            copy.start()

    def wait():
        for copy in copies(j):
            copy.wait()

    return lax.rem(j, 2), wait


def fetch_last(j, steps, src, dst, sem):
    copy = pltpu.make_async_copy(src, dst, sem)

    @pl.when(j == 0)
    def _():
        copy.start()

    @pl.when(j == steps - 1)
    def _():
        copy.wait()


def mix_kernel(
    kb, n, len_ref, taps_ref, x_ref, u_ref, lag_ref, gain_ref, stu_hbm, ar_hbm,
    hid_ref, nt_ref, ta_ref, tb_ref, tc_ref, td_ref, c_ref, acc_ref, w_buf, ar_ref, sems, ar_sem,
):
    j, steps = pl.program_id(0), pl.num_programs(0)
    half, width = u_ref.shape[1:]
    share, step = x_ref.shape[0], n // 2
    m = lax.axis_index("mp")
    shift, is_odd = m // 2, lax.rem(m, 2)
    depth = ta_ref.shape[1]
    first = ta_ref.shape[0] // kb
    rest = share - first
    row = lax.broadcasted_iota(jnp.int32, (share, half), 0) * step + shift
    col = lax.broadcasted_iota(jnp.int32, (share, half), 1)
    upto, below = col <= row, col <= row - 1 + is_odd
    slot, wait = fetch_matrices(j, stu_hbm.shape[0] // (2 * kb), kb, stu_hbm, w_buf, sems)

    @pl.when(j == 0)
    def _():
        acc_ref[...] = jnp.zeros((share, width), F32)

    for k in range(kb):
        for which, valid, short, full in ((0, upto, ta_ref, tc_ref), (1, below, tb_ref, td_ref)):
            base = taps_ref[which, pl.ds(j * kb + k, 1), :]
            t = toeplitz(base, first, 0, step)
            t = jnp.where(valid[:first], t, 0.0).astype(BF)
            short[k * first : (k + 1) * first, :] = t[:, :depth]
            t = toeplitz(base, rest, step * first, step)
            full[k * rest : (k + 1) * rest, :] = jnp.where(valid[first:], t, 0.0).astype(BF)
    ca, cb = dot(ta_ref[...], u_ref[0, :depth]), dot(tb_ref[...], u_ref[1, :depth])
    cc, cd = dot(tc_ref[...], u_ref[0]), dot(td_ref[...], u_ref[1])
    sign = jnp.where(is_odd == 0, 1.0, -1.0)
    for k in range(kb):
        plus = slice(k * width, (k + 1) * width)
        minus = slice((kb + k) * width, (kb + k + 1) * width)
        pa, pb = ca[k * first : (k + 1) * first], cb[k * first : (k + 1) * first]
        c_ref[:first, plus] = (pa + pb).astype(BF)
        c_ref[:first, minus] = ((pa - pb) * sign).astype(BF)
        pa, pb = cc[k * rest : (k + 1) * rest], cd[k * rest : (k + 1) * rest]
        c_ref[first:, plus] = (pa + pb).astype(BF)
        c_ref[first:, minus] = ((pa - pb) * sign).astype(BF)
    wait()
    acc_ref[...] += dot(c_ref[...], w_buf[slot].reshape(2 * kb * width, width))
    fetch_last(j, steps, ar_hbm, ar_ref, ar_sem)

    @pl.when(j == steps - 1)
    def _():
        total = acc_ref[...] + dot(lag_ref[...], ar_ref[...].reshape(lag_ref.shape[1], width))
        hidden = x_ref[...] + total
        hid_ref[...] = hidden
        r2 = lax.rsqrt(jnp.mean(hidden * hidden, axis=-1, keepdims=True) + EPS)
        pos = n * lax.broadcasted_iota(jnp.int32, (share, 1), 0) + m
        mask = (pos < len_ref[0]).astype(F32)
        nt_ref[...] = (mask * hidden * r2 * gain_ref[1:2, :]).astype(BF)


def matrix_scratch(kb, ar):
    width = ar.shape[1]
    return [
        pltpu.VMEM((2, 2, kb, width, width), BF),
        pltpu.VMEM(ar.shape, BF),
        pltpu.SemaphoreType.DMA((2, 2)),
        pltpu.SemaphoreType.DMA,
    ]


def spectral_mix(lengths, taps, x, u, lags, gains, stu, ar, n, kb):
    share, width = x.shape
    half = u.shape[1]
    filt = taps.shape[1]
    depth = min(256, half)
    first = depth // (n // 2)
    return pl.pallas_call(
        functools.partial(mix_kernel, kb, n),
        grid=(filt // kb,),
        in_specs=[smem()] + [whole()] * 5 + [outside()] * 2,
        out_specs=[whole()] * 2,
        out_shape=[
            jax.ShapeDtypeStruct((share, width), F32),
            jax.ShapeDtypeStruct((share, width), BF),
        ],
        scratch_shapes=[pltpu.VMEM((kb * first, depth), BF)] * 2
        + [pltpu.VMEM((kb * (share - first), half), BF)] * 2
        + [pltpu.VMEM((share, 2 * kb * width), BF), pltpu.VMEM((share, width), F32)]
        + matrix_scratch(kb, ar),
        compiler_params=params(51 << 20),
        cost_estimate=cost(0, 0),
        name="spectral_mix",
    )(lengths, taps, x, u, lags, gains, stu, ar)


def dealt_kernel(n, in_ref, out_ref, scr):
    share = out_ref.shape[0] // n
    put_columns(scr, in_ref[...].astype(F32))
    for m in range(n):
        out_ref[m * share : (m + 1) * share, :] = every_nth(scr, m, share, n).astype(BF)


def dealt_rows(value, n):
    length, width = value.shape
    return pl.pallas_call(
        functools.partial(dealt_kernel, n),
        in_specs=[whole()],
        out_specs=whole(),
        out_shape=jax.ShapeDtypeStruct(value.shape, BF),
        scratch_shapes=[pltpu.VMEM((width // 128, length + 16, 128), F32)],
        compiler_params=params(),
        cost_estimate=cost(value.size, 4 * value.size),
        name="dealt_rows",
    )(value)


def half_kernel(gate_hbm, up_hbm, down_hbm, out_ref, sems):
    rows = gate_hbm.shape[0] // 2
    start = pl.multiple_of(lax.rem(lax.axis_index("dp"), 2) * rows, 16)
    copies = [
        pltpu.make_async_copy(src.at[pl.ds(start, rows)], out_ref.at[k], sems.at[k])
        for k, src in enumerate((gate_hbm, up_hbm, down_hbm))
    ]
    for copy in copies:
        copy.start()
    for copy in copies:
        copy.wait()


def half_weights(gate, up, down):
    rows, width = gate.shape
    return pl.pallas_call(
        half_kernel,
        in_specs=[outside()] * 3,
        out_specs=whole(),
        out_shape=jax.ShapeDtypeStruct((3, rows // 2, width), BF),
        scratch_shapes=[pltpu.SemaphoreType.DMA((3,))],
        compiler_params=params(58 << 20),
        cost_estimate=cost(0, 6 * gate.size),
        name="half_weights",
    )(gate, up, down)


def both_halves_kernel(own_ref, other_ref, *out_refs):
    rows = own_ref.shape[1]
    core = lax.rem(lax.axis_index("dp"), 2)
    for ref, which in ((own_ref, core), (other_ref, 1 - core)):
        start = pl.multiple_of(which * rows, 16)
        for k, out in enumerate(out_refs):
            out[pl.ds(start, rows), :] = ref[k]


def both_halves(own, other):
    count, rows, width = own.shape
    return pl.pallas_call(
        both_halves_kernel,
        in_specs=[whole()] * 2,
        out_specs=[whole()] * count,
        out_shape=[jax.ShapeDtypeStruct((2 * rows, width), BF)] * count,
        compiler_params=params(),
        cost_estimate=cost(0, 4 * own.size),
        name="both_halves",
    )(own, other)


def hidden_part(nt, cot, gw, uw, dw):
    gate = dot(nt, gw)
    upper = dot(nt, uw)
    back_act = dot_cols(cot, dw)
    square = gate * gate
    th = jnp.tanh(SQRT_2_PI * (gate + CUBIC * square * gate))
    half = 0.5 * (1.0 + th)
    gelu = gate * half
    slope = half + 0.5 * gate * (1.0 - th * th) * (SQRT_2_PI * (1.0 + 3.0 * CUBIC * square))
    act = (gelu * upper).astype(BF)
    return act, (back_act * upper * slope).astype(BF), (back_act * gelu).astype(BF)


def rows_of(cot_ref, which, share):
    return cot_ref[pl.ds(pl.multiple_of(which * share, 16), share), :]


def ffn_kernel(shift, n, nt_ref, cot_ref, *refs):
    w_refs, (bn_ref, out_ref, act_ref, bg_ref, bu_ref) = refs[:6], refs[6:]
    nt = nt_ref[...]
    cot = rows_of(cot_ref, lax.rem(lax.axis_index("mp") + shift, n), nt.shape[0])
    bn, out = 0.0, 0.0
    for k in range(2):
        gw, uw, dw = (ref[...] for ref in w_refs[3 * k : 3 * k + 3])
        act, bg, bu = hidden_part(nt, cot, gw, uw, dw)
        bn = bn + dot_cols(bg, gw) + dot_cols(bu, uw)
        out = out + dot(act, dw)
        if k == 0:
            act_ref[...] = act
            bg_ref[...] = bg
            bu_ref[...] = bu
    bn_ref[...] = bn.astype(BF)
    out_ref[...] = out.astype(BF)


def feed_forward(shift, n, nt, cot, own, other):
    share, width = nt.shape
    hid = own[0].shape[1]
    return pl.pallas_call(
        functools.partial(ffn_kernel, shift, n),
        in_specs=[whole()] * 8,
        out_specs=[whole()] * 5,
        out_shape=[jax.ShapeDtypeStruct((share, width), BF)] * 2
        + [jax.ShapeDtypeStruct((share, hid), BF)] * 3,
        compiler_params=params(),
        cost_estimate=cost(24 * share * width * hid, 2 * (6 * width * hid + 6 * share * width)),
        name="feed_forward",
    )(nt, cot, *own, *other)


def hidden_kernel(shift, n, nt_ref, cot_ref, gw_ref, uw_ref, dw_ref, act_ref, bg_ref, bu_ref):
    nt = nt_ref[...]
    which = lax.rem((lax.axis_index("mp") ^ 1) + shift, n)
    cot = rows_of(cot_ref, which, nt.shape[0])
    act_ref[...], bg_ref[...], bu_ref[...] = hidden_part(
        nt, cot, gw_ref[...], uw_ref[...], dw_ref[...]
    )


def hidden_rows(shift, n, nt, cot, own):
    share, width = nt.shape
    hid = own[0].shape[1]
    return pl.pallas_call(
        functools.partial(hidden_kernel, shift, n),
        in_specs=[whole()] * 5,
        out_specs=[whole()] * 3,
        out_shape=[jax.ShapeDtypeStruct((share, hid), BF)] * 3,
        compiler_params=params(),
        cost_estimate=cost(6 * share * width * hid, 2 * (3 * width * hid + 6 * share * width)),
        name="hidden_rows",
    )(nt, cot, *own)


def ffn_grad_kernel(n, share, groups, cot_ref, *refs):
    nt_refs, act_refs, bg_refs, bu_refs = (refs[i * n : (i + 1) * n] for i in range(4))
    grad_refs = refs[4 * n :]
    m = lax.axis_index("mp")
    nt = jnp.concatenate([ref[...] for ref in nt_refs], axis=0)
    act = jnp.concatenate([ref[...] for ref in act_refs], axis=0)
    bg = jnp.concatenate([ref[...] for ref in bg_refs], axis=0)
    bu = jnp.concatenate([ref[...] for ref in bu_refs], axis=0)
    cot = jnp.concatenate(
        [
            rows_of(cot_ref, lax.rem(first + shift, n), share)
            for first in (m, m ^ 1)
            for shift in range(0, n, 2)
        ],
        axis=0,
    )
    nt_t = nt.T
    grads = (dot(nt_t, bg), dot(nt_t, bu), dot(act.T, cot))
    if not groups:
        for ref, grad in zip(grad_refs, grads):
            ref[...] = grad.astype(BF)
        return
    keep_ref, send_ref, scr = grad_refs
    for i in range(3):
        scr[i] = grads[i].astype(BF)
    rows = scr.shape[1] // (2 * groups)
    d = lax.axis_index("dp")
    core = lax.rem(d, 2)
    for r in range(groups):
        chip = ((d // 2) ^ r) * 2
        for i in range(3):
            mine = pl.multiple_of((chip + core) * rows, 16)
            other = pl.multiple_of((chip + 1 - core) * rows, 16)
            at = (3 * r + i) * rows
            keep_ref[at : at + rows, :] = scr[i, pl.ds(mine, rows), :]
            send_ref[at : at + rows, :] = scr[i, pl.ds(other, rows), :]


def ffn_grads(cot, nts, acts, bgs, bus, groups):
    n = len(nts)
    share, width = nts[0].shape
    hid = acts[0].shape[1]
    length = cot.shape[0]
    scratch = []
    if groups:
        out_shape = [jax.ShapeDtypeStruct((3 * width // 2, width), BF)] * 2
        scratch = [pltpu.VMEM((3, width, width), BF)]
    else:
        out_shape = [
            jax.ShapeDtypeStruct((width, hid), BF),
            jax.ShapeDtypeStruct((width, hid), BF),
            jax.ShapeDtypeStruct((hid, width), BF),
        ]
    args = [cot, *nts, *acts, *bgs, *bus]
    return pl.pallas_call(
        functools.partial(ffn_grad_kernel, n, share, groups),
        in_specs=[whole()] * len(args),
        out_specs=[whole()] * len(out_shape),
        out_shape=out_shape,
        scratch_shapes=scratch,
        compiler_params=params(),
        cost_estimate=cost(6 * length * width * hid, 12 * length * width),
        name="ffn_grads",
    )(*args)


def mid_kernel(n, share, mp, len_ref, hid_ref, cot_ref, gain_ref, *refs):
    bn_refs, (bh_ref, b_ref, gg_ref) = refs[:n], refs[n:]
    m = lax.axis_index("mp")
    bn = bn_refs[0][...].astype(F32)
    for ref in bn_refs[1:]:
        bn = bn + ref[...].astype(F32)
    hidden = hid_ref[...]
    r2 = lax.rsqrt(jnp.mean(hidden * hidden, axis=-1, keepdims=True) + EPS)
    pos = mp * lax.broadcasted_iota(jnp.int32, (share, 1), 0) + m
    bn = bn * (pos < len_ref[0]).astype(F32)
    z = hidden * r2
    gg_ref[...] = jnp.broadcast_to(jnp.sum(bn * z, axis=0, keepdims=True), gg_ref.shape)
    q = bn * gain_ref[1:2, :]
    start = pl.multiple_of(m * share, 16)
    dout = cot_ref[pl.ds(start, share), :].astype(F32)
    back = dout + r2 * (q - z * jnp.mean(q * z, axis=-1, keepdims=True))
    bh_ref[...] = back
    b_ref[...] = back.astype(BF)


def mid_norm(lengths, hidden, cot, gain, pieces):
    share, width = hidden.shape
    n = len(pieces)
    return pl.pallas_call(
        functools.partial(mid_kernel, n, share, cot.shape[0] // share),
        in_specs=[smem()] + [whole()] * (3 + n),
        out_specs=[whole()] * 3,
        out_shape=[
            jax.ShapeDtypeStruct(hidden.shape, F32),
            jax.ShapeDtypeStruct(hidden.shape, BF),
            jax.ShapeDtypeStruct((8, width), F32),
        ],
        compiler_params=params(),
        cost_estimate=cost(20 * hidden.size, 20 * hidden.size),
        name="second_norm_back",
    )(lengths, hidden, cot, gain, *pieces)


def unmix_kernel(
    kb, n, len_ref, taps_ref, x_ref, bh_ref, gg_ref, gain_ref, stu_hbm, ar_hbm, *refs
):
    b_refs, (ig_ref, gain_out) = refs[:n], refs[n : n + 2]
    ta_ref, tb_ref, tc_ref, td_ref, b_scr, lag_ref, acc_ref, scr = refs[n + 2 : n + 10]
    w_buf, ar_ref, sems, ar_sem = refs[n + 10 :]
    j, steps = pl.program_id(0), pl.num_programs(0)
    share, width = bh_ref.shape
    half, step = n * share // 2, n // 2
    m = lax.axis_index("mp")
    shift, is_odd = m // 2, lax.rem(m, 2)
    depth = tc_ref.shape[1]
    start = half - depth
    first = ta_ref.shape[0] // kb
    rest = share - first
    row = lax.broadcasted_iota(jnp.int32, (share, half), 0) * step + shift
    col = lax.broadcasted_iota(jnp.int32, (share, half), 1)
    above, upto = col >= row + is_odd, col >= row
    slot, wait = fetch_matrices(j, stu_hbm.shape[0] // (2 * kb), kb, stu_hbm, w_buf, sems)

    @pl.when(j == 0)
    def _():
        for r in range(n):
            c = lax.rem(m + r, n)
            value = b_refs[r][...].astype(F32)
            put_every_nth(scr.at[lax.rem(c, 2)], value, c // 2, step)
            if r < lag_ref.shape[1] // width:
                moved = pltpu.roll(value, share - 1, 0)
                last = lax.broadcasted_iota(jnp.int32, (share, 1), 0) == share - 1
                moved = jnp.where(last, 0.0, moved)
                value = jnp.where(m + r >= n, moved, value)
                lag_ref[:, r * width : (r + 1) * width] = value.astype(BF)
        for odd in range(2):
            b_scr[odd] = columns_of(scr.at[odd], half).astype(BF)
        acc_ref[...] = jnp.zeros((share, width), F32)

    for k in range(kb):
        for which, valid, full, short in ((2, above, ta_ref, tc_ref), (3, upto, tb_ref, td_ref)):
            base = taps_ref[which, pl.ds(j * kb + k, 1), :]
            t = toeplitz(base, first, 0, step)
            full[k * first : (k + 1) * first, :] = jnp.where(valid[:first], t, 0.0).astype(BF)
            t = toeplitz(base, rest, step * first, step)
            t = jnp.where(valid[first:], t, 0.0).astype(BF)
            short[k * rest : (k + 1) * rest, :] = t[:, start:]
    ca, cb = dot(ta_ref[...], b_scr[0]), dot(tb_ref[...], b_scr[1])
    cc, cd = dot(tc_ref[...], b_scr[0, start:]), dot(td_ref[...], b_scr[1, start:])
    sign = jnp.where(is_odd == 0, 1.0, -1.0)
    wait()
    total = acc_ref[...]
    for k in range(kb):
        upper, lower = slice(k * first, (k + 1) * first), slice(k * rest, (k + 1) * rest)
        pa = jnp.concatenate([ca[upper], cc[lower]], axis=0)
        pb = jnp.concatenate([cb[upper], cd[lower]], axis=0)
        total = total + dot_cols((pa + pb).astype(BF), w_buf[slot, 0, k])
        total = total + dot_cols(((pa - pb) * sign).astype(BF), w_buf[slot, 1, k])
    acc_ref[...] = total
    fetch_last(j, steps, ar_hbm, ar_ref, ar_sem)

    @pl.when(j == steps - 1)
    def _():
        total = acc_ref[...]
        for lag in range(ar_ref.shape[0]):
            total = total + dot_cols(lag_ref[:, lag * width : (lag + 1) * width], ar_ref[lag])
        x = x_ref[...]
        r1 = lax.rsqrt(jnp.mean(x * x, axis=-1, keepdims=True) + EPS)
        pos = n * lax.broadcasted_iota(jnp.int32, (share, 1), 0) + m
        masked = total * (pos < len_ref[0]).astype(F32)
        y = x * r1
        p = masked * gain_ref[0:1, :]
        ig = bh_ref[...] + r1 * (p - y * jnp.mean(p * y, axis=-1, keepdims=True))
        ig_ref[...] = ig.astype(BF)
        gain_out[0:8, :] = jnp.broadcast_to(jnp.sum(masked * y, axis=0, keepdims=True), (8, width))
        gain_out[8:16, :] = gg_ref[...]


def spectral_unmix(lengths, taps, x, back_hidden, gg, gains, stu, ar, pieces, kb):
    share, width = back_hidden.shape
    n = len(pieces)
    half = n * share // 2
    count = taps.shape[1]
    depth = min(256, half)
    first = (half - depth) // (n // 2)
    return pl.pallas_call(
        functools.partial(unmix_kernel, kb, n),
        grid=(count // kb,),
        in_specs=[smem()] + [whole()] * 5 + [outside()] * 2 + [whole()] * n,
        out_specs=[whole()] * 2,
        out_shape=[
            jax.ShapeDtypeStruct((share, width), BF),
            jax.ShapeDtypeStruct((16, width), F32),
        ],
        scratch_shapes=[pltpu.VMEM((kb * first, half), BF)] * 2
        + [pltpu.VMEM((kb * (share - first), depth), BF)] * 2
        + [
            pltpu.VMEM((2, half, width), BF),
            pltpu.VMEM((share, ar.shape[0] * width), BF),
            pltpu.VMEM((share, width), F32),
            pltpu.VMEM((2, width // 128, half + 8, 128), F32),
        ]
        + matrix_scratch(kb, ar),
        compiler_params=params(30 << 20),
        cost_estimate=cost(4 * count * share * width * (half + width), 2 * stu.size),
        name="spectral_unmix",
    )(lengths, taps, x, back_hidden, gg, gains, stu, ar, *pieces)


def conv_kernel(groups, tile, own, first, filt_ref, *refs):
    ut_refs, (conv_ref, tt_ref, ut_scr) = refs[:groups], refs[groups:]
    j = pl.program_id(0)
    filt, length = filt_ref.shape
    block = conv_ref.shape[1]
    count = length // tile
    chip = lax.axis_index("dp") // 2

    @pl.when(j == 0)
    def _():
        start = pl.multiple_of(chip * block, 16)
        for r in range(groups):
            ut_scr[r * block : (r + 1) * block, :] = ut_refs[r][pl.ds(start, block), :]

    which = lax.axis_index("mp") * own + first + j
    strip = toeplitz(filt_ref[pl.ds(lax.rem(which, filt), 1), :], tile)
    row = lax.broadcasted_iota(jnp.int32, (tile, length), 0)
    col = lax.broadcasted_iota(jnp.int32, (tile, length), 1)
    flip = ((col - row) % 2 == 1) & (which >= filt)
    strip = jnp.where(col >= row, jnp.where(flip, -strip, strip), 0.0).astype(BF)
    for b in range(count):
        tt_ref[b * tile : (b + 1) * tile, b * tile :] = strip[:, : length - b * tile]
    for c in range(count):
        end = (c + 1) * tile
        part = dot(ut_scr[:, :end], tt_ref[:end, c * tile : end]).astype(BF)
        for r in range(groups):
            start = pl.multiple_of((lax.rem(chip, groups) ^ r) * length + c * tile, 128)
            conv_ref[0, :, pl.ds(start, tile)] = part[r * block : (r + 1) * block, :]


def convolutions(filt, uts, own, chips, first, last):
    length = filt.shape[1]
    groups = len(uts)
    block = uts[0].shape[0] // chips
    tile = 256 if length % 256 == 0 else length
    return pl.pallas_call(
        functools.partial(conv_kernel, groups, tile, own, first),
        grid=(last - first,),
        in_specs=[whole()] * (1 + groups),
        out_specs=pl.BlockSpec((1, block, groups * length), lambda j: (j, 0, 0)),
        out_shape=jax.ShapeDtypeStruct((last - first, block, groups * length), BF),
        scratch_shapes=[
            pltpu.VMEM((length, length), BF),
            pltpu.VMEM((groups * block, length), BF),
        ],
        compiler_params=params(),
        cost_estimate=cost(0, 0),
        name="convolutions",
    )(filt, *uts)


def lag_kernel(groups, *refs):
    ut_refs, out_refs = refs[:groups], refs[groups:]
    width, length = ut_refs[0].shape
    chip = lax.rem(lax.axis_index("dp") // 2, groups)
    col = lax.broadcasted_iota(jnp.int32, (width, length), 1)
    for r in range(groups):
        start = pl.multiple_of((chip ^ r) * length, 128)
        out_refs[0][:, pl.ds(start, length)] = ut_refs[r][:width, :]
        value = ut_refs[r][:width, :].astype(F32)
        for lag in range(1, len(out_refs)):
            moved = pltpu.roll(value, lag, 1)
            out_refs[lag][:, pl.ds(start, length)] = jnp.where(col >= lag, moved, 0.0).astype(BF)


def lagged(uts, order):
    groups = len(uts)
    width, length = uts[0].shape
    shape = jax.ShapeDtypeStruct((width, groups * length), BF)
    return pl.pallas_call(
        functools.partial(lag_kernel, groups),
        in_specs=[whole()] * groups,
        out_specs=[whole()] * order,
        out_shape=[shape] * order,
        compiler_params=params(),
        cost_estimate=cost(0, 0),
        name="lagged",
    )(*uts)


def grads_kernel(steps, order, groups, rows, conv_ref, conv_two_ref, *refs):
    lag_refs, b_refs = refs[:order], refs[order : order + len(rows)]
    keep_ref, send_ref, b_scr, scr = refs[order + len(rows) :]
    g = pl.program_id(0)
    d = lax.axis_index("dp")
    chip, core = lax.rem(d // 2, groups), lax.rem(d, 2)
    step, block, depth = conv_ref.shape
    width, length = b_scr.shape[1], depth // groups
    half = block // 2

    @pl.when(g == 0)
    def _():
        for ref, (r, at, size) in zip(b_refs, rows):
            start = pl.multiple_of((chip ^ r) * length + at, 16)
            b_scr[pl.ds(start, size), :] = ref[:size, :]

    for k, ref in enumerate((conv_ref, conv_two_ref)):

        @pl.when((g >= k * steps // 2) & (g < (k + 1) * steps // 2))
        def _():
            part = dot(ref[...].reshape(step * block, depth), b_scr[...])
            scr[...] = part.reshape(step, block, width)

    @pl.when(g < steps)
    def _():
        mine = pl.multiple_of(core * half, 16)
        other = pl.multiple_of((1 - core) * half, 16)
        keep_ref[pl.ds(g * step, step)] = scr[:, pl.ds(mine, half), :]
        for k in range(step):
            start = pl.multiple_of((g * step + k) * half, 16)
            send_ref[pl.ds(start, half), :] = scr[k, pl.ds(other, half), :].astype(BF)

    for lag in range(order):

        @pl.when(g == steps + lag)
        def _():
            at = steps * step * half + lag * width
            send_ref[at : at + width, :] = dot(lag_refs[lag][...], b_scr[...]).astype(BF)


def matrix_grads(convs, lags, backs, rows):
    part, block, depth = convs[0].shape
    own = 2 * part
    order, width = len(lags), lags[0].shape[0]
    groups = 1 + max(r for r, _, _ in rows)
    step = next(s for s in (3, 2, 1) if part % s == 0)
    steps = own // step
    half = block // 2
    return pl.pallas_call(
        functools.partial(grads_kernel, steps, order, groups, rows),
        grid=(steps + order,),
        in_specs=[
            pl.BlockSpec((step, block, depth), lambda g: (jnp.minimum(g, steps // 2 - 1), 0, 0)),
            pl.BlockSpec(
                (step, block, depth), lambda g: (jnp.clip(g - steps // 2, 0, steps // 2 - 1), 0, 0)
            ),
        ]
        + [whole()] * (order + len(backs)),
        out_specs=[whole()] * 2,
        out_shape=[
            jax.ShapeDtypeStruct((own, half, width), F32),
            jax.ShapeDtypeStruct((own * half + order * width, width), BF),
        ],
        scratch_shapes=[
            pltpu.VMEM((depth, width), BF),
            pltpu.VMEM((step, block, width), F32),
        ],
        compiler_params=params(),
        cost_estimate=cost(0, 0),
        name="matrix_grads",
    )(*convs, *lags, *backs)


def rows_message_kernel(ig_ref, hid_ref, *refs):
    share = ig_ref.shape[0]
    total = hid_ref[...]
    for ref in refs[:-1]:
        total = total + ref[...].astype(F32)
    refs[-1][:share, :] = ig_ref[...]
    refs[-1][share:, :] = total.astype(BF)


def rows_message(ig, hidden, pieces):
    share, width = ig.shape
    return pl.pallas_call(
        rows_message_kernel,
        in_specs=[whole()] * (2 + len(pieces)),
        out_specs=whole(),
        out_shape=jax.ShapeDtypeStruct((2 * share, width), BF),
        compiler_params=params(),
        cost_estimate=cost(4 * ig.size, 10 * ig.size),
        name="rows_message",
    )(ig, hidden, *pieces)


def finish_rows_kernel(n, share, at, *refs):
    pieces, (out_ref, scr) = refs[:n], refs[n:]
    m = lax.axis_index("mp")
    for r in range(n):
        value = pieces[r][at : at + share, :].astype(F32)
        put_every_nth(scr, value, lax.rem(m + r, n), n)
    out_ref[...] = columns_of(scr, n * share).astype(out_ref.dtype)


def finish_rows(pieces, at, dtype, weight):
    n = len(pieces)
    share, width = pieces[0].shape[0] // 2, pieces[0].shape[1]
    return pl.pallas_call(
        functools.partial(finish_rows_kernel, n, share, at),
        in_specs=[whole()] * n,
        out_specs=whole(),
        out_shape=jax.ShapeDtypeStruct((n * share, width), dtype),
        scratch_shapes=[pltpu.VMEM((width // 128, n * share + 16, 128), F32)],
        compiler_params=params(),
        cost_estimate=cost(weight, weight),
        name="finish_rows",
    )(*pieces)


def ordered_sum_kernel(n, axis, step, *refs):
    pieces, (out_ref, scr) = refs[:n], refs[n:]
    me = lax.axis_index(axis)
    for r in range(n):
        who = lax.rem(me + r, n) if step == 0 else (me // step) ^ r
        scr[who] = pieces[r][...]
    total = scr[0]
    for r in range(1, n):
        total = total + scr[r]
    out_ref[...] = total


def ordered_sum(pieces, axis, step):
    n = len(pieces)
    shape = pieces[0].shape
    return pl.pallas_call(
        functools.partial(ordered_sum_kernel, n, axis, step),
        in_specs=[whole()] * n,
        out_specs=whole(),
        out_shape=jax.ShapeDtypeStruct(shape, F32),
        scratch_shapes=[pltpu.VMEM((n,) + shape, F32)],
        compiler_params=params(),
        cost_estimate=cost(n * pieces[0].size, 4 * n * pieces[0].size),
        name="ordered_sum",
    )(*pieces)


def gains_sum_kernel(n, *refs):
    pieces, (first_ref, second_ref, scr) = refs[:n], refs[n:]
    me = lax.axis_index("mp")
    for r in range(n):
        scr[lax.rem(me + r, n)] = pieces[r][...]
    total = scr[0]
    for r in range(1, n):
        total = total + scr[r]
    first_ref[...] = total[0]
    second_ref[...] = total[8]


def gains_sum(pieces):
    n = len(pieces)
    shape = pieces[0].shape
    return pl.pallas_call(
        functools.partial(gains_sum_kernel, n),
        in_specs=[whole()] * n,
        out_specs=[whole()] * 2,
        out_shape=[jax.ShapeDtypeStruct(shape[1:], F32)] * 2,
        scratch_shapes=[pltpu.VMEM((n,) + shape, F32)],
        compiler_params=params(),
        cost_estimate=cost(n * pieces[0].size, 4 * n * pieces[0].size),
        name="gains_sum",
    )(*pieces)


def cores_sum_kernel(keep_ref, recv_ref, upper_ref, lower_ref):
    total = (keep_ref[...].astype(F32) + recv_ref[...].astype(F32)).astype(BF)
    half = total.shape[0] // 8
    for r in range(4):
        at = 2 * r * half
        upper_ref[r * half : (r + 1) * half, :] = total[at : at + half]
        lower_ref[r * half : (r + 1) * half, :] = total[at + half : at + 2 * half]


def cores_sum(keep, recv):
    size, width = keep.shape
    return pl.pallas_call(
        cores_sum_kernel,
        in_specs=[whole()] * 2,
        out_specs=[whole()] * 2,
        out_shape=[jax.ShapeDtypeStruct((size // 2, width), BF)] * 2,
        compiler_params=params(),
        cost_estimate=cost(keep.size, 8 * keep.size),
        name="cores_sum",
    )(keep, recv)


def pack_kernel(n, share, *refs):
    pieces, (out_ref, scr) = refs[:n], refs[n:]
    m = lax.axis_index("mp")
    for r in range(n):
        put_every_nth(scr, pieces[r][...].astype(F32), lax.rem(m + r, n), n)
    out_ref[...] = columns_of(scr, n * share).astype(BF)


def pack_rows(pieces):
    n = len(pieces)
    share, width = pieces[0].shape
    return pl.pallas_call(
        functools.partial(pack_kernel, n, share),
        in_specs=[whole()] * n,
        out_specs=whole(),
        out_shape=jax.ShapeDtypeStruct((n * share, width), BF),
        scratch_shapes=[pltpu.VMEM((width // 128, n * share + 16, 128), F32)],
        compiler_params=params(),
        cost_estimate=cost(n * share * width, 6 * n * share * width),
        name="pack_rows",
    )(*pieces)


def turn_kernel(x_ref, y_ref, upper_ref, lower_ref, gain_ref, to_y, to_x):
    half, size = x_ref.shape[0] // 2, upper_ref.shape[0]
    gains = split_gains(gain_ref[...])
    for ref, rows, w_ref in ((to_y, x_ref[:half, :], lower_ref), (to_x, y_ref[half:, :], upper_ref)):
        ref[:half, :] = rows
        ref[half : half + size, :] = w_ref[...]
        ref[half + size :, :] = gains


def turn(over_x, over_y, upper, lower, gains):
    rows = over_x.shape[0] // 2 + upper.shape[0] + 32
    return pl.pallas_call(
        turn_kernel,
        in_specs=[whole()] * 5,
        out_specs=[whole()] * 2,
        out_shape=[jax.ShapeDtypeStruct((rows, over_x.shape[1]), BF)] * 2,
        compiler_params=params(),
        cost_estimate=cost(over_x.size, 8 * over_x.size),
        name="turn",
    )(over_x, over_y, upper, lower, gains)


def half_sums_kernel(upper_ref, lower_ref, from_y, from_x, to_y, to_x):
    size = to_y.shape[0]
    half = size // 4
    at = from_y.shape[0] - 32 - size
    for ref, own, came, bits in ((to_y, upper_ref, from_x, 1), (to_x, lower_ref, from_y, 2)):
        for r in range(4):
            there = at + (r ^ bits) * half
            ref[r * half : (r + 1) * half, :] = (
                own[r * half : (r + 1) * half, :].astype(F32)
                + came[there : there + half, :].astype(F32)
            ).astype(BF)
    to_x[size:, :] = from_y[at + size :, :]


def half_sums(upper, lower, from_y, from_x):
    size, width = upper.shape
    return pl.pallas_call(
        half_sums_kernel,
        in_specs=[whole()] * 4,
        out_specs=[whole()] * 2,
        out_shape=[jax.ShapeDtypeStruct((rows, width), BF) for rows in (size, size + 32)],
        compiler_params=params(),
        cost_estimate=cost(upper.size, 8 * upper.size),
        name="half_sums",
    )(upper, lower, from_y, from_x)


def chunks_kernel(upper_ref, from_y, lower_ref, from_x, more_ref, out_ref):
    half = upper_ref.shape[0] // 4
    for own, came, bits, lower in ((upper_ref, from_y, 2, 0), (lower_ref, from_x, 1, 1)):
        for r in range(4):
            at, there = (2 * r + lower) * half, (r ^ bits) * half
            out_ref[at : at + half, :] = (
                own[r * half : (r + 1) * half, :].astype(F32)
                + came[there : there + half, :].astype(F32)
            ).astype(BF)
    out_ref[8 * half :, :] = more_ref[...]


def whole_chunks(upper, from_y, lower, from_x, more):
    size, width = upper.shape
    return pl.pallas_call(
        chunks_kernel,
        in_specs=[whole()] * 5,
        out_specs=whole(),
        out_shape=jax.ShapeDtypeStruct((2 * size + more.shape[0], width), BF),
        compiler_params=params(),
        cost_estimate=cost(upper.size, 8 * upper.size),
        name="whole_chunks",
    )(upper, from_y, lower, from_x, more)


def split_gains(both):
    high = both.astype(BF)
    low = (both - high.astype(F32)).astype(BF)
    return jnp.concatenate([high, low], axis=0)


def joined(gains):
    return gains[:16].astype(F32) + gains[16:].astype(F32)


def chips_sum_kernel(gain_ref, from_x, from_y, recv_ref, out_ref, scr):
    chip = lax.axis_index("dp") // 2
    scr[chip] = joined(split_gains(gain_ref[...]))
    for ref, bits in ((from_x, 1), (from_y, 2), (recv_ref, 3)):
        scr[chip ^ bits] = joined(ref[ref.shape[0] - 32 :, :])
    out_ref[...] = ((scr[0] + scr[1]) + scr[2]) + scr[3]


def chips_sum(gains, from_x, from_y, recv):
    return pl.pallas_call(
        chips_sum_kernel,
        in_specs=[whole()] * 4,
        out_specs=whole(),
        out_shape=jax.ShapeDtypeStruct(gains.shape, F32),
        scratch_shapes=[pltpu.VMEM((4,) + gains.shape, F32)],
        compiler_params=params(),
        cost_estimate=cost(4 * gains.size, 16 * gains.size),
        name="chips_sum",
    )(gains, from_x, from_y, recv)


def finish_kernel(custom, keep_ref, send_ref, recv_ref, stu_ref, ar_ref, *w_refs):
    own, half, width = keep_ref.shape
    base = 0
    if custom:
        d = lax.axis_index("dp")
        core = lax.rem(d, 2)
        rows = width // 8
        base = 12 * rows
        for r in range(4):
            chip = ((d // 2) ^ r) * 2
            for ref, which in ((send_ref, chip + core), (recv_ref, chip + 1 - core)):
                start = pl.multiple_of(which * rows, 16)
                for i, out in enumerate(w_refs):
                    at = (3 * r + i) * rows
                    out[pl.ds(start, rows), :] = ref[at : at + rows, :].astype(F32)
    for k in range(own):
        at = base + k * half
        stu_ref[k] = keep_ref[k] + recv_ref[at : at + half, :].astype(F32)
    for i in range(ar_ref.shape[0]):
        at = base + own * half + i * width
        ar_ref[i] = send_ref[at : at + width, :].astype(F32) + recv_ref[
            at : at + width, :
        ].astype(F32)


def finish(keep, send, recv, order, custom):
    width = keep.shape[2]
    more = [jax.ShapeDtypeStruct((width, width), F32)] * (3 if custom else 0)
    return pl.pallas_call(
        functools.partial(finish_kernel, custom),
        in_specs=[whole()] * 3,
        out_specs=[whole()] * (2 + len(more)),
        out_shape=[
            jax.ShapeDtypeStruct(keep.shape, F32),
            jax.ShapeDtypeStruct((order, width, width), F32),
        ]
        + more,
        compiler_params=params(),
        cost_estimate=cost(keep.size, 10 * keep.size),
        name="finish",
    )(keep, send, recv)


def fetch_shifted(value, axis, n, step=1):
    pieces = {0: value}
    for r in sorted(range(step, n, step), key=lambda r: min(r, n - r)):
        pieces[r] = lax.ppermute(value, axis, [(i, (i - r) % n) for i in range(n)])
    return [pieces[r] for r in range(0, n, step)]


def send_shifted(pieces, axis, n, step):
    moved = {0: pieces[0]}
    for r in sorted(range(step, n, step), key=lambda r: min(r, n - r)):
        moved[r] = lax.ppermute(pieces[r // step], axis, [(i, (i + r) % n) for i in range(n)])
    return [moved[r] for r in range(0, n, step)]


def swap(value, axis, n, bits):
    return lax.ppermute(value, axis, [(i, i ^ bits) for i in range(n)])


def swap_sum(value, n):
    return ordered_sum([value, swap(value, "dp", n, 1)], "dp", 0)


def after(values, first):
    flat, tree = jax.tree.flatten(values)
    out = lax.optimization_barrier((*flat, *jax.tree.leaves(first)))
    return jax.tree.unflatten(tree, out[: len(flat)])


def shards(
    inputs, lengths, filters, first_gain, stu_weight, ar_weight, second_gain,
    gate_weight, up_weight, down_weight, cotangent,
):
    n = lax.axis_size("mp")
    n_dp = lax.axis_size("dp")
    groups = n_dp // 2
    length, width = inputs.shape
    share = length // n
    order = ar_weight.shape[0]
    own = stu_weight.shape[0] // n
    lengths = lengths.astype(jnp.int32)
    both_gains = jnp.stack([first_gain, second_gain])

    own_w = (gate_weight, up_weight, down_weight)
    custom = n_dp == 8 and gate_weight.shape[1] == width
    if custom:
        half_w = half_weights(*own_w)
        both_gains = after(both_gains, half_w)
        half_w = swap(half_w, "mp", n, 1)
    u, ut, ut_two, x_own, u_lags, taps, natural = first_norm(
        lengths, inputs, both_gains, filters.T, n, order
    )
    uts = [ut, swap(ut, "dp", n_dp, 2), swap(ut_two, "dp", n_dp, 4)]
    hidden, nt = spectral_mix(
        lengths, taps, x_own, u, u_lags, both_gains, stu_weight, ar_weight, n, 8
    )
    cotangent = dealt_rows(cotangent, n)
    nts = fetch_shifted(nt, "mp", n, 2)
    others = [swap(piece, "mp", n, 1) for piece in nts]
    if custom:
        other_w = both_halves(half_w, swap(after(half_w, nt), "dp", n_dp, 1))
    else:
        other_w = [swap(w, "mp", n, 1) for w in own_w]
    parts = [feed_forward(0, n, after(nt, uts[1:3]), cotangent, own_w, other_w)]
    for k in range(1, n // 2):
        piece = after(nts[k], parts[-1][0])
        parts.append(feed_forward(2 * k, n, piece, cotangent, own_w, other_w))
    uts += [swap(after(ut, nt), "dp", n_dp, 2 * r) for r in range(3, groups)]
    bns = send_shifted([p[0] for p in parts], "mp", n, 2)
    out_parts = [p[1] for p in parts]
    bns[1:] = after(bns[1:], uts)
    back_hidden, back_rows, second_part = mid_norm(lengths, hidden, cotangent, both_gains, bns)
    backs = fetch_shifted(back_rows, "mp", n)
    more = [
        hidden_rows(2 * k, n, after(piece, back_rows), cotangent, own_w)
        for k, piece in enumerate(others)
    ]
    acts, bgs, bus = ([p[i + 2] for p in parts] + [p[i] for p in more] for i in range(3))
    grads = ffn_grads(cotangent, nts + others, acts, bgs, bus, groups if custom else 0)
    uts = after(uts, back_rows)
    fours = [uts[r : r + 4] for r in range(0, groups, 4)]
    lags = [lagged(some, order) for some in fours]
    conv = [convolutions(natural, some, own, groups, 0, own // 2) for some in fours]
    backs = after(backs, (lags, conv))
    own_back = pack_rows(backs)
    if custom:
        over_x, over_y = swap(own_back, "dp", n_dp, 2), swap(own_back, "dp", n_dp, 4)
        w_came = swap(after(grads[1], own_back), "dp", n_dp, 1)
    out_sums = send_shifted(after(out_parts, own_back), "mp", n, 2)
    ig, gains = spectral_unmix(
        lengths, taps, x_own, back_hidden, second_part, both_gains, stu_weight, ar_weight, backs, 8
    )
    uts, hidden = after((uts, hidden), ig)
    fours = [uts[r : r + 4] for r in range(0, groups, 4)]
    conv_two = [convolutions(natural, some, own, groups, own // 2, own) for some in fours]
    message = rows_message(ig, hidden, out_sums)
    messages = fetch_shifted(message, "mp", n)
    if custom:
        upper, lower = cores_sum(grads[0], after(w_came, message))
        to_y, to_x = turn(after(over_x, message), over_y, upper, lower, gains)
        from_y, from_x = swap(to_y, "dp", n_dp, 4), swap(to_x, "dp", n_dp, 2)
        all_backs = [own_back, over_x, over_y, from_y, from_x]
        half = length // 2
        rows = ((0, 0, length), (1, 0, length), (2, 0, length), (3, 0, half), (3, half, half))
        upper, lower = half_sums(after(upper, conv_two), lower, from_y, from_x)
        from_y_two, from_x_two = swap(upper, "dp", n_dp, 4), swap(lower, "dp", n_dp, 2)
        conv_two = after(conv_two, upper)
        gains_parts = (gains, from_x, from_y)
    else:
        all_backs = [own_back] + [swap(own_back, "dp", n_dp, 2 * r) for r in range(1, groups)]
        rows = tuple((r, 0, length) for r in range(min(groups, 4)))
        gains = ordered_sum([gains] + [swap(gains, "dp", n_dp, r) for r in range(1, n_dp)], "dp", 1)
    conv = after(list(zip(conv, conv_two)), message)
    if len(conv) == 1:
        keep, send = matrix_grads(conv[0], lags[0], all_backs, rows)
    else:
        some = [
            matrix_grads(c, lags[k], all_backs[4 * k : 4 * k + 4], rows)
            for k, c in enumerate(conv)
        ]
        keep = ordered_sum([k for k, _ in some], "dp", 8)
        send = ordered_sum([k.astype(F32) for _, k in some], "dp", 8).astype(BF)
    messages = after(messages, send)
    output = finish_rows(messages, share, BF, 1e9)
    input_grad = finish_rows(after(messages, output), 0, F32, 1e6)
    if custom:
        from_y_two, from_x_two = after((from_y_two, from_x_two), output)
        gains = chips_sum(*gains_parts, after(from_x_two, send))
        gains = [gains, after(swap(gains, "dp", n_dp, 1), input_grad)]
        gains = ordered_sum(gains, "dp", 0)
        send = whole_chunks(upper, from_y_two, lower, from_x_two, after(send, gains))
    gains = fetch_shifted(gains, "mp", n)
    recv = swap(send, "dp", n_dp, 1)
    stu_grad, ar_grad, *w_grads = finish(keep, send, recv, order, custom)
    first_grad, second_grad = gains_sum(after(gains, stu_grad))
    if custom:
        gate_grad, up_grad, down_grad = w_grads
    else:
        gate_grad, up_grad, down_grad = (g.astype(F32) for g in lax.psum(tuple(grads), "dp"))
    return (
        output, input_grad, stu_grad, ar_grad, first_grad, second_grad, gate_grad, up_grad, down_grad,
    )


def solution(mesh):
    in_specs = (
        P("dp", None), P("dp"), P(), P(), P(), P(), P(),
        P(None, "mp"), P(None, "mp"), P("mp", None), P("dp", None),
    )
    out_specs = (
        P("dp", None), P("dp", None), P("mp", "dp", None), P(), P(), P(),
        P(None, "mp"), P(None, "mp"), P("mp", None),
    )
    return jax.shard_map(shards, mesh=mesh, in_specs=in_specs, out_specs=out_specs, check_vma=False)
```
